32 devices in a mesh: dp: 8 (over z, y), mp: 4 (over x, core).
Axes of the slice: x: 2, y: 2, z: 4, core: 2. Of those that a mesh axis runs over, the one named last changes fastest.
Arguments:
- tokens: bfloat16 [8192, 768], P('dp'), may hold values from -12 to 12
- w_qkv: bfloat16 [3, 768, 768], P(None, 'dp', 'mp'), may hold values from -0.21875 to 0.21875
- w_out: bfloat16 [768, 768], P('mp', 'dp'), may hold values from -1.5 to 1.5
- w_up: bfloat16 [768, 3072], P('dp', 'mp'), may hold values from -0.21875 to 0.21875
- w_down: bfloat16 [3072, 768], P('mp', 'dp'), may hold values from -0.109375 to 0.109375
- b_qv: bfloat16 [2, 12, 64], P(None, 'mp', 'dp'), may hold values from -3 to 3
- b_up: bfloat16 [12, 256], P('mp', 'dp'), may hold values from -3 to 3
- vectors: bfloat16 [6, 768], P(None, 'dp'), may hold values from -1.2 to 1.4, as said below
- ema_ranges: float32 [4], replicated, may hold values from 1 to 4
- key_mask: int32 [8192], P('dp'), may hold values from 0 to 1, as said below
- long_rows: int32 [16], P('dp'), may hold values 0 or 1
- grad_out: bfloat16 [8192, 768], P(('dp', 'mp')), may hold values from -6 to 6
Outputs:
- layer_out: bfloat16 [8192, 768], P(('dp', 'mp'))
- grad_tokens: float32 [8192, 768], P('dp')
- grad_qkv: float32 [3, 768, 768], P(None, 'dp', 'mp')
- grad_wout: float32 [768, 768], P('mp', 'dp')
- grad_wup: float32 [768, 3072], P('dp', 'mp')
- grad_wdown: float32 [3072, 768], P('mp', 'dp')
- grad_bqv: float32 [2, 12, 64], P(None, 'mp', 'dp')
- grad_bup: float32 [12, 256], P('mp', 'dp')
- grad_vectors: float32 [6, 768], P(None, 'dp')
- new_ranges: float32 [4], replicated
The draws below stay inside these ranges and needn't reach their ends.
Inputs may be any that keep to these rules, and one draw needn't show every extreme that they name: `key_mask`: the first of every 128 positions is 1. `vectors`: rows 2 and 4 lie near 1.
All inputs are finite; a program needn't handle non-finite values. No bound on the sum of `long_rows` on one device may be relied on, other than what follows from the above.
Results may differ from the reference program's by a relative error of at most 0.014.
Values may be sent and summed in bfloat16 or wider, within the bound.
A program may use at most 128 MiB of HBM per device.

```python
import math
import jax
import jax.numpy as jnp
from jax import lax

D = 768
H = 12
HD = 64
FF = 3072
BLOCK = 512
SEG = 128
TOKENS = 8192
NBLOCKS = 16


def draw_tokens(key, part):
    key = jax.random.fold_in(key, 11)
    rising = 1.0 + 2.0 * jnp.arange(TOKENS, dtype=jnp.float32)[:, None] / TOKENS
    base = jnp.clip(jax.random.normal(key, (TOKENS, D), jnp.float32), -4.0, 4.0)
    return (base * rising).astype(jnp.bfloat16)


def draw_vectors(key, part):
    key = jax.random.fold_in(key, 12)
    noise = jnp.clip(jax.random.normal(key, (6, D), jnp.float32), -4.0, 4.0)
    row_ids = jnp.arange(6)
    gain_rows = (row_ids % 2 == 0) & (row_ids >= 2)
    return jnp.where(gain_rows[:, None], 1.0 + 0.1 * noise, 0.3 * noise).astype(jnp.bfloat16)


def draw_key_mask(key, part):
    key = jax.random.fold_in(key, 13)
    picks = jax.random.randint(key, (TOKENS,), 0, 8)
    leading = jnp.arange(TOKENS) % SEG == 0
    return jnp.where(leading | (picks < 7), 1, 0).astype(jnp.int32)


def touch_ends(values, key, least, top_value):
    longest = values.shape.index(max(values.shape))
    spots = []
    for shift in (0, 1):
        where = [jax.random.randint(jax.random.fold_in(key, axis), (), 0, length) for axis, length in enumerate(values.shape)]
        where[longest] = (where[longest] + shift) % values.shape[longest]
        spots.append(tuple(where))
    return values.at[spots[0]].set(least).at[spots[1]].set(top_value)


def block_scale(key, dims, cuts, low, largest):
    factor_of = 1.0
    for dim, shards_of in cuts:
        heights = jax.random.uniform(jax.random.fold_in(jax.random.fold_in(key, 6), dim), (shards_of,), jnp.float32, low / len(cuts), largest / len(cuts))
        factor_of = factor_of * jnp.repeat(jnp.exp(heights), dims[dim] // shards_of).reshape((-1,) + (1,) * (len(dims) - 1 - dim))
    return factor_of


def normal_values(stream_key, shape, scale, most, split=(), held_as=jnp.bfloat16):
    values = jax.random.normal(stream_key, shape, jnp.float32) * scale
    if len(split) > 0:
        values = block_scale(stream_key, shape, split, -0.22, 0.18) * values
    return jnp.clip(values, min=-most, max=most).astype(held_as)


def setup_inputs(seed: int = 0) -> dict:
    seeds = jax.random.split(jax.random.key(seed), 13)
    tokens = draw_tokens(jax.random.fold_in(seeds[12], 71), 0)
    w_qkv = normal_values(seeds[1], (3, D, D), D ** -0.5, 0.21875, ((1, 8), (2, 4)))
    w_out = normal_values(seeds[2], (D, D), (D // 48) ** -0.5, 1.5, ((0, 4), (1, 8)))
    w_up = normal_values(seeds[3], (D, FF), D ** -0.5, 0.21875, ((0, 8), (1, 4)))
    w_down = normal_values(seeds[4], (FF, D), FF ** -0.5, 0.109375, ((0, 4), (1, 8)))
    b_qv = normal_values(seeds[5], (2, H, HD), 0.5, 3.0, ((1, 4), (2, 8)))
    b_up = normal_values(seeds[6], (H, FF // H), 0.5, 3.0, ((0, 4), (1, 8)))
    vectors = draw_vectors(jax.random.fold_in(seeds[12], 71), 0)
    ema_ranges = jnp.clip(jnp.exp(jax.random.uniform(seeds[8], (4,), jnp.float32, math.log(1.0), math.log(4.0))), 1.0, 4.0)
    key_mask = draw_key_mask(jax.random.fold_in(seeds[12], 71), 0)
    long_rows = touch_ends((jax.random.randint(seeds[10], (NBLOCKS,), 0, 2) < 1).astype(jnp.int32), jax.random.fold_in(seeds[10], 1), 0, 1)
    grad_out = normal_values(seeds[11], (TOKENS, D), 1.0, 6.0, ((0, 32),))
    return {"tokens": tokens, "w_qkv": w_qkv, "w_out": w_out, "w_up": w_up, "w_down": w_down, "b_qv": b_qv, "b_up": b_up, "vectors": vectors, "ema_ranges": ema_ranges, "key_mask": key_mask, "long_rows": long_rows, "grad_out": grad_out}


@jax.custom_vjp
def low(v):
    return lax.optimization_barrier(v.astype(jnp.bfloat16)).astype(jnp.float32)

@jax.custom_vjp
def low_back(v):
    return v

def low_keep(v):
    return (low(v), None)

def low_pass(kept, grad):
    return (grad,)

def back_keep(v):
    return (v, None)

def back_low(kept, grad):
    return (low(grad),)
low.defvjp(low_keep, low_pass)
low_back.defvjp(back_keep, back_low)
eps_norm = 1e-12

def matmul(left, right):
    return jnp.dot(left, right, precision=lax.Precision.HIGHEST, preferred_element_type=jnp.float32)

def squash(values, limit):
    return limit * jnp.tanh(values / limit)

def layer_norm(values, gain, shift):
    center = values - lax.optimization_barrier(jnp.mean(values, axis=-1, keepdims=True))
    spread = lax.optimization_barrier(jnp.mean(center * center, axis=-1, keepdims=True))
    return center * lax.rsqrt(spread + eps_norm) * gain + shift

def attend(pieces):
    queries, keys_in, values, live, long_flag = pieces
    scores = low_back(jnp.einsum('qhd,khd->hqk', queries, keys_in, precision=lax.Precision.HIGHEST))
    places = jnp.arange(BLOCK) // SEG
    allowed = (live[None, :] > 0) & ((long_flag > 0) | (places[:, None] == places[None, :]))
    scores = jnp.where(allowed[None], scores, -1e+30)
    top_score = lax.optimization_barrier(jnp.max(scores, axis=-1, keepdims=True))
    weights = jnp.exp(scores - top_score)
    attn_probs = weights / lax.optimization_barrier(jnp.sum(weights, axis=-1, keepdims=True))
    return jnp.einsum('hqk,khd->qhd', low(attn_probs), values, precision=lax.Precision.HIGHEST)

def forward(tokens, w_qkv, w_out, w_up, w_down, b_qv, b_up, vectors, key_mask, long_rows, ranges, w_peaks):
    tok_quant = low(squash(tokens, ranges[0]))
    qkv_quant = low(squash(w_qkv, w_peaks[0]))
    queries = low(low_back((matmul(tok_quant, qkv_quant[0]) + b_qv[0].reshape(D)) * HD ** (-0.5)))
    keys_all = low(low_back(matmul(tok_quant, qkv_quant[1])))
    values = low(low_back(matmul(tok_quant, qkv_quant[2]) + b_qv[1].reshape(D)))
    blocks = TOKENS // BLOCK
    shape_four = (blocks, BLOCK, H, HD)
    context = lax.map(jax.checkpoint(attend), (queries.reshape(shape_four), keys_all.reshape(shape_four), values.reshape(shape_four), key_mask.reshape(blocks, BLOCK), long_rows))
    context = low_back(context.reshape(TOKENS, D))
    ctx_quant = low(squash(context, ranges[1]))
    attn = low_back(matmul(ctx_quant, low(squash(w_out, w_peaks[1]))) + vectors[0])
    first = tokens + attn
    normed = layer_norm(first, vectors[2], vectors[3])
    hid_quant = low(squash(normed, ranges[2]))
    hidden = low_back(matmul(hid_quant, low(squash(w_up, w_peaks[2]))) + b_up.reshape(FF))
    active = jax.nn.gelu(hidden, approximate=False)
    act_quant = low(squash(active, ranges[3]))
    branch = low_back(matmul(act_quant, low(squash(w_down, w_peaks[3]))) + vectors[1])
    result = layer_norm(first + branch, vectors[4], vectors[5])
    maxima = jnp.stack([jnp.max(jnp.abs(tokens)), jnp.max(jnp.abs(context)), jnp.max(jnp.abs(normed)), jnp.max(jnp.abs(active))])
    return (result, maxima)

def reference(tokens, w_qkv, w_out, w_up, w_down, b_qv, b_up, vectors, ema_ranges, key_mask, long_rows, grad_out):
    floats = tuple((array.astype(jnp.float32) for array in (tokens, w_qkv, w_out, w_up, w_down, b_qv, b_up, vectors)))
    w_peaks = jnp.stack([jnp.max(jnp.abs(floats[1])), jnp.max(jnp.abs(floats[2])), jnp.max(jnp.abs(floats[3])), jnp.max(jnp.abs(floats[4]))])

    def run(*params):
        return forward(*params, key_mask, long_rows, ema_ranges, w_peaks)
    result, pull, maxima = jax.vjp(run, *floats, has_aux=True)
    grads = pull(grad_out.astype(jnp.float32))
    new_ranges = 0.9 * ema_ranges + 0.1 * maxima
    return (result.astype(jnp.bfloat16), grads[0], grads[1], grads[2], grads[3], grads[4], grads[5], grads[6], grads[7], new_ranges)
```

```python
import jax
import jax.numpy as jnp
from jax import lax
from jax.experimental import pallas as pl
from jax.experimental.pallas import tpu as pltpu
from jax.sharding import PartitionSpec as P

HD = 64
BLOCK = 512
SEG = 128


eps_norm = 1e-12
root_half = 0.7071067811865476
inv_root_tau = 0.3989422804014327


def squash(values, limit):
    return limit * jnp.tanh(values / limit)


def slope(values, limit):
    bent = jnp.tanh(values / limit)
    return 1.0 - bent * bent


def peak_of(values):
    return jnp.max(jnp.abs(values.astype(jnp.float32)))


def product(left, right):
    return jnp.dot(left, right, preferred_element_type=jnp.float32)


def contract_rows(left, right):
    return lax.dot_general(
        left, right, (((0,), (0,)), ((), ())), preferred_element_type=jnp.float32
    )


def contract_cols(left, right):
    return lax.dot_general(
        left, right, (((1,), (1,)), ((), ())), preferred_element_type=jnp.float32
    )


def normalize(values):
    center = values - jnp.mean(values, axis=-1, keepdims=True)
    factor = lax.rsqrt(jnp.mean(center * center, axis=-1, keepdims=True) + eps_norm)
    return (center * factor, factor)


def norm_back(grad_normed, normed, factor):
    first_mean = jnp.mean(grad_normed, axis=-1, keepdims=True)
    cross_mean = jnp.mean(grad_normed * normed, axis=-1, keepdims=True)
    return factor * (grad_normed - first_mean - normed * cross_mean)


def allowed_keys(live, long_flag):
    places = jnp.arange(BLOCK) // SEG
    return (live[None, :] > 0) & ((long_flag > 0) | (places[:, None] == places[None, :]))


def block_scores(queries, keys_in, live, long_flag):
    scores = jnp.einsum("qhd,khd->hqk", queries, keys_in, preferred_element_type=jnp.float32)
    return jnp.where(allowed_keys(live, long_flag)[None], scores, -1e30)


def attend_block(pieces):
    queries, keys_in, values, live, long_flag = pieces
    scores = block_scores(queries, keys_in, live, long_flag)
    top_score = jnp.max(scores, axis=-1, keepdims=True)
    weights = jnp.exp(scores - top_score)
    totals = jnp.sum(weights, axis=-1, keepdims=True)
    attn_probs = (weights / totals).astype(jnp.bfloat16)
    context = jnp.einsum("hqk,khd->qhd", attn_probs, values, preferred_element_type=jnp.float32)
    return (context, top_score + jnp.log(totals))


def attend_back(pieces):
    queries, keys_in, values, live, long_flag, log_total, grad_ctx = pieces
    attn_probs = jnp.exp(block_scores(queries, keys_in, live, long_flag) - log_total)
    grad_probs = jnp.einsum("qhd,khd->hqk", grad_ctx, values, preferred_element_type=jnp.float32)
    grad_values = jnp.einsum(
        "hqk,qhd->khd",
        attn_probs.astype(jnp.bfloat16),
        grad_ctx,
        preferred_element_type=jnp.float32,
    )
    inner = jnp.sum(grad_probs * attn_probs, axis=-1, keepdims=True)
    grad_scores = (attn_probs * (grad_probs - inner)).astype(jnp.bfloat16)
    grad_queries = jnp.einsum(
        "hqk,khd->qhd", grad_scores, keys_in, preferred_element_type=jnp.float32
    )
    grad_keys = jnp.einsum("hqk,qhd->khd", grad_scores, queries, preferred_element_type=jnp.float32)
    return (
        grad_queries.astype(jnp.bfloat16),
        grad_keys.astype(jnp.bfloat16),
        grad_values.astype(jnp.bfloat16),
    )


def prepare(gathered, w_peaks):
    return tuple(
        (
            squash(gathered[index].astype(jnp.float32), w_peaks[index]).astype(jnp.bfloat16)
            for index in range(4)
        )
    )


def peak_all(values):
    return lax.pmax(peak_of(values), ("dp", "mp"))


def per_device(
    tokens,
    w_qkv,
    w_out,
    w_up,
    w_down,
    b_qv,
    b_up,
    vectors,
    ema_ranges,
    key_mask,
    long_rows,
    grad_out,
):
    row_count = tokens.shape[0]
    quarter = row_count // lax.axis_size("mp")
    row_start = lax.axis_index("mp") * quarter
    blocks = row_count // BLOCK
    w_peaks = lax.pmax(
        (peak_of(w_qkv), peak_of(w_out), peak_of(w_up), peak_of(w_down)), ("dp", "mp")
    )
    gathered = (
        lax.all_gather(w_qkv, "dp", axis=1, tiled=True),
        lax.all_gather(w_out, "dp", axis=1, tiled=True),
        lax.all_gather(w_up, "dp", axis=0, tiled=True),
        lax.all_gather(w_down, "dp", axis=1, tiled=True),
        lax.all_gather(b_qv, "dp", axis=2, tiled=True),
        lax.all_gather(b_up, "dp", axis=1, tiled=True),
        lax.all_gather(vectors, "dp", axis=1, tiled=True),
    )
    qkv_q, out_q, up_q, down_q = prepare(gathered, w_peaks)
    bias_qv = gathered[4].astype(jnp.float32).reshape(2, -1)
    bias_up = gathered[5].astype(jnp.float32).reshape(-1)
    vec = gathered[6].astype(jnp.float32)
    head_width = bias_qv.shape[1]
    heads_here = head_width // HD
    scale_q = HD ** (-0.5)
    tok_float = tokens.astype(jnp.float32)
    peak_tok = peak_all(tok_float)
    tok_quant = squash(tok_float, ema_ranges[0]).astype(jnp.bfloat16)
    projected = jnp.einsum("td,jde->jte", tok_quant, qkv_q, preferred_element_type=jnp.float32)
    queries = ((projected[0] + bias_qv[0]) * scale_q).astype(jnp.bfloat16)
    keys_all = projected[1].astype(jnp.bfloat16)
    values = (projected[2] + bias_qv[1]).astype(jnp.bfloat16)
    shape_four = (blocks, BLOCK, heads_here, HD)
    mask_blocks = key_mask.reshape(blocks, BLOCK)
    block_inputs = (
        queries.reshape(shape_four),
        keys_all.reshape(shape_four),
        values.reshape(shape_four),
        mask_blocks,
        long_rows,
    )
    context, log_total = lax.map(attend_block, block_inputs)
    context = context.reshape(row_count, head_width)
    peak_ctx = peak_all(context)
    ctx_quant = squash(context, ema_ranges[1]).astype(jnp.bfloat16)
    partial_attn = product(ctx_quant, out_q)
    attn = lax.psum_scatter(partial_attn, "mp", scatter_dimension=0, tiled=True) + vec[0]
    first_own = lax.dynamic_slice_in_dim(tok_float, row_start, quarter, 0) + attn
    normed, factor_one = normalize(first_own)
    hidden_in = normed * vec[2] + vec[3]
    hid_quant = lax.all_gather(
        squash(hidden_in, ema_ranges[2]).astype(jnp.bfloat16), "mp", axis=0, tiled=True
    )
    peak_hid = peak_all(hidden_in)
    pre_act = product(hid_quant, up_q) + bias_up
    active = pre_act * 0.5 * (1.0 + lax.erf(pre_act * root_half))
    peak_act = peak_all(active)
    act_quant = squash(active, ema_ranges[3]).astype(jnp.bfloat16)
    branch = (
        lax.psum_scatter(product(act_quant, down_q), "mp", scatter_dimension=0, tiled=True) + vec[1]
    )
    second = first_own + branch
    normed_two, factor_two = normalize(second)
    layer_out = (normed_two * vec[4] + vec[5]).astype(jnp.bfloat16)
    new_ranges = 0.9 * ema_ranges + 0.1 * jnp.stack([peak_tok, peak_ctx, peak_hid, peak_act])
    gathered = (
        lax.all_gather(w_qkv, "dp", axis=1, tiled=True),
        lax.all_gather(w_out, "dp", axis=1, tiled=True),
        lax.all_gather(w_up, "dp", axis=0, tiled=True),
        lax.all_gather(w_down, "dp", axis=1, tiled=True),
        lax.all_gather(b_qv, "dp", axis=2, tiled=True),
        lax.all_gather(b_up, "dp", axis=1, tiled=True),
        lax.all_gather(vectors, "dp", axis=1, tiled=True),
    )
    qkv_q, out_q, up_q, down_q = prepare(gathered, w_peaks)
    grad_y = grad_out.astype(jnp.float32)
    grad_gain_two = jnp.sum(grad_y * normed_two, axis=0)
    grad_shift_two = jnp.sum(grad_y, axis=0)
    grad_second = norm_back(grad_y * vec[4], normed_two, factor_two)
    grad_resid = lax.all_gather(grad_second.astype(jnp.bfloat16), "mp", axis=0, tiled=True).astype(
        grad_second.dtype
    )
    grad_branch = grad_resid.astype(jnp.bfloat16)
    grad_bias_down = jnp.sum(grad_branch.astype(jnp.float32), axis=0)
    grad_down_w = contract_rows(act_quant, grad_branch)
    grad_active = contract_cols(grad_branch, down_q) * slope(active, ema_ranges[3])
    normal_cdf = 0.5 * (1.0 + lax.erf(pre_act * root_half))
    normal_pdf = inv_root_tau * jnp.exp(-0.5 * pre_act * pre_act)
    grad_pre = (grad_active * (normal_cdf + pre_act * normal_pdf)).astype(jnp.bfloat16)
    grad_bias_up = jnp.sum(grad_pre.astype(jnp.float32), axis=0)
    grad_up_w = contract_rows(hid_quant, grad_pre)
    partial_hid = contract_cols(grad_pre, up_q)
    grad_hid_q = lax.psum_scatter(partial_hid, "mp", scatter_dimension=0, tiled=True)
    grad_hidden = grad_hid_q * slope(hidden_in, ema_ranges[2])
    grad_gain_one = jnp.sum(grad_hidden * normed, axis=0)
    grad_shift_one = jnp.sum(grad_hidden, axis=0)
    grad_first = norm_back(grad_hidden * vec[2], normed, factor_one) + grad_second
    grad_attn = lax.all_gather(grad_first.astype(jnp.bfloat16), "mp", axis=0, tiled=True)
    grad_bias_out = jnp.sum(grad_attn.astype(jnp.float32), axis=0)
    grad_out_w = contract_rows(ctx_quant, grad_attn)
    grad_ctx = (contract_cols(grad_attn, out_q) * slope(context, ema_ranges[1])).astype(
        jnp.bfloat16
    )
    back_inputs = block_inputs + (log_total, grad_ctx.reshape(shape_four))
    grad_q, grad_k, grad_v = lax.map(attend_back, back_inputs)
    stacked = jnp.stack(
        [
            grad_q.reshape(row_count, head_width) * jnp.bfloat16(scale_q),
            grad_k.reshape(row_count, head_width),
            grad_v.reshape(row_count, head_width),
        ]
    )
    grad_qkv_w = jnp.einsum("td,jte->jde", tok_quant, stacked, preferred_element_type=jnp.float32)
    stacked_float = stacked.astype(jnp.float32)
    grad_bias_qv = jnp.stack([jnp.sum(stacked_float[0], axis=0), jnp.sum(stacked_float[2], axis=0)])
    part_input = jnp.einsum("jte,jde->td", stacked, qkv_q, preferred_element_type=jnp.float32)
    own_term = part_input * slope(tok_float, ema_ranges[0])
    own_rows = lax.dynamic_slice_in_dim(own_term, row_start, quarter, 0) + grad_first
    own_term = lax.dynamic_update_slice_in_dim(own_term, own_rows, row_start, 0)
    grad_tokens, norm_tail = (
        lax.psum(own_term.astype(jnp.bfloat16), "mp").astype(jnp.float32),
        lax.psum(
            jnp.stack([grad_gain_one, grad_shift_one, grad_gain_two, grad_shift_two]).astype(
                jnp.bfloat16
            ),
            "mp",
        ).astype(jnp.float32),
    )
    grad_vec = jnp.stack(
        [grad_bias_out, grad_bias_down, norm_tail[0], norm_tail[1], norm_tail[2], norm_tail[3]]
    )
    summed = (
        lax.psum_scatter(
            grad_qkv_w * slope(gathered[0].astype(jnp.float32), w_peaks[0]),
            "dp",
            scatter_dimension=1,
            tiled=True,
        ),
        lax.psum_scatter(
            grad_out_w * slope(gathered[1].astype(jnp.float32), w_peaks[1]),
            "dp",
            scatter_dimension=1,
            tiled=True,
        ),
        lax.psum_scatter(
            grad_up_w * slope(gathered[2].astype(jnp.float32), w_peaks[2]),
            "dp",
            scatter_dimension=0,
            tiled=True,
        ),
        lax.psum_scatter(
            grad_down_w * slope(gathered[3].astype(jnp.float32), w_peaks[3]),
            "dp",
            scatter_dimension=1,
            tiled=True,
        ),
        lax.psum_scatter(
            grad_bias_qv.reshape(gathered[4].shape), "dp", scatter_dimension=2, tiled=True
        ),
        lax.psum_scatter(
            grad_bias_up.reshape(gathered[5].shape), "dp", scatter_dimension=1, tiled=True
        ),
        lax.psum_scatter(grad_vec, "dp", scatter_dimension=1, tiled=True),
    )
    return (
        layer_out,
        grad_tokens,
        summed[0],
        summed[1],
        summed[2],
        summed[3],
        summed[4],
        summed[5],
        summed[6],
        new_ranges,
    )


BF = jnp.bfloat16
F32 = jnp.float32
MESH = pl.DeviceIdType.MESH
WIDE = 768
PIECE = 96
CUT = 48
OWN = 256
HERE = 384


def nn(left, right):
    return lax.dot_general(left, right, (((1,), (0,)), ((), ())), preferred_element_type=F32)


def nt(left, right):
    return lax.dot_general(left, right, (((1,), (1,)), ((), ())), preferred_element_type=F32)


def mul8(value, step):
    return pl.multiple_of(value, step)


def loop(count, body):
    def step(index, carry):
        body(index)
        return carry

    lax.fori_loop(0, count, step, 0)


def layer_kernel(
    tok,
    w_qkv,
    w_out,
    w_up,
    w_down,
    b_qv,
    b_up,
    vectors,
    ranges,
    mask,
    long_rows,
    grad_out,
    o_layer,
    o_tok,
    o_qkv,
    o_out,
    o_up,
    o_down,
    o_bqv,
    o_bup,
    o_vec,
    o_rng,
    wts,
    wff,
    wc,
    wo,
    rdx,
    rdy,
    rxx,
    ryy,
    rzz,
    sm,
    smc,
    vec,
    bup,
    bqv,
    xq,
    xqt,
    bias,
    qs,
    ks,
    vs,
    kt,
    vt,
    probs,
    ds,
    ctxt,
    cq,
    slc,
    exa_s,
    exa_r,
    exb_s,
    exb_r,
    hq,
    hqt,
    r1,
    n1,
    rstd1,
    sl1,
    aq,
    fac,
    gu,
    gf,
    rowt,
    gr2,
    gc,
    gct,
    dsum,
    grads,
    gqt,
    gwo,
    tot,
    tot_c,
    tot_x,
    tot_y,
    tot_z,
    zs,
    zr,
    xs,
    xr,
    ys,
    yr,
    dxs,
    dxr,
    dys,
    dyr,
    rs_s,
    rs_r,
    sm_s,
    sm_r,
    ex_s,
    ex_r,
    tt_s,
    tt_r,
    gx_s,
    gx_r,
):
    dp = lax.axis_index("dp")
    mp = lax.axis_index("mp")
    z, y = dp // 2, dp % 2
    x, c = mp // 2, mp % 2
    nx, ny, nc = 1 - x, 1 - y, 1 - c
    to_x = (dp, nx * 2 + c)
    to_y = (z * 2 + ny, mp)
    to_c = (dp, x * 2 + nc)
    to_z = [None] + [((z + k) % 4 * 2 + y, mp) for k in (1, 2, 3)]
    zk = [z] + [(z + 4 - k) % 4 for k in (1, 2, 3)]
    zf = [z] + [(z + k) % 4 for k in (1, 2, 3)]
    mine = mul8(c * OWN, OWN)
    theirs = mul8(nc * OWN, OWN)
    started = {}

    def copy(src, dst, send, recv, device):
        return pltpu.make_async_remote_copy(
            src_ref=src, dst_ref=dst, send_sem=send, recv_sem=recv, device_id=device, device_id_type=MESH
        )

    def send(group, *args):
        made = copy(*args)
        made.start()
        started.setdefault(group, []).append(made)

    def sent(group):
        for made in started.pop(group, []):
            made.wait_send()

    range_of = [ranges[i] for i in range(4)]
    inv_of = [1.0 / r for r in range_of]

    wts[1, x, z, y] = w_up[...]
    wts[2, x, z, y] = w_down[...].T
    turned = w_out[...].T
    for j, part in enumerate((w_qkv[0], w_qkv[1], w_qkv[2], turned)):
        wts[0, x, z, y, :, j * 128 : j * 128 + 128] = part[:, 0:128]
        wts[0, x, z, y, :, 512 + j * 64 : 576 + j * 64] = part[:, 128:192]

    sm[x, z, y] = jnp.zeros((16, 128), F32)
    sm[x, z, y, 0:6, 0:96] = vectors[...].astype(F32)
    sm[x, z, y, 6:9, 0:32] = b_up[...].astype(F32)
    sm[x, z, y, 9:12, 0:8] = b_qv[0].astype(F32)
    sm[x, z, y, 12:15, 0:8] = b_qv[1].astype(F32)
    lane = lax.broadcasted_iota(jnp.int32, (1, 128), 1)
    peak_row = jnp.zeros((1, 128), F32)
    for g, ref in enumerate((w_qkv, w_out, w_up, w_down)):
        most = jnp.abs(ref[...].astype(F32))
        if most.ndim == 3:
            most = jnp.max(most, axis=0)
        most = jnp.max(jnp.max(most, axis=0, keepdims=True), axis=1, keepdims=True)
        peak_row = jnp.where(lane == g, most, peak_row)
    sm[x, z, y, 15:16] = peak_row

    barrier = pltpu.get_barrier_semaphore()
    for device in (to_c, to_x, to_y, *to_z[1:]):
        pl.semaphore_signal(barrier, inc=1, device_id=device, device_id_type=MESH)
    pl.semaphore_wait(barrier, 6)

    def ag_z_send(g):
        for k in (1, 2, 3):
            own = wts.at[g, x, z, y]
            send(("ag", g), own, own, zs.at[g, k - 1], zr.at[g, k - 1], to_z[k])

    def ag_xy_send(g, k):
        own = wts.at[g, x, zk[k], y]
        if k > 0:
            copy(own, own, zs.at[g, k - 1], zr.at[g, k - 1], to_z[k]).wait_recv()
        send(("ag", g), own, own, xs.at[g, k], xr.at[g, k], to_x)
        send(("ag", g), own, own, ys.at[g, k], yr.at[g, k], to_y)

    def ag_diag(g, k):
        got = wts.at[g, x, zk[k], ny]
        copy(got, got, ys.at[g, k], yr.at[g, k], to_y).wait_recv()
        half = wts.at[g, x, zk[k], ny, pl.ds(0, CUT)]
        send(("ag", g), half, half, dxs.at[g, k], dxr.at[g, k], to_x)
        got = wts.at[g, nx, zk[k], y]
        copy(got, got, xs.at[g, k], xr.at[g, k], to_x).wait_recv()
        half = wts.at[g, nx, zk[k], y, pl.ds(CUT, PIECE - CUT)]
        send(("ag", g), half, half, dys.at[g, k], dyr.at[g, k], to_y)

    def ag_last(g, k):
        half = wts.at[g, nx, zk[k], ny, pl.ds(0, CUT)]
        copy(half, half, dxs.at[g, k], dxr.at[g, k], to_x).wait_recv()
        half = wts.at[g, nx, zk[k], ny, pl.ds(CUT, PIECE - CUT)]
        copy(half, half, dys.at[g, k], dyr.at[g, k], to_y).wait_recv()

    small_c = copy(sm.at[x, z, y], smc, sm_s.at[0], sm_r.at[0], to_c)
    small_c.start()
    ag_z_send(0)
    ag_xy_send(0, 0)

    base = mul8(x * 512, 512)

    def do_tokens(i):
        rows = pl.ds(mul8(i * 128, 128), 128)
        v = tok[pl.ds(mul8(base + i * 128, 128), 128), :].astype(F32)
        xq[rows, :] = (range_of[0] * jnp.tanh(v * inv_of[0])).astype(BF)

    loop(4, do_tokens)
    small_c.wait()
    sm[x, z, y, 15:16] = jnp.maximum(sm[x, z, y, 15:16], smc[15:16])
    small_x = copy(sm.at[x, z, y], sm.at[x, z, y], sm_s.at[1], sm_r.at[1], to_x)
    small_x.start()
    ag_xy_send(0, 1)

    def do_turn(j):
        cols = pl.ds(mul8(j * 128, 128), 128)
        xqt[cols, :] = xq[:, cols].T

    loop(6, do_turn)
    copy(sm.at[nx, z, y], sm.at[nx, z, y], sm_s.at[1], sm_r.at[1], to_x).wait_recv()
    small_y = copy(sm.at[:, z, y], sm.at[:, z, y], sm_s.at[2], sm_r.at[2], to_y)
    small_y.start()
    ag_diag(0, 0)
    ag_xy_send(0, 2)

    long_flag = long_rows[x].astype(F32)
    for r in range(4):
        row = mask[pl.ds(x * 4 + r, 1), :].astype(F32)
        column = jnp.broadcast_to(row, (128, 128)).T
        for s in range(4):
            seen = column * (1.0 if r == s else long_flag)
            bias[r * 128 : r * 128 + 128, s * 128 : s * 128 + 128] = jnp.where(seen > 0.5, 0.0, -1e30)

    copy(sm.at[:, z, ny], sm.at[:, z, ny], sm_s.at[2], sm_r.at[2], to_y).wait_recv()
    small_z = []
    for k in (1, 2, 3):
        made = copy(sm.at[:, z], sm.at[:, z], sm_s.at[2 + k], sm_r.at[2 + k], to_z[k])
        made.start()
        small_z.append(made)
    ag_diag(0, 1)
    ag_xy_send(0, 3)
    ag_z_send(1)
    ag_diag(0, 2)
    for k in (1, 2, 3):
        copy(sm.at[:, zk[k]], sm.at[:, zk[k]], sm_s.at[2 + k], sm_r.at[2 + k], to_z[k]).wait_recv()
    ag_diag(0, 3)
    small_x.wait_send()
    small_y.wait_send()
    for made in small_z:
        made.wait_send()

    peaks = jnp.max(jnp.max(jnp.max(sm[:, :, :, 15:16, :], axis=0), axis=0), axis=0)
    w_peak = [jnp.max(jnp.where(lane == g, peaks, 0.0)) for g in range(4)]
    w_inv = [1.0 / r for r in w_peak]

    def spread(xx, width, step):
        total = None
        for place in range(8):
            tile = sm[xx, place // 2, place % 2]
            if width > 128:
                tile = jnp.concatenate([tile, jnp.zeros((16, width - 128), F32)], axis=1)
            if place:
                tile = pltpu.roll(tile, place * step, 1)
            total = tile if total is None else total + tile
        return total

    vec[...] = spread(0, WIDE, 96)
    heads = []
    for xx in range(2):
        wide = spread(xx, 256, 32)
        for h in range(3):
            bup[xx : xx + 1, h * 256 : h * 256 + 256] = wide[6 + h : 7 + h, :]
        narrow = spread(xx, 128, 8)
        heads.append((narrow, pltpu.roll(narrow, 64, 1)))
    for j, first in enumerate((9, 12)):
        for xx in range(2):
            bqv[j : j + 1, xx * 128 : xx * 128 + 128] = (
                heads[xx][0][first : first + 1] + heads[xx][1][first + 1 : first + 2]
            )
        bqv[j : j + 1, 256:384] = heads[0][0][first + 2 : first + 3] + heads[1][1][first + 2 : first + 3]

    for k in range(4):
        ag_xy_send(1, k)
    ag_z_send(2)
    for k in range(4):
        ag_last(0, k)

    left = lax.broadcasted_iota(jnp.int32, (PIECE, 128), 1) < 64

    def squash_heads(place):
        rows = pl.ds(mul8(place * PIECE, PIECE), PIECE)
        tiles = []
        for xx in range(2):
            v = wts[0, xx, place // 2, place % 2].astype(F32)
            inner = [w_peak[0] * jnp.tanh(v[:, t * 128 : t * 128 + 128] * w_inv[0]) for t in (0, 1, 2)]
            inner.append(w_peak[1] * jnp.tanh(v[:, 384:512] * w_inv[1]))
            mixed = jnp.where(left, w_peak[0], w_peak[1])
            mixed_inv = jnp.where(left, w_inv[0], w_inv[1])
            inner.append(w_peak[0] * jnp.tanh(v[:, 512:640] * w_inv[0]))
            inner.append(mixed * jnp.tanh(v[:, 640:768] * mixed_inv))
            tiles.append(inner)
        for t in range(3):
            for xx in range(2):
                wc[rows, t * HERE + xx * 128 : t * HERE + xx * 128 + 128] = tiles[xx][t].astype(BF)
        for xx in range(2):
            wo[rows, xx * 128 : xx * 128 + 128] = tiles[xx][3].astype(BF)
        for t, first, second in ((4, 0, 1), (5, 2, 3)):
            one, two = tiles[0][t], tiles[1][t]
            wc[rows, first * HERE + 256 : first * HERE + 384] = jnp.where(left, one, pltpu.roll(two, 64, 1)).astype(BF)
            other = jnp.where(left, pltpu.roll(one, 64, 1), two).astype(BF)
            if second == 1:
                wc[rows, HERE + 256 : HERE + 384] = other
            else:
                wo[rows, 256:384] = other

    loop(8, squash_heads)

    def squash_ff(g, xx):
        def body(place):
            v = wts[g, xx, place // 2, place % 2].astype(F32)
            wff[g - 1, xx, pl.ds(mul8(place * PIECE, PIECE), PIECE), :] = (
                w_peak[g + 1] * jnp.tanh(v * w_inv[g + 1])
            ).astype(BF)

        loop(8, body)

    for j, held in enumerate((qs, ks, vs)):

        def project(i, j=j, held=held):
            rows = pl.ds(mul8(i * 256, 256), 256)
            got = nn(xq[rows, :], wc[:, j * HERE : (j + 1) * HERE])
            if j == 0:
                got = (got + bqv[0:1, :]) * 0.125
            elif j == 2:
                got = got + bqv[1:2, :]
            held[rows, :] = got.astype(BF)

        loop(2, project)
    for p in range(3):
        cols = slice(p * 128, p * 128 + 128)
        kt[cols, :] = ks[:, cols].T
        vt[cols, :] = vs[:, cols].T
    ag_diag(1, 0)

    half_of = lax.broadcasted_iota(jnp.int32, (1, 128), 1) // 64

    def attend(p):
        cols = pl.ds(mul8(p * 128, 128), 128)
        for e in range(2):
            feats = pl.ds(mul8(p * 128 + e * 64, 64), 64)
            for n in range(2):
                q = qs[n * 256 : n * 256 + 256, cols]
                q = jnp.where(half_of == e, q, jnp.zeros_like(q))
                s = nt(ks[:, cols], q) + bias[:, n * 256 : n * 256 + 256]
                s = jnp.exp(s - jnp.max(s, axis=0, keepdims=True))
                s = (s * (1.0 / jnp.sum(s, axis=0, keepdims=True))).astype(BF)
                probs[p * 2 + e, :, n * 256 : n * 256 + 256] = s
                ctxt[feats, n * 256 : n * 256 + 256] = nn(vt[feats, :], s)

    for p in range(3):
        attend(p)
        ag_diag(1, p + 1)

    for p in range(3):
        cols = slice(p * 128, p * 128 + 128)
        bent = jnp.tanh(ctxt[cols, :].T * inv_of[1])
        cq[:, cols] = (range_of[1] * bent).astype(BF)
        slc[:, cols] = 1.0 - bent * bent
    tot[0] = jnp.zeros((16, WIDE), F32)
    most = jnp.max(jnp.max(jnp.abs(ctxt[...]), axis=0, keepdims=True), axis=1, keepdims=True)
    tot[0, 10:11, :] = jnp.broadcast_to(most, (1, WIDE))

    def out_part(start, held):
        def body(n):
            cols = pl.ds(mul8(n * 256, 256), 256)
            held[:, cols] = nt(cq[pl.ds(start, OWN), :], wo[cols, :])

        loop(3, body)

    out_part(theirs, exa_s)
    ex1 = copy(exa_s, exa_r, ex_s.at[0], ex_r.at[0], to_c)
    ex1.start()
    for k in range(4):
        ag_xy_send(2, k)
    out_part(mine, r1)
    ex1.wait()

    def sum_rows(v):
        return jnp.sum(v, axis=0, keepdims=True)

    def mean_of(v):
        return jnp.sum(v, axis=-1, keepdims=True) * (1.0 / WIDE)

    def first_norm(i):
        rows = pl.ds(mul8(i * 64, 64), 64)
        v = tok[pl.ds(mul8(base + mine + i * 64, 64), 64), :].astype(F32)
        v = v + (r1[rows, :] + exa_r[rows, :] + vec[0:1, :])
        r1[rows, :] = v
        center = v - mean_of(v)
        factor = lax.rsqrt(mean_of(center * center) + 1e-12)
        normed = center * factor
        n1[rows, :] = normed
        rstd1[rows, :] = factor
        h = normed * vec[2:3, :] + vec[3:4, :]
        tot[0, 11:12, :] = jnp.maximum(tot[0, 11:12, :], jnp.max(jnp.abs(h), axis=0, keepdims=True))
        bent = jnp.tanh(h * inv_of[2])
        sl1[rows, :] = 1.0 - bent * bent
        hq[pl.ds(mul8(mine + i * 64, 64), 64), :] = (range_of[2] * bent).astype(BF)

    loop(4, first_norm)

    def share_rows(held, number):
        own = held.at[pl.ds(mine, OWN)]
        made = copy(own, own, ex_s.at[number], ex_r.at[number], to_c)
        made.start()
        started.setdefault("share", []).append(made)

    def got_rows(held, number):
        other = held.at[pl.ds(theirs, OWN)]
        copy(other, other, ex_s.at[number], ex_r.at[number], to_c).wait_recv()

    def turn_rows(held, out, start):
        def body(j):
            cols = pl.ds(mul8(j * 128, 128), 128)
            out[cols, pl.ds(start, OWN)] = held[pl.ds(start, OWN), cols].T

        loop(6, body)

    share_rows(hq, 1)
    for k in range(4):
        ag_last(1, k)
    squash_ff(1, 0)
    squash_ff(1, 1)
    ag_diag(2, 0)
    got_rows(hq, 1)
    turn_rows(hq, hqt, 0)
    turn_rows(hq, hqt, OWN)

    def expand(xx):
        def body(j):
            n, i = j // 2, j % 2
            cols = pl.ds(mul8(n * 256, 256), 256)
            wide = pl.ds(mul8(xx * WIDE + n * 256, 256), 256)
            rows = pl.ds(mul8(i * 256, 256), 256)
            u = nn(hq[rows, :], wff[0, xx, :, cols]) + bup[xx : xx + 1, cols]
            cdf = 0.5 * (1.0 + lax.erf(u * 0.7071067811865476))
            a = u * cdf
            tot[0, 12:13, 0:256] = jnp.maximum(tot[0, 12:13, 0:256], jnp.max(jnp.abs(a), axis=0, keepdims=True))
            bent = jnp.tanh(a * inv_of[3])
            aq[rows, wide] = (range_of[3] * bent).astype(BF)
            pdf = 0.3989422804014327 * jnp.exp(-0.5 * u * u)
            fac[rows, wide] = ((1.0 - bent * bent) * (cdf + u * pdf)).astype(fac.dtype)

        loop(6, body)

    expand(0)
    ag_diag(2, 1)
    expand(1)
    ag_diag(2, 2)
    ag_diag(2, 3)

    def down_part(start, held, xx, first):
        def body(n):
            cols = pl.ds(mul8(n * 256, 256), 256)
            got = nt(aq[pl.ds(start, OWN), pl.ds(mul8(xx * WIDE, WIDE), WIDE)], wff[1, xx, cols, :])
            held[:, cols] = got if first else held[:, cols] + got

        loop(3, body)

    squash_ff(2, x)
    down_part(theirs, exb_s, x, True)
    down_part(mine, gr2, x, True)
    for k in range(4):
        ag_last(2, k)
    squash_ff(2, nx)
    down_part(theirs, exb_s, nx, False)
    ex2 = copy(exb_s, exb_r, ex_s.at[2], ex_r.at[2], to_c)
    ex2.start()
    down_part(mine, gr2, nx, False)
    ex2.wait()

    def second_norm(i):
        rows = pl.ds(mul8(i * 64, 64), 64)
        v = r1[rows, :] + (gr2[rows, :] + exb_r[rows, :] + vec[1:2, :])
        center = v - mean_of(v)
        factor = lax.rsqrt(mean_of(center * center) + 1e-12)
        normed = center * factor
        o_layer[rows, :] = (normed * vec[4:5, :] + vec[5:6, :]).astype(BF)
        gy = grad_out[rows, :].astype(F32)
        tot[0, 4:5, :] += sum_rows(gy * normed)
        tot[0, 5:6, :] += sum_rows(gy)
        gn = gy * vec[4:5, :]
        back = factor * (gn - mean_of(gn) - normed * mean_of(gn * normed))
        gr2[rows, :] = back
        low = back.astype(BF)
        tot[0, 1:2, :] += sum_rows(low.astype(F32))
        gf[pl.ds(mul8(mine + i * 64, 64), 64), :] = low

    loop(4, second_norm)
    share_rows(gf, 3)
    turn_rows(gf, rowt, mine)
    for g in range(3):
        sent(("ag", g))
    got_rows(gf, 3)
    turn_rows(gf, rowt, theirs)

    def rs_send(g, number, src, dst, device):
        send("rs", src, dst, rs_s.at[g, number], rs_r.at[g, number], device)

    def rs_wait(g, number, dst, device):
        copy(dst, dst, rs_s.at[g, number], rs_r.at[g, number], device).wait_recv()

    top, low_half = pl.ds(0, CUT), pl.ds(CUT, PIECE - CUT)

    def rs_first(g):
        rs_send(g, 0, wts.at[g, nx, :, ny, top], rdx.at[g], to_x)
        rs_send(g, 1, wts.at[g, nx, :, ny, low_half], rdy.at[g], to_y)
        rs_send(g, 2, wts.at[g, nx, :, y, top], rxx.at[g, :, top], to_x)

    def rs_second(g):
        rs_send(g, 3, wts.at[g, x, :, ny, low_half], ryy.at[g, :, low_half], to_y)

    def rs_third(g):
        rs_wait(g, 0, rdx.at[g], to_x)

        def add_x(i):
            wts[g, x, i, ny, top] = (wts[g, x, i, ny, top].astype(F32) + rdx[g, i].astype(F32)).astype(BF)

        loop(4, add_x)
        rs_send(g, 4, wts.at[g, x, :, ny, top], ryy.at[g, :, top], to_y)
        rs_wait(g, 1, rdy.at[g], to_y)

        def add_y(i):
            wts[g, nx, i, y, low_half] = (
                wts[g, nx, i, y, low_half].astype(F32) + rdy[g, i].astype(F32)
            ).astype(BF)

        loop(4, add_y)
        rs_send(g, 5, wts.at[g, nx, :, y, low_half], rxx.at[g, :, low_half], to_x)

    def plane(g, zz):
        return wts[g, x, zz, y].astype(F32) + rxx[g, zz].astype(F32) + ryy[g, zz].astype(F32)

    def rs_fourth(g):
        rs_wait(g, 2, rxx.at[g, :, top], to_x)
        rs_wait(g, 3, ryy.at[g, :, low_half], to_y)
        rs_wait(g, 4, ryy.at[g, :, top], to_y)
        rs_wait(g, 5, rxx.at[g, :, low_half], to_x)
        for k in (1, 2, 3):
            wts[g, x, zf[k], y] = plane(g, zf[k]).astype(BF)
            rs_send(g, 5 + k, wts.at[g, x, zf[k], y], rzz.at[g, k - 1], to_z[k])

    def rs_total(g):
        for k in (1, 2, 3):
            rs_wait(g, 5 + k, rzz.at[g, k - 1], to_z[k])
        total = plane(g, z)
        for k in range(3):
            total = total + rzz[g, k].astype(F32)
        return total

    def ff_grad(g, turned, held, xx):
        def body(j):
            n, i = j // 2, j % 2
            cols = pl.ds(mul8(n * 256, 256), 256)
            wide = pl.ds(mul8(xx * WIDE + n * 256, 256), 256)
            got = nn(turned[pl.ds(mul8(i * HERE, HERE), HERE), :], held[:, wide])
            wts[g, xx, pl.ds(i * 2, 2), :, :, cols] = got.reshape(2, 2, PIECE, 256).astype(BF)

        loop(6, body)

    ff_grad(2, rowt, aq, nx)
    rs_first(2)
    ff_grad(2, rowt, aq, x)
    rs_second(2)

    for xx in range(2):

        def hidden_grad(j, xx=xx):
            n, i = j // 2, j % 2
            cols = pl.ds(mul8(n * 256, 256), 256)
            wide = pl.ds(mul8(xx * WIDE + n * 256, 256), 256)
            rows = pl.ds(mul8(i * 256, 256), 256)
            got = (nn(gf[rows, :], wff[1, xx, :, cols]) * fac[rows, wide].astype(F32)).astype(BF)
            gu[rows, wide] = got
            tot[0, 6 + xx : 7 + xx, cols] += sum_rows(got.astype(F32))

        loop(6, hidden_grad)
    ff_grad(1, hqt, gu, nx)
    rs_first(1)
    ff_grad(1, hqt, gu, x)
    rs_second(1)

    def up_part(start, held):
        def body(n):
            cols = pl.ds(mul8(n * 256, 256), 256)
            held[:, cols] = nt(gu[pl.ds(start, OWN), 0:WIDE], wff[0, 0, cols, :]) + nt(
                gu[pl.ds(start, OWN), WIDE : 2 * WIDE], wff[0, 1, cols, :]
            )

        loop(3, body)

    up_part(theirs, exa_s)
    ex3 = copy(exa_s, exa_r, ex_s.at[4], ex_r.at[4], to_c)
    ex3.start()
    up_part(mine, r1)
    rs_third(2)
    ex3.wait()

    def first_back(i):
        rows = pl.ds(mul8(i * 64, 64), 64)
        normed = n1[rows, :]
        gh = (r1[rows, :] + exa_r[rows, :]) * sl1[rows, :]
        tot[0, 2:3, :] += sum_rows(gh * normed)
        tot[0, 3:4, :] += sum_rows(gh)
        gn = gh * vec[2:3, :]
        back = rstd1[rows, :] * (gn - mean_of(gn) - normed * mean_of(gn * normed)) + gr2[rows, :]
        gr2[rows, :] = back
        low = back.astype(BF)
        tot[0, 0:1, :] += sum_rows(low.astype(F32))
        gf[pl.ds(mul8(mine + i * 64, 64), 64), :] = low

    sent("share")
    loop(4, first_back)
    share_rows(gf, 5)
    turn_rows(gf, rowt, mine)
    got_rows(gf, 5)
    turn_rows(gf, rowt, theirs)

    def out_grad(i):
        rows = pl.ds(mul8(i * 256, 256), 256)
        gwo[rows, :] = nn(rowt[rows, :], cq[...])

    loop(3, out_grad)

    def ctx_grad(i):
        rows = pl.ds(mul8(i * 256, 256), 256)
        gc[rows, :] = (nn(gf[rows, :], wo[...]) * slc[rows, :]).astype(BF)

    loop(2, ctx_grad)
    for p in range(3):
        cols = slice(p * 128, p * 128 + 128)
        gct[cols, :] = gc[:, cols].T
        for e in range(2):
            feats = slice(p * 128 + e * 64, p * 128 + e * 64 + 64)
            dsum[p * 2 + e : p * 2 + e + 1, :] = sum_rows(gct[feats, :].astype(F32) * ctxt[feats, :])
    rs_third(1)

    row_half = lax.broadcasted_iota(jnp.int32, (128, 1), 0) // 64

    def attend_back(p):
        cols = pl.ds(mul8(p * 128, 128), 128)
        grad_k = grad_v = None
        for e in range(2):
            feats = pl.ds(mul8(p * 128 + e * 64, 64), 64)
            for n in range(2):
                part = slice(n * 256, n * 256 + 256)
                g = gct[cols, part]
                g = jnp.where(row_half == e, g, jnp.zeros_like(g))
                dpr = nn(vs[:, cols], g)
                ds[:, part] = (probs[p * 2 + e, :, part].astype(F32) * (dpr - dsum[pl.ds(p * 2 + e, 1), part])).astype(BF)
            g = gc[:, cols]
            g = jnp.where(half_of == e, g, jnp.zeros_like(g))
            more_v = nn(probs[p * 2 + e], g)
            q = qs[:, cols]
            q = jnp.where(half_of == e, q, jnp.zeros_like(q))
            more_k = nn(ds[...], q)
            grad_v = more_v if e == 0 else grad_v + more_v
            grad_k = more_k if e == 0 else grad_k + more_k
            gqt[feats, :] = nn(kt[feats, :], ds[...])
        grads[:, pl.ds(mul8(HERE + p * 128, 128), 128)] = grad_k.astype(BF)
        grads[:, pl.ds(mul8(2 * HERE + p * 128, 128), 128)] = grad_v.astype(BF)
        grads[:, cols] = (gqt[cols, :].astype(BF).astype(F32) * 0.125).T.astype(BF)

    attend_back(0)
    attend_back(1)
    rs_fourth(2)
    attend_back(2)
    for j, part in ((0, 0), (2, HERE)):
        tot[0, 8:9, part : part + HERE] = sum_rows(grads[:, j * HERE : (j + 1) * HERE].astype(F32))

    left_two = lax.broadcasted_iota(jnp.int32, (2 * PIECE, 128), 1) < 64

    def head_grad(i):
        rows = pl.ds(mul8(i * 2 * PIECE, 2 * PIECE), 2 * PIECE)
        gq, gk, gv = (nn(xqt[rows, :], grads[:, j * HERE : (j + 1) * HERE]) for j in range(3))
        parts = (gq, gk, gv, gwo[rows, :])

        def put(xx, t, v):
            wts[0, xx, i, :, :, t * 128 : t * 128 + 128] = v.reshape(2, PIECE, 128).astype(BF)

        for xx in range(2):
            for t in range(4):
                put(xx, t, parts[t][:, xx * 128 : xx * 128 + 128])
        for t, first, second in ((4, gq, gk), (5, gv, gwo[rows, :])):
            one, two = first[:, 256:384], second[:, 256:384]
            put(0, t, jnp.where(left_two, one, pltpu.roll(two, 64, 1)))
            put(1, t, jnp.where(left_two, pltpu.roll(one, 64, 1), two))

    loop(4, head_grad)
    rs_first(0)
    rs_second(0)

    def token_part(start, held):
        def body(n):
            cols = pl.ds(mul8(n * 256, 256), 256)
            held[:, cols] = nt(grads[pl.ds(start, OWN), :], wc[cols, :])

        loop(3, body)

    token_part(theirs, exb_s)
    ex4 = copy(exb_s, exb_r, ex_s.at[6], ex_r.at[6], to_c)
    ex4.start()
    token_part(mine, r1)
    rs_fourth(1)

    def most_x(i):
        v = jnp.abs(tok[pl.ds(mul8(base + i * 128, 128), 128), :].astype(F32))
        tot[0, 9:10, :] = jnp.maximum(tot[0, 9:10, :], jnp.max(v, axis=0, keepdims=True))

    loop(4, most_x)
    row_of = lax.broadcasted_iota(jnp.int32, (16, 1), 0)
    small = copy(tot.at[0], tot_c, tt_s.at[0], tt_r.at[0], to_c)
    small.start()
    ex4.wait()

    def token_grad(i):
        rows = pl.ds(mul8(i * 64, 64), 64)
        v = tok[pl.ds(mul8(base + mine + i * 64, 64), 64), :].astype(F32)
        bent = jnp.tanh(v * inv_of[0])
        got = gr2[rows, :] + (r1[rows, :] + exb_r[rows, :]) * (1.0 - bent * bent)
        o_tok[pl.ds(mul8(mp * OWN + i * 64, 64), 64), :] = got.astype(BF)

    loop(4, token_grad)
    own = o_tok.at[pl.ds(mul8(mp * OWN, OWN), OWN)]
    send("tok", own, own, gx_s.at[0], gx_r.at[0], to_x)
    send("tok", own, own, gx_s.at[1], gx_r.at[1], to_c)

    small.wait()
    mixed = jnp.where(row_of < 6, tot[0] + tot_c[...], jnp.maximum(tot[0], tot_c[...]))
    tot[1] = jnp.where((row_of >= 6) & (row_of < 9), tot[0], mixed)
    small = copy(tot.at[1], tot_x, tt_s.at[1], tt_r.at[1], to_x)
    small.start()
    rs_third(0)
    small.wait()
    tot[2] = jnp.where(row_of < 9, tot[1] + tot_x[...], jnp.maximum(tot[1], tot_x[...]))
    small = copy(tot.at[2], tot_y, tt_s.at[2], tt_r.at[2], to_y)
    small.start()
    o_up[...] = rs_total(1) * _slope(w_up[...], w_inv[2])
    small.wait()
    tot[3] = jnp.where(row_of < 9, tot[2] + tot_y[...], jnp.maximum(tot[2], tot_y[...]))
    smalls = []
    for k in (1, 2, 3):
        made = copy(tot.at[3], tot_z.at[k - 1], tt_s.at[2 + k], tt_r.at[2 + k], to_z[k])
        made.start()
        smalls.append(made)
    o_down[...] = rs_total(2).T * _slope(w_down[...], w_inv[3])
    rs_fourth(0)

    far = o_tok.at[pl.ds(mul8((nx * 2 + c) * OWN, OWN), OWN)]
    copy(far, far, gx_s.at[0], gx_r.at[0], to_x).wait_recv()
    send("tok", far, far, gx_s.at[2], gx_r.at[2], to_c)

    for made in smalls:
        made.wait()
    done = tot[3]
    for k in range(3):
        done = jnp.where(row_of < 9, done + tot_z[k], jnp.maximum(done, tot_z[k]))
    back = pltpu.roll(done, (8 - dp) * 96, 1)
    o_vec[...] = back[0:6, 0:96]
    ups = jnp.where(x == 0, done[6:7, :], done[7:8, :])
    for h in range(3):
        tile = jnp.broadcast_to(ups[:, h * 256 : h * 256 + 256], (8, 256))
        o_bup[h : h + 1, :] = pltpu.roll(tile, (8 - dp) * 32, 1)[0:1, 0:32]
    for j in range(2):
        row = jnp.broadcast_to(done[8:9, j * HERE : (j + 1) * HERE], (8, HERE))
        pair = jnp.where(x == 0, row[:, 0:128], row[:, 128:256])
        for h, tile, shift in ((0, pair, 0), (1, pair, 64), (2, row[:, 256:384], 64 * x)):
            o_bqv[j, h : h + 1, :] = pltpu.roll(tile, (256 - shift - dp * 8) % 128, 1)[0:1, 0:8]
    for i in range(4):
        o_rng[i] = 0.9 * range_of[i] + 0.1 * jnp.max(done[9 + i : 10 + i, :])

    total = rs_total(0)
    for j in range(4):
        main = total[:, j * 128 : j * 128 + 128]
        pair = total[:, 512 + j // 2 * 128 : 640 + j // 2 * 128]
        if j % 2:
            pair = pltpu.roll(pair, 64, 1)
        whole = jnp.concatenate([main, pair], axis=1)[:, 0:192]
        if j < 3:
            o_qkv[j] = whole * _slope(w_qkv[j], w_inv[0])
        else:
            o_out[...] = whole.T * _slope(w_out[...], w_inv[1])
    near = o_tok.at[pl.ds(mul8((x * 2 + nc) * OWN, OWN), OWN)]
    copy(near, near, gx_s.at[1], gx_r.at[1], to_c).wait_recv()
    far = o_tok.at[pl.ds(mul8((nx * 2 + nc) * OWN, OWN), OWN)]
    copy(far, far, gx_s.at[2], gx_r.at[2], to_c).wait_recv()
    for group in list(started):
        sent(group)


def _slope(values, inverse):
    bent = jnp.tanh(values.astype(F32) * inverse)
    return 1.0 - bent * bent


def layer_on_chips(
    tokens, w_qkv, w_out, w_up, w_down, b_qv, b_up, vectors, ema_ranges, key_mask, long_rows, grad_out
):
    vmem = pltpu.VMEM
    rows = tokens.shape[0]
    half = rows // 2

    def buffer(*shape, dtype=BF):
        return vmem(shape, dtype)

    def f32(*shape):
        return vmem(shape, F32)

    sems = pltpu.SemaphoreType.DMA
    scratch = [
        buffer(3, 2, 4, 2, PIECE, WIDE),
        buffer(2, 2, WIDE, WIDE),
        buffer(WIDE, 3 * HERE),
        buffer(WIDE, HERE),
        buffer(3, 4, CUT, WIDE),
        buffer(3, 4, PIECE - CUT, WIDE),
        buffer(3, 4, PIECE, WIDE),
        buffer(3, 4, PIECE, WIDE),
        buffer(3, 3, PIECE, WIDE),
        f32(2, 4, 2, 16, 128),
        f32(16, 128),
        f32(16, WIDE),
        f32(8, WIDE),
        f32(8, HERE),
        buffer(half, WIDE),
        buffer(WIDE, half),
        f32(half, half),
        buffer(half, HERE),
        buffer(half, HERE),
        buffer(half, HERE),
        buffer(HERE, half),
        buffer(HERE, half),
        buffer(6, half, half),
        buffer(half, half),
        f32(HERE, half),
        buffer(half, HERE),
        f32(half, HERE),
        f32(OWN, WIDE),
        f32(OWN, WIDE),
        f32(OWN, WIDE),
        f32(OWN, WIDE),
        buffer(half, WIDE),
        buffer(WIDE, half),
        f32(OWN, WIDE),
        f32(OWN, WIDE),
        f32(OWN, 1),
        f32(OWN, WIDE),
        buffer(half, 2 * WIDE),
        buffer(half, 2 * WIDE),
        buffer(half, 2 * WIDE),
        buffer(half, WIDE),
        buffer(WIDE, half),
        f32(OWN, WIDE),
        buffer(half, HERE),
        buffer(HERE, half),
        f32(8, half),
        buffer(half, 3 * HERE),
        f32(HERE, half),
        f32(WIDE, HERE),
        f32(4, 16, WIDE),
        f32(16, WIDE),
        f32(16, WIDE),
        f32(16, WIDE),
        f32(3, 16, WIDE),
        sems((3, 3)),
        sems((3, 3)),
        sems((3, 4)),
        sems((3, 4)),
        sems((3, 4)),
        sems((3, 4)),
        sems((3, 4)),
        sems((3, 4)),
        sems((3, 4)),
        sems((3, 4)),
        sems((3, 9)),
        sems((3, 9)),
        sems((6,)),
        sems((6,)),
        sems((7,)),
        sems((7,)),
        sems((6,)),
        sems((6,)),
        sems((3,)),
        sems((3,)),
    ]
    whole = pl.BlockSpec(memory_space=vmem)
    scalars = pl.BlockSpec(memory_space=pltpu.SMEM)
    shape = jax.ShapeDtypeStruct
    outs = pl.pallas_call(
        layer_kernel,
        out_shape=[
            shape(grad_out.shape, BF),
            shape(tokens.shape, BF),
            shape(w_qkv.shape, F32),
            shape(w_out.shape, F32),
            shape(w_up.shape, F32),
            shape(w_down.shape, F32),
            shape(b_qv.shape, F32),
            shape(b_up.shape, F32),
            shape(vectors.shape, F32),
            shape(ema_ranges.shape, F32),
        ],
        in_specs=[whole] * 8 + [scalars, whole, scalars, whole],
        out_specs=[whole] * 9 + [scalars],
        scratch_shapes=scratch,
        compiler_params=pltpu.CompilerParams(
            collective_id=0, has_side_effects=True, vmem_limit_bytes=VMEM_LIMIT
        ),
        name="encoder_layer",
    )(
        tokens,
        w_qkv,
        w_out,
        w_up,
        w_down,
        b_qv,
        b_up,
        vectors,
        ema_ranges,
        key_mask.reshape(rows // 128, 128),
        long_rows,
        grad_out,
    )
    return (outs[0], outs[1].astype(F32), *outs[2:])


VMEM_LIMIT = 64 * 1024 * 1024


def solution(mesh):
    placed = (
        P("dp", None),
        P(None, "dp", "mp"),
        P("mp", "dp"),
        P("dp", "mp"),
        P("mp", "dp"),
        P(None, "mp", "dp"),
        P("mp", "dp"),
        P(None, "dp"),
        P(),
        P("dp"),
        P("dp"),
        P(("dp", "mp"), None),
    )
    on_chips = dict(mesh.shape) == {"dp": 8, "mp": 4}
    return jax.shard_map(
        layer_on_chips if on_chips else per_device,
        mesh=mesh,
        in_specs=placed,
        out_specs=(
            P(("dp", "mp"), None),
            P("dp", None),
            P(None, "dp", "mp"),
            P("mp", "dp"),
            P("dp", "mp"),
            P("mp", "dp"),
            P(None, "mp", "dp"),
            P("mp", "dp"),
            P(None, "dp"),
            P(),
        ),
        check_vma=False,
    )
```

```python
import jax
import jax.numpy as jnp
from jax import lax
from jax.experimental import pallas as pl
from jax.experimental.pallas import tpu as pltpu
from jax.sharding import PartitionSpec as P

HD = 64
BLOCK = 512
SEG = 128


eps_norm = 1e-12
root_half = 0.7071067811865476
inv_root_tau = 0.3989422804014327


def squash(values, limit):
    return limit * jnp.tanh(values / limit)


def slope(values, limit):
    bent = jnp.tanh(values / limit)
    return 1.0 - bent * bent


def peak_of(values):
    return jnp.max(jnp.abs(values.astype(jnp.float32)))


def product(left, right):
    return jnp.dot(left, right, preferred_element_type=jnp.float32)


def contract_rows(left, right):
    return lax.dot_general(
        left, right, (((0,), (0,)), ((), ())), preferred_element_type=jnp.float32
    )


def contract_cols(left, right):
    return lax.dot_general(
        left, right, (((1,), (1,)), ((), ())), preferred_element_type=jnp.float32
    )


def normalize(values):
    center = values - jnp.mean(values, axis=-1, keepdims=True)
    factor = lax.rsqrt(jnp.mean(center * center, axis=-1, keepdims=True) + eps_norm)
    return (center * factor, factor)


def norm_back(grad_normed, normed, factor):
    first_mean = jnp.mean(grad_normed, axis=-1, keepdims=True)
    cross_mean = jnp.mean(grad_normed * normed, axis=-1, keepdims=True)
    return factor * (grad_normed - first_mean - normed * cross_mean)


def allowed_keys(live, long_flag):
    places = jnp.arange(BLOCK) // SEG
    return (live[None, :] > 0) & ((long_flag > 0) | (places[:, None] == places[None, :]))


def block_scores(queries, keys_in, live, long_flag):
    scores = jnp.einsum("qhd,khd->hqk", queries, keys_in, preferred_element_type=jnp.float32)
    return jnp.where(allowed_keys(live, long_flag)[None], scores, -1e30)


def attend_block(pieces):
    queries, keys_in, values, live, long_flag = pieces
    scores = block_scores(queries, keys_in, live, long_flag)
    top_score = jnp.max(scores, axis=-1, keepdims=True)
    weights = jnp.exp(scores - top_score)
    totals = jnp.sum(weights, axis=-1, keepdims=True)
    attn_probs = (weights / totals).astype(jnp.bfloat16)
    context = jnp.einsum("hqk,khd->qhd", attn_probs, values, preferred_element_type=jnp.float32)
    return (context, top_score + jnp.log(totals))


def attend_back(pieces):
    queries, keys_in, values, live, long_flag, log_total, grad_ctx = pieces
    attn_probs = jnp.exp(block_scores(queries, keys_in, live, long_flag) - log_total)
    grad_probs = jnp.einsum("qhd,khd->hqk", grad_ctx, values, preferred_element_type=jnp.float32)
    grad_values = jnp.einsum(
        "hqk,qhd->khd",
        attn_probs.astype(jnp.bfloat16),
        grad_ctx,
        preferred_element_type=jnp.float32,
    )
    inner = jnp.sum(grad_probs * attn_probs, axis=-1, keepdims=True)
    grad_scores = (attn_probs * (grad_probs - inner)).astype(jnp.bfloat16)
    grad_queries = jnp.einsum(
        "hqk,khd->qhd", grad_scores, keys_in, preferred_element_type=jnp.float32
    )
    grad_keys = jnp.einsum("hqk,qhd->khd", grad_scores, queries, preferred_element_type=jnp.float32)
    return (
        grad_queries.astype(jnp.bfloat16),
        grad_keys.astype(jnp.bfloat16),
        grad_values.astype(jnp.bfloat16),
    )


def prepare(gathered, w_peaks):
    return tuple(
        (
            squash(gathered[index].astype(jnp.float32), w_peaks[index]).astype(jnp.bfloat16)
            for index in range(4)
        )
    )


def peak_all(values):
    return lax.pmax(peak_of(values), ("dp", "mp"))


def per_device(
    tokens,
    w_qkv,
    w_out,
    w_up,
    w_down,
    b_qv,
    b_up,
    vectors,
    ema_ranges,
    key_mask,
    long_rows,
    grad_out,
):
    row_count = tokens.shape[0]
    quarter = row_count // lax.axis_size("mp")
    row_start = lax.axis_index("mp") * quarter
    blocks = row_count // BLOCK
    w_peaks = lax.pmax(
        (peak_of(w_qkv), peak_of(w_out), peak_of(w_up), peak_of(w_down)), ("dp", "mp")
    )
    gathered = (
        lax.all_gather(w_qkv, "dp", axis=1, tiled=True),
        lax.all_gather(w_out, "dp", axis=1, tiled=True),
        lax.all_gather(w_up, "dp", axis=0, tiled=True),
        lax.all_gather(w_down, "dp", axis=1, tiled=True),
        lax.all_gather(b_qv, "dp", axis=2, tiled=True),
        lax.all_gather(b_up, "dp", axis=1, tiled=True),
        lax.all_gather(vectors, "dp", axis=1, tiled=True),
    )
    qkv_q, out_q, up_q, down_q = prepare(gathered, w_peaks)
    bias_qv = gathered[4].astype(jnp.float32).reshape(2, -1)
    bias_up = gathered[5].astype(jnp.float32).reshape(-1)
    vec = gathered[6].astype(jnp.float32)
    head_width = bias_qv.shape[1]
    heads_here = head_width // HD
    scale_q = HD ** (-0.5)
    tok_float = tokens.astype(jnp.float32)
    peak_tok = peak_all(tok_float)
    tok_quant = squash(tok_float, ema_ranges[0]).astype(jnp.bfloat16)
    projected = jnp.einsum("td,jde->jte", tok_quant, qkv_q, preferred_element_type=jnp.float32)
    queries = ((projected[0] + bias_qv[0]) * scale_q).astype(jnp.bfloat16)
    keys_all = projected[1].astype(jnp.bfloat16)
    values = (projected[2] + bias_qv[1]).astype(jnp.bfloat16)
    shape_four = (blocks, BLOCK, heads_here, HD)
    mask_blocks = key_mask.reshape(blocks, BLOCK)
    block_inputs = (
        queries.reshape(shape_four),
        keys_all.reshape(shape_four),
        values.reshape(shape_four),
        mask_blocks,
        long_rows,
    )
    context, log_total = lax.map(attend_block, block_inputs)
    context = context.reshape(row_count, head_width)
    peak_ctx = peak_all(context)
    ctx_quant = squash(context, ema_ranges[1]).astype(jnp.bfloat16)
    partial_attn = product(ctx_quant, out_q)
    attn = lax.psum_scatter(partial_attn, "mp", scatter_dimension=0, tiled=True) + vec[0]
    first_own = lax.dynamic_slice_in_dim(tok_float, row_start, quarter, 0) + attn
    normed, factor_one = normalize(first_own)
    hidden_in = normed * vec[2] + vec[3]
    hid_quant = lax.all_gather(
        squash(hidden_in, ema_ranges[2]).astype(jnp.bfloat16), "mp", axis=0, tiled=True
    )
    peak_hid = peak_all(hidden_in)
    pre_act = product(hid_quant, up_q) + bias_up
    active = pre_act * 0.5 * (1.0 + lax.erf(pre_act * root_half))
    peak_act = peak_all(active)
    act_quant = squash(active, ema_ranges[3]).astype(jnp.bfloat16)
    branch = (
        lax.psum_scatter(product(act_quant, down_q), "mp", scatter_dimension=0, tiled=True) + vec[1]
    )
    second = first_own + branch
    normed_two, factor_two = normalize(second)
    layer_out = (normed_two * vec[4] + vec[5]).astype(jnp.bfloat16)
    new_ranges = 0.9 * ema_ranges + 0.1 * jnp.stack([peak_tok, peak_ctx, peak_hid, peak_act])
    gathered = (
        lax.all_gather(w_qkv, "dp", axis=1, tiled=True),
        lax.all_gather(w_out, "dp", axis=1, tiled=True),
        lax.all_gather(w_up, "dp", axis=0, tiled=True),
        lax.all_gather(w_down, "dp", axis=1, tiled=True),
        lax.all_gather(b_qv, "dp", axis=2, tiled=True),
        lax.all_gather(b_up, "dp", axis=1, tiled=True),
        lax.all_gather(vectors, "dp", axis=1, tiled=True),
    )
    qkv_q, out_q, up_q, down_q = prepare(gathered, w_peaks)
    grad_y = grad_out.astype(jnp.float32)
    grad_gain_two = jnp.sum(grad_y * normed_two, axis=0)
    grad_shift_two = jnp.sum(grad_y, axis=0)
    grad_second = norm_back(grad_y * vec[4], normed_two, factor_two)
    grad_resid = lax.all_gather(grad_second.astype(jnp.bfloat16), "mp", axis=0, tiled=True).astype(
        grad_second.dtype
    )
    grad_branch = grad_resid.astype(jnp.bfloat16)
    grad_bias_down = jnp.sum(grad_branch.astype(jnp.float32), axis=0)
    grad_down_w = contract_rows(act_quant, grad_branch)
    grad_active = contract_cols(grad_branch, down_q) * slope(active, ema_ranges[3])
    normal_cdf = 0.5 * (1.0 + lax.erf(pre_act * root_half))
    normal_pdf = inv_root_tau * jnp.exp(-0.5 * pre_act * pre_act)
    grad_pre = (grad_active * (normal_cdf + pre_act * normal_pdf)).astype(jnp.bfloat16)
    grad_bias_up = jnp.sum(grad_pre.astype(jnp.float32), axis=0)
    grad_up_w = contract_rows(hid_quant, grad_pre)
    partial_hid = contract_cols(grad_pre, up_q)
    grad_hid_q = lax.psum_scatter(partial_hid, "mp", scatter_dimension=0, tiled=True)
    grad_hidden = grad_hid_q * slope(hidden_in, ema_ranges[2])
    grad_gain_one = jnp.sum(grad_hidden * normed, axis=0)
    grad_shift_one = jnp.sum(grad_hidden, axis=0)
    grad_first = norm_back(grad_hidden * vec[2], normed, factor_one) + grad_second
    grad_attn = lax.all_gather(grad_first.astype(jnp.bfloat16), "mp", axis=0, tiled=True)
    grad_bias_out = jnp.sum(grad_attn.astype(jnp.float32), axis=0)
    grad_out_w = contract_rows(ctx_quant, grad_attn)
    grad_ctx = (contract_cols(grad_attn, out_q) * slope(context, ema_ranges[1])).astype(
        jnp.bfloat16
    )
    back_inputs = block_inputs + (log_total, grad_ctx.reshape(shape_four))
    grad_q, grad_k, grad_v = lax.map(attend_back, back_inputs)
    stacked = jnp.stack(
        [
            grad_q.reshape(row_count, head_width) * jnp.bfloat16(scale_q),
            grad_k.reshape(row_count, head_width),
            grad_v.reshape(row_count, head_width),
        ]
    )
    grad_qkv_w = jnp.einsum("td,jte->jde", tok_quant, stacked, preferred_element_type=jnp.float32)
    stacked_float = stacked.astype(jnp.float32)
    grad_bias_qv = jnp.stack([jnp.sum(stacked_float[0], axis=0), jnp.sum(stacked_float[2], axis=0)])
    part_input = jnp.einsum("jte,jde->td", stacked, qkv_q, preferred_element_type=jnp.float32)
    own_term = part_input * slope(tok_float, ema_ranges[0])
    own_rows = lax.dynamic_slice_in_dim(own_term, row_start, quarter, 0) + grad_first
    own_term = lax.dynamic_update_slice_in_dim(own_term, own_rows, row_start, 0)
    grad_tokens, norm_tail = (
        lax.psum(own_term.astype(jnp.bfloat16), "mp").astype(jnp.float32),
        lax.psum(
            jnp.stack([grad_gain_one, grad_shift_one, grad_gain_two, grad_shift_two]).astype(
                jnp.bfloat16
            ),
            "mp",
        ).astype(jnp.float32),
    )
    grad_vec = jnp.stack(
        [grad_bias_out, grad_bias_down, norm_tail[0], norm_tail[1], norm_tail[2], norm_tail[3]]
    )
    summed = (
        lax.psum_scatter(
            grad_qkv_w * slope(gathered[0].astype(jnp.float32), w_peaks[0]),
            "dp",
            scatter_dimension=1,
            tiled=True,
        ),
        lax.psum_scatter(
            grad_out_w * slope(gathered[1].astype(jnp.float32), w_peaks[1]),
            "dp",
            scatter_dimension=1,
            tiled=True,
        ),
        lax.psum_scatter(
            grad_up_w * slope(gathered[2].astype(jnp.float32), w_peaks[2]),
            "dp",
            scatter_dimension=0,
            tiled=True,
        ),
        lax.psum_scatter(
            grad_down_w * slope(gathered[3].astype(jnp.float32), w_peaks[3]),
            "dp",
            scatter_dimension=1,
            tiled=True,
        ),
        lax.psum_scatter(
            grad_bias_qv.reshape(gathered[4].shape), "dp", scatter_dimension=2, tiled=True
        ),
        lax.psum_scatter(
            grad_bias_up.reshape(gathered[5].shape), "dp", scatter_dimension=1, tiled=True
        ),
        lax.psum_scatter(grad_vec, "dp", scatter_dimension=1, tiled=True),
    )
    return (
        layer_out,
        grad_tokens,
        summed[0],
        summed[1],
        summed[2],
        summed[3],
        summed[4],
        summed[5],
        summed[6],
        new_ranges,
    )


BF = jnp.bfloat16
F32 = jnp.float32
MESH = pl.DeviceIdType.MESH
WIDE = 768
PIECE = 96
AG_CUTS = ((16, 32, 48), (16, 48, 32), (16, 32, 48))
RS_CUTS = ((16, 48, 32), (32, 32, 32), (32, 32, 32))
OWN = 256
HERE = 384


def nn(left, right):
    return lax.dot_general(left, right, (((1,), (0,)), ((), ())), preferred_element_type=F32)


def nt(left, right):
    return lax.dot_general(left, right, (((1,), (1,)), ((), ())), preferred_element_type=F32)


def mul8(value, step):
    return pl.multiple_of(value, step)


def loop(count, body):
    def step(index, carry):
        body(index)
        return carry

    lax.fori_loop(0, count, step, 0)


def layer_kernel(
    tok,
    w_qkv,
    w_out,
    w_up,
    w_down,
    b_qv,
    b_up,
    vectors,
    ranges,
    mask,
    long_rows,
    grad_out,
    o_layer,
    o_tok,
    o_qkv,
    o_out,
    o_up,
    o_down,
    o_bqv,
    o_bup,
    o_vec,
    o_rng,
    wts,
    wff,
    wc,
    wo,
    rdx,
    rdy,
    rxx,
    ryy,
    rz,
    rzf,
    rz2,
    rzf2,
    rst,
    sm,
    smc,
    vec,
    bup,
    bqv,
    xq,
    xqt,
    bias,
    qs,
    ks,
    vs,
    kt,
    vt,
    probs,
    ds,
    ctxt,
    cq,
    slc,
    exa_s,
    exa_r,
    exb_s,
    exb_r,
    hq,
    hqt,
    r1,
    n1,
    rstd1,
    sl1,
    aq,
    fac,
    gu,
    gf,
    rowt,
    gr2,
    gc,
    gct,
    dsum,
    grads,
    gqt,
    gwo,
    tot,
    tot_c,
    tot_x,
    tot_y,
    tot_z,
    zs,
    zf,
    zr,
    z2s,
    z2f,
    z2r,
    sts,
    str_,
    xs,
    xr,
    ys,
    yr,
    dxs,
    dxr,
    dys,
    dyr,
    rs_s,
    rs_r,
    rf_s,
    rf_r,
    sm_s,
    sm_r,
    ex_s,
    ex_r,
    tt_s,
    tt_r,
    gx_s,
    gx_r,
):
    dp = lax.axis_index("dp")
    mp = lax.axis_index("mp")
    z, y = dp // 2, dp % 2
    x, c = mp // 2, mp % 2
    nx, ny, nc = 1 - x, 1 - y, 1 - c
    to_x = (dp, nx * 2 + c)
    to_y = (z * 2 + ny, mp)
    to_c = (dp, x * 2 + nc)
    to_xy = (z * 2 + ny, nx * 2 + c)
    to_z = [None] + [((z + k) % 4 * 2 + y, mp) for k in (1, 2, 3)]
    from_z = [z] + [(z + 4 - k) % 4 for k in (1, 2, 3)]
    zk = [z, z + 1 - 2 * (z % 2), 2 - z // 2, 3 - 3 * (z // 2)]
    outer = (z * z - 3 * z + 2) // 2
    to_zk = [None] + [(zk[k] * 2 + y, mp) for k in (1, 2, 3)]
    mine = mul8(c * OWN, OWN)
    theirs = mul8(nc * OWN, OWN)
    started = {}

    def copy(src, dst, send, recv, device):
        return pltpu.make_async_remote_copy(
            src_ref=src, dst_ref=dst, send_sem=send, recv_sem=recv, device_id=device, device_id_type=MESH
        )

    def send(group, *args):
        made = copy(*args)
        made.start()
        started.setdefault(group, []).append((made, None))

    def send_if(which, group, *args):
        made = copy(*args)
        pl.when(outer == which)(made.start)
        started.setdefault(group, []).append((made, which))

    def sent(group):
        for made, which in started.pop(group, []):
            if which is None:
                made.wait_send()
            else:
                pl.when(outer == which)(made.wait_send)

    range_of = [ranges[i] for i in range(4)]
    inv_of = [1.0 / r for r in range_of]

    barrier = pltpu.get_barrier_semaphore()
    for device in (to_c, to_x, to_y, to_xy, *to_z[1:]):
        pl.semaphore_signal(barrier, inc=1, device_id=device, device_id_type=MESH)
    wts[1, x, z, y] = w_up[...]
    wts[2, x, z, y] = w_down[...]
    turned = w_out[...].T
    for j, part in enumerate((w_qkv[0], w_qkv[1], w_qkv[2], turned)):
        wts[0, x, z, y, :, j * 128 : j * 128 + 128] = part[:, 0:128]
        wts[0, x, z, y, :, 512 + j * 64 : 576 + j * 64] = part[:, 128:192]

    sm[x, z, y] = jnp.zeros((16, 128), F32)
    sm[x, z, y, 0:6, 0:96] = vectors[...].astype(F32)
    sm[x, z, y, 6:9, 0:32] = b_up[...].astype(F32)
    sm[x, z, y, 9:12, 0:8] = b_qv[:, 0, :].astype(F32)
    sm[x, z, y, 12:15, 0:8] = b_qv[:, 1, :].astype(F32)
    lane = lax.broadcasted_iota(jnp.int32, (1, 128), 1)
    peak_row = jnp.zeros((1, 128), F32)
    for g, ref in enumerate((w_qkv, w_out, w_up, w_down)):
        most = jnp.abs(ref[...].astype(F32))
        if most.ndim == 3:
            most = jnp.max(most, axis=0)
        most = jnp.max(jnp.max(most, axis=0, keepdims=True), axis=1, keepdims=True)
        peak_row = jnp.where(lane == g, most, peak_row)
    sm[x, z, y, 15:16] = peak_row

    pl.semaphore_wait(barrier, 7)

    def ag_rows(g, xx, zz, yy, part):
        strip, one, two = AG_CUTS[g]
        first = (0, strip, strip + one, strip)[part]
        return wts.at[g, xx, zz, yy, pl.ds(first, (strip, one, two, one + two)[part])]

    def ag_strips(g, zz):
        return wts.at[g, :, zz, :, pl.ds(0, AG_CUTS[g][0])]

    def ag_strip_xy(g):
        own = ag_rows(g, x, z, y, 0)
        for i, device in enumerate((to_x, to_y, to_xy)):
            send(("ag", g), own, own, sts.at[g, i], str_.at[g, i], device)

    def ag_strip_z(g):
        for i, (xx, yy, device) in enumerate(((nx, y, to_x), (x, ny, to_y), (nx, ny, to_xy))):
            got = ag_rows(g, xx, z, yy, 0)
            copy(got, got, sts.at[g, i], str_.at[g, i], device).wait_recv()
        own = ag_strips(g, z)
        send(("ag", g), own, own, z2s.at[g, 0], z2r.at[g, 0], to_zk[1])
        send(("ag", g), own, own, z2s.at[g, 1], z2r.at[g, 1 + outer], to_zk[2])

    def ag_strip_got(g, k):
        got = ag_strips(g, zk[k])
        copy(got, got, z2s.at[g, 0], z2r.at[g, k - 1], to_zk[k]).wait_recv()
        if k > 1:
            send_if(0, ("ag", g), got, got, z2f.at[g, k - 2], z2r.at[g, k - 1], to_zk[1])

    def ag_z_send(g):
        own = ag_rows(g, x, z, y, 3)
        send(("ag", g), own, own, zs.at[g, 0], zr.at[g, 0], to_zk[1])
        send(("ag", g), own, own, zs.at[g, 1], zr.at[g, 1 + outer], to_zk[2])

    def ag_xy_send(g, k):
        own = ag_rows(g, x, zk[k], y, 3)
        if k > 0:
            copy(own, own, zs.at[g, 0], zr.at[g, k - 1], to_zk[k]).wait_recv()
            if k > 1:
                send_if(0, ("ag", g), own, own, zf.at[g, k - 2], zr.at[g, k - 1], to_zk[1])
        send(("ag", g), own, own, xs.at[g, k], xr.at[g, k], to_x)
        send(("ag", g), own, own, ys.at[g, k], yr.at[g, k], to_y)

    def ag_diag(g, k):
        got = ag_rows(g, x, zk[k], ny, 3)
        copy(got, got, ys.at[g, k], yr.at[g, k], to_y).wait_recv()
        half = ag_rows(g, x, zk[k], ny, 1)
        send(("ag", g), half, half, dxs.at[g, k], dxr.at[g, k], to_x)
        got = ag_rows(g, nx, zk[k], y, 3)
        copy(got, got, xs.at[g, k], xr.at[g, k], to_x).wait_recv()
        half = ag_rows(g, nx, zk[k], y, 2)
        send(("ag", g), half, half, dys.at[g, k], dyr.at[g, k], to_y)

    def ag_last(g, k):
        half = ag_rows(g, nx, zk[k], ny, 1)
        copy(half, half, dxs.at[g, k], dxr.at[g, k], to_x).wait_recv()
        half = ag_rows(g, nx, zk[k], ny, 2)
        copy(half, half, dys.at[g, k], dyr.at[g, k], to_y).wait_recv()

    small_c = copy(sm.at[x, z, y], smc, sm_s.at[0], sm_r.at[0], to_c)
    small_c.start()
    ag_strip_xy(0)
    ag_z_send(0)
    ag_xy_send(0, 0)

    base = mul8(x * 512, 512)

    def do_tokens(i):
        rows = pl.ds(mul8(i * 128, 128), 128)
        v = tok[pl.ds(mul8(base + i * 128, 128), 128), :].astype(F32)
        xq[rows, :] = (range_of[0] * jnp.tanh(v * inv_of[0])).astype(BF)

    loop(4, do_tokens)
    small_c.wait()
    sm[x, z, y, 15:16] = jnp.maximum(sm[x, z, y, 15:16], smc[15:16])
    small_x = copy(sm.at[x, z, y], sm.at[x, z, y], sm_s.at[1], sm_r.at[1], to_x)
    small_x.start()
    ag_strip_z(0)
    ag_xy_send(0, 1)

    def do_turn(j):
        cols = pl.ds(mul8(j * 128, 128), 128)
        xqt[cols, :] = xq[:, cols].T

    loop(6, do_turn)
    copy(sm.at[nx, z, y], sm.at[nx, z, y], sm_s.at[1], sm_r.at[1], to_x).wait_recv()
    small_y = copy(sm.at[:, z, y], sm.at[:, z, y], sm_s.at[2], sm_r.at[2], to_y)
    small_y.start()
    ag_diag(0, 0)
    ag_xy_send(0, 2)

    long_flag = long_rows[x].astype(F32)
    for r in range(4):
        row = mask[pl.ds(x * 4 + r, 1), :].astype(F32)
        column = jnp.broadcast_to(row, (128, 128)).T
        for s in range(4):
            seen = column * (1.0 if r == s else long_flag)
            bias[r * 128 : r * 128 + 128, s * 128 : s * 128 + 128] = jnp.where(seen > 0.5, 0.0, -1e30)

    copy(sm.at[:, z, ny], sm.at[:, z, ny], sm_s.at[2], sm_r.at[2], to_y).wait_recv()
    small_z = []
    for k in (1, 2, 3):
        made = copy(sm.at[:, z], sm.at[:, z], sm_s.at[2 + k], sm_r.at[2 + k], to_z[k])
        made.start()
        small_z.append(made)
    ag_diag(0, 1)
    ag_xy_send(0, 3)
    ag_strip_xy(1)
    ag_z_send(1)
    for k in (1, 2, 3):
        ag_strip_got(0, k)
    ag_diag(0, 2)
    ag_xy_send(1, 0)
    ag_diag(0, 3)
    for k in (1, 2, 3):
        copy(sm.at[:, from_z[k]], sm.at[:, from_z[k]], sm_s.at[2 + k], sm_r.at[2 + k], to_z[k]).wait_recv()
    small_x.wait_send()
    small_y.wait_send()
    for made in small_z:
        made.wait_send()

    peaks = jnp.max(jnp.max(jnp.max(sm[:, :, :, 15:16, :], axis=0), axis=0), axis=0)
    w_peak = [jnp.max(jnp.where(lane == g, peaks, 0.0)) for g in range(4)]
    w_inv = [1.0 / r for r in w_peak]

    def spread(xx, width, step):
        total = None
        for place in range(8):
            tile = sm[xx, place // 2, place % 2]
            if width > 128:
                tile = jnp.concatenate([tile, jnp.zeros((16, width - 128), F32)], axis=1)
            if place:
                tile = pltpu.roll(tile, place * step, 1)
            total = tile if total is None else total + tile
        return total

    vec[...] = spread(0, WIDE, 96)
    heads = []
    for xx in range(2):
        wide = spread(xx, 256, 32)
        for h in range(3):
            bup[xx : xx + 1, h * 256 : h * 256 + 256] = wide[6 + h : 7 + h, :]
        narrow = spread(xx, 128, 8)
        heads.append((narrow, pltpu.roll(narrow, 64, 1)))
    for j, first in enumerate((9, 12)):
        for xx in range(2):
            bqv[j : j + 1, xx * 128 : xx * 128 + 128] = (
                heads[xx][0][first : first + 1] + heads[xx][1][first + 1 : first + 2]
            )
        bqv[j : j + 1, 256:384] = heads[0][0][first + 2 : first + 3] + heads[1][1][first + 2 : first + 3]

    ag_xy_send(1, 1)
    ag_strip_z(1)
    for k in range(4):
        ag_last(0, k)

    left = lax.broadcasted_iota(jnp.int32, (PIECE, 128), 1) < 64

    def squash_heads(place):
        rows = pl.ds(mul8(place * PIECE, PIECE), PIECE)
        tiles = []
        for xx in range(2):
            v = wts[0, xx, place // 2, place % 2].astype(F32)
            inner = [w_peak[0] * jnp.tanh(v[:, t * 128 : t * 128 + 128] * w_inv[0]) for t in (0, 1, 2)]
            inner.append(w_peak[1] * jnp.tanh(v[:, 384:512] * w_inv[1]))
            mixed = jnp.where(left, w_peak[0], w_peak[1])
            mixed_inv = jnp.where(left, w_inv[0], w_inv[1])
            inner.append(w_peak[0] * jnp.tanh(v[:, 512:640] * w_inv[0]))
            inner.append(mixed * jnp.tanh(v[:, 640:768] * mixed_inv))
            tiles.append(inner)
        for t in range(3):
            for xx in range(2):
                wc[rows, t * HERE + xx * 128 : t * HERE + xx * 128 + 128] = tiles[xx][t].astype(BF)
        for xx in range(2):
            wo[rows, xx * 128 : xx * 128 + 128] = tiles[xx][3].astype(BF)
        for t, first, second in ((4, 0, 1), (5, 2, 3)):
            one, two = tiles[0][t], tiles[1][t]
            wc[rows, first * HERE + 256 : first * HERE + 384] = jnp.where(left, one, pltpu.roll(two, 64, 1)).astype(BF)
            other = jnp.where(left, pltpu.roll(one, 64, 1), two).astype(BF)
            if second == 1:
                wc[rows, HERE + 256 : HERE + 384] = other
            else:
                wo[rows, 256:384] = other

    loop(8, squash_heads)
    ag_xy_send(1, 2)

    def squash_ff(g, xx):
        def body(place):
            v = wts[g, xx, place // 2, place % 2].astype(F32)
            wff[g - 1, xx, pl.ds(mul8(place * PIECE, PIECE), PIECE), :] = (
                w_peak[g + 1] * jnp.tanh(v * w_inv[g + 1])
            ).astype(BF)

        loop(8, body)

    for j, held in enumerate((qs, ks, vs)):

        def project(i, j=j, held=held):
            rows = pl.ds(mul8(i * 256, 256), 256)
            got = nn(xq[rows, :], wc[:, j * HERE : (j + 1) * HERE])
            if j == 0:
                got = (got + bqv[0:1, :]) * 0.125
            elif j == 2:
                got = got + bqv[1:2, :]
            held[rows, :] = got.astype(BF)

        loop(2, project)
    ag_xy_send(1, 3)
    ag_strip_xy(2)
    ag_z_send(2)
    for p in range(3):
        cols = slice(p * 128, p * 128 + 128)
        kt[cols, :] = ks[:, cols].T
        vt[cols, :] = vs[:, cols].T
    ag_diag(1, 0)

    half_of = lax.broadcasted_iota(jnp.int32, (1, 128), 1) // 64

    def attend(p):
        cols = pl.ds(mul8(p * 128, 128), 128)
        for e in range(2):
            feats = pl.ds(mul8(p * 128 + e * 64, 64), 64)
            for n in range(2):
                q = qs[n * 256 : n * 256 + 256, cols]
                q = jnp.where(half_of == e, q, jnp.zeros_like(q))
                s = nt(ks[:, cols], q) + bias[:, n * 256 : n * 256 + 256]
                s = jnp.exp(s - jnp.max(s, axis=0, keepdims=True))
                s = (s * (1.0 / jnp.sum(s, axis=0, keepdims=True))).astype(BF)
                probs[p * 2 + e, :, n * 256 : n * 256 + 256] = s
                ctxt[feats, n * 256 : n * 256 + 256] = nn(vt[feats, :], s)

    attend(0)
    ag_diag(1, 1)
    for k in (1, 2, 3):
        ag_strip_got(1, k)
    attend(1)
    ag_xy_send(2, 0)
    ag_strip_z(2)
    attend(2)
    ag_diag(1, 2)
    ag_xy_send(2, 1)

    for p in range(3):
        cols = slice(p * 128, p * 128 + 128)
        bent = jnp.tanh(ctxt[cols, :].T * inv_of[1])
        cq[:, cols] = (range_of[1] * bent).astype(BF)
        slc[:, cols] = 1.0 - bent * bent
    tot[0] = jnp.zeros((16, WIDE), F32)
    most = jnp.max(jnp.max(jnp.abs(ctxt[...]), axis=0, keepdims=True), axis=1, keepdims=True)
    tot[0, 10:11, :] = jnp.broadcast_to(most, (1, WIDE))
    ag_diag(1, 3)
    ag_xy_send(2, 2)

    def out_part(start, held):
        def body(n):
            cols = pl.ds(mul8(n * 256, 256), 256)
            held[:, cols] = nt(cq[pl.ds(start, OWN), :], wo[cols, :])

        loop(3, body)

    out_part(theirs, exa_s)
    ex1 = copy(exa_s, exa_r, ex_s.at[0], ex_r.at[0], to_c)
    ex1.start()
    ag_xy_send(2, 3)
    out_part(mine, r1)
    ex1.wait()

    def sum_rows(v):
        return jnp.sum(v, axis=0, keepdims=True)

    def mean_of(v):
        return jnp.sum(v, axis=-1, keepdims=True) * (1.0 / WIDE)

    def first_norm(i):
        rows = pl.ds(mul8(i * 64, 64), 64)
        v = tok[pl.ds(mul8(base + mine + i * 64, 64), 64), :].astype(F32)
        v = v + (r1[rows, :] + exa_r[rows, :] + vec[0:1, :])
        r1[rows, :] = v
        center = v - mean_of(v)
        factor = lax.rsqrt(mean_of(center * center) + 1e-12)
        normed = center * factor
        n1[rows, :] = normed
        rstd1[rows, :] = factor
        h = normed * vec[2:3, :] + vec[3:4, :]
        tot[0, 11:12, :] = jnp.maximum(tot[0, 11:12, :], jnp.max(jnp.abs(h), axis=0, keepdims=True))
        bent = jnp.tanh(h * inv_of[2])
        sl1[rows, :] = 1.0 - bent * bent
        hq[pl.ds(mul8(mine + i * 64, 64), 64), :] = (range_of[2] * bent).astype(BF)

    loop(4, first_norm)

    def share_rows(held, number):
        own = held.at[pl.ds(mine, OWN)]
        made = copy(own, own, ex_s.at[number], ex_r.at[number], to_c)
        made.start()
        started.setdefault("share", []).append((made, None))

    def got_rows(held, number):
        other = held.at[pl.ds(theirs, OWN)]
        copy(other, other, ex_s.at[number], ex_r.at[number], to_c).wait_recv()

    def turn_rows(held, out, start):
        def body(j):
            cols = pl.ds(mul8(j * 128, 128), 128)
            out[cols, pl.ds(start, OWN)] = held[pl.ds(start, OWN), cols].T

        loop(6, body)

    share_rows(hq, 1)
    for k in range(4):
        ag_last(1, k)
    squash_ff(1, 0)
    squash_ff(1, 1)
    ag_diag(2, 0)
    got_rows(hq, 1)
    turn_rows(hq, hqt, 0)
    turn_rows(hq, hqt, OWN)

    def expand(xx):
        def body(j):
            n, i = j // 2, j % 2
            cols = pl.ds(mul8(n * 256, 256), 256)
            wide = pl.ds(mul8(xx * WIDE + n * 256, 256), 256)
            rows = pl.ds(mul8(i * 256, 256), 256)
            u = nn(hq[rows, :], wff[0, xx, :, cols]) + bup[xx : xx + 1, cols]
            cdf = 0.5 * (1.0 + lax.erf(u * 0.7071067811865476))
            a = u * cdf
            tot[0, 12:13, 0:256] = jnp.maximum(tot[0, 12:13, 0:256], jnp.max(jnp.abs(a), axis=0, keepdims=True))
            bent = jnp.tanh(a * inv_of[3])
            aq[rows, wide] = (range_of[3] * bent).astype(BF)
            pdf = 0.3989422804014327 * jnp.exp(-0.5 * u * u)
            fac[rows, wide] = ((1.0 - bent * bent) * (cdf + u * pdf)).astype(fac.dtype)

        loop(6, body)

    expand(0)
    ag_diag(2, 1)
    for k in (1, 2, 3):
        ag_strip_got(2, k)
    expand(1)
    ag_diag(2, 2)
    ag_diag(2, 3)

    def down_part(start, held, xx, first):
        def body(n):
            cols = pl.ds(mul8(n * 256, 256), 256)
            got = nt(aq[pl.ds(start, OWN), pl.ds(mul8(xx * WIDE, WIDE), WIDE)], wff[1, xx, cols, :])
            held[:, cols] = got if first else held[:, cols] + got

        loop(3, body)

    squash_ff(2, x)
    down_part(theirs, exb_s, x, True)
    down_part(mine, gr2, x, True)
    for k in range(4):
        ag_last(2, k)
    squash_ff(2, nx)
    down_part(theirs, exb_s, nx, False)
    ex2 = copy(exb_s, exb_r, ex_s.at[2], ex_r.at[2], to_c)
    ex2.start()
    down_part(mine, gr2, nx, False)
    ex2.wait()

    def second_norm(i):
        rows = pl.ds(mul8(i * 64, 64), 64)
        v = r1[rows, :] + (gr2[rows, :] + exb_r[rows, :] + vec[1:2, :])
        center = v - mean_of(v)
        factor = lax.rsqrt(mean_of(center * center) + 1e-12)
        normed = center * factor
        o_layer[rows, :] = (normed * vec[4:5, :] + vec[5:6, :]).astype(BF)
        gy = grad_out[rows, :].astype(F32)
        tot[0, 4:5, :] += sum_rows(gy * normed)
        tot[0, 5:6, :] += sum_rows(gy)
        gn = gy * vec[4:5, :]
        back = factor * (gn - mean_of(gn) - normed * mean_of(gn * normed))
        gr2[rows, :] = back
        low = back.astype(BF)
        tot[0, 1:2, :] += sum_rows(low.astype(F32))
        gf[pl.ds(mul8(mine + i * 64, 64), 64), :] = low

    loop(4, second_norm)
    share_rows(gf, 3)
    turn_rows(gf, rowt, mine)
    for g in range(3):
        sent(("ag", g))
    got_rows(gf, 3)
    turn_rows(gf, rowt, theirs)

    def rs_send(g, number, src, dst, device):
        send("rs", src, dst, rs_s.at[g, number], rs_r.at[g, number], device)

    def rs_send_if(which, g, number, src, dst, device, slot):
        send_if(which, "rs", src, dst, rf_s.at[g, number], slot, device)

    def rs_wait(g, number, dst, device):
        copy(dst, dst, rs_s.at[g, number], rs_r.at[g, number], device).wait_recv()

    def rs_rows(g, part):
        strip, one, two = RS_CUTS[g]
        return pl.ds((0, strip, strip + one, strip)[part], (strip, one, two, one + two)[part])

    def rs_part(g, part):
        _, one, two = RS_CUTS[g]
        return pl.ds((0, 0, one, 0)[part], (0, one, two, one + two)[part])

    def rs_first(g):
        one, two = rs_part(g, 1), rs_part(g, 2)
        rs_send(g, 0, wts.at[g, nx, :, ny, rs_rows(g, 1)], rdx.at[g, :, one], to_x)
        rs_send(g, 1, wts.at[g, nx, :, ny, rs_rows(g, 2)], rdy.at[g, :, pl.ds(0, RS_CUTS[g][2])], to_y)
        rs_send(g, 2, wts.at[g, nx, :, y, rs_rows(g, 1)], rxx.at[g, :, one], to_x)

    def rs_second(g):
        rs_send(g, 3, wts.at[g, x, :, ny, rs_rows(g, 2)], ryy.at[g, :, rs_part(g, 2)], to_y)

    def rs_third(g):
        one, two = rs_part(g, 1), rs_part(g, 2)
        far = pl.ds(0, RS_CUTS[g][2])
        rs_wait(g, 0, rdx.at[g, :, one], to_x)

        def add_x(i):
            here = rs_rows(g, 1)
            wts[g, x, i, ny, here] = (wts[g, x, i, ny, here].astype(F32) + rdx[g, i, one].astype(F32)).astype(BF)

        loop(4, add_x)
        rs_send(g, 4, wts.at[g, x, :, ny, rs_rows(g, 1)], ryy.at[g, :, one], to_y)
        rs_wait(g, 1, rdy.at[g, :, far], to_y)

        def add_y(i):
            here = rs_rows(g, 2)
            wts[g, nx, i, y, here] = (wts[g, nx, i, y, here].astype(F32) + rdy[g, i, far].astype(F32)).astype(BF)

        loop(4, add_y)
        rs_send(g, 5, wts.at[g, nx, :, y, rs_rows(g, 2)], rxx.at[g, :, two], to_x)

    def plane(g, zz):
        rest, here = rs_rows(g, 3), rs_part(g, 3)
        return wts[g, x, zz, y, rest].astype(F32) + rxx[g, zz, here].astype(F32) + ryy[g, zz, here].astype(F32)

    def rs_fourth(g):
        one, two, both, rest = rs_part(g, 1), rs_part(g, 2), rs_part(g, 3), rs_rows(g, 3)
        rs_wait(g, 2, rxx.at[g, :, one], to_x)
        rs_wait(g, 3, ryy.at[g, :, two], to_y)
        rs_wait(g, 4, ryy.at[g, :, one], to_y)
        rs_wait(g, 5, rxx.at[g, :, two], to_x)
        for k in (2, 3):
            wts[g, x, zk[k], y, rest] = plane(g, zk[k]).astype(BF)
            rs_send_if(
                1, g, k - 2, wts.at[g, x, zk[k], y, rest], rzf.at[g, k - 2, both], to_zk[1], rf_r.at[g, k - 2]
            )
        wts[g, x, zk[1], y, rest] = plane(g, zk[1]).astype(BF)
        rs_send(g, 6, wts.at[g, x, zk[1], y, rest], rz.at[g, 0, both], to_zk[1])

    def rs_fifth(g):
        both, rest = rs_part(g, 3), rs_rows(g, 3)

        @pl.when(outer == 0)
        def _():
            for k in (2, 3):
                copy(
                    rzf.at[g, k - 2, both], rzf.at[g, k - 2, both], rf_s.at[g, 0], rf_r.at[g, k - 2], to_zk[1]
                ).wait_recv()
                wts[g, x, zk[k], y, rest] = (
                    wts[g, x, zk[k], y, rest].astype(F32) + rzf[g, k - 2, both].astype(F32)
                ).astype(BF)

        for k in (2, 3):
            rs_send_if(
                0, g, k, wts.at[g, x, zk[k], y, rest], rz.at[g, 1, both], to_zk[k], rs_r.at[g, 7]
            )

    def strips(g, zz):
        return wts.at[g, :, zz, :, pl.ds(0, RS_CUTS[g][0])]

    def rs_strip_z(g):
        here = pl.ds(0, RS_CUTS[g][0])
        for k in (2, 3):
            rs_send_if(1, g, 2 + k, strips(g, zk[k]), rzf2.at[g, k - 2, :, :, here], to_zk[1], rf_r.at[g, k])
        rs_send(g, 8, strips(g, zk[1]), rz2.at[g, 0, :, :, here], to_zk[1])

    def rs_strip_fwd(g):
        here = pl.ds(0, RS_CUTS[g][0])

        @pl.when(outer == 0)
        def _():
            for k in (2, 3):
                held = rzf2.at[g, k - 2, :, :, here]
                copy(held, held, rf_s.at[g, 0], rf_r.at[g, k], to_zk[1]).wait_recv()
                wts[g, :, zk[k], :, here] = (
                    wts[g, :, zk[k], :, here].astype(F32) + rzf2[g, k - 2, :, :, here].astype(F32)
                ).astype(BF)

        for k in (2, 3):
            rs_send_if(0, g, 4 + k, strips(g, zk[k]), rz2.at[g, 1, :, :, here], to_zk[k], rs_r.at[g, 9])

    def rs_strip_xy(g):
        here = pl.ds(0, RS_CUTS[g][0])
        for k in (0, 1):
            rs_wait(g, 8 + k, rz2.at[g, k, :, :, here], to_zk[1 + k])
        wts[g, :, z, :, here] = (
            wts[g, :, z, :, here].astype(F32)
            + rz2[g, 0, :, :, here].astype(F32)
            + rz2[g, 1, :, :, here].astype(F32)
        ).astype(BF)
        for i, (xx, yy, device) in enumerate(((nx, y, to_x), (x, ny, to_y), (nx, ny, to_xy))):
            rs_send(g, 10 + i, wts.at[g, xx, z, yy, here], rst.at[g, i, here], device)

    def rs_total(g):
        here, both = pl.ds(0, RS_CUTS[g][0]), rs_part(g, 3)
        for k in (0, 1):
            rs_wait(g, 6 + k, rz.at[g, k, both], to_zk[1 + k])
        for i, device in enumerate((to_x, to_y, to_xy)):
            rs_wait(g, 10 + i, rst.at[g, i, here], device)
        strip = wts[g, x, z, y, here].astype(F32)
        for i in range(3):
            strip = strip + rst[g, i, here].astype(F32)
        total = plane(g, z)
        for k in range(2):
            total = total + rz[g, k, both].astype(F32)
        return jnp.concatenate([strip, total], axis=0)

    def ff_grad(g, turned, held, xx):
        def body(j):
            n, i = j // 2, j % 2
            cols = pl.ds(mul8(n * 256, 256), 256)
            wide = pl.ds(mul8(xx * WIDE + n * 256, 256), 256)
            got = nn(turned[pl.ds(mul8(i * HERE, HERE), HERE), :], held[:, wide])
            wts[g, xx, pl.ds(i * 2, 2), :, :, cols] = got.reshape(2, 2, PIECE, 256).astype(BF)

        loop(6, body)

    ff_grad(2, rowt, aq, nx)
    rs_first(2)
    ff_grad(2, rowt, aq, x)
    rs_second(2)
    rs_strip_z(2)

    for xx in range(2):

        def hidden_grad(j, xx=xx):
            n, i = j // 2, j % 2
            cols = pl.ds(mul8(n * 256, 256), 256)
            wide = pl.ds(mul8(xx * WIDE + n * 256, 256), 256)
            rows = pl.ds(mul8(i * 256, 256), 256)
            got = (nn(gf[rows, :], wff[1, xx, :, cols]) * fac[rows, wide].astype(F32)).astype(BF)
            gu[rows, wide] = got
            tot[0, 6 + xx : 7 + xx, cols] += sum_rows(got.astype(F32))

        loop(6, hidden_grad)
    ff_grad(1, hqt, gu, nx)
    rs_first(1)
    ff_grad(1, hqt, gu, x)
    rs_second(1)
    rs_strip_z(1)

    def up_part(start, held):
        def body(n):
            cols = pl.ds(mul8(n * 256, 256), 256)
            held[:, cols] = nt(gu[pl.ds(start, OWN), 0:WIDE], wff[0, 0, cols, :]) + nt(
                gu[pl.ds(start, OWN), WIDE : 2 * WIDE], wff[0, 1, cols, :]
            )

        loop(3, body)

    up_part(theirs, exa_s)
    ex3 = copy(exa_s, exa_r, ex_s.at[4], ex_r.at[4], to_c)
    ex3.start()
    up_part(mine, r1)
    rs_third(2)
    ex3.wait()

    def first_back(i):
        rows = pl.ds(mul8(i * 64, 64), 64)
        normed = n1[rows, :]
        gh = (r1[rows, :] + exa_r[rows, :]) * sl1[rows, :]
        tot[0, 2:3, :] += sum_rows(gh * normed)
        tot[0, 3:4, :] += sum_rows(gh)
        gn = gh * vec[2:3, :]
        back = rstd1[rows, :] * (gn - mean_of(gn) - normed * mean_of(gn * normed)) + gr2[rows, :]
        gr2[rows, :] = back
        low = back.astype(BF)
        tot[0, 0:1, :] += sum_rows(low.astype(F32))
        gf[pl.ds(mul8(mine + i * 64, 64), 64), :] = low

    sent("share")
    loop(4, first_back)
    share_rows(gf, 5)
    turn_rows(gf, rowt, mine)
    got_rows(gf, 5)
    turn_rows(gf, rowt, theirs)

    def out_grad(i):
        rows = pl.ds(mul8(i * 256, 256), 256)
        gwo[rows, :] = nn(rowt[rows, :], cq[...])

    loop(3, out_grad)

    def ctx_grad(i):
        rows = pl.ds(mul8(i * 256, 256), 256)
        gc[rows, :] = (nn(gf[rows, :], wo[...]) * slc[rows, :]).astype(BF)

    loop(2, ctx_grad)
    for p in range(3):
        cols = slice(p * 128, p * 128 + 128)
        gct[cols, :] = gc[:, cols].T
        for e in range(2):
            feats = slice(p * 128 + e * 64, p * 128 + e * 64 + 64)
            dsum[p * 2 + e : p * 2 + e + 1, :] = sum_rows(gct[feats, :].astype(F32) * ctxt[feats, :])
    rs_strip_fwd(2)

    row_half = lax.broadcasted_iota(jnp.int32, (128, 1), 0) // 64

    def attend_back(p):
        cols = pl.ds(mul8(p * 128, 128), 128)
        grad_k = grad_v = None
        for e in range(2):
            feats = pl.ds(mul8(p * 128 + e * 64, 64), 64)
            for n in range(2):
                part = slice(n * 256, n * 256 + 256)
                g = gct[cols, part]
                g = jnp.where(row_half == e, g, jnp.zeros_like(g))
                dpr = nn(vs[:, cols], g)
                ds[:, part] = (probs[p * 2 + e, :, part].astype(F32) * (dpr - dsum[pl.ds(p * 2 + e, 1), part])).astype(BF)
            g = gc[:, cols]
            g = jnp.where(half_of == e, g, jnp.zeros_like(g))
            more_v = nn(probs[p * 2 + e], g)
            q = qs[:, cols]
            q = jnp.where(half_of == e, q, jnp.zeros_like(q))
            more_k = nn(ds[...], q)
            grad_v = more_v if e == 0 else grad_v + more_v
            grad_k = more_k if e == 0 else grad_k + more_k
            gqt[feats, :] = nn(kt[feats, :], ds[...])
        grads[:, pl.ds(mul8(HERE + p * 128, 128), 128)] = grad_k.astype(BF)
        grads[:, pl.ds(mul8(2 * HERE + p * 128, 128), 128)] = grad_v.astype(BF)
        grads[:, cols] = (gqt[cols, :].astype(BF).astype(F32) * 0.125).T.astype(BF)

    attend_back(0)
    attend_back(1)
    attend_back(2)
    rs_third(1)
    for j, part in ((0, 0), (2, HERE)):
        tot[0, 8:9, part : part + HERE] = sum_rows(grads[:, j * HERE : (j + 1) * HERE].astype(F32))

    left_two = lax.broadcasted_iota(jnp.int32, (2 * PIECE, 128), 1) < 64

    def head_grad(i):
        rows = pl.ds(mul8(i * 2 * PIECE, 2 * PIECE), 2 * PIECE)
        gq, gk, gv = (nn(xqt[rows, :], grads[:, j * HERE : (j + 1) * HERE]) for j in range(3))
        parts = (gq, gk, gv, gwo[rows, :])

        def put(xx, t, v):
            wts[0, xx, i, :, :, t * 128 : t * 128 + 128] = v.reshape(2, PIECE, 128).astype(BF)

        for xx in range(2):
            for t in range(4):
                put(xx, t, parts[t][:, xx * 128 : xx * 128 + 128])
        for t, first, second in ((4, gq, gk), (5, gv, gwo[rows, :])):
            one, two = first[:, 256:384], second[:, 256:384]
            put(0, t, jnp.where(left_two, one, pltpu.roll(two, 64, 1)))
            put(1, t, jnp.where(left_two, pltpu.roll(one, 64, 1), two))

    loop(4, head_grad)

    def most_x(i):
        v = jnp.abs(tok[pl.ds(mul8(base + i * 128, 128), 128), :].astype(F32))
        tot[0, 9:10, :] = jnp.maximum(tot[0, 9:10, :], jnp.max(v, axis=0, keepdims=True))

    loop(4, most_x)
    row_of = lax.broadcasted_iota(jnp.int32, (16, 1), 0)
    small = copy(tot.at[0], tot_c, tt_s.at[0], tt_r.at[0], to_c)
    small.start()
    rs_first(0)
    rs_second(0)
    rs_strip_z(0)

    def token_part(start, held):
        def body(n):
            cols = pl.ds(mul8(n * 256, 256), 256)
            held[:, cols] = nt(grads[pl.ds(start, OWN), :], wc[cols, :])

        loop(3, body)

    token_part(theirs, exb_s)
    ex4 = copy(exb_s, exb_r, ex_s.at[6], ex_r.at[6], to_c)
    ex4.start()
    small.wait()
    mixed = jnp.where(row_of < 6, tot[0] + tot_c[...], jnp.maximum(tot[0], tot_c[...]))
    tot[1] = jnp.where((row_of >= 6) & (row_of < 9), tot[0], mixed)
    small = copy(tot.at[1], tot_x, tt_s.at[1], tt_r.at[1], to_x)
    small.start()
    token_part(mine, r1)
    rs_fourth(2)
    rs_strip_fwd(1)
    rs_strip_xy(2)
    rs_fifth(2)
    ex4.wait()

    def token_grad(i):
        rows = pl.ds(mul8(i * 64, 64), 64)
        v = tok[pl.ds(mul8(base + mine + i * 64, 64), 64), :].astype(F32)
        bent = jnp.tanh(v * inv_of[0])
        got = gr2[rows, :] + (r1[rows, :] + exb_r[rows, :]) * (1.0 - bent * bent)
        o_tok[pl.ds(mul8(mp * OWN + i * 64, 64), 64), :] = got.astype(BF)

    loop(4, token_grad)
    rs_third(0)
    own = o_tok.at[pl.ds(mul8(mp * OWN, OWN), OWN)]
    send("tok", own, own, gx_s.at[1], gx_r.at[1], to_c)
    send("tok", own, own, gx_s.at[0], gx_r.at[0], to_x)
    rs_strip_fwd(0)
    small.wait()
    tot[2] = jnp.where(row_of < 9, tot[1] + tot_x[...], jnp.maximum(tot[1], tot_x[...]))
    small = copy(tot.at[2], tot_y, tt_s.at[2], tt_r.at[2], to_y)
    small.start()
    rs_fourth(1)
    rs_strip_xy(1)
    rs_fifth(1)
    rs_strip_xy(0)
    small.wait()
    tot[3] = jnp.where(row_of < 9, tot[2] + tot_y[...], jnp.maximum(tot[2], tot_y[...]))
    smalls = []
    for k in (1, 2, 3):
        made = copy(tot.at[3], tot_z.at[k - 1], tt_s.at[2 + k], tt_r.at[2 + k], to_z[k])
        made.start()
        smalls.append(made)
    o_down[...] = rs_total(2) * _slope(w_down[...], w_inv[3])
    rs_fourth(0)
    rs_fifth(0)
    o_up[...] = rs_total(1) * _slope(w_up[...], w_inv[2])

    far = o_tok.at[pl.ds(mul8((nx * 2 + c) * OWN, OWN), OWN)]
    copy(far, far, gx_s.at[0], gx_r.at[0], to_x).wait_recv()
    send("tok", far, far, gx_s.at[2], gx_r.at[2], to_c)

    for made in smalls:
        made.wait()
    done = tot[3]
    for k in range(3):
        done = jnp.where(row_of < 9, done + tot_z[k], jnp.maximum(done, tot_z[k]))
    back = pltpu.roll(done, (8 - dp) * 96, 1)
    o_vec[...] = back[0:6, 0:96]
    ups = jnp.where(x == 0, done[6:7, :], done[7:8, :])
    for h in range(3):
        tile = jnp.broadcast_to(ups[:, h * 256 : h * 256 + 256], (8, 256))
        o_bup[h : h + 1, :] = pltpu.roll(tile, (8 - dp) * 32, 1)[0:1, 0:32]
    for j in range(2):
        row = jnp.broadcast_to(done[8:9, j * HERE : (j + 1) * HERE], (8, HERE))
        pair = jnp.where(x == 0, row[:, 0:128], row[:, 128:256])
        for h, tile, shift in ((0, pair, 0), (1, pair, 64), (2, row[:, 256:384], 64 * x)):
            o_bqv[h, j : j + 1, :] = pltpu.roll(tile, (256 - shift - dp * 8) % 128, 1)[0:1, 0:8]
    for i in range(4):
        o_rng[i] = 0.9 * range_of[i] + 0.1 * jnp.max(done[9 + i : 10 + i, :])

    total = rs_total(0)
    for j in range(4):
        main = total[:, j * 128 : j * 128 + 128]
        pair = total[:, 512 + j // 2 * 128 : 640 + j // 2 * 128]
        if j % 2:
            pair = pltpu.roll(pair, 64, 1)
        whole = jnp.concatenate([main, pair], axis=1)[:, 0:192]
        if j < 3:
            o_qkv[j] = whole * _slope(w_qkv[j], w_inv[0])
        else:
            o_out[...] = whole.T * _slope(w_out[...], w_inv[1])
    near = o_tok.at[pl.ds(mul8((x * 2 + nc) * OWN, OWN), OWN)]
    copy(near, near, gx_s.at[1], gx_r.at[1], to_c).wait_recv()
    far = o_tok.at[pl.ds(mul8((nx * 2 + nc) * OWN, OWN), OWN)]
    copy(far, far, gx_s.at[2], gx_r.at[2], to_c).wait_recv()
    for group in list(started):
        sent(group)


def _slope(values, inverse):
    bent = jnp.tanh(values.astype(F32) * inverse)
    return 1.0 - bent * bent


def layer_on_chips(
    tokens, w_qkv, w_out, w_up, w_down, b_qv, b_up, vectors, ema_ranges, key_mask, long_rows, grad_out
):
    vmem = pltpu.VMEM
    rows = tokens.shape[0]
    half = rows // 2

    def buffer(*shape, dtype=BF):
        return vmem(shape, dtype)

    def f32(*shape):
        return vmem(shape, F32)

    sems = pltpu.SemaphoreType.DMA
    scratch = [
        buffer(3, 2, 4, 2, PIECE, WIDE),
        buffer(2, 2, WIDE, WIDE),
        buffer(WIDE, 3 * HERE),
        buffer(WIDE, HERE),
        buffer(3, 4, 48, WIDE),
        buffer(3, 4, 32, WIDE),
        buffer(3, 4, 80, WIDE),
        buffer(3, 4, 80, WIDE),
        buffer(3, 2, 80, WIDE),
        buffer(3, 2, 80, WIDE),
        buffer(3, 2, 2, 2, 32, WIDE),
        buffer(3, 2, 2, 2, 32, WIDE),
        buffer(3, 3, 32, WIDE),
        f32(2, 4, 2, 16, 128),
        f32(16, 128),
        f32(16, WIDE),
        f32(8, WIDE),
        f32(8, HERE),
        buffer(half, WIDE),
        buffer(WIDE, half),
        f32(half, half),
        buffer(half, HERE),
        buffer(half, HERE),
        buffer(half, HERE),
        buffer(HERE, half),
        buffer(HERE, half),
        buffer(6, half, half),
        buffer(half, half),
        f32(HERE, half),
        buffer(half, HERE),
        f32(half, HERE),
        f32(OWN, WIDE),
        f32(OWN, WIDE),
        f32(OWN, WIDE),
        f32(OWN, WIDE),
        buffer(half, WIDE),
        buffer(WIDE, half),
        f32(OWN, WIDE),
        f32(OWN, WIDE),
        f32(OWN, 1),
        f32(OWN, WIDE),
        buffer(half, 2 * WIDE),
        buffer(half, 2 * WIDE),
        buffer(half, 2 * WIDE),
        buffer(half, WIDE),
        buffer(WIDE, half),
        f32(OWN, WIDE),
        buffer(half, HERE),
        buffer(HERE, half),
        f32(8, half),
        buffer(half, 3 * HERE),
        f32(HERE, half),
        f32(WIDE, HERE),
        f32(4, 16, WIDE),
        f32(16, WIDE),
        f32(16, WIDE),
        f32(16, WIDE),
        f32(3, 16, WIDE),
        sems((3, 2)),
        sems((3, 2)),
        sems((3, 3)),
        sems((3, 2)),
        sems((3, 2)),
        sems((3, 3)),
        sems((3, 3)),
        sems((3, 3)),
        sems((3, 4)),
        sems((3, 4)),
        sems((3, 4)),
        sems((3, 4)),
        sems((3, 4)),
        sems((3, 4)),
        sems((3, 4)),
        sems((3, 4)),
        sems((3, 13)),
        sems((3, 13)),
        sems((3, 8)),
        sems((3, 4)),
        sems((6,)),
        sems((6,)),
        sems((7,)),
        sems((7,)),
        sems((6,)),
        sems((6,)),
        sems((3,)),
        sems((3,)),
    ]
    whole = pl.BlockSpec(memory_space=vmem)
    scalars = pl.BlockSpec(memory_space=pltpu.SMEM)
    shape = jax.ShapeDtypeStruct
    outs = pl.pallas_call(
        layer_kernel,
        out_shape=[
            shape(grad_out.shape, BF),
            shape(tokens.shape, BF),
            shape(w_qkv.shape, F32),
            shape(w_out.shape, F32),
            shape(w_up.shape, F32),
            shape(w_down.shape[::-1], F32),
            shape((b_qv.shape[1], b_qv.shape[0], b_qv.shape[2]), F32),
            shape(b_up.shape, F32),
            shape(vectors.shape, F32),
            shape(ema_ranges.shape, F32),
        ],
        in_specs=[whole] * 8 + [scalars, whole, scalars, whole],
        out_specs=[whole] * 9 + [scalars],
        scratch_shapes=scratch,
        compiler_params=pltpu.CompilerParams(
            collective_id=0, has_side_effects=True, vmem_limit_bytes=VMEM_LIMIT
        ),
        name="encoder_layer",
    )(
        tokens,
        w_qkv,
        w_out,
        w_up,
        w_down.T,
        b_qv.transpose(1, 0, 2),
        b_up,
        vectors,
        ema_ranges,
        key_mask.reshape(rows // 128, 128),
        long_rows,
        grad_out,
    )
    outs = finish(outs)
    return (*outs[:5], outs[5].T, outs[6].transpose(1, 0, 2), *outs[7:])


def finish_kernel(*refs):
    ins, outs, held, wide, sem = refs[:10], refs[10:20], refs[20:29], refs[29], refs[30]
    parts = [pl.ds(i * OWN, OWN) for i in range(ins[1].shape[0] // OWN)]
    arriving = [pltpu.make_async_copy(ins[1].at[p], held[1].at[p], sem.at[9 + i]) for i, p in enumerate(parts)]
    moved = [i for i in range(9) if i != 1]
    arriving += [pltpu.make_async_copy(ins[i], held[i], sem.at[i]) for i in moved]
    leaving = [pltpu.make_async_copy(wide.at[p], outs[1].at[p], sem.at[9 + i]) for i, p in enumerate(parts)]
    leaving += [pltpu.make_async_copy(held[i], outs[i], sem.at[i]) for i in moved]
    for made in arriving:
        made.start()
    for i in range(4):
        outs[9][i] = ins[9][i]
    for i, (here, there) in enumerate(zip(arriving, leaving)):
        here.wait()
        if i < len(parts):
            wide[parts[i], :] = held[1][parts[i], :].astype(F32)
        there.start()
    for made in leaving:
        made.wait()


def finish(held):
    shape = jax.ShapeDtypeStruct
    far = pl.BlockSpec(memory_space=pltpu.HBM)
    scalars = pl.BlockSpec(memory_space=pltpu.SMEM)
    return pl.pallas_call(
        finish_kernel,
        out_shape=[shape(v.shape, F32 if i == 1 else v.dtype) for i, v in enumerate(held)],
        in_specs=[far] * 9 + [scalars],
        out_specs=[far] * 9 + [scalars],
        scratch_shapes=[pltpu.VMEM(v.shape, v.dtype) for v in held[:9]]
        + [pltpu.VMEM(held[1].shape, F32), pltpu.SemaphoreType.DMA((9 + held[1].shape[0] // OWN,))],
        compiler_params=pltpu.CompilerParams(vmem_limit_bytes=VMEM_LIMIT),
        name="write_results",
    )(*held)


VMEM_LIMIT = 64 * 1024 * 1024


def solution(mesh):
    placed = (
        P("dp", None),
        P(None, "dp", "mp"),
        P("mp", "dp"),
        P("dp", "mp"),
        P("mp", "dp"),
        P(None, "mp", "dp"),
        P("mp", "dp"),
        P(None, "dp"),
        P(),
        P("dp"),
        P("dp"),
        P(("dp", "mp"), None),
    )
    on_chips = dict(mesh.shape) == {"dp": 8, "mp": 4}
    return jax.shard_map(
        layer_on_chips if on_chips else per_device,
        mesh=mesh,
        in_specs=placed,
        out_specs=(
            P(("dp", "mp"), None),
            P("dp", None),
            P(None, "dp", "mp"),
            P("mp", "dp"),
            P("dp", "mp"),
            P("mp", "dp"),
            P(None, "mp", "dp"),
            P("mp", "dp"),
            P(None, "dp"),
            P(),
        ),
        check_vma=False,
    )
```

```python
import jax
import jax.numpy as jnp
from jax import lax
from jax.experimental import pallas as pl
from jax.experimental.pallas import tpu as pltpu
from jax.sharding import PartitionSpec as P

HD = 64
BLOCK = 512
SEG = 128


eps_norm = 1e-12
root_half = 0.7071067811865476
inv_root_tau = 0.3989422804014327


def squash(values, limit):
    return limit * jnp.tanh(values / limit)


def slope(values, limit):
    bent = jnp.tanh(values / limit)
    return 1.0 - bent * bent


def peak_of(values):
    return jnp.max(jnp.abs(values.astype(jnp.float32)))


def product(left, right):
    return jnp.dot(left, right, preferred_element_type=jnp.float32)


def contract_rows(left, right):
    return lax.dot_general(
        left, right, (((0,), (0,)), ((), ())), preferred_element_type=jnp.float32
    )


def contract_cols(left, right):
    return lax.dot_general(
        left, right, (((1,), (1,)), ((), ())), preferred_element_type=jnp.float32
    )


def normalize(values):
    center = values - jnp.mean(values, axis=-1, keepdims=True)
    factor = lax.rsqrt(jnp.mean(center * center, axis=-1, keepdims=True) + eps_norm)
    return (center * factor, factor)


def norm_back(grad_normed, normed, factor):
    first_mean = jnp.mean(grad_normed, axis=-1, keepdims=True)
    cross_mean = jnp.mean(grad_normed * normed, axis=-1, keepdims=True)
    return factor * (grad_normed - first_mean - normed * cross_mean)


def allowed_keys(live, long_flag):
    places = jnp.arange(BLOCK) // SEG
    return (live[None, :] > 0) & ((long_flag > 0) | (places[:, None] == places[None, :]))


def block_scores(queries, keys_in, live, long_flag):
    scores = jnp.einsum("qhd,khd->hqk", queries, keys_in, preferred_element_type=jnp.float32)
    return jnp.where(allowed_keys(live, long_flag)[None], scores, -1e30)


def attend_block(pieces):
    queries, keys_in, values, live, long_flag = pieces
    scores = block_scores(queries, keys_in, live, long_flag)
    top_score = jnp.max(scores, axis=-1, keepdims=True)
    weights = jnp.exp(scores - top_score)
    totals = jnp.sum(weights, axis=-1, keepdims=True)
    attn_probs = (weights / totals).astype(jnp.bfloat16)
    context = jnp.einsum("hqk,khd->qhd", attn_probs, values, preferred_element_type=jnp.float32)
    return (context, top_score + jnp.log(totals))


def attend_back(pieces):
    queries, keys_in, values, live, long_flag, log_total, grad_ctx = pieces
    attn_probs = jnp.exp(block_scores(queries, keys_in, live, long_flag) - log_total)
    grad_probs = jnp.einsum("qhd,khd->hqk", grad_ctx, values, preferred_element_type=jnp.float32)
    grad_values = jnp.einsum(
        "hqk,qhd->khd",
        attn_probs.astype(jnp.bfloat16),
        grad_ctx,
        preferred_element_type=jnp.float32,
    )
    inner = jnp.sum(grad_probs * attn_probs, axis=-1, keepdims=True)
    grad_scores = (attn_probs * (grad_probs - inner)).astype(jnp.bfloat16)
    grad_queries = jnp.einsum(
        "hqk,khd->qhd", grad_scores, keys_in, preferred_element_type=jnp.float32
    )
    grad_keys = jnp.einsum("hqk,qhd->khd", grad_scores, queries, preferred_element_type=jnp.float32)
    return (
        grad_queries.astype(jnp.bfloat16),
        grad_keys.astype(jnp.bfloat16),
        grad_values.astype(jnp.bfloat16),
    )


def prepare(gathered, w_peaks):
    return tuple(
        (
            squash(gathered[index].astype(jnp.float32), w_peaks[index]).astype(jnp.bfloat16)
            for index in range(4)
        )
    )


def peak_all(values):
    return lax.pmax(peak_of(values), ("dp", "mp"))


def per_device(
    tokens,
    w_qkv,
    w_out,
    w_up,
    w_down,
    b_qv,
    b_up,
    vectors,
    ema_ranges,
    key_mask,
    long_rows,
    grad_out,
):
    row_count = tokens.shape[0]
    quarter = row_count // lax.axis_size("mp")
    row_start = lax.axis_index("mp") * quarter
    blocks = row_count // BLOCK
    w_peaks = lax.pmax(
        (peak_of(w_qkv), peak_of(w_out), peak_of(w_up), peak_of(w_down)), ("dp", "mp")
    )
    gathered = (
        lax.all_gather(w_qkv, "dp", axis=1, tiled=True),
        lax.all_gather(w_out, "dp", axis=1, tiled=True),
        lax.all_gather(w_up, "dp", axis=0, tiled=True),
        lax.all_gather(w_down, "dp", axis=1, tiled=True),
        lax.all_gather(b_qv, "dp", axis=2, tiled=True),
        lax.all_gather(b_up, "dp", axis=1, tiled=True),
        lax.all_gather(vectors, "dp", axis=1, tiled=True),
    )
    qkv_q, out_q, up_q, down_q = prepare(gathered, w_peaks)
    bias_qv = gathered[4].astype(jnp.float32).reshape(2, -1)
    bias_up = gathered[5].astype(jnp.float32).reshape(-1)
    vec = gathered[6].astype(jnp.float32)
    head_width = bias_qv.shape[1]
    heads_here = head_width // HD
    scale_q = HD ** (-0.5)
    tok_float = tokens.astype(jnp.float32)
    peak_tok = peak_all(tok_float)
    tok_quant = squash(tok_float, ema_ranges[0]).astype(jnp.bfloat16)
    projected = jnp.einsum("td,jde->jte", tok_quant, qkv_q, preferred_element_type=jnp.float32)
    queries = ((projected[0] + bias_qv[0]) * scale_q).astype(jnp.bfloat16)
    keys_all = projected[1].astype(jnp.bfloat16)
    values = (projected[2] + bias_qv[1]).astype(jnp.bfloat16)
    shape_four = (blocks, BLOCK, heads_here, HD)
    mask_blocks = key_mask.reshape(blocks, BLOCK)
    block_inputs = (
        queries.reshape(shape_four),
        keys_all.reshape(shape_four),
        values.reshape(shape_four),
        mask_blocks,
        long_rows,
    )
    context, log_total = lax.map(attend_block, block_inputs)
    context = context.reshape(row_count, head_width)
    peak_ctx = peak_all(context)
    ctx_quant = squash(context, ema_ranges[1]).astype(jnp.bfloat16)
    partial_attn = product(ctx_quant, out_q)
    attn = lax.psum_scatter(partial_attn, "mp", scatter_dimension=0, tiled=True) + vec[0]
    first_own = lax.dynamic_slice_in_dim(tok_float, row_start, quarter, 0) + attn
    normed, factor_one = normalize(first_own)
    hidden_in = normed * vec[2] + vec[3]
    hid_quant = lax.all_gather(
        squash(hidden_in, ema_ranges[2]).astype(jnp.bfloat16), "mp", axis=0, tiled=True
    )
    peak_hid = peak_all(hidden_in)
    pre_act = product(hid_quant, up_q) + bias_up
    active = pre_act * 0.5 * (1.0 + lax.erf(pre_act * root_half))
    peak_act = peak_all(active)
    act_quant = squash(active, ema_ranges[3]).astype(jnp.bfloat16)
    branch = (
        lax.psum_scatter(product(act_quant, down_q), "mp", scatter_dimension=0, tiled=True) + vec[1]
    )
    second = first_own + branch
    normed_two, factor_two = normalize(second)
    layer_out = (normed_two * vec[4] + vec[5]).astype(jnp.bfloat16)
    new_ranges = 0.9 * ema_ranges + 0.1 * jnp.stack([peak_tok, peak_ctx, peak_hid, peak_act])
    gathered = (
        lax.all_gather(w_qkv, "dp", axis=1, tiled=True),
        lax.all_gather(w_out, "dp", axis=1, tiled=True),
        lax.all_gather(w_up, "dp", axis=0, tiled=True),
        lax.all_gather(w_down, "dp", axis=1, tiled=True),
        lax.all_gather(b_qv, "dp", axis=2, tiled=True),
        lax.all_gather(b_up, "dp", axis=1, tiled=True),
        lax.all_gather(vectors, "dp", axis=1, tiled=True),
    )
    qkv_q, out_q, up_q, down_q = prepare(gathered, w_peaks)
    grad_y = grad_out.astype(jnp.float32)
    grad_gain_two = jnp.sum(grad_y * normed_two, axis=0)
    grad_shift_two = jnp.sum(grad_y, axis=0)
    grad_second = norm_back(grad_y * vec[4], normed_two, factor_two)
    grad_resid = lax.all_gather(grad_second.astype(jnp.bfloat16), "mp", axis=0, tiled=True).astype(
        grad_second.dtype
    )
    grad_branch = grad_resid.astype(jnp.bfloat16)
    grad_bias_down = jnp.sum(grad_branch.astype(jnp.float32), axis=0)
    grad_down_w = contract_rows(act_quant, grad_branch)
    grad_active = contract_cols(grad_branch, down_q) * slope(active, ema_ranges[3])
    normal_cdf = 0.5 * (1.0 + lax.erf(pre_act * root_half))
    normal_pdf = inv_root_tau * jnp.exp(-0.5 * pre_act * pre_act)
    grad_pre = (grad_active * (normal_cdf + pre_act * normal_pdf)).astype(jnp.bfloat16)
    grad_bias_up = jnp.sum(grad_pre.astype(jnp.float32), axis=0)
    grad_up_w = contract_rows(hid_quant, grad_pre)
    partial_hid = contract_cols(grad_pre, up_q)
    grad_hid_q = lax.psum_scatter(partial_hid, "mp", scatter_dimension=0, tiled=True)
    grad_hidden = grad_hid_q * slope(hidden_in, ema_ranges[2])
    grad_gain_one = jnp.sum(grad_hidden * normed, axis=0)
    grad_shift_one = jnp.sum(grad_hidden, axis=0)
    grad_first = norm_back(grad_hidden * vec[2], normed, factor_one) + grad_second
    grad_attn = lax.all_gather(grad_first.astype(jnp.bfloat16), "mp", axis=0, tiled=True)
    grad_bias_out = jnp.sum(grad_attn.astype(jnp.float32), axis=0)
    grad_out_w = contract_rows(ctx_quant, grad_attn)
    grad_ctx = (contract_cols(grad_attn, out_q) * slope(context, ema_ranges[1])).astype(
        jnp.bfloat16
    )
    back_inputs = block_inputs + (log_total, grad_ctx.reshape(shape_four))
    grad_q, grad_k, grad_v = lax.map(attend_back, back_inputs)
    stacked = jnp.stack(
        [
            grad_q.reshape(row_count, head_width) * jnp.bfloat16(scale_q),
            grad_k.reshape(row_count, head_width),
            grad_v.reshape(row_count, head_width),
        ]
    )
    grad_qkv_w = jnp.einsum("td,jte->jde", tok_quant, stacked, preferred_element_type=jnp.float32)
    stacked_float = stacked.astype(jnp.float32)
    grad_bias_qv = jnp.stack([jnp.sum(stacked_float[0], axis=0), jnp.sum(stacked_float[2], axis=0)])
    part_input = jnp.einsum("jte,jde->td", stacked, qkv_q, preferred_element_type=jnp.float32)
    own_term = part_input * slope(tok_float, ema_ranges[0])
    own_rows = lax.dynamic_slice_in_dim(own_term, row_start, quarter, 0) + grad_first
    own_term = lax.dynamic_update_slice_in_dim(own_term, own_rows, row_start, 0)
    grad_tokens, norm_tail = (
        lax.psum(own_term.astype(jnp.bfloat16), "mp").astype(jnp.float32),
        lax.psum(
            jnp.stack([grad_gain_one, grad_shift_one, grad_gain_two, grad_shift_two]).astype(
                jnp.bfloat16
            ),
            "mp",
        ).astype(jnp.float32),
    )
    grad_vec = jnp.stack(
        [grad_bias_out, grad_bias_down, norm_tail[0], norm_tail[1], norm_tail[2], norm_tail[3]]
    )
    summed = (
        lax.psum_scatter(
            grad_qkv_w * slope(gathered[0].astype(jnp.float32), w_peaks[0]),
            "dp",
            scatter_dimension=1,
            tiled=True,
        ),
        lax.psum_scatter(
            grad_out_w * slope(gathered[1].astype(jnp.float32), w_peaks[1]),
            "dp",
            scatter_dimension=1,
            tiled=True,
        ),
        lax.psum_scatter(
            grad_up_w * slope(gathered[2].astype(jnp.float32), w_peaks[2]),
            "dp",
            scatter_dimension=0,
            tiled=True,
        ),
        lax.psum_scatter(
            grad_down_w * slope(gathered[3].astype(jnp.float32), w_peaks[3]),
            "dp",
            scatter_dimension=1,
            tiled=True,
        ),
        lax.psum_scatter(
            grad_bias_qv.reshape(gathered[4].shape), "dp", scatter_dimension=2, tiled=True
        ),
        lax.psum_scatter(
            grad_bias_up.reshape(gathered[5].shape), "dp", scatter_dimension=1, tiled=True
        ),
        lax.psum_scatter(grad_vec, "dp", scatter_dimension=1, tiled=True),
    )
    return (
        layer_out,
        grad_tokens,
        summed[0],
        summed[1],
        summed[2],
        summed[3],
        summed[4],
        summed[5],
        summed[6],
        new_ranges,
    )


BF = jnp.bfloat16
F32 = jnp.float32
MESH = pl.DeviceIdType.MESH
WIDE = 768
PIECE = 96
AG_CUTS = ((0, 48, 48), (16, 32, 48), (32, 32, 32))
RS_CUTS = ((16, 32, 48), (16, 32, 48), (32, 32, 32))
OWN = 256
HERE = 384


def nn(left, right):
    return lax.dot_general(left, right, (((1,), (0,)), ((), ())), preferred_element_type=F32)


def nt(left, right):
    return lax.dot_general(left, right, (((1,), (1,)), ((), ())), preferred_element_type=F32)


def mul8(value, step):
    return pl.multiple_of(value, step)


def loop(count, body):
    def step(index, carry):
        body(index)
        return carry

    lax.fori_loop(0, count, step, 0)


def layer_kernel(
    h_tok,
    h_qkv,
    h_out,
    h_up,
    h_down,
    h_bqv,
    h_bup,
    h_vec,
    ranges,
    h_mask,
    long_rows,
    h_grad,
    r_layer,
    r_tok,
    r_qkv,
    r_out,
    r_up,
    r_down,
    r_bqv,
    r_bup,
    r_vec,
    o_rng,
    tok,
    w_qkv,
    w_out,
    w_up,
    w_down,
    b_qv,
    b_up,
    vectors,
    mask,
    grad_out,
    o_layer,
    o_tok,
    o_qkv,
    o_out,
    o_up,
    o_down,
    o_bqv,
    o_bup,
    o_vec,
    wts,
    wff,
    wc,
    wo,
    rdx,
    rdy,
    rxx,
    ryy,
    rz,
    rzf,
    rz2,
    rzf2,
    rst,
    sm,
    smc,
    vec,
    bup,
    bqv,
    xq,
    xqt,
    bias,
    qs,
    ks,
    vs,
    kt,
    vt,
    probs,
    ds,
    ctxt,
    cq,
    slc,
    exa_s,
    exa_r,
    exb_s,
    exb_r,
    hq,
    hqt,
    r1,
    n1,
    rstd1,
    sl1,
    aq,
    fac,
    gu,
    gf,
    rowt,
    gr2,
    gc,
    gct,
    dsum,
    grads,
    gqt,
    gwo,
    tot,
    tot_c,
    tot_x,
    tot_y,
    tot_z,
    zs,
    zf,
    zr,
    z2s,
    z2f,
    z2r,
    sts,
    str_,
    xs,
    xr,
    ys,
    yr,
    dxs,
    dxr,
    dys,
    dyr,
    rs_s,
    rs_r,
    rf_s,
    rf_r,
    sm_s,
    sm_r,
    ex_s,
    ex_r,
    tt_s,
    tt_r,
    gx_s,
    gx_r,
    in_s,
    out_s,
):
    dp = lax.axis_index("dp")
    mp = lax.axis_index("mp")
    z, y = dp // 2, dp % 2
    x, c = mp // 2, mp % 2
    nx, ny, nc = 1 - x, 1 - y, 1 - c
    to_x = (dp, nx * 2 + c)
    to_y = (z * 2 + ny, mp)
    to_c = (dp, x * 2 + nc)
    to_xy = (z * 2 + ny, nx * 2 + c)
    to_z = [None] + [((z + k) % 4 * 2 + y, mp) for k in (1, 2, 3)]
    from_z = [z] + [(z + 4 - k) % 4 for k in (1, 2, 3)]
    zk = [z, z + 1 - 2 * (z % 2), 2 - z // 2, 3 - 3 * (z // 2)]
    outer = (z * z - 3 * z + 2) // 2
    to_zk = [None] + [(zk[k] * 2 + y, mp) for k in (1, 2, 3)]
    mine = mul8(c * OWN, OWN)
    theirs = mul8(nc * OWN, OWN)
    started = {}

    def copy(src, dst, send, recv, device):
        return pltpu.make_async_remote_copy(
            src_ref=src, dst_ref=dst, send_sem=send, recv_sem=recv, device_id=device, device_id_type=MESH
        )

    def send(group, *args):
        made = copy(*args)
        made.start()
        started.setdefault(group, []).append((made, None))

    def send_if(which, group, *args):
        made = copy(*args)
        pl.when(outer == which)(made.start)
        started.setdefault(group, []).append((made, which))

    def sent(group):
        for made, which in started.pop(group, []):
            if which is None:
                made.wait_send()
            else:
                pl.when(outer == which)(made.wait_send)

    base = mul8(x * 512, 512)
    arriving = [
        pltpu.make_async_copy(there, here, in_s.at[i])
        for i, (there, here) in enumerate(
            (
                (h_up, w_up),
                (h_down, w_down),
                (h_qkv, w_qkv),
                (h_out, w_out),
                (h_vec, vectors),
                (h_bup, b_up),
                (h_bqv, b_qv),
                (h_tok.at[pl.ds(base, 512)], tok),
                (h_mask, mask),
                (h_grad, grad_out),
            )
        )
    ]
    for made in arriving:
        made.start()
    leaving = []

    def leave(here, there):
        made = pltpu.make_async_copy(here, there, out_s.at[len(leaving)])
        made.start()
        leaving.append(made)

    range_of = [ranges[i] for i in range(4)]
    inv_of = [1.0 / r for r in range_of]

    barrier = pltpu.get_barrier_semaphore()
    for device in (to_c, to_x, to_y, to_xy, *to_z[1:]):
        pl.semaphore_signal(barrier, inc=1, device_id=device, device_id_type=MESH)
    for made in arriving[:7]:
        made.wait()
    wts[1, x, z, y] = w_up[...]
    wts[2, x, z, y] = w_down[...]
    turned = w_out[...].T
    for j, part in enumerate((w_qkv[0], w_qkv[1], w_qkv[2], turned)):
        wts[0, x, z, y, :, j * 128 : j * 128 + 128] = part[:, 0:128]
        wts[0, x, z, y, :, 512 + j * 64 : 576 + j * 64] = part[:, 128:192]

    sm[x, z, y] = jnp.zeros((16, 128), F32)
    sm[x, z, y, 0:6, 0:96] = vectors[...].astype(F32)
    sm[x, z, y, 6:9, 0:32] = b_up[...].astype(F32)
    sm[x, z, y, 9:12, 0:8] = b_qv[:, 0, :].astype(F32)
    sm[x, z, y, 12:15, 0:8] = b_qv[:, 1, :].astype(F32)
    lane = lax.broadcasted_iota(jnp.int32, (1, 128), 1)
    peak_row = jnp.zeros((1, 128), F32)
    for g, ref in enumerate((w_qkv, w_out, w_up, w_down)):
        most = jnp.abs(ref[...].astype(F32))
        if most.ndim == 3:
            most = jnp.max(most, axis=0)
        most = jnp.max(jnp.max(most, axis=0, keepdims=True), axis=1, keepdims=True)
        peak_row = jnp.where(lane == g, most, peak_row)
    sm[x, z, y, 15:16] = peak_row

    pl.semaphore_wait(barrier, 7)

    def ag_rows(g, xx, zz, yy, part):
        strip, one, two = AG_CUTS[g]
        first = (0, strip, strip + one, strip)[part]
        return wts.at[g, xx, zz, yy, pl.ds(first, (strip, one, two, one + two)[part])]

    def ag_strips(g, zz):
        return wts.at[g, :, zz, :, pl.ds(0, AG_CUTS[g][0])]

    def ag_strip_xy(g):
        own = ag_rows(g, x, z, y, 0)
        for i, device in enumerate((to_x, to_y, to_xy)):
            send(("ag", g), own, own, sts.at[g, i], str_.at[g, i], device)

    def ag_strip_z(g):
        for i, (xx, yy, device) in enumerate(((nx, y, to_x), (x, ny, to_y), (nx, ny, to_xy))):
            got = ag_rows(g, xx, z, yy, 0)
            copy(got, got, sts.at[g, i], str_.at[g, i], device).wait_recv()
        own = ag_strips(g, z)
        send(("ag", g), own, own, z2s.at[g, 0], z2r.at[g, 0], to_zk[1])
        send(("ag", g), own, own, z2s.at[g, 1], z2r.at[g, 1 + outer], to_zk[2])

    def ag_strip_fwd(g):
        @pl.when(outer == 0)
        def _():
            for k in (2, 3):
                got = ag_strips(g, zk[k])
                copy(got, got, z2s.at[g, 0], z2r.at[g, k - 1], to_zk[k]).wait_recv()

        for k in (2, 3):
            got = ag_strips(g, zk[k])
            send_if(0, ("ag", g), got, got, z2f.at[g, k - 2], z2r.at[g, k - 1], to_zk[1])

    def ag_strip_got(g):
        got = ag_strips(g, zk[1])
        copy(got, got, z2s.at[g, 0], z2r.at[g, 0], to_zk[1]).wait_recv()

        @pl.when(outer == 1)
        def _():
            for k in (2, 3):
                got = ag_strips(g, zk[k])
                copy(got, got, z2s.at[g, 0], z2r.at[g, k - 1], to_zk[1]).wait_recv()

    def ag_z_send(g):
        own = ag_rows(g, x, z, y, 3)
        send(("ag", g), own, own, zs.at[g, 0], zr.at[g, 0], to_zk[1])
        send(("ag", g), own, own, zs.at[g, 1], zr.at[g, 1 + outer], to_zk[2])

    def ag_z_fwd(g, k):
        got = ag_rows(g, x, zk[k], y, 3)
        pl.when(outer == 0)(copy(got, got, zs.at[g, 0], zr.at[g, k - 1], to_zk[k]).wait_recv)
        send_if(0, ("ag", g), got, got, zf.at[g, k - 2], zr.at[g, k - 1], to_zk[1])

    def ag_xy_send(g, k):
        own = ag_rows(g, x, zk[k], y, 3)
        if k > 0:
            arrived = copy(own, own, zs.at[g, 0], zr.at[g, k - 1], to_zk[1]).wait_recv
            if k > 1:
                pl.when(outer == 1)(arrived)
            else:
                arrived()
        send(("ag", g), own, own, xs.at[g, k], xr.at[g, k], to_x)
        send(("ag", g), own, own, ys.at[g, k], yr.at[g, k], to_y)

    def ag_diag(g, k):
        got = ag_rows(g, x, zk[k], ny, 3)
        copy(got, got, ys.at[g, k], yr.at[g, k], to_y).wait_recv()
        half = ag_rows(g, x, zk[k], ny, 1)
        send(("ag", g), half, half, dxs.at[g, k], dxr.at[g, k], to_x)
        got = ag_rows(g, nx, zk[k], y, 3)
        copy(got, got, xs.at[g, k], xr.at[g, k], to_x).wait_recv()
        half = ag_rows(g, nx, zk[k], y, 2)
        send(("ag", g), half, half, dys.at[g, k], dyr.at[g, k], to_y)

    def ag_last(g, k):
        half = ag_rows(g, nx, zk[k], ny, 1)
        copy(half, half, dxs.at[g, k], dxr.at[g, k], to_x).wait_recv()
        half = ag_rows(g, nx, zk[k], ny, 2)
        copy(half, half, dys.at[g, k], dyr.at[g, k], to_y).wait_recv()

    small_c = copy(sm.at[x, z, y], smc, sm_s.at[0], sm_r.at[0], to_c)
    small_c.start()
    ag_z_send(0)
    ag_xy_send(0, 0)
    small_c.wait()
    sm[x, z, y, 15:16] = jnp.maximum(sm[x, z, y, 15:16], smc[15:16])
    small_x = copy(sm.at[x, z, y], sm.at[x, z, y], sm_s.at[1], sm_r.at[1], to_x)
    small_x.start()
    ag_strip_xy(1)
    ag_xy_send(1, 0)

    for made in arriving[7:]:
        made.wait()

    def do_tokens(i):
        rows = pl.ds(mul8(i * 128, 128), 128)
        v = tok[pl.ds(mul8(i * 128, 128), 128), :].astype(F32)
        xq[rows, :] = (range_of[0] * jnp.tanh(v * inv_of[0])).astype(BF)

    loop(4, do_tokens)
    copy(sm.at[nx, z, y], sm.at[nx, z, y], sm_s.at[1], sm_r.at[1], to_x).wait_recv()
    small_y = copy(sm.at[:, z, y], sm.at[:, z, y], sm_s.at[2], sm_r.at[2], to_y)
    small_y.start()
    ag_strip_xy(2)
    ag_xy_send(2, 0)
    ag_z_send(1)

    def do_turn(j):
        cols = pl.ds(mul8(j * 128, 128), 128)
        xqt[cols, :] = xq[:, cols].T

    loop(6, do_turn)
    ag_xy_send(0, 1)
    ag_z_fwd(0, 2)

    long_flag = long_rows[x].astype(F32)
    for r in range(4):
        row = mask[pl.ds(x * 4 + r, 1), :].astype(F32)
        column = jnp.broadcast_to(row, (128, 128)).T
        for s in range(4):
            seen = column * (1.0 if r == s else long_flag)
            bias[r * 128 : r * 128 + 128, s * 128 : s * 128 + 128] = jnp.where(seen > 0.5, 0.0, -1e30)

    copy(sm.at[:, z, ny], sm.at[:, z, ny], sm_s.at[2], sm_r.at[2], to_y).wait_recv()
    small_z = []
    for k in (1, 2, 3):
        made = copy(sm.at[:, z], sm.at[:, z], sm_s.at[2 + k], sm_r.at[2 + k], to_z[k])
        made.start()
        small_z.append(made)
    ag_z_fwd(0, 3)
    ag_xy_send(0, 2)
    ag_strip_z(1)
    ag_xy_send(0, 3)
    ag_diag(0, 0)
    ag_diag(0, 1)
    ag_z_send(2)
    ag_xy_send(1, 1)
    ag_z_fwd(1, 2)
    ag_diag(0, 2)
    for k in (1, 2, 3):
        copy(sm.at[:, from_z[k]], sm.at[:, from_z[k]], sm_s.at[2 + k], sm_r.at[2 + k], to_z[k]).wait_recv()
    small_x.wait_send()
    small_y.wait_send()
    for made in small_z:
        made.wait_send()

    peaks = jnp.max(jnp.max(jnp.max(sm[:, :, :, 15:16, :], axis=0), axis=0), axis=0)
    w_peak = [jnp.max(jnp.where(lane == g, peaks, 0.0)) for g in range(4)]
    w_inv = [1.0 / r for r in w_peak]

    def spread(xx, width, step):
        total = None
        for place in range(8):
            tile = sm[xx, place // 2, place % 2]
            if width > 128:
                tile = jnp.concatenate([tile, jnp.zeros((16, width - 128), F32)], axis=1)
            if place:
                tile = pltpu.roll(tile, place * step, 1)
            total = tile if total is None else total + tile
        return total

    vec[...] = spread(0, WIDE, 96)
    heads = []
    for xx in range(2):
        wide = spread(xx, 256, 32)
        for h in range(3):
            bup[xx : xx + 1, h * 256 : h * 256 + 256] = wide[6 + h : 7 + h, :]
        narrow = spread(xx, 128, 8)
        heads.append((narrow, pltpu.roll(narrow, 64, 1)))
    for j, first in enumerate((9, 12)):
        for xx in range(2):
            bqv[j : j + 1, xx * 128 : xx * 128 + 128] = (
                heads[xx][0][first : first + 1] + heads[xx][1][first + 1 : first + 2]
            )
        bqv[j : j + 1, 256:384] = heads[0][0][first + 2 : first + 3] + heads[1][1][first + 2 : first + 3]

    ag_z_fwd(1, 3)
    ag_strip_z(2)
    ag_strip_fwd(1)
    ag_diag(0, 3)
    for k in range(4):
        ag_last(0, k)

    left = lax.broadcasted_iota(jnp.int32, (PIECE, 128), 1) < 64

    def squash_heads(place):
        rows = pl.ds(mul8(place * PIECE, PIECE), PIECE)
        tiles = []
        for xx in range(2):
            v = wts[0, xx, place // 2, place % 2].astype(F32)
            inner = [w_peak[0] * jnp.tanh(v[:, t * 128 : t * 128 + 128] * w_inv[0]) for t in (0, 1, 2)]
            inner.append(w_peak[1] * jnp.tanh(v[:, 384:512] * w_inv[1]))
            mixed = jnp.where(left, w_peak[0], w_peak[1])
            mixed_inv = jnp.where(left, w_inv[0], w_inv[1])
            inner.append(w_peak[0] * jnp.tanh(v[:, 512:640] * w_inv[0]))
            inner.append(mixed * jnp.tanh(v[:, 640:768] * mixed_inv))
            tiles.append(inner)
        for t in range(3):
            for xx in range(2):
                wc[rows, t * HERE + xx * 128 : t * HERE + xx * 128 + 128] = tiles[xx][t].astype(BF)
        for xx in range(2):
            wo[rows, xx * 128 : xx * 128 + 128] = tiles[xx][3].astype(BF)
        for t, first, second in ((4, 0, 1), (5, 2, 3)):
            one, two = tiles[0][t], tiles[1][t]
            wc[rows, first * HERE + 256 : first * HERE + 384] = jnp.where(left, one, pltpu.roll(two, 64, 1)).astype(BF)
            other = jnp.where(left, pltpu.roll(one, 64, 1), two).astype(BF)
            if second == 1:
                wc[rows, HERE + 256 : HERE + 384] = other
            else:
                wo[rows, 256:384] = other

    loop(8, squash_heads)
    ag_xy_send(1, 2)
    ag_xy_send(1, 3)

    def squash_ff(g, xx):
        def body(place):
            v = wts[g, xx, place // 2, place % 2].astype(F32)
            wff[g - 1, xx, pl.ds(mul8(place * PIECE, PIECE), PIECE), :] = (
                w_peak[g + 1] * jnp.tanh(v * w_inv[g + 1])
            ).astype(BF)

        loop(8, body)

    for j, held in enumerate((qs, ks, vs)):

        got = nn(xq[...], wc[:, j * HERE : (j + 1) * HERE])
        if j == 0:
            got = (got + bqv[0:1, :]) * 0.125
        elif j == 2:
            got = got + bqv[1:2, :]
        held[...] = got.astype(BF)
    ag_diag(1, 0)
    ag_z_fwd(2, 2)
    ag_z_fwd(2, 3)
    for p in range(3):
        cols = slice(p * 128, p * 128 + 128)
        kt[cols, :] = ks[:, cols].T
        vt[cols, :] = vs[:, cols].T
    ag_diag(1, 1)
    ag_xy_send(2, 1)

    half_of = lax.broadcasted_iota(jnp.int32, (1, 128), 1) // 64

    def attend(p):
        cols = pl.ds(mul8(p * 128, 128), 128)
        for e in range(2):
            feats = pl.ds(mul8(p * 128 + e * 64, 64), 64)
            for n in range(2):
                q = qs[n * 256 : n * 256 + 256, cols]
                q = jnp.where(half_of == e, q, jnp.zeros_like(q))
                s = nt(ks[:, cols], q) + bias[:, n * 256 : n * 256 + 256]
                s = jnp.exp(s - jnp.max(s, axis=0, keepdims=True))
                s = (s * (1.0 / jnp.sum(s, axis=0, keepdims=True))).astype(BF)
                probs[p * 2 + e, :, n * 256 : n * 256 + 256] = s
                ctxt[feats, n * 256 : n * 256 + 256] = nn(vt[feats, :], s)

    attend(0)
    ag_xy_send(2, 2)
    attend(1)
    ag_diag(1, 2)
    ag_strip_fwd(2)
    attend(2)
    ag_xy_send(2, 3)
    ag_diag(1, 3)

    for p in range(3):
        cols = slice(p * 128, p * 128 + 128)
        bent = jnp.tanh(ctxt[cols, :].T * inv_of[1])
        cq[:, cols] = (range_of[1] * bent).astype(BF)
        slc[:, cols] = 1.0 - bent * bent
    tot[0] = jnp.zeros((16, WIDE), F32)
    most = jnp.max(jnp.max(jnp.abs(ctxt[...]), axis=0, keepdims=True), axis=1, keepdims=True)
    tot[0, 10:11, :] = jnp.broadcast_to(most, (1, WIDE))

    def out_part(start, held):
        held[...] = nt(cq[pl.ds(start, OWN), :], wo[...])

    out_part(theirs, exa_s)
    ex1 = copy(exa_s, exa_r, ex_s.at[0], ex_r.at[0], to_c)
    ex1.start()
    ag_diag(2, 0)
    out_part(mine, r1)
    ex1.wait()

    def sum_rows(v):
        return jnp.sum(v, axis=0, keepdims=True)

    def mean_of(v):
        return jnp.sum(v, axis=-1, keepdims=True) * (1.0 / WIDE)

    def first_norm(i):
        rows = pl.ds(mul8(i * 64, 64), 64)
        v = tok[pl.ds(mul8(mine + i * 64, 64), 64), :].astype(F32)
        v = v + (r1[rows, :] + exa_r[rows, :] + vec[0:1, :])
        r1[rows, :] = v
        center = v - mean_of(v)
        factor = lax.rsqrt(mean_of(center * center) + 1e-12)
        normed = center * factor
        n1[rows, :] = normed
        rstd1[rows, :] = factor
        h = normed * vec[2:3, :] + vec[3:4, :]
        tot[0, 11:12, :] = jnp.maximum(tot[0, 11:12, :], jnp.max(jnp.abs(h), axis=0, keepdims=True))
        bent = jnp.tanh(h * inv_of[2])
        sl1[rows, :] = 1.0 - bent * bent
        hq[pl.ds(mul8(mine + i * 64, 64), 64), :] = (range_of[2] * bent).astype(BF)

    loop(4, first_norm)

    def share_rows(held, number):
        own = held.at[pl.ds(mine, OWN)]
        made = copy(own, own, ex_s.at[number], ex_r.at[number], to_c)
        made.start()
        started.setdefault("share", []).append((made, None))

    def got_rows(held, number):
        other = held.at[pl.ds(theirs, OWN)]
        copy(other, other, ex_s.at[number], ex_r.at[number], to_c).wait_recv()

    def turn_rows(held, out, start):
        out[:, pl.ds(start, OWN)] = held[pl.ds(start, OWN), :].T

    share_rows(hq, 1)
    ag_strip_got(1)
    ag_diag(2, 1)
    got_rows(hq, 1)
    turn_rows(hq, hqt, 0)
    turn_rows(hq, hqt, OWN)
    squash_ff(1, x)

    def expand(xx):
        wide = pl.ds(mul8(xx * WIDE, WIDE), WIDE)

        def body(i):
            rows = pl.ds(mul8(i * 256, 256), 256)
            u = nn(hq[rows, :], wff[0, xx]) + bup[pl.ds(xx, 1), :]
            cdf = 0.5 * (1.0 + lax.erf(u * 0.7071067811865476))
            a = u * cdf
            tot[0, 12:13, :] = jnp.maximum(tot[0, 12:13, :], jnp.max(jnp.abs(a), axis=0, keepdims=True))
            bent = jnp.tanh(a * inv_of[3])
            aq[rows, wide] = (range_of[3] * bent).astype(BF)
            pdf = 0.3989422804014327 * jnp.exp(-0.5 * u * u)
            fac[rows, wide] = ((1.0 - bent * bent) * (cdf + u * pdf)).astype(fac.dtype)

        loop(2, body)

    expand(x)
    ag_diag(2, 2)
    for k in range(4):
        ag_last(1, k)
    squash_ff(1, nx)
    expand(nx)
    ag_diag(2, 3)
    ag_strip_got(2)

    def down_part(start, held, xx, first):
        got = nt(aq[pl.ds(start, OWN), pl.ds(mul8(xx * WIDE, WIDE), WIDE)], wff[1, xx])
        held[...] = got if first else held[...] + got

    squash_ff(2, x)
    down_part(theirs, exb_s, x, True)
    down_part(mine, gr2, x, True)
    for k in range(4):
        ag_last(2, k)
    squash_ff(2, nx)
    down_part(theirs, exb_s, nx, False)
    ex2 = copy(exb_s, exb_r, ex_s.at[2], ex_r.at[2], to_c)
    ex2.start()
    down_part(mine, gr2, nx, False)
    ex2.wait()

    def second_norm(i):
        rows = pl.ds(mul8(i * 64, 64), 64)
        v = r1[rows, :] + (gr2[rows, :] + exb_r[rows, :] + vec[1:2, :])
        center = v - mean_of(v)
        factor = lax.rsqrt(mean_of(center * center) + 1e-12)
        normed = center * factor
        o_layer[rows, :] = (normed * vec[4:5, :] + vec[5:6, :]).astype(BF)
        gy = grad_out[rows, :].astype(F32)
        tot[0, 4:5, :] += sum_rows(gy * normed)
        tot[0, 5:6, :] += sum_rows(gy)
        gn = gy * vec[4:5, :]
        back = factor * (gn - mean_of(gn) - normed * mean_of(gn * normed))
        gr2[rows, :] = back
        low = back.astype(BF)
        tot[0, 1:2, :] += sum_rows(low.astype(F32))
        gf[pl.ds(mul8(mine + i * 64, 64), 64), :] = low

    loop(4, second_norm)
    leave(o_layer, r_layer)
    share_rows(gf, 3)
    turn_rows(gf, rowt, mine)
    for g in range(3):
        sent(("ag", g))
    got_rows(gf, 3)
    turn_rows(gf, rowt, theirs)

    def rs_send(g, number, src, dst, device):
        send("rs", src, dst, rs_s.at[g, number], rs_r.at[g, number], device)

    def rs_send_if(which, g, number, src, dst, device, slot):
        send_if(which, "rs", src, dst, rf_s.at[g, number], slot, device)

    def rs_wait(g, number, dst, device):
        copy(dst, dst, rs_s.at[g, number], rs_r.at[g, number], device).wait_recv()

    def rs_rows(g, part):
        strip, one, two = RS_CUTS[g]
        return pl.ds((0, strip, strip + one, strip)[part], (strip, one, two, one + two)[part])

    def rs_part(g, part):
        _, one, two = RS_CUTS[g]
        return pl.ds((0, 0, one, 0)[part], (0, one, two, one + two)[part])

    far_z, near_z = pl.ds(2 - z // 2 * 2, 2), pl.ds(z // 2 * 2, 2)

    def rs_first(g, near):
        one, two = rs_part(g, 1), rs_part(g, 2)
        rs_send(g, 0, wts.at[g, nx, :, ny, rs_rows(g, 1)], rdx.at[g, :, one], to_x)
        rs_send(g, 1, wts.at[g, nx, :, ny, rs_rows(g, 2)], rdy.at[g, :, pl.ds(0, RS_CUTS[g][2])], to_y)
        rs_send(g, 2, wts.at[g, nx, far_z, y, rs_rows(g, 1)], rxx.at[g, far_z, one], to_x)
        if near:
            rs_send(g, 15, wts.at[g, nx, near_z, y, rs_rows(g, 1)], rxx.at[g, near_z, one], to_x)

    def rs_second(g, near):
        two = rs_part(g, 2)
        rs_send(g, 3, wts.at[g, x, far_z, ny, rs_rows(g, 2)], ryy.at[g, far_z, two], to_y)
        if near:
            rs_send(g, 16, wts.at[g, x, near_z, ny, rs_rows(g, 2)], ryy.at[g, near_z, two], to_y)

    def rs_third_x(g, near):
        one, two = rs_part(g, 1), rs_part(g, 2)
        rs_wait(g, 0, rdx.at[g, :, one], to_x)

        def add_x(i):
            here = rs_rows(g, 1)
            wts[g, x, i, ny, here] = (wts[g, x, i, ny, here].astype(F32) + rdx[g, i, one].astype(F32)).astype(BF)

        loop(4, add_x)
        rs_send(g, 4, wts.at[g, x, far_z, ny, rs_rows(g, 1)], ryy.at[g, far_z, one], to_y)
        rs_send(g, 13, wts.at[g, x, near_z, ny, rs_rows(g, 1)], ryy.at[g, near_z, one], to_y)
        if not near:
            rs_send(g, 16, wts.at[g, x, near_z, ny, rs_rows(g, 2)], ryy.at[g, near_z, two], to_y)

    def rs_third_y(g, near):
        one, two = rs_part(g, 1), rs_part(g, 2)
        far = pl.ds(0, RS_CUTS[g][2])
        rs_wait(g, 1, rdy.at[g, :, far], to_y)

        def add_y(i):
            here = rs_rows(g, 2)
            wts[g, nx, i, y, here] = (wts[g, nx, i, y, here].astype(F32) + rdy[g, i, far].astype(F32)).astype(BF)

        loop(4, add_y)
        rs_send(g, 5, wts.at[g, nx, far_z, y, rs_rows(g, 2)], rxx.at[g, far_z, two], to_x)
        rs_send(g, 14, wts.at[g, nx, near_z, y, rs_rows(g, 2)], rxx.at[g, near_z, two], to_x)
        if not near:
            rs_send(g, 15, wts.at[g, nx, near_z, y, rs_rows(g, 1)], rxx.at[g, near_z, one], to_x)

    def plane(g, zz):
        rest, here = rs_rows(g, 3), rs_part(g, 3)
        return wts[g, x, zz, y, rest].astype(F32) + rxx[g, zz, here].astype(F32) + ryy[g, zz, here].astype(F32)

    def rs_fourth(g):
        one, two, both, rest = rs_part(g, 1), rs_part(g, 2), rs_part(g, 3), rs_rows(g, 3)
        rs_wait(g, 2, rxx.at[g, far_z, one], to_x)
        rs_wait(g, 3, ryy.at[g, far_z, two], to_y)
        rs_wait(g, 4, ryy.at[g, far_z, one], to_y)
        rs_wait(g, 5, rxx.at[g, far_z, two], to_x)
        for k in (3, 2):
            wts[g, x, zk[k], y, rest] = plane(g, zk[k]).astype(BF)
            rs_send_if(
                1, g, k - 2, wts.at[g, x, zk[k], y, rest], rzf.at[g, k - 2, both], to_zk[1], rf_r.at[g, k - 2]
            )

    def rs_near(g):
        one, two, both, rest = rs_part(g, 1), rs_part(g, 2), rs_part(g, 3), rs_rows(g, 3)
        rs_wait(g, 13, ryy.at[g, near_z, one], to_y)
        rs_wait(g, 14, rxx.at[g, near_z, two], to_x)
        rs_wait(g, 15, rxx.at[g, near_z, one], to_x)
        rs_wait(g, 16, ryy.at[g, near_z, two], to_y)
        wts[g, x, zk[1], y, rest] = plane(g, zk[1]).astype(BF)
        rs_send(g, 6, wts.at[g, x, zk[1], y, rest], rz.at[g, 0, both], to_zk[1])

    def rs_fifth(g):
        both, rest = rs_part(g, 3), rs_rows(g, 3)
        for k in (3, 2):

            @pl.when(outer == 0)
            def _(k=k):
                held = rzf.at[g, k - 2, both]
                copy(held, held, rf_s.at[g, 0], rf_r.at[g, k - 2], to_zk[1]).wait_recv()
                wts[g, x, zk[k], y, rest] = (
                    wts[g, x, zk[k], y, rest].astype(F32) + rzf[g, k - 2, both].astype(F32)
                ).astype(BF)

            rs_send_if(0, g, k, wts.at[g, x, zk[k], y, rest], rz.at[g, 1, both], to_zk[k], rs_r.at[g, 7])

    def strips(g, zz):
        return wts.at[g, :, zz, :, pl.ds(0, RS_CUTS[g][0])]

    def rs_strip_z(g):
        here = pl.ds(0, RS_CUTS[g][0])
        for k in (3, 2):
            rs_send_if(1, g, 2 + k, strips(g, zk[k]), rzf2.at[g, k - 2, :, :, here], to_zk[1], rf_r.at[g, k])
        rs_send(g, 8, strips(g, zk[1]), rz2.at[g, 0, :, :, here], to_zk[1])

    def rs_strip_fwd(g):
        here = pl.ds(0, RS_CUTS[g][0])
        for k in (3, 2):

            @pl.when(outer == 0)
            def _(k=k):
                held = rzf2.at[g, k - 2, :, :, here]
                copy(held, held, rf_s.at[g, 0], rf_r.at[g, k], to_zk[1]).wait_recv()
                wts[g, :, zk[k], :, here] = (
                    wts[g, :, zk[k], :, here].astype(F32) + rzf2[g, k - 2, :, :, here].astype(F32)
                ).astype(BF)

            rs_send_if(0, g, 4 + k, strips(g, zk[k]), rz2.at[g, 1, :, :, here], to_zk[k], rs_r.at[g, 9])

    def rs_strip_xy(g):
        here = pl.ds(0, RS_CUTS[g][0])
        for k in (0, 1):
            rs_wait(g, 8 + k, rz2.at[g, k, :, :, here], to_zk[1 + k])
        wts[g, :, z, :, here] = (
            wts[g, :, z, :, here].astype(F32)
            + rz2[g, 0, :, :, here].astype(F32)
            + rz2[g, 1, :, :, here].astype(F32)
        ).astype(BF)
        rs_send(g, 10, wts.at[g, nx, z, y, here], rst.at[g, 0, here], to_x)
        rs_send(g, 12, wts.at[g, nx, z, ny, here], rst.at[g, 2, here], to_xy)

    def rs_strip_y(g):
        here = pl.ds(0, RS_CUTS[g][0])
        rs_send(g, 11, wts.at[g, x, z, ny, here], rst.at[g, 1, here], to_y)

    def rs_total(g):
        here, both = pl.ds(0, RS_CUTS[g][0]), rs_part(g, 3)
        for k in (0, 1):
            rs_wait(g, 6 + k, rz.at[g, k, both], to_zk[1 + k])
        for i, device in enumerate((to_x, to_y, to_xy)):
            rs_wait(g, 10 + i, rst.at[g, i, here], device)
        strip = wts[g, x, z, y, here].astype(F32)
        for i in range(3):
            strip = strip + rst[g, i, here].astype(F32)
        total = plane(g, z)
        for k in range(2):
            total = total + rz[g, k, both].astype(F32)
        return jnp.concatenate([strip, total], axis=0)

    def ff_grad(g, turned, held, xx):
        got = nn(turned[...], held[:, pl.ds(mul8(xx * WIDE, WIDE), WIDE)])
        wts[g, xx] = got.reshape(4, 2, PIECE, WIDE).astype(BF)

    ff_grad(2, rowt, aq, nx)
    rs_first(2, True)
    ff_grad(2, rowt, aq, x)
    rs_second(2, True)
    rs_strip_z(2)

    for xx in range(2):

        def hidden_grad(i, xx=xx):
            wide = slice(xx * WIDE, xx * WIDE + WIDE)
            rows = pl.ds(mul8(i * 256, 256), 256)
            got = (nn(gf[rows, :], wff[1, xx]) * fac[rows, wide].astype(F32)).astype(BF)
            gu[rows, wide] = got
            tot[0, 6 + xx : 7 + xx, :] += sum_rows(got.astype(F32))

        loop(2, hidden_grad)
    def up_part(start, held):
        held[...] = nt(gu[pl.ds(start, OWN), 0:WIDE], wff[0, 0]) + nt(
            gu[pl.ds(start, OWN), WIDE : 2 * WIDE], wff[0, 1]
        )

    up_part(theirs, exa_s)
    ex3 = copy(exa_s, exa_r, ex_s.at[4], ex_r.at[4], to_c)
    ex3.start()
    up_part(mine, r1)
    ff_grad(1, hqt, gu, nx)
    rs_third_x(2, True)
    rs_third_y(2, True)
    rs_first(1, True)
    ff_grad(1, hqt, gu, x)
    rs_second(1, True)
    rs_strip_z(1)
    ex3.wait()

    def first_back(i):
        rows = pl.ds(mul8(i * 64, 64), 64)
        normed = n1[rows, :]
        gh = (r1[rows, :] + exa_r[rows, :]) * sl1[rows, :]
        tot[0, 2:3, :] += sum_rows(gh * normed)
        tot[0, 3:4, :] += sum_rows(gh)
        gn = gh * vec[2:3, :]
        back = rstd1[rows, :] * (gn - mean_of(gn) - normed * mean_of(gn * normed)) + gr2[rows, :]
        gr2[rows, :] = back
        low = back.astype(BF)
        tot[0, 0:1, :] += sum_rows(low.astype(F32))
        gf[pl.ds(mul8(mine + i * 64, 64), 64), :] = low

    sent("share")
    loop(4, first_back)
    share_rows(gf, 5)
    turn_rows(gf, rowt, mine)
    got_rows(gf, 5)
    turn_rows(gf, rowt, theirs)

    gwo[...] = nn(rowt[...], cq[...])
    gc[...] = (nn(gf[...], wo[...]) * slc[...]).astype(BF)
    for p in range(3):
        cols = slice(p * 128, p * 128 + 128)
        gct[cols, :] = gc[:, cols].T
        for e in range(2):
            feats = slice(p * 128 + e * 64, p * 128 + e * 64 + 64)
            dsum[p * 2 + e : p * 2 + e + 1, :] = sum_rows(gct[feats, :].astype(F32) * ctxt[feats, :])

    row_half = lax.broadcasted_iota(jnp.int32, (128, 1), 0) // 64

    def attend_back(p):
        cols = pl.ds(mul8(p * 128, 128), 128)
        grad_k = grad_v = None
        for e in range(2):
            feats = pl.ds(mul8(p * 128 + e * 64, 64), 64)
            for n in range(2):
                part = slice(n * 256, n * 256 + 256)
                g = gct[cols, part]
                g = jnp.where(row_half == e, g, jnp.zeros_like(g))
                dpr = nn(vs[:, cols], g)
                ds[:, part] = (probs[p * 2 + e, :, part].astype(F32) * (dpr - dsum[pl.ds(p * 2 + e, 1), part])).astype(BF)
            g = gc[:, cols]
            g = jnp.where(half_of == e, g, jnp.zeros_like(g))
            more_v = nn(probs[p * 2 + e], g)
            q = qs[:, cols]
            q = jnp.where(half_of == e, q, jnp.zeros_like(q))
            more_k = nn(ds[...], q)
            grad_v = more_v if e == 0 else grad_v + more_v
            grad_k = more_k if e == 0 else grad_k + more_k
            gqt[feats, :] = nn(kt[feats, :], ds[...])
        grads[:, pl.ds(mul8(HERE + p * 128, 128), 128)] = grad_k.astype(BF)
        grads[:, pl.ds(mul8(2 * HERE + p * 128, 128), 128)] = grad_v.astype(BF)
        grads[:, cols] = (gqt[cols, :].astype(BF).astype(F32) * 0.125).T.astype(BF)

    attend_back(0)
    attend_back(1)
    attend_back(2)
    rs_strip_fwd(2)
    rs_fourth(2)
    rs_near(2)
    for j, part in ((0, 0), (2, HERE)):
        tot[0, 8:9, part : part + HERE] = sum_rows(grads[:, j * HERE : (j + 1) * HERE].astype(F32))

    left_four = lax.broadcasted_iota(jnp.int32, (4 * PIECE, 128), 1) < 64

    def head_grad(i):
        rows = pl.ds(mul8(i * 4 * PIECE, 4 * PIECE), 4 * PIECE)
        gq, gk, gv = (nn(xqt[rows, :], grads[:, j * HERE : (j + 1) * HERE]) for j in range(3))
        parts = (gq, gk, gv, gwo[rows, :])

        def put(xx, t, v):
            wts[0, xx, pl.ds(i * 2, 2), :, :, t * 128 : t * 128 + 128] = v.reshape(2, 2, PIECE, 128).astype(BF)

        for xx in range(2):
            for t in range(4):
                put(xx, t, parts[t][:, xx * 128 : xx * 128 + 128])
        for t, first, second in ((4, gq, gk), (5, gv, gwo[rows, :])):
            one, two = first[:, 256:384], second[:, 256:384]
            put(0, t, jnp.where(left_four, one, pltpu.roll(two, 64, 1)))
            put(1, t, jnp.where(left_four, pltpu.roll(one, 64, 1), two))

    def most_x(i):
        v = jnp.abs(tok[pl.ds(mul8(i * 128, 128), 128), :].astype(F32))
        tot[0, 9:10, :] = jnp.maximum(tot[0, 9:10, :], jnp.max(v, axis=0, keepdims=True))

    loop(4, most_x)
    row_of = lax.broadcasted_iota(jnp.int32, (16, 1), 0)
    small = copy(tot.at[0], tot_c, tt_s.at[0], tt_r.at[0], to_c)
    small.start()
    loop(2, head_grad)
    small.wait()
    mixed = jnp.where(row_of < 6, tot[0] + tot_c[...], jnp.maximum(tot[0], tot_c[...]))
    tot[1] = jnp.where((row_of >= 6) & (row_of < 9), tot[0], mixed)
    small = copy(tot.at[1], tot_x, tt_s.at[1], tt_r.at[1], to_x)
    small.start()
    rs_first(0, False)
    rs_second(0, False)
    rs_strip_z(0)

    def token_part(start, held):
        held[...] = nt(grads[pl.ds(start, OWN), :], wc[...])

    token_part(theirs, exb_s)
    ex4 = copy(exb_s, exb_r, ex_s.at[6], ex_r.at[6], to_c)
    ex4.start()
    rs_third_x(1, True)
    rs_third_y(1, True)
    token_part(mine, r1)
    ex4.wait()

    def token_grad(i):
        rows = pl.ds(mul8(i * 64, 64), 64)
        v = tok[pl.ds(mul8(mine + i * 64, 64), 64), :].astype(F32)
        bent = jnp.tanh(v * inv_of[0])
        got = gr2[rows, :] + (r1[rows, :] + exb_r[rows, :]) * (1.0 - bent * bent)
        o_tok[pl.ds(mul8(mp * OWN + i * 64, 64), 64), :] = got.astype(BF)

    loop(4, token_grad)
    own = o_tok.at[pl.ds(mul8(mp * OWN, OWN), OWN)]
    send("tok", own, own, gx_s.at[1], gx_r.at[1], to_c)
    rs_strip_fwd(1)
    small.wait()
    tot[2] = jnp.where(row_of < 9, tot[1] + tot_x[...], jnp.maximum(tot[1], tot_x[...]))
    small = copy(tot.at[2], tot_y, tt_s.at[2], tt_r.at[2], to_y)
    small.start()
    rs_strip_xy(2)
    rs_third_x(0, False)
    rs_fifth(2)
    rs_strip_xy(1)
    rs_third_y(0, False)
    rs_strip_y(2)
    rs_strip_y(1)
    send("tok", own, own, gx_s.at[0], gx_r.at[0], to_x)
    rs_strip_fwd(0)
    rs_fourth(1)
    rs_near(1)
    small.wait()
    tot[3] = jnp.where(row_of < 9, tot[2] + tot_y[...], jnp.maximum(tot[2], tot_y[...]))
    smalls = []
    for k in (1, 2, 3):
        made = copy(tot.at[3], tot_z.at[k - 1], tt_s.at[2 + k], tt_r.at[2 + k], to_z[k])
        made.start()
        smalls.append(made)
    rs_fourth(0)
    rs_strip_xy(0)
    rs_strip_y(0)
    rs_fifth(1)
    rs_near(0)
    rs_fifth(0)
    o_down[...] = rs_total(2) * _slope(w_down[...], w_inv[3])
    leave(o_down, r_down)
    o_up[...] = rs_total(1) * _slope(w_up[...], w_inv[2])
    leave(o_up, r_up)

    far = o_tok.at[pl.ds(mul8((nx * 2 + c) * OWN, OWN), OWN)]
    copy(far, far, gx_s.at[0], gx_r.at[0], to_x).wait_recv()
    send("tok", far, far, gx_s.at[2], gx_r.at[2], to_c)

    for made in smalls:
        made.wait()
    done = tot[3]
    for k in range(3):
        done = jnp.where(row_of < 9, done + tot_z[k], jnp.maximum(done, tot_z[k]))
    back = pltpu.roll(done, (8 - dp) * 96, 1)
    o_vec[...] = back[0:6, 0:96]
    ups = jnp.where(x == 0, done[6:7, :], done[7:8, :])
    for h in range(3):
        tile = jnp.broadcast_to(ups[:, h * 256 : h * 256 + 256], (8, 256))
        o_bup[h : h + 1, :] = pltpu.roll(tile, (8 - dp) * 32, 1)[0:1, 0:32]
    for j in range(2):
        row = jnp.broadcast_to(done[8:9, j * HERE : (j + 1) * HERE], (8, HERE))
        pair = jnp.where(x == 0, row[:, 0:128], row[:, 128:256])
        for h, tile, shift in ((0, pair, 0), (1, pair, 64), (2, row[:, 256:384], 64 * x)):
            o_bqv[h, j : j + 1, :] = pltpu.roll(tile, (256 - shift - dp * 8) % 128, 1)[0:1, 0:8]
    for i in range(4):
        o_rng[i] = 0.9 * range_of[i] + 0.1 * jnp.max(done[9 + i : 10 + i, :])

    for here, there in ((o_vec, r_vec), (o_bup, r_bup), (o_bqv, r_bqv)):
        leave(here, there)
    near = pl.ds(mul8((x * 2 + nc) * OWN, OWN), OWN)
    copy(o_tok.at[near], o_tok.at[near], gx_s.at[1], gx_r.at[1], to_c).wait_recv()
    far = pl.ds(mul8((nx * 2 + nc) * OWN, OWN), OWN)
    copy(o_tok.at[far], o_tok.at[far], gx_s.at[2], gx_r.at[2], to_c).wait_recv()
    leave(o_tok, r_tok)
    total = rs_total(0)
    for j in range(4):
        main = total[:, j * 128 : j * 128 + 128]
        pair = total[:, 512 + j // 2 * 128 : 640 + j // 2 * 128]
        if j % 2:
            pair = pltpu.roll(pair, 64, 1)
        whole = jnp.concatenate([main, pair], axis=1)[:, 0:192]
        if j < 3:
            o_qkv[j] = whole * _slope(w_qkv[j], w_inv[0])
        else:
            o_out[...] = whole.T * _slope(w_out[...], w_inv[1])
    leave(o_qkv, r_qkv)
    leave(o_out, r_out)
    for group in list(started):
        sent(group)
    for made in leaving:
        made.wait()


def _slope(values, inverse):
    bent = jnp.tanh(values.astype(F32) * inverse)
    return 1.0 - bent * bent


def layer_on_chips(
    tokens, w_qkv, w_out, w_up, w_down, b_qv, b_up, vectors, ema_ranges, key_mask, long_rows, grad_out
):
    vmem = pltpu.VMEM
    rows = tokens.shape[0]
    half = rows // 2

    def buffer(*shape, dtype=BF):
        return vmem(shape, dtype)

    def f32(*shape):
        return vmem(shape, F32)

    sems = pltpu.SemaphoreType.DMA
    ins = (w_qkv, w_out, w_up, w_down.T, b_qv.transpose(1, 0, 2), b_up, vectors)
    mask = key_mask.reshape(rows // 128, 128)
    kinds = [
        jax.ShapeDtypeStruct(grad_out.shape, BF),
        jax.ShapeDtypeStruct(tokens.shape, BF),
        *(jax.ShapeDtypeStruct(v.shape, F32) for v in ins),
    ]
    scratch = [
        buffer(half, WIDE),
        *(vmem(v.shape, v.dtype) for v in (*ins, mask, grad_out)),
        *(vmem(v.shape, v.dtype) for v in kinds),
        buffer(3, 2, 4, 2, PIECE, WIDE),
        buffer(2, 2, WIDE, WIDE),
        buffer(WIDE, 3 * HERE),
        buffer(WIDE, HERE),
        buffer(3, 4, 48, WIDE),
        buffer(3, 4, 48, WIDE),
        buffer(3, 4, 80, WIDE),
        buffer(3, 4, 80, WIDE),
        buffer(3, 2, 80, WIDE),
        buffer(3, 2, 80, WIDE),
        buffer(3, 2, 2, 2, 32, WIDE),
        buffer(3, 2, 2, 2, 32, WIDE),
        buffer(3, 3, 32, WIDE),
        f32(2, 4, 2, 16, 128),
        f32(16, 128),
        f32(16, WIDE),
        f32(8, WIDE),
        f32(8, HERE),
        buffer(half, WIDE),
        buffer(WIDE, half),
        f32(half, half),
        buffer(half, HERE),
        buffer(half, HERE),
        buffer(half, HERE),
        buffer(HERE, half),
        buffer(HERE, half),
        buffer(6, half, half),
        buffer(half, half),
        f32(HERE, half),
        buffer(half, HERE),
        f32(half, HERE),
        f32(OWN, WIDE),
        f32(OWN, WIDE),
        f32(OWN, WIDE),
        f32(OWN, WIDE),
        buffer(half, WIDE),
        buffer(WIDE, half),
        f32(OWN, WIDE),
        f32(OWN, WIDE),
        f32(OWN, 1),
        f32(OWN, WIDE),
        buffer(half, 2 * WIDE),
        buffer(half, 2 * WIDE),
        buffer(half, 2 * WIDE),
        buffer(half, WIDE),
        buffer(WIDE, half),
        f32(OWN, WIDE),
        buffer(half, HERE),
        buffer(HERE, half),
        f32(8, half),
        buffer(half, 3 * HERE),
        f32(HERE, half),
        f32(WIDE, HERE),
        f32(4, 16, WIDE),
        f32(16, WIDE),
        f32(16, WIDE),
        f32(16, WIDE),
        f32(3, 16, WIDE),
        sems((3, 2)),
        sems((3, 2)),
        sems((3, 3)),
        sems((3, 2)),
        sems((3, 2)),
        sems((3, 3)),
        sems((3, 3)),
        sems((3, 3)),
        sems((3, 4)),
        sems((3, 4)),
        sems((3, 4)),
        sems((3, 4)),
        sems((3, 4)),
        sems((3, 4)),
        sems((3, 4)),
        sems((3, 4)),
        sems((3, 17)),
        sems((3, 17)),
        sems((3, 8)),
        sems((3, 4)),
        sems((6,)),
        sems((6,)),
        sems((7,)),
        sems((7,)),
        sems((6,)),
        sems((6,)),
        sems((3,)),
        sems((3,)),
        sems((10,)),
        sems((9,)),
    ]
    far = pl.BlockSpec(memory_space=pltpu.HBM)
    scalars = pl.BlockSpec(memory_space=pltpu.SMEM)
    outs = pl.pallas_call(
        layer_kernel,
        out_shape=[*kinds, jax.ShapeDtypeStruct(ema_ranges.shape, F32)],
        in_specs=[far] * 8 + [scalars, far, scalars, far],
        out_specs=[far] * 9 + [scalars],
        scratch_shapes=scratch,
        compiler_params=pltpu.CompilerParams(
            collective_id=0, has_side_effects=True, vmem_limit_bytes=VMEM_LIMIT
        ),
        name="encoder_layer",
    )(tokens, *ins, ema_ranges, mask, long_rows, grad_out)
    outs = finish(outs)
    return (*outs[:5], outs[5].T, outs[6].transpose(1, 0, 2), *outs[7:])


def finish_kernel(*refs):
    ins, outs, held, wide, sem = refs[:10], refs[10:20], refs[20:29], refs[29], refs[30]
    parts = [pl.ds(i * OWN, OWN) for i in range(ins[1].shape[0] // OWN)]
    arriving = [pltpu.make_async_copy(ins[1].at[p], held[1].at[p], sem.at[9 + i]) for i, p in enumerate(parts)]
    moved = [i for i in range(9) if i != 1]
    arriving += [pltpu.make_async_copy(ins[i], held[i], sem.at[i]) for i in moved]
    leaving = [pltpu.make_async_copy(wide.at[p], outs[1].at[p], sem.at[9 + i]) for i, p in enumerate(parts)]
    leaving += [pltpu.make_async_copy(held[i], outs[i], sem.at[i]) for i in moved]
    for made in arriving:
        made.start()
    for i in range(4):
        outs[9][i] = ins[9][i]
    for i, (here, there) in enumerate(zip(arriving, leaving)):
        here.wait()
        if i < len(parts):
            wide[parts[i], :] = held[1][parts[i], :].astype(F32)
        there.start()
    for made in leaving:
        made.wait()


def finish(held):
    shape = jax.ShapeDtypeStruct
    far = pl.BlockSpec(memory_space=pltpu.HBM)
    scalars = pl.BlockSpec(memory_space=pltpu.SMEM)
    return pl.pallas_call(
        finish_kernel,
        out_shape=[shape(v.shape, F32 if i == 1 else v.dtype) for i, v in enumerate(held)],
        in_specs=[far] * 9 + [scalars],
        out_specs=[far] * 9 + [scalars],
        scratch_shapes=[pltpu.VMEM(v.shape, v.dtype) for v in held[:9]]
        + [pltpu.VMEM(held[1].shape, F32), pltpu.SemaphoreType.DMA((9 + held[1].shape[0] // OWN,))],
        compiler_params=pltpu.CompilerParams(vmem_limit_bytes=VMEM_LIMIT),
        name="write_results",
    )(*held)


VMEM_LIMIT = 64 * 1024 * 1024


def solution(mesh):
    placed = (
        P("dp", None),
        P(None, "dp", "mp"),
        P("mp", "dp"),
        P("dp", "mp"),
        P("mp", "dp"),
        P(None, "mp", "dp"),
        P("mp", "dp"),
        P(None, "dp"),
        P(),
        P("dp"),
        P("dp"),
        P(("dp", "mp"), None),
    )
    on_chips = dict(mesh.shape) == {"dp": 8, "mp": 4}
    return jax.shard_map(
        layer_on_chips if on_chips else per_device,
        mesh=mesh,
        in_specs=placed,
        out_specs=(
            P(("dp", "mp"), None),
            P("dp", None),
            P(None, "dp", "mp"),
            P("mp", "dp"),
            P("dp", "mp"),
            P("mp", "dp"),
            P(None, "mp", "dp"),
            P("mp", "dp"),
            P(None, "dp"),
            P(),
        ),
        check_vma=False,
    )
```

```python
import jax
import jax.numpy as jnp
from jax import lax
from jax.experimental import pallas as pl
from jax.experimental.pallas import tpu as pltpu
from jax.sharding import PartitionSpec as P

HD = 64
BLOCK = 512
SEG = 128


eps_norm = 1e-12
root_half = 0.7071067811865476
inv_root_tau = 0.3989422804014327


def squash(values, limit):
    return limit * jnp.tanh(values / limit)


def slope(values, limit):
    bent = jnp.tanh(values / limit)
    return 1.0 - bent * bent


def peak_of(values):
    return jnp.max(jnp.abs(values.astype(jnp.float32)))


def product(left, right):
    return jnp.dot(left, right, preferred_element_type=jnp.float32)


def contract_rows(left, right):
    return lax.dot_general(
        left, right, (((0,), (0,)), ((), ())), preferred_element_type=jnp.float32
    )


def contract_cols(left, right):
    return lax.dot_general(
        left, right, (((1,), (1,)), ((), ())), preferred_element_type=jnp.float32
    )


def normalize(values):
    center = values - jnp.mean(values, axis=-1, keepdims=True)
    factor = lax.rsqrt(jnp.mean(center * center, axis=-1, keepdims=True) + eps_norm)
    return (center * factor, factor)


def norm_back(grad_normed, normed, factor):
    first_mean = jnp.mean(grad_normed, axis=-1, keepdims=True)
    cross_mean = jnp.mean(grad_normed * normed, axis=-1, keepdims=True)
    return factor * (grad_normed - first_mean - normed * cross_mean)


def allowed_keys(live, long_flag):
    places = jnp.arange(BLOCK) // SEG
    return (live[None, :] > 0) & ((long_flag > 0) | (places[:, None] == places[None, :]))


def block_scores(queries, keys_in, live, long_flag):
    scores = jnp.einsum("qhd,khd->hqk", queries, keys_in, preferred_element_type=jnp.float32)
    return jnp.where(allowed_keys(live, long_flag)[None], scores, -1e30)


def attend_block(pieces):
    queries, keys_in, values, live, long_flag = pieces
    scores = block_scores(queries, keys_in, live, long_flag)
    top_score = jnp.max(scores, axis=-1, keepdims=True)
    weights = jnp.exp(scores - top_score)
    totals = jnp.sum(weights, axis=-1, keepdims=True)
    attn_probs = (weights / totals).astype(jnp.bfloat16)
    context = jnp.einsum("hqk,khd->qhd", attn_probs, values, preferred_element_type=jnp.float32)
    return (context, top_score + jnp.log(totals))


def attend_back(pieces):
    queries, keys_in, values, live, long_flag, log_total, grad_ctx = pieces
    attn_probs = jnp.exp(block_scores(queries, keys_in, live, long_flag) - log_total)
    grad_probs = jnp.einsum("qhd,khd->hqk", grad_ctx, values, preferred_element_type=jnp.float32)
    grad_values = jnp.einsum(
        "hqk,qhd->khd",
        attn_probs.astype(jnp.bfloat16),
        grad_ctx,
        preferred_element_type=jnp.float32,
    )
    inner = jnp.sum(grad_probs * attn_probs, axis=-1, keepdims=True)
    grad_scores = (attn_probs * (grad_probs - inner)).astype(jnp.bfloat16)
    grad_queries = jnp.einsum(
        "hqk,khd->qhd", grad_scores, keys_in, preferred_element_type=jnp.float32
    )
    grad_keys = jnp.einsum("hqk,qhd->khd", grad_scores, queries, preferred_element_type=jnp.float32)
    return (
        grad_queries.astype(jnp.bfloat16),
        grad_keys.astype(jnp.bfloat16),
        grad_values.astype(jnp.bfloat16),
    )


def prepare(gathered, w_peaks):
    return tuple(
        (
            squash(gathered[index].astype(jnp.float32), w_peaks[index]).astype(jnp.bfloat16)
            for index in range(4)
        )
    )


def peak_all(values):
    return lax.pmax(peak_of(values), ("dp", "mp"))


def per_device(
    tokens,
    w_qkv,
    w_out,
    w_up,
    w_down,
    b_qv,
    b_up,
    vectors,
    ema_ranges,
    key_mask,
    long_rows,
    grad_out,
):
    row_count = tokens.shape[0]
    quarter = row_count // lax.axis_size("mp")
    row_start = lax.axis_index("mp") * quarter
    blocks = row_count // BLOCK
    w_peaks = lax.pmax(
        (peak_of(w_qkv), peak_of(w_out), peak_of(w_up), peak_of(w_down)), ("dp", "mp")
    )
    gathered = (
        lax.all_gather(w_qkv, "dp", axis=1, tiled=True),
        lax.all_gather(w_out, "dp", axis=1, tiled=True),
        lax.all_gather(w_up, "dp", axis=0, tiled=True),
        lax.all_gather(w_down, "dp", axis=1, tiled=True),
        lax.all_gather(b_qv, "dp", axis=2, tiled=True),
        lax.all_gather(b_up, "dp", axis=1, tiled=True),
        lax.all_gather(vectors, "dp", axis=1, tiled=True),
    )
    qkv_q, out_q, up_q, down_q = prepare(gathered, w_peaks)
    bias_qv = gathered[4].astype(jnp.float32).reshape(2, -1)
    bias_up = gathered[5].astype(jnp.float32).reshape(-1)
    vec = gathered[6].astype(jnp.float32)
    head_width = bias_qv.shape[1]
    heads_here = head_width // HD
    scale_q = HD ** (-0.5)
    tok_float = tokens.astype(jnp.float32)
    peak_tok = peak_all(tok_float)
    tok_quant = squash(tok_float, ema_ranges[0]).astype(jnp.bfloat16)
    projected = jnp.einsum("td,jde->jte", tok_quant, qkv_q, preferred_element_type=jnp.float32)
    queries = ((projected[0] + bias_qv[0]) * scale_q).astype(jnp.bfloat16)
    keys_all = projected[1].astype(jnp.bfloat16)
    values = (projected[2] + bias_qv[1]).astype(jnp.bfloat16)
    shape_four = (blocks, BLOCK, heads_here, HD)
    mask_blocks = key_mask.reshape(blocks, BLOCK)
    block_inputs = (
        queries.reshape(shape_four),
        keys_all.reshape(shape_four),
        values.reshape(shape_four),
        mask_blocks,
        long_rows,
    )
    context, log_total = lax.map(attend_block, block_inputs)
    context = context.reshape(row_count, head_width)
    peak_ctx = peak_all(context)
    ctx_quant = squash(context, ema_ranges[1]).astype(jnp.bfloat16)
    partial_attn = product(ctx_quant, out_q)
    attn = lax.psum_scatter(partial_attn, "mp", scatter_dimension=0, tiled=True) + vec[0]
    first_own = lax.dynamic_slice_in_dim(tok_float, row_start, quarter, 0) + attn
    normed, factor_one = normalize(first_own)
    hidden_in = normed * vec[2] + vec[3]
    hid_quant = lax.all_gather(
        squash(hidden_in, ema_ranges[2]).astype(jnp.bfloat16), "mp", axis=0, tiled=True
    )
    peak_hid = peak_all(hidden_in)
    pre_act = product(hid_quant, up_q) + bias_up
    active = pre_act * 0.5 * (1.0 + lax.erf(pre_act * root_half))
    peak_act = peak_all(active)
    act_quant = squash(active, ema_ranges[3]).astype(jnp.bfloat16)
    branch = (
        lax.psum_scatter(product(act_quant, down_q), "mp", scatter_dimension=0, tiled=True) + vec[1]
    )
    second = first_own + branch
    normed_two, factor_two = normalize(second)
    layer_out = (normed_two * vec[4] + vec[5]).astype(jnp.bfloat16)
    new_ranges = 0.9 * ema_ranges + 0.1 * jnp.stack([peak_tok, peak_ctx, peak_hid, peak_act])
    gathered = (
        lax.all_gather(w_qkv, "dp", axis=1, tiled=True),
        lax.all_gather(w_out, "dp", axis=1, tiled=True),
        lax.all_gather(w_up, "dp", axis=0, tiled=True),
        lax.all_gather(w_down, "dp", axis=1, tiled=True),
        lax.all_gather(b_qv, "dp", axis=2, tiled=True),
        lax.all_gather(b_up, "dp", axis=1, tiled=True),
        lax.all_gather(vectors, "dp", axis=1, tiled=True),
    )
    qkv_q, out_q, up_q, down_q = prepare(gathered, w_peaks)
    grad_y = grad_out.astype(jnp.float32)
    grad_gain_two = jnp.sum(grad_y * normed_two, axis=0)
    grad_shift_two = jnp.sum(grad_y, axis=0)
    grad_second = norm_back(grad_y * vec[4], normed_two, factor_two)
    grad_resid = lax.all_gather(grad_second.astype(jnp.bfloat16), "mp", axis=0, tiled=True).astype(
        grad_second.dtype
    )
    grad_branch = grad_resid.astype(jnp.bfloat16)
    grad_bias_down = jnp.sum(grad_branch.astype(jnp.float32), axis=0)
    grad_down_w = contract_rows(act_quant, grad_branch)
    grad_active = contract_cols(grad_branch, down_q) * slope(active, ema_ranges[3])
    normal_cdf = 0.5 * (1.0 + lax.erf(pre_act * root_half))
    normal_pdf = inv_root_tau * jnp.exp(-0.5 * pre_act * pre_act)
    grad_pre = (grad_active * (normal_cdf + pre_act * normal_pdf)).astype(jnp.bfloat16)
    grad_bias_up = jnp.sum(grad_pre.astype(jnp.float32), axis=0)
    grad_up_w = contract_rows(hid_quant, grad_pre)
    partial_hid = contract_cols(grad_pre, up_q)
    grad_hid_q = lax.psum_scatter(partial_hid, "mp", scatter_dimension=0, tiled=True)
    grad_hidden = grad_hid_q * slope(hidden_in, ema_ranges[2])
    grad_gain_one = jnp.sum(grad_hidden * normed, axis=0)
    grad_shift_one = jnp.sum(grad_hidden, axis=0)
    grad_first = norm_back(grad_hidden * vec[2], normed, factor_one) + grad_second
    grad_attn = lax.all_gather(grad_first.astype(jnp.bfloat16), "mp", axis=0, tiled=True)
    grad_bias_out = jnp.sum(grad_attn.astype(jnp.float32), axis=0)
    grad_out_w = contract_rows(ctx_quant, grad_attn)
    grad_ctx = (contract_cols(grad_attn, out_q) * slope(context, ema_ranges[1])).astype(
        jnp.bfloat16
    )
    back_inputs = block_inputs + (log_total, grad_ctx.reshape(shape_four))
    grad_q, grad_k, grad_v = lax.map(attend_back, back_inputs)
    stacked = jnp.stack(
        [
            grad_q.reshape(row_count, head_width) * jnp.bfloat16(scale_q),
            grad_k.reshape(row_count, head_width),
            grad_v.reshape(row_count, head_width),
        ]
    )
    grad_qkv_w = jnp.einsum("td,jte->jde", tok_quant, stacked, preferred_element_type=jnp.float32)
    stacked_float = stacked.astype(jnp.float32)
    grad_bias_qv = jnp.stack([jnp.sum(stacked_float[0], axis=0), jnp.sum(stacked_float[2], axis=0)])
    part_input = jnp.einsum("jte,jde->td", stacked, qkv_q, preferred_element_type=jnp.float32)
    own_term = part_input * slope(tok_float, ema_ranges[0])
    own_rows = lax.dynamic_slice_in_dim(own_term, row_start, quarter, 0) + grad_first
    own_term = lax.dynamic_update_slice_in_dim(own_term, own_rows, row_start, 0)
    grad_tokens, norm_tail = (
        lax.psum(own_term.astype(jnp.bfloat16), "mp").astype(jnp.float32),
        lax.psum(
            jnp.stack([grad_gain_one, grad_shift_one, grad_gain_two, grad_shift_two]).astype(
                jnp.bfloat16
            ),
            "mp",
        ).astype(jnp.float32),
    )
    grad_vec = jnp.stack(
        [grad_bias_out, grad_bias_down, norm_tail[0], norm_tail[1], norm_tail[2], norm_tail[3]]
    )
    summed = (
        lax.psum_scatter(
            grad_qkv_w * slope(gathered[0].astype(jnp.float32), w_peaks[0]),
            "dp",
            scatter_dimension=1,
            tiled=True,
        ),
        lax.psum_scatter(
            grad_out_w * slope(gathered[1].astype(jnp.float32), w_peaks[1]),
            "dp",
            scatter_dimension=1,
            tiled=True,
        ),
        lax.psum_scatter(
            grad_up_w * slope(gathered[2].astype(jnp.float32), w_peaks[2]),
            "dp",
            scatter_dimension=0,
            tiled=True,
        ),
        lax.psum_scatter(
            grad_down_w * slope(gathered[3].astype(jnp.float32), w_peaks[3]),
            "dp",
            scatter_dimension=1,
            tiled=True,
        ),
        lax.psum_scatter(
            grad_bias_qv.reshape(gathered[4].shape), "dp", scatter_dimension=2, tiled=True
        ),
        lax.psum_scatter(
            grad_bias_up.reshape(gathered[5].shape), "dp", scatter_dimension=1, tiled=True
        ),
        lax.psum_scatter(grad_vec, "dp", scatter_dimension=1, tiled=True),
    )
    return (
        layer_out,
        grad_tokens,
        summed[0],
        summed[1],
        summed[2],
        summed[3],
        summed[4],
        summed[5],
        summed[6],
        new_ranges,
    )


BF = jnp.bfloat16
F32 = jnp.float32
MESH = pl.DeviceIdType.MESH
WIDE = 768
PIECE = 96
AG_CUTS = ((0, 48, 48), (16, 32, 48), (32, 32, 32))
RS_CUTS = ((16, 32, 48), (32, 32, 32), (32, 32, 32))
OWN = 256
HERE = 384


def nn(left, right):
    return lax.dot_general(left, right, (((1,), (0,)), ((), ())), preferred_element_type=F32)


def nt(left, right):
    return lax.dot_general(left, right, (((1,), (1,)), ((), ())), preferred_element_type=F32)


def mul8(value, step):
    return pl.multiple_of(value, step)


def loop(count, body):
    def step(index, carry):
        body(index)
        return carry

    lax.fori_loop(0, count, step, 0)


def layer_kernel(
    h_tok,
    h_qkv,
    h_out,
    h_up,
    h_down,
    h_bqv,
    h_bup,
    h_vec,
    h_rng,
    h_mask,
    h_long,
    h_grad,
    r_layer,
    r_tok,
    r_qkv,
    r_out,
    r_up,
    r_down,
    r_bqv,
    r_bup,
    r_vec,
    r_rng,
    tok,
    w_qkv,
    w_out,
    w_up,
    w_down,
    b_qv,
    b_up,
    vectors,
    mask,
    grad_out,
    o_layer,
    o_tok,
    o_qkv,
    o_out,
    o_up,
    o_down,
    o_bqv,
    o_bup,
    o_vec,
    ranges,
    long_rows,
    o_rng,
    wts,
    wff,
    wc,
    wo,
    rdx,
    rdy,
    rxx,
    ryy,
    rz,
    rzf,
    rz2,
    rzf2,
    rst,
    sm,
    smc,
    vec,
    bup,
    bqv,
    xq,
    xqt,
    bias,
    qs,
    ks,
    vs,
    kt,
    vt,
    probs,
    ds,
    ctxt,
    cq,
    slc,
    exa_s,
    exa_r,
    exb_s,
    exb_r,
    hq,
    hqt,
    r1,
    n1,
    rstd1,
    sl1,
    aq,
    fac,
    gu,
    gf,
    rowt,
    gr2,
    gc,
    gct,
    dsum,
    grads,
    gqt,
    gwo,
    tot,
    tot_c,
    tot_x,
    tot_y,
    tot_z,
    zs,
    zf,
    zr,
    z2s,
    z2f,
    z2r,
    sts,
    str_,
    xs,
    xr,
    ys,
    yr,
    dxs,
    dxr,
    dys,
    dyr,
    rs_s,
    rs_r,
    rf_s,
    rf_r,
    sm_s,
    sm_r,
    ex_s,
    ex_r,
    tt_s,
    tt_r,
    gx_s,
    gx_r,
    in_s,
    out_s,
):
    dp = lax.axis_index("dp")
    mp = lax.axis_index("mp")
    z, y = dp // 2, dp % 2
    x, c = mp // 2, mp % 2
    nx, ny, nc = 1 - x, 1 - y, 1 - c
    to_x = (dp, nx * 2 + c)
    to_y = (z * 2 + ny, mp)
    to_c = (dp, x * 2 + nc)
    to_xy = (z * 2 + ny, nx * 2 + c)
    to_z = [None] + [((z + k) % 4 * 2 + y, mp) for k in (1, 2, 3)]
    from_z = [z] + [(z + 4 - k) % 4 for k in (1, 2, 3)]
    zk = [z, z + 1 - 2 * (z % 2), 2 - z // 2, 3 - 3 * (z // 2)]
    outer = (z * z - 3 * z + 2) // 2
    to_zk = [None] + [(zk[k] * 2 + y, mp) for k in (1, 2, 3)]
    mine = mul8(c * OWN, OWN)
    theirs = mul8(nc * OWN, OWN)
    started = {}

    def copy(src, dst, send, recv, device):
        return pltpu.make_async_remote_copy(
            src_ref=src, dst_ref=dst, send_sem=send, recv_sem=recv, device_id=device, device_id_type=MESH
        )

    def send(group, *args):
        made = copy(*args)
        made.start()
        started.setdefault(group, []).append((made, None))

    def send_if(which, group, *args):
        made = copy(*args)
        pl.when(outer == which)(made.start)
        started.setdefault(group, []).append((made, which))

    def sent(group):
        for made, which in started.pop(group, []):
            if which is None:
                made.wait_send()
            else:
                pl.when(outer == which)(made.wait_send)

    barrier = pltpu.get_barrier_semaphore()
    for device in (to_c, to_x, to_y, to_xy, *to_z[1:]):
        pl.semaphore_signal(barrier, inc=1, device_id=device, device_id_type=MESH)

    base = mul8(x * 512, 512)
    arriving = [
        pltpu.make_async_copy(there, here, in_s.at[i])
        for i, (there, here) in enumerate(
            (
                (h_qkv, w_qkv),
                (h_out, w_out),
                (h_up, w_up),
                (h_down, w_down),
                (h_vec, vectors),
                (h_bup, b_up),
                (h_bqv, b_qv),
                (h_rng, ranges),
                (h_tok.at[pl.ds(base, 512)], tok),
                (h_mask, mask),
                (h_long, long_rows),
                (h_grad, grad_out),
                (h_up, wts.at[1, x, z, y]),
                (h_down, wts.at[2, x, z, y]),
            )
        )
    ]
    for made in arriving:
        made.start()
    leaving = []

    def leave_rows(place):
        part = pl.ds(mul8(place * OWN, OWN), OWN)
        leave(o_tok.at[part], r_tok.at[part])

    def leave(here, there):
        made = pltpu.make_async_copy(here, there, out_s.at[len(leaving)])
        made.start()
        leaving.append(made)

    pl.semaphore_wait(barrier, 7)

    def ag_rows(g, xx, zz, yy, part):
        strip, one, two = AG_CUTS[g]
        first = (0, strip, strip + one, strip)[part]
        return wts.at[g, xx, zz, yy, pl.ds(first, (strip, one, two, one + two)[part])]

    def ag_own(g, part):
        if g == 0:
            return ag_rows(g, x, z, y, part)
        strip, one, two = AG_CUTS[g]
        return (h_up, h_down)[g - 1].at[pl.ds(*((0, strip), None, None, (strip, one + two))[part])]

    def ag_strips(g, zz):
        return wts.at[g, :, zz, :, pl.ds(0, AG_CUTS[g][0])]

    def ag_strip_xy(g):
        own = ag_rows(g, x, z, y, 0)
        for i, device in enumerate((to_x, to_y, to_xy)):
            send(("ag", g), ag_own(g, 0), own, sts.at[g, i], str_.at[g, i], device)

    def ag_strip_z(g):
        for i, (xx, yy, device) in enumerate(((nx, y, to_x), (x, ny, to_y), (nx, ny, to_xy))):
            got = ag_rows(g, xx, z, yy, 0)
            copy(got, got, sts.at[g, i], str_.at[g, i], device).wait_recv()
        own = ag_strips(g, z)
        send(("ag", g), own, own, z2s.at[g, 0], z2r.at[g, 0], to_zk[1])
        send(("ag", g), own, own, z2s.at[g, 1], z2r.at[g, 1 + outer], to_zk[2])

    def ag_strip_fwd(g):
        @pl.when(outer == 0)
        def _():
            for k in (2, 3):
                got = ag_strips(g, zk[k])
                copy(got, got, z2s.at[g, 0], z2r.at[g, k - 1], to_zk[k]).wait_recv()

        for k in (2, 3):
            got = ag_strips(g, zk[k])
            send_if(0, ("ag", g), got, got, z2f.at[g, k - 2], z2r.at[g, k - 1], to_zk[1])

    def ag_strip_got(g):
        got = ag_strips(g, zk[1])
        copy(got, got, z2s.at[g, 0], z2r.at[g, 0], to_zk[1]).wait_recv()

        @pl.when(outer == 1)
        def _():
            for k in (2, 3):
                got = ag_strips(g, zk[k])
                copy(got, got, z2s.at[g, 0], z2r.at[g, k - 1], to_zk[1]).wait_recv()

    def ag_z_send(g):
        own, held = ag_rows(g, x, z, y, 3), ag_own(g, 3)
        send(("ag", g), held, own, zs.at[g, 0], zr.at[g, 0], to_zk[1])
        send(("ag", g), held, own, zs.at[g, 1], zr.at[g, 1 + outer], to_zk[2])

    def ag_z_fwd(g, k):
        got = ag_rows(g, x, zk[k], y, 3)
        pl.when(outer == 0)(copy(got, got, zs.at[g, 0], zr.at[g, k - 1], to_zk[k]).wait_recv)
        send_if(0, ("ag", g), got, got, zf.at[g, k - 2], zr.at[g, k - 1], to_zk[1])

    def ag_xy_send(g, k, which=None):
        own = ag_rows(g, x, zk[k], y, 3)
        if which is not None:
            send_if(which, ("ag", g), own, own, xs.at[g, k], xr.at[g, k], to_x)
            send_if(which, ("ag", g), own, own, ys.at[g, k], yr.at[g, k], to_y)
            return
        if k > 0:
            arrived = copy(own, own, zs.at[g, 0], zr.at[g, k - 1], to_zk[1]).wait_recv
            if k > 1:
                pl.when(outer == 1)(arrived)
            else:
                arrived()
        held = own if k else ag_own(g, 3)
        send(("ag", g), held, own, xs.at[g, k], xr.at[g, k], to_x)
        send(("ag", g), held, own, ys.at[g, k], yr.at[g, k], to_y)

    def ag_diag(g, k):
        got = ag_rows(g, x, zk[k], ny, 3)
        copy(got, got, ys.at[g, k], yr.at[g, k], to_y).wait_recv()
        half = ag_rows(g, x, zk[k], ny, 1)
        send(("ag", g), half, half, dxs.at[g, k], dxr.at[g, k], to_x)
        got = ag_rows(g, nx, zk[k], y, 3)
        copy(got, got, xs.at[g, k], xr.at[g, k], to_x).wait_recv()
        half = ag_rows(g, nx, zk[k], y, 2)
        send(("ag", g), half, half, dys.at[g, k], dyr.at[g, k], to_y)

    def ag_last(g, k):
        half = ag_rows(g, nx, zk[k], ny, 1)
        copy(half, half, dxs.at[g, k], dxr.at[g, k], to_x).wait_recv()
        half = ag_rows(g, nx, zk[k], ny, 2)
        copy(half, half, dys.at[g, k], dyr.at[g, k], to_y).wait_recv()

    ag_strip_xy(1)
    ag_xy_send(1, 0)

    arriving[0].wait()
    arriving[1].wait()
    turned = w_out[...].T
    for j, part in enumerate((w_qkv[0], w_qkv[1], w_qkv[2], turned)):
        wts[0, x, z, y, :, j * 128 : j * 128 + 128] = part[:, 0:128]
        wts[0, x, z, y, :, 512 + j * 64 : 576 + j * 64] = part[:, 128:192]
    ag_z_send(0)
    ag_xy_send(0, 0)

    for made in arriving[2:8]:
        made.wait()
    range_of = [ranges[i] for i in range(4)]
    inv_of = [1.0 / r for r in range_of]

    sm[x, z, y] = jnp.zeros((16, 128), F32)
    sm[x, z, y, 0:6, 0:96] = vectors[...].astype(F32)
    sm[x, z, y, 6:9, 0:32] = b_up[...].astype(F32)
    sm[x, z, y, 9:12, 0:8] = b_qv[:, 0, :].astype(F32)
    sm[x, z, y, 12:15, 0:8] = b_qv[:, 1, :].astype(F32)
    lane = lax.broadcasted_iota(jnp.int32, (1, 128), 1)
    peak_row = jnp.zeros((1, 128), F32)
    for g, ref in enumerate((w_qkv, w_out, w_up, w_down)):
        most = jnp.abs(ref[...].astype(F32))
        if most.ndim == 3:
            most = jnp.max(most, axis=0)
        most = jnp.max(jnp.max(most, axis=0, keepdims=True), axis=1, keepdims=True)
        peak_row = jnp.where(lane == g, most, peak_row)
    sm[x, z, y, 15:16] = peak_row

    small_c = copy(sm.at[x, z, y], smc, sm_s.at[0], sm_r.at[0], to_c)
    small_c.start()
    ag_z_send(1)
    small_c.wait()
    sm[x, z, y, 15:16] = jnp.maximum(sm[x, z, y, 15:16], smc[15:16])
    small_xy = ((nx, y, to_x), (x, ny, to_y), (nx, ny, to_xy))
    for i, (_, _, device) in enumerate(small_xy):
        send("sm", sm.at[x, z, y], sm.at[x, z, y], sm_s.at[1 + i], sm_r.at[1 + i], device)
    ag_strip_xy(2)

    for made in arriving[8:]:
        made.wait()

    def do_tokens(i):
        rows = pl.ds(mul8(i * 128, 128), 128)
        v = tok[pl.ds(mul8(i * 128, 128), 128), :].astype(F32)
        xq[rows, :] = (range_of[0] * jnp.tanh(v * inv_of[0])).astype(BF)

    loop(4, do_tokens)
    def do_turn(j):
        cols = pl.ds(mul8(j * 128, 128), 128)
        xqt[cols, :] = xq[:, cols].T

    loop(6, do_turn)
    ag_xy_send(0, 1)
    ag_z_fwd(0, 2)
    ag_z_fwd(0, 3)

    long_flag = long_rows[x].astype(F32)
    for r in range(4):
        row = mask[pl.ds(x * 4 + r, 1), :].astype(F32)
        column = jnp.broadcast_to(row, (128, 128)).T
        for s in range(4):
            seen = column * (1.0 if r == s else long_flag)
            bias[r * 128 : r * 128 + 128, s * 128 : s * 128 + 128] = jnp.where(seen > 0.5, 0.0, -1e30)

    for i, (xx, yy, device) in enumerate(small_xy):
        copy(sm.at[xx, z, yy], sm.at[xx, z, yy], sm_s.at[1 + i], sm_r.at[1 + i], device).wait_recv()
    for k in (1, 2, 3):
        send("sm", sm.at[:, z], sm.at[:, z], sm_s.at[3 + k], sm_r.at[3 + k], to_z[k])
    ag_strip_z(1)
    ag_z_send(2)
    ag_diag(0, 0)
    got = ag_rows(1, x, zk[1], y, 3)
    copy(got, got, zs.at[1, 0], zr.at[1, 0], to_zk[1]).wait_recv()
    ag_xy_send(1, 1, 1)
    ag_xy_send(0, 2)
    ag_z_fwd(1, 2)
    ag_diag(0, 1)
    ag_xy_send(0, 3)
    ag_xy_send(1, 1, 0)
    ag_z_fwd(1, 3)
    ag_strip_z(2)
    for k in (1, 2, 3):
        copy(sm.at[:, from_z[k]], sm.at[:, from_z[k]], sm_s.at[3 + k], sm_r.at[3 + k], to_z[k]).wait_recv()
    sent("sm")

    peaks = jnp.max(jnp.max(jnp.max(sm[:, :, :, 15:16, :], axis=0), axis=0), axis=0)
    w_peak = [jnp.max(jnp.where(lane == g, peaks, 0.0)) for g in range(4)]
    w_inv = [1.0 / r for r in w_peak]

    def spread(xx, width, step):
        total = None
        for place in range(8):
            tile = sm[xx, place // 2, place % 2]
            if width > 128:
                tile = jnp.concatenate([tile, jnp.zeros((16, width - 128), F32)], axis=1)
            if place:
                tile = pltpu.roll(tile, place * step, 1)
            total = tile if total is None else total + tile
        return total

    vec[...] = spread(0, WIDE, 96)
    heads = []
    for xx in range(2):
        wide = spread(xx, 256, 32)
        for h in range(3):
            bup[xx : xx + 1, h * 256 : h * 256 + 256] = wide[6 + h : 7 + h, :]
        narrow = spread(xx, 128, 8)
        heads.append((narrow, pltpu.roll(narrow, 64, 1)))
    for j, first in enumerate((9, 12)):
        for xx in range(2):
            bqv[j : j + 1, xx * 128 : xx * 128 + 128] = (
                heads[xx][0][first : first + 1] + heads[xx][1][first + 1 : first + 2]
            )
        bqv[j : j + 1, 256:384] = heads[0][0][first + 2 : first + 3] + heads[1][1][first + 2 : first + 3]

    ag_diag(0, 2)
    ag_xy_send(2, 0)
    ag_strip_fwd(1)
    ag_diag(0, 3)
    ag_xy_send(1, 2)
    ag_xy_send(1, 3)
    ag_diag(1, 0)
    ag_diag(1, 1)

    left = lax.broadcasted_iota(jnp.int32, (PIECE, 128), 1) < 64

    def squash_heads(zz, yy):
        place = zz * 2 + yy
        rows = pl.ds(mul8(place * PIECE, PIECE), PIECE)
        tiles = []
        for xx in range(2):
            v = wts[0, xx, zz, yy].astype(F32)
            inner = [w_peak[0] * jnp.tanh(v[:, t * 128 : t * 128 + 128] * w_inv[0]) for t in (0, 1, 2)]
            inner.append(w_peak[1] * jnp.tanh(v[:, 384:512] * w_inv[1]))
            mixed = jnp.where(left, w_peak[0], w_peak[1])
            mixed_inv = jnp.where(left, w_inv[0], w_inv[1])
            inner.append(w_peak[0] * jnp.tanh(v[:, 512:640] * w_inv[0]))
            inner.append(mixed * jnp.tanh(v[:, 640:768] * mixed_inv))
            tiles.append(inner)
        for t in range(3):
            for xx in range(2):
                wc[rows, t * HERE + xx * 128 : t * HERE + xx * 128 + 128] = tiles[xx][t].astype(BF)
        for xx in range(2):
            wo[rows, xx * 128 : xx * 128 + 128] = tiles[xx][3].astype(BF)
        for t, first, second in ((4, 0, 1), (5, 2, 3)):
            one, two = tiles[0][t], tiles[1][t]
            wc[rows, first * HERE + 256 : first * HERE + 384] = jnp.where(left, one, pltpu.roll(two, 64, 1)).astype(BF)
            other = jnp.where(left, pltpu.roll(one, 64, 1), two).astype(BF)
            if second == 1:
                wc[rows, HERE + 256 : HERE + 384] = other
            else:
                wo[rows, 256:384] = other

    loop(4, lambda zz: squash_heads(zz, y))
    for k in range(4):
        ag_last(0, k)
    loop(4, lambda zz: squash_heads(zz, ny))
    ag_z_fwd(2, 2)
    ag_z_fwd(2, 3)
    ag_diag(1, 2)

    def squash_ff(g, xx):
        def body(place):
            v = wts[g, xx, place // 2, place % 2].astype(F32)
            wff[g - 1, xx, pl.ds(mul8(place * PIECE, PIECE), PIECE), :] = (
                w_peak[g + 1] * jnp.tanh(v * w_inv[g + 1])
            ).astype(BF)

        loop(8, body)

    for j, held in enumerate((qs, ks, vs)):

        got = nn(xq[...], wc[:, j * HERE : (j + 1) * HERE])
        if j == 0:
            got = (got + bqv[0:1, :]) * 0.125
        elif j == 2:
            got = got + bqv[1:2, :]
        held[...] = got.astype(BF)
    ag_diag(1, 3)
    for p in range(3):
        cols = slice(p * 128, p * 128 + 128)
        kt[cols, :] = ks[:, cols].T
        vt[cols, :] = vs[:, cols].T
    ag_xy_send(2, 1)

    half_of = lax.broadcasted_iota(jnp.int32, (1, 128), 1) // 64

    def attend(p):
        cols = pl.ds(mul8(p * 128, 128), 128)
        for e in range(2):
            feats = pl.ds(mul8(p * 128 + e * 64, 64), 64)
            for n in range(2):
                q = qs[n * 256 : n * 256 + 256, cols]
                q = jnp.where(half_of == e, q, jnp.zeros_like(q))
                s = nt(ks[:, cols], q) + bias[:, n * 256 : n * 256 + 256]
                s = jnp.exp(s - jnp.max(s, axis=0, keepdims=True))
                s = (s * (1.0 / jnp.sum(s, axis=0, keepdims=True))).astype(BF)
                probs[p * 2 + e, :, n * 256 : n * 256 + 256] = s
                ctxt[feats, n * 256 : n * 256 + 256] = nn(vt[feats, :], s)

    ag_strip_fwd(2)
    attend(0)
    ag_xy_send(2, 2)
    ag_diag(2, 0)
    attend(1)
    ag_xy_send(2, 3)
    attend(2)

    for p in range(3):
        cols = slice(p * 128, p * 128 + 128)
        bent = jnp.tanh(ctxt[cols, :].T * inv_of[1])
        cq[:, cols] = (range_of[1] * bent).astype(BF)
        slc[:, cols] = 1.0 - bent * bent
    tot[0] = jnp.zeros((16, WIDE), F32)
    most = jnp.max(jnp.max(jnp.abs(ctxt[...]), axis=0, keepdims=True), axis=1, keepdims=True)
    tot[0, 10:11, :] = jnp.broadcast_to(most, (1, WIDE))

    def out_part(start, held, cols=slice(0, WIDE)):
        held[:, cols] = nt(cq[pl.ds(start, OWN), :], wo[cols, :])

    ex1 = []
    for i in range(2):
        cols = slice(i * HERE, i * HERE + HERE)
        out_part(theirs, exa_s, cols)
        made = copy(exa_s.at[:, cols], exa_r.at[:, cols], ex_s.at[(0, 9)[i]], ex_r.at[(0, 9)[i]], to_c)
        made.start()
        ex1.append(made)
    out_part(mine, r1)
    ag_diag(2, 1)
    ag_strip_got(1)
    for k in range(4):
        ag_last(1, k)
    squash_ff(1, 0)
    squash_ff(1, 1)
    for made in ex1:
        made.wait()

    def sum_rows(v):
        return jnp.sum(v, axis=0, keepdims=True)

    def mean_of(v):
        return jnp.sum(v, axis=-1, keepdims=True) * (1.0 / WIDE)

    def first_norm(i):
        rows = pl.ds(mul8(i * 128, 128), 128)
        v = tok[pl.ds(mul8(mine + i * 128, 128), 128), :].astype(F32)
        v = v + (r1[rows, :] + exa_r[rows, :] + vec[0:1, :])
        r1[rows, :] = v
        center = v - mean_of(v)
        factor = lax.rsqrt(mean_of(center * center) + 1e-12)
        normed = center * factor
        n1[rows, :] = normed
        rstd1[rows, :] = factor
        h = normed * vec[2:3, :] + vec[3:4, :]
        tot[0, 11:12, :] = jnp.maximum(tot[0, 11:12, :], jnp.max(jnp.abs(h), axis=0, keepdims=True))
        bent = jnp.tanh(h * inv_of[2])
        sl1[rows, :] = 1.0 - bent * bent
        hq[pl.ds(mul8(mine + i * 128, 128), 128), :] = (range_of[2] * bent).astype(BF)

    def half_rows(start, i):
        return pl.ds(mul8(start + i * 128, 128), 128)

    for i in range(2):
        first_norm(i)
        own = hq.at[half_rows(mine, i)]
        made = copy(own, own, ex_s.at[(1, 10)[i]], ex_r.at[(1, 10)[i]], to_c)
        made.start()
        started.setdefault("share", []).append((made, None))

    def share_rows(held, number):
        own = held.at[pl.ds(mine, OWN)]
        made = copy(own, own, ex_s.at[number], ex_r.at[number], to_c)
        made.start()
        started.setdefault("share", []).append((made, None))

    def got_rows(held, number):
        other = held.at[pl.ds(theirs, OWN)]
        copy(other, other, ex_s.at[number], ex_r.at[number], to_c).wait_recv()

    def turn_rows(held, out, start):
        out[:, pl.ds(start, OWN)] = held[pl.ds(start, OWN), :].T

    ag_diag(2, 2)
    turn_rows(hq, hqt, mine)
    for i in range(2):
        other = hq.at[half_rows(theirs, i)]
        copy(other, other, ex_s.at[(1, 10)[i]], ex_r.at[(1, 10)[i]], to_c).wait_recv()
    turn_rows(hq, hqt, theirs)

    def expand(xx):
        wide = pl.ds(mul8(xx * WIDE, WIDE), WIDE)

        def body(i):
            rows = pl.ds(mul8(i * 256, 256), 256)
            u = nn(hq[rows, :], wff[0, xx]) + bup[pl.ds(xx, 1), :]
            cdf = 0.5 * (1.0 + lax.erf(u * 0.7071067811865476))
            a = u * cdf
            tot[0, 12:13, :] = jnp.maximum(tot[0, 12:13, :], jnp.max(jnp.abs(a), axis=0, keepdims=True))
            bent = jnp.tanh(a * inv_of[3])
            aq[rows, wide] = (range_of[3] * bent).astype(BF)
            pdf = 0.3989422804014327 * jnp.exp(-0.5 * u * u)
            fac[rows, wide] = ((1.0 - bent * bent) * (cdf + u * pdf)).astype(fac.dtype)

        loop(2, body)

    expand(x)
    ag_diag(2, 3)
    expand(nx)
    ag_strip_got(2)

    def down_part(start, held, xx, first, cols=slice(0, WIDE)):
        got = nt(aq[pl.ds(start, OWN), pl.ds(mul8(xx * WIDE, WIDE), WIDE)], wff[1, xx, cols, :])
        held[:, cols] = got if first else held[:, cols] + got

    squash_ff(2, x)
    down_part(theirs, exb_s, x, True)
    down_part(mine, gr2, x, True)
    for k in range(4):
        ag_last(2, k)
    squash_ff(2, nx)
    ex2 = []
    for i in range(2):
        cols = slice(i * HERE, i * HERE + HERE)
        down_part(theirs, exb_s, nx, False, cols)
        made = copy(exb_s.at[:, cols], exb_r.at[:, cols], ex_s.at[(2, 7)[i]], ex_r.at[(2, 7)[i]], to_c)
        made.start()
        ex2.append(made)
    down_part(mine, gr2, nx, False)
    for made in ex2:
        made.wait()

    def second_norm(i):
        rows = pl.ds(mul8(i * 128, 128), 128)
        v = r1[rows, :] + (gr2[rows, :] + exb_r[rows, :] + vec[1:2, :])
        center = v - mean_of(v)
        factor = lax.rsqrt(mean_of(center * center) + 1e-12)
        normed = center * factor
        o_layer[rows, :] = (normed * vec[4:5, :] + vec[5:6, :]).astype(BF)
        gy = grad_out[rows, :].astype(F32)
        tot[0, 4:5, :] += sum_rows(gy * normed)
        tot[0, 5:6, :] += sum_rows(gy)
        gn = gy * vec[4:5, :]
        back = factor * (gn - mean_of(gn) - normed * mean_of(gn * normed))
        gr2[rows, :] = back
        low = back.astype(BF)
        tot[0, 1:2, :] += sum_rows(low.astype(F32))
        gf[pl.ds(mul8(mine + i * 128, 128), 128), :] = low

    for i in range(2):
        second_norm(i)
        own = gf.at[half_rows(mine, i)]
        made = copy(own, own, ex_s.at[(3, 8)[i]], ex_r.at[(3, 8)[i]], to_c)
        made.start()
        started.setdefault("share", []).append((made, None))
    leave(o_layer, r_layer)
    turn_rows(gf, rowt, mine)
    for g in range(3):
        sent(("ag", g))
    for i in range(2):
        other = gf.at[half_rows(theirs, i)]
        copy(other, other, ex_s.at[(3, 8)[i]], ex_r.at[(3, 8)[i]], to_c).wait_recv()
    turn_rows(gf, rowt, theirs)

    def rs_send(g, number, src, dst, device):
        send("rs", src, dst, rs_s.at[g, number], rs_r.at[g, number], device)

    def rs_send_if(which, g, number, src, dst, device, slot):
        send_if(which, "rs", src, dst, rf_s.at[g, number], slot, device)

    def rs_wait(g, number, dst, device):
        copy(dst, dst, rs_s.at[g, number], rs_r.at[g, number], device).wait_recv()

    def rs_rows(g, part):
        strip, one, two = RS_CUTS[g]
        return pl.ds((0, strip, strip + one, strip)[part], (strip, one, two, one + two)[part])

    def rs_part(g, part):
        _, one, two = RS_CUTS[g]
        return pl.ds((0, 0, one, 0)[part], (0, one, two, one + two)[part])

    far_z, near_z = pl.ds(2 - z // 2 * 2, 2), pl.ds(z // 2 * 2, 2)

    def rs_first(g, near):
        one, two = rs_part(g, 1), rs_part(g, 2)
        rs_send(g, 0, wts.at[g, nx, :, ny, rs_rows(g, 1)], rdx.at[g, :, one], to_x)
        rs_send(g, 1, wts.at[g, nx, :, ny, rs_rows(g, 2)], rdy.at[g, :, pl.ds(0, RS_CUTS[g][2])], to_y)
        rs_send(g, 2, wts.at[g, nx, far_z, y, rs_rows(g, 1)], rxx.at[g, far_z, one], to_x)
        if near:
            rs_send(g, 15, wts.at[g, nx, near_z, y, rs_rows(g, 1)], rxx.at[g, near_z, one], to_x)

    def rs_second(g, near):
        two = rs_part(g, 2)
        rs_send(g, 3, wts.at[g, x, far_z, ny, rs_rows(g, 2)], ryy.at[g, far_z, two], to_y)
        if near:
            rs_send(g, 16, wts.at[g, x, near_z, ny, rs_rows(g, 2)], ryy.at[g, near_z, two], to_y)

    def rs_third_x(g, near):
        one, two = rs_part(g, 1), rs_part(g, 2)
        rs_wait(g, 0, rdx.at[g, :, one], to_x)

        def add_x(i):
            here = rs_rows(g, 1)
            wts[g, x, i, ny, here] = (wts[g, x, i, ny, here].astype(F32) + rdx[g, i, one].astype(F32)).astype(BF)

        loop(4, add_x)
        rs_send(g, 4, wts.at[g, x, far_z, ny, rs_rows(g, 1)], ryy.at[g, far_z, one], to_y)
        rs_send(g, 13, wts.at[g, x, near_z, ny, rs_rows(g, 1)], ryy.at[g, near_z, one], to_y)
        if not near:
            rs_send(g, 16, wts.at[g, x, near_z, ny, rs_rows(g, 2)], ryy.at[g, near_z, two], to_y)

    def rs_third_y(g, near):
        one, two = rs_part(g, 1), rs_part(g, 2)
        far = pl.ds(0, RS_CUTS[g][2])
        rs_wait(g, 1, rdy.at[g, :, far], to_y)

        def add_y(i):
            here = rs_rows(g, 2)
            wts[g, nx, i, y, here] = (wts[g, nx, i, y, here].astype(F32) + rdy[g, i, far].astype(F32)).astype(BF)

        loop(4, add_y)
        rs_send(g, 5, wts.at[g, nx, far_z, y, rs_rows(g, 2)], rxx.at[g, far_z, two], to_x)
        rs_send(g, 14, wts.at[g, nx, near_z, y, rs_rows(g, 2)], rxx.at[g, near_z, two], to_x)
        if not near:
            rs_send(g, 15, wts.at[g, nx, near_z, y, rs_rows(g, 1)], rxx.at[g, near_z, one], to_x)

    def plane(g, zz):
        rest, here = rs_rows(g, 3), rs_part(g, 3)
        return wts[g, x, zz, y, rest].astype(F32) + rxx[g, zz, here].astype(F32) + ryy[g, zz, here].astype(F32)

    def rs_fourth(g):
        one, two, both, rest = rs_part(g, 1), rs_part(g, 2), rs_part(g, 3), rs_rows(g, 3)
        rs_wait(g, 2, rxx.at[g, far_z, one], to_x)
        rs_wait(g, 3, ryy.at[g, far_z, two], to_y)
        rs_wait(g, 4, ryy.at[g, far_z, one], to_y)
        rs_wait(g, 5, rxx.at[g, far_z, two], to_x)
        for k in (3, 2):
            wts[g, x, zk[k], y, rest] = plane(g, zk[k]).astype(BF)
            rs_send_if(
                1, g, k - 2, wts.at[g, x, zk[k], y, rest], rzf.at[g, k - 2, both], to_zk[1], rf_r.at[g, k - 2]
            )

    def rs_near(g):
        one, two, both, rest = rs_part(g, 1), rs_part(g, 2), rs_part(g, 3), rs_rows(g, 3)
        rs_wait(g, 13, ryy.at[g, near_z, one], to_y)
        rs_wait(g, 14, rxx.at[g, near_z, two], to_x)
        rs_wait(g, 15, rxx.at[g, near_z, one], to_x)
        rs_wait(g, 16, ryy.at[g, near_z, two], to_y)
        wts[g, x, zk[1], y, rest] = plane(g, zk[1]).astype(BF)
        rs_send(g, 6, wts.at[g, x, zk[1], y, rest], rz.at[g, 0, both], to_zk[1])

    def rs_fifth(g):
        both, rest = rs_part(g, 3), rs_rows(g, 3)
        for k in (3, 2):

            @pl.when(outer == 0)
            def _(k=k):
                held = rzf.at[g, k - 2, both]
                copy(held, held, rf_s.at[g, 0], rf_r.at[g, k - 2], to_zk[1]).wait_recv()
                wts[g, x, zk[k], y, rest] = (
                    wts[g, x, zk[k], y, rest].astype(F32) + rzf[g, k - 2, both].astype(F32)
                ).astype(BF)

            rs_send_if(0, g, k, wts.at[g, x, zk[k], y, rest], rz.at[g, 1, both], to_zk[k], rs_r.at[g, 7])

    def strips(g, zz):
        return wts.at[g, :, zz, :, pl.ds(0, RS_CUTS[g][0])]

    def rs_strip_z(g):
        here = pl.ds(0, RS_CUTS[g][0])
        for k in (3, 2):
            rs_send_if(1, g, 2 + k, strips(g, zk[k]), rzf2.at[g, k - 2, :, :, here], to_zk[1], rf_r.at[g, k])
        rs_send(g, 8, strips(g, zk[1]), rz2.at[g, 0, :, :, here], to_zk[1])

    def rs_strip_fwd(g):
        here = pl.ds(0, RS_CUTS[g][0])
        for k in (3, 2):

            @pl.when(outer == 0)
            def _(k=k):
                held = rzf2.at[g, k - 2, :, :, here]
                copy(held, held, rf_s.at[g, 0], rf_r.at[g, k], to_zk[1]).wait_recv()
                wts[g, :, zk[k], :, here] = (
                    wts[g, :, zk[k], :, here].astype(F32) + rzf2[g, k - 2, :, :, here].astype(F32)
                ).astype(BF)

            rs_send_if(0, g, 4 + k, strips(g, zk[k]), rz2.at[g, 1, :, :, here], to_zk[k], rs_r.at[g, 9])

    def rs_strip_sum(g):
        here = pl.ds(0, RS_CUTS[g][0])
        for k in (0, 1):
            rs_wait(g, 8 + k, rz2.at[g, k, :, :, here], to_zk[1 + k])
        wts[g, :, z, :, here] = (
            wts[g, :, z, :, here].astype(F32)
            + rz2[g, 0, :, :, here].astype(F32)
            + rz2[g, 1, :, :, here].astype(F32)
        ).astype(BF)

    def rs_strip_send(g):
        here = pl.ds(0, RS_CUTS[g][0])
        rs_send(g, 12, wts.at[g, nx, z, ny, here], rst.at[g, 2, here], to_xy)
        rs_send(g, 10, wts.at[g, nx, z, y, here], rst.at[g, 0, here], to_x)
        rs_send(g, 11, wts.at[g, x, z, ny, here], rst.at[g, 1, here], to_y)

    def rs_total(g):
        here, both = pl.ds(0, RS_CUTS[g][0]), rs_part(g, 3)
        for k in (0, 1):
            rs_wait(g, 6 + k, rz.at[g, k, both], to_zk[1 + k])
        for i, device in enumerate((to_x, to_y, to_xy)):
            rs_wait(g, 10 + i, rst.at[g, i, here], device)
        strip = wts[g, x, z, y, here].astype(F32)
        for i in range(3):
            strip = strip + rst[g, i, here].astype(F32)
        total = plane(g, z)
        for k in range(2):
            total = total + rz[g, k, both].astype(F32)
        return jnp.concatenate([strip, total], axis=0)

    def ff_grad(g, turned, held, xx):
        got = nn(turned[...], held[:, pl.ds(mul8(xx * WIDE, WIDE), WIDE)])
        wts[g, xx] = got.reshape(4, 2, PIECE, WIDE).astype(BF)

    ff_grad(2, rowt, aq, nx)
    rs_first(2, True)
    ff_grad(2, rowt, aq, x)
    rs_second(2, True)
    rs_strip_z(2)

    for xx in range(2):

        def hidden_grad(i, xx=xx):
            wide = slice(xx * WIDE, xx * WIDE + WIDE)
            rows = pl.ds(mul8(i * 256, 256), 256)
            got = (nn(gf[rows, :], wff[1, xx]) * fac[rows, wide].astype(F32)).astype(BF)
            gu[rows, wide] = got
            tot[0, 6 + xx : 7 + xx, :] += sum_rows(got.astype(F32))

        loop(2, hidden_grad)
    def up_part(start, held):
        held[...] = nt(gu[pl.ds(start, OWN), 0:WIDE], wff[0, 0]) + nt(
            gu[pl.ds(start, OWN), WIDE : 2 * WIDE], wff[0, 1]
        )

    up_part(theirs, exa_s)
    ex3 = copy(exa_s, exa_r, ex_s.at[4], ex_r.at[4], to_c)
    ex3.start()
    up_part(mine, r1)
    ff_grad(1, hqt, gu, nx)
    rs_third_x(2, True)
    rs_third_y(2, True)
    rs_first(1, True)
    ff_grad(1, hqt, gu, x)
    rs_second(1, True)
    rs_strip_z(1)
    ex3.wait()

    def first_back(i):
        rows = pl.ds(mul8(i * 64, 64), 64)
        normed = n1[rows, :]
        gh = (r1[rows, :] + exa_r[rows, :]) * sl1[rows, :]
        tot[0, 2:3, :] += sum_rows(gh * normed)
        tot[0, 3:4, :] += sum_rows(gh)
        gn = gh * vec[2:3, :]
        back = rstd1[rows, :] * (gn - mean_of(gn) - normed * mean_of(gn * normed)) + gr2[rows, :]
        gr2[rows, :] = back
        low = back.astype(BF)
        tot[0, 0:1, :] += sum_rows(low.astype(F32))
        gf[pl.ds(mul8(mine + i * 64, 64), 64), :] = low

    sent("share")
    loop(4, first_back)
    share_rows(gf, 5)
    turn_rows(gf, rowt, mine)
    got_rows(gf, 5)
    turn_rows(gf, rowt, theirs)

    gwo[...] = nn(rowt[...], cq[...])
    gc[...] = (nn(gf[...], wo[...]) * slc[...]).astype(BF)
    for p in range(3):
        cols = slice(p * 128, p * 128 + 128)
        gct[cols, :] = gc[:, cols].T
        for e in range(2):
            feats = slice(p * 128 + e * 64, p * 128 + e * 64 + 64)
            dsum[p * 2 + e : p * 2 + e + 1, :] = sum_rows(gct[feats, :].astype(F32) * ctxt[feats, :])

    row_half = lax.broadcasted_iota(jnp.int32, (128, 1), 0) // 64

    def attend_back(p):
        cols = pl.ds(mul8(p * 128, 128), 128)
        grad_k = grad_v = None
        for e in range(2):
            feats = pl.ds(mul8(p * 128 + e * 64, 64), 64)
            for n in range(2):
                part = slice(n * 256, n * 256 + 256)
                g = gct[cols, part]
                g = jnp.where(row_half == e, g, jnp.zeros_like(g))
                dpr = nn(vs[:, cols], g)
                ds[:, part] = (probs[p * 2 + e, :, part].astype(F32) * (dpr - dsum[pl.ds(p * 2 + e, 1), part])).astype(BF)
            g = gc[:, cols]
            g = jnp.where(half_of == e, g, jnp.zeros_like(g))
            more_v = nn(probs[p * 2 + e], g)
            q = qs[:, cols]
            q = jnp.where(half_of == e, q, jnp.zeros_like(q))
            more_k = nn(ds[...], q)
            grad_v = more_v if e == 0 else grad_v + more_v
            grad_k = more_k if e == 0 else grad_k + more_k
            gqt[feats, :] = nn(kt[feats, :], ds[...])
        grads[:, pl.ds(mul8(HERE + p * 128, 128), 128)] = grad_k.astype(BF)
        grads[:, pl.ds(mul8(2 * HERE + p * 128, 128), 128)] = grad_v.astype(BF)
        grads[:, cols] = (gqt[cols, :].astype(BF).astype(F32) * 0.125).T.astype(BF)

    attend_back(0)
    attend_back(1)
    attend_back(2)
    rs_strip_fwd(2)
    rs_fourth(2)
    rs_near(2)
    for j, part in ((0, 0), (2, HERE)):
        tot[0, 8:9, part : part + HERE] = sum_rows(grads[:, j * HERE : (j + 1) * HERE].astype(F32))

    left_four = lax.broadcasted_iota(jnp.int32, (4 * PIECE, 128), 1) < 64

    def head_grad(i):
        rows = pl.ds(mul8(i * 4 * PIECE, 4 * PIECE), 4 * PIECE)
        gq, gk, gv = (nn(xqt[rows, :], grads[:, j * HERE : (j + 1) * HERE]) for j in range(3))
        parts = (gq, gk, gv, gwo[rows, :])

        def put(xx, t, v):
            wts[0, xx, pl.ds(i * 2, 2), :, :, t * 128 : t * 128 + 128] = v.reshape(2, 2, PIECE, 128).astype(BF)

        for xx in range(2):
            for t in range(4):
                put(xx, t, parts[t][:, xx * 128 : xx * 128 + 128])
        for t, first, second in ((4, gq, gk), (5, gv, gwo[rows, :])):
            one, two = first[:, 256:384], second[:, 256:384]
            put(0, t, jnp.where(left_four, one, pltpu.roll(two, 64, 1)))
            put(1, t, jnp.where(left_four, pltpu.roll(one, 64, 1), two))

    def most_x(i):
        v = jnp.abs(tok[pl.ds(mul8(i * 128, 128), 128), :].astype(F32))
        tot[0, 9:10, :] = jnp.maximum(tot[0, 9:10, :], jnp.max(v, axis=0, keepdims=True))

    loop(4, most_x)
    row_of = lax.broadcasted_iota(jnp.int32, (16, 1), 0)
    small = copy(tot.at[0], tot_c, tt_s.at[0], tt_r.at[0], to_c)
    small.start()
    loop(2, head_grad)
    small.wait()
    mixed = jnp.where(row_of < 6, tot[0] + tot_c[...], jnp.maximum(tot[0], tot_c[...]))
    tot[1] = jnp.where((row_of >= 6) & (row_of < 9), tot[0], mixed)
    small = copy(tot.at[1], tot_x, tt_s.at[1], tt_r.at[1], to_x)
    small.start()
    rs_first(0, False)
    rs_second(0, False)
    rs_strip_z(0)

    def token_part(start, held):
        held[...] = nt(grads[pl.ds(start, OWN), :], wc[...])

    token_part(theirs, exb_s)
    ex4 = copy(exb_s, exb_r, ex_s.at[6], ex_r.at[6], to_c)
    ex4.start()
    rs_third_x(1, True)
    rs_third_y(1, True)
    token_part(mine, r1)
    ex4.wait()

    def token_grad(i):
        rows = pl.ds(mul8(i * 64, 64), 64)
        v = tok[pl.ds(mul8(mine + i * 64, 64), 64), :].astype(F32)
        bent = jnp.tanh(v * inv_of[0])
        got = gr2[rows, :] + (r1[rows, :] + exb_r[rows, :]) * (1.0 - bent * bent)
        o_tok[pl.ds(mul8(mp * OWN + i * 64, 64), 64), :] = got.astype(BF)

    loop(4, token_grad)
    own = o_tok.at[pl.ds(mul8(mp * OWN, OWN), OWN)]
    send("tok", own, own, gx_s.at[1], gx_r.at[1], to_c)
    leave_rows(mp)
    rs_strip_fwd(1)
    small.wait()
    tot[2] = jnp.where(row_of < 9, tot[1] + tot_x[...], jnp.maximum(tot[1], tot_x[...]))
    small = copy(tot.at[2], tot_y, tt_s.at[2], tt_r.at[2], to_y)
    small.start()
    rs_third_x(0, False)
    rs_fifth(2)
    rs_third_y(0, False)
    send("tok", own, own, gx_s.at[0], gx_r.at[0], to_x)
    for g in (2, 1):
        rs_strip_sum(g)
        rs_strip_send(g)
    rs_strip_fwd(0)
    rs_fourth(1)
    rs_near(1)
    small.wait()
    tot[3] = jnp.where(row_of < 9, tot[2] + tot_y[...], jnp.maximum(tot[2], tot_y[...]))
    smalls = []
    for k in (1, 2, 3):
        made = copy(tot.at[3], tot_z.at[k - 1], tt_s.at[2 + k], tt_r.at[2 + k], to_z[k])
        made.start()
        smalls.append(made)
    rs_fourth(0)
    rs_strip_sum(0)
    rs_strip_send(0)
    rs_fifth(1)
    rs_near(0)
    rs_fifth(0)
    o_down[...] = rs_total(2) * _slope(w_down[...], w_inv[3])
    leave(o_down, r_down)
    o_up[...] = rs_total(1) * _slope(w_up[...], w_inv[2])
    leave(o_up, r_up)

    far = o_tok.at[pl.ds(mul8((nx * 2 + c) * OWN, OWN), OWN)]
    copy(far, far, gx_s.at[0], gx_r.at[0], to_x).wait_recv()
    send("tok", far, far, gx_s.at[2], gx_r.at[2], to_c)
    leave_rows(nx * 2 + c)

    for made in smalls:
        made.wait()
    done = tot[3]
    for k in range(3):
        done = jnp.where(row_of < 9, done + tot_z[k], jnp.maximum(done, tot_z[k]))
    back = pltpu.roll(done, (8 - dp) * 96, 1)
    o_vec[...] = back[0:6, 0:96]
    ups = jnp.where(x == 0, done[6:7, :], done[7:8, :])
    for h in range(3):
        tile = jnp.broadcast_to(ups[:, h * 256 : h * 256 + 256], (8, 256))
        o_bup[h : h + 1, :] = pltpu.roll(tile, (8 - dp) * 32, 1)[0:1, 0:32]
    for j in range(2):
        row = jnp.broadcast_to(done[8:9, j * HERE : (j + 1) * HERE], (8, HERE))
        pair = jnp.where(x == 0, row[:, 0:128], row[:, 128:256])
        for h, tile, shift in ((0, pair, 0), (1, pair, 64), (2, row[:, 256:384], 64 * x)):
            o_bqv[h, j : j + 1, :] = pltpu.roll(tile, (256 - shift - dp * 8) % 128, 1)[0:1, 0:8]
    for i in range(4):
        most = jnp.max(done[9 + i : 10 + i, :], axis=1, keepdims=True)
        o_rng[i : i + 1, :] = jnp.broadcast_to(0.9 * range_of[i] + 0.1 * most, (1, 128))

    for here, there in ((o_vec, r_vec), (o_bup, r_bup), (o_bqv, r_bqv), (o_rng, r_rng)):
        leave(here, there)
    near = pl.ds(mul8((x * 2 + nc) * OWN, OWN), OWN)
    copy(o_tok.at[near], o_tok.at[near], gx_s.at[1], gx_r.at[1], to_c).wait_recv()
    leave_rows(x * 2 + nc)
    total = rs_total(0)
    for j in range(4):
        main = total[:, j * 128 : j * 128 + 128]
        pair = total[:, 512 + j // 2 * 128 : 640 + j // 2 * 128]
        if j % 2:
            pair = pltpu.roll(pair, 64, 1)
        whole = jnp.concatenate([main, pair], axis=1)[:, 0:192]
        if j < 3:
            o_qkv[j] = whole * _slope(w_qkv[j], w_inv[0])
        else:
            o_out[...] = whole.T * _slope(w_out[...], w_inv[1])
    leave(o_qkv, r_qkv)
    leave(o_out, r_out)
    far = pl.ds(mul8((nx * 2 + nc) * OWN, OWN), OWN)
    copy(o_tok.at[far], o_tok.at[far], gx_s.at[2], gx_r.at[2], to_c).wait_recv()
    leave_rows(nx * 2 + nc)
    for group in list(started):
        sent(group)
    for made in leaving:
        made.wait()


def _slope(values, inverse):
    bent = jnp.tanh(values.astype(F32) * inverse)
    return 1.0 - bent * bent


def layer_on_chips(
    tokens, w_qkv, w_out, w_up, w_down, b_qv, b_up, vectors, ema_ranges, key_mask, long_rows, grad_out
):
    vmem = pltpu.VMEM
    rows = tokens.shape[0]
    half = rows // 2

    def buffer(*shape, dtype=BF):
        return vmem(shape, dtype)

    def f32(*shape):
        return vmem(shape, F32)

    sems = pltpu.SemaphoreType.DMA
    ins = (w_qkv, w_out, w_up, w_down.T, b_qv.transpose(1, 0, 2), b_up, vectors)
    mask = key_mask.reshape(rows // 128, 128)
    kinds = [
        jax.ShapeDtypeStruct(grad_out.shape, BF),
        jax.ShapeDtypeStruct(tokens.shape, BF),
        *(jax.ShapeDtypeStruct(v.shape, F32) for v in ins),
    ]
    scratch = [
        buffer(half, WIDE),
        *(vmem(v.shape, v.dtype) for v in (*ins, mask, grad_out)),
        *(vmem(v.shape, v.dtype) for v in kinds),
        pltpu.SMEM(ema_ranges.shape, F32),
        pltpu.SMEM(long_rows.shape, jnp.int32),
        f32(8, 128),
        buffer(3, 2, 4, 2, PIECE, WIDE),
        buffer(2, 2, WIDE, WIDE),
        buffer(WIDE, 3 * HERE),
        buffer(WIDE, HERE),
        buffer(3, 4, 48, WIDE),
        buffer(3, 4, 48, WIDE),
        buffer(3, 4, 80, WIDE),
        buffer(3, 4, 80, WIDE),
        buffer(3, 2, 80, WIDE),
        buffer(3, 2, 80, WIDE),
        buffer(3, 2, 2, 2, 32, WIDE),
        buffer(3, 2, 2, 2, 32, WIDE),
        buffer(3, 3, 32, WIDE),
        f32(2, 4, 2, 16, 128),
        f32(16, 128),
        f32(16, WIDE),
        f32(8, WIDE),
        f32(8, HERE),
        buffer(half, WIDE),
        buffer(WIDE, half),
        f32(half, half),
        buffer(half, HERE),
        buffer(half, HERE),
        buffer(half, HERE),
        buffer(HERE, half),
        buffer(HERE, half),
        buffer(6, half, half),
        buffer(half, half),
        f32(HERE, half),
        buffer(half, HERE),
        f32(half, HERE),
        f32(OWN, WIDE),
        f32(OWN, WIDE),
        f32(OWN, WIDE),
        f32(OWN, WIDE),
        buffer(half, WIDE),
        buffer(WIDE, half),
        f32(OWN, WIDE),
        f32(OWN, WIDE),
        f32(OWN, 1),
        f32(OWN, WIDE),
        buffer(half, 2 * WIDE),
        buffer(half, 2 * WIDE),
        buffer(half, 2 * WIDE),
        buffer(half, WIDE),
        buffer(WIDE, half),
        f32(OWN, WIDE),
        buffer(half, HERE),
        buffer(HERE, half),
        f32(8, half),
        buffer(half, 3 * HERE),
        f32(HERE, half),
        f32(WIDE, HERE),
        f32(4, 16, WIDE),
        f32(16, WIDE),
        f32(16, WIDE),
        f32(16, WIDE),
        f32(3, 16, WIDE),
        sems((3, 2)),
        sems((3, 2)),
        sems((3, 3)),
        sems((3, 2)),
        sems((3, 2)),
        sems((3, 3)),
        sems((3, 3)),
        sems((3, 3)),
        sems((3, 4)),
        sems((3, 4)),
        sems((3, 4)),
        sems((3, 4)),
        sems((3, 4)),
        sems((3, 4)),
        sems((3, 4)),
        sems((3, 4)),
        sems((3, 17)),
        sems((3, 17)),
        sems((3, 8)),
        sems((3, 4)),
        sems((7,)),
        sems((7,)),
        sems((11,)),
        sems((11,)),
        sems((6,)),
        sems((6,)),
        sems((3,)),
        sems((3,)),
        sems((14,)),
        sems((13,)),
    ]
    far = pl.BlockSpec(memory_space=pltpu.HBM)
    outs = pl.pallas_call(
        layer_kernel,
        out_shape=[*kinds, jax.ShapeDtypeStruct((8, 128), F32)],
        in_specs=[far] * 12,
        out_specs=[far] * 10,
        scratch_shapes=scratch,
        compiler_params=pltpu.CompilerParams(
            collective_id=0, has_side_effects=True, vmem_limit_bytes=VMEM_LIMIT
        ),
        name="encoder_layer",
    )(tokens, *ins, ema_ranges, mask, long_rows, grad_out)
    outs = finish(outs, ema_ranges)
    return (*outs[:5], outs[5].T, outs[6].transpose(1, 0, 2), *outs[7:])


def finish_kernel(*refs):
    ins, outs, held, wide, sem = refs[:10], refs[10:20], refs[20:30], refs[30], refs[31]
    step = OWN // 2
    parts = [pl.ds(i * step, step) for i in range(ins[1].shape[0] // step)]
    arriving = [pltpu.make_async_copy(ins[1].at[p], held[1].at[p], sem.at[10 + i]) for i, p in enumerate(parts)]
    moved = [i for i in range(10) if i != 1]
    arriving += [pltpu.make_async_copy(ins[i], held[i], sem.at[i]) for i in moved]
    leaving = [pltpu.make_async_copy(wide.at[p], outs[1].at[p], sem.at[10 + i]) for i, p in enumerate(parts)]
    leaving += [pltpu.make_async_copy(held[i], outs[i], sem.at[i]) for i in moved[:-1]]
    for made in arriving:
        made.start()
    for i, (here, there) in enumerate(zip(arriving, leaving)):
        here.wait()
        if i < len(parts):
            wide[parts[i], :] = held[1][parts[i], :].astype(F32)
        there.start()
    arriving[-1].wait()
    for i in range(4):
        outs[9][i] = held[9][i, 0]
    for made in leaving:
        made.wait()


def finish(held, ranges):
    shape = jax.ShapeDtypeStruct
    far = pl.BlockSpec(memory_space=pltpu.HBM)
    return pl.pallas_call(
        finish_kernel,
        out_shape=[shape(v.shape, F32 if i == 1 else v.dtype) for i, v in enumerate(held[:9])]
        + [shape(ranges.shape, F32)],
        in_specs=[far] * 10,
        out_specs=[far] * 9 + [pl.BlockSpec(memory_space=pltpu.SMEM)],
        scratch_shapes=[pltpu.VMEM(v.shape, v.dtype) for v in held]
        + [pltpu.VMEM(held[1].shape, F32), pltpu.SemaphoreType.DMA((10 + held[1].shape[0] * 2 // OWN,))],
        compiler_params=pltpu.CompilerParams(vmem_limit_bytes=VMEM_LIMIT),
        name="write_results",
    )(*held)


VMEM_LIMIT = 64 * 1024 * 1024


def solution(mesh):
    placed = (
        P("dp", None),
        P(None, "dp", "mp"),
        P("mp", "dp"),
        P("dp", "mp"),
        P("mp", "dp"),
        P(None, "mp", "dp"),
        P("mp", "dp"),
        P(None, "dp"),
        P(),
        P("dp"),
        P("dp"),
        P(("dp", "mp"), None),
    )
    on_chips = dict(mesh.shape) == {"dp": 8, "mp": 4}
    return jax.shard_map(
        layer_on_chips if on_chips else per_device,
        mesh=mesh,
        in_specs=placed,
        out_specs=(
            P(("dp", "mp"), None),
            P("dp", None),
            P(None, "dp", "mp"),
            P("mp", "dp"),
            P("dp", "mp"),
            P("mp", "dp"),
            P(None, "mp", "dp"),
            P("mp", "dp"),
            P(None, "dp"),
            P(),
        ),
        check_vma=False,
    )
```

```python
import functools
import math

import jax
import jax.numpy as jnp
from jax import lax
from jax.experimental import pallas as pl
from jax.experimental.pallas import tpu as pltpu
from jax.sharding import PartitionSpec as P

HD = 64
BLOCK = 512
SEG = 128


eps_norm = 1e-12
root_half = 0.7071067811865476
inv_root_tau = 0.3989422804014327


def squash(values, limit):
    return limit * jnp.tanh(values / limit)


def slope(values, limit):
    bent = jnp.tanh(values / limit)
    return 1.0 - bent * bent


def peak_of(values):
    return jnp.max(jnp.abs(values.astype(jnp.float32)))


def product(left, right):
    return jnp.dot(left, right, preferred_element_type=jnp.float32)


def contract_rows(left, right):
    return lax.dot_general(
        left, right, (((0,), (0,)), ((), ())), preferred_element_type=jnp.float32
    )


def contract_cols(left, right):
    return lax.dot_general(
        left, right, (((1,), (1,)), ((), ())), preferred_element_type=jnp.float32
    )


def normalize(values):
    center = values - jnp.mean(values, axis=-1, keepdims=True)
    factor = lax.rsqrt(jnp.mean(center * center, axis=-1, keepdims=True) + eps_norm)
    return (center * factor, factor)


def norm_back(grad_normed, normed, factor):
    first_mean = jnp.mean(grad_normed, axis=-1, keepdims=True)
    cross_mean = jnp.mean(grad_normed * normed, axis=-1, keepdims=True)
    return factor * (grad_normed - first_mean - normed * cross_mean)


def allowed_keys(live, long_flag):
    places = jnp.arange(BLOCK) // SEG
    return (live[None, :] > 0) & ((long_flag > 0) | (places[:, None] == places[None, :]))


def block_scores(queries, keys_in, live, long_flag):
    scores = jnp.einsum("qhd,khd->hqk", queries, keys_in, preferred_element_type=jnp.float32)
    return jnp.where(allowed_keys(live, long_flag)[None], scores, -1e30)


def attend_block(pieces):
    queries, keys_in, values, live, long_flag = pieces
    scores = block_scores(queries, keys_in, live, long_flag)
    top_score = jnp.max(scores, axis=-1, keepdims=True)
    weights = jnp.exp(scores - top_score)
    totals = jnp.sum(weights, axis=-1, keepdims=True)
    attn_probs = (weights / totals).astype(jnp.bfloat16)
    context = jnp.einsum("hqk,khd->qhd", attn_probs, values, preferred_element_type=jnp.float32)
    return (context, top_score + jnp.log(totals))


def attend_back(pieces):
    queries, keys_in, values, live, long_flag, log_total, grad_ctx = pieces
    attn_probs = jnp.exp(block_scores(queries, keys_in, live, long_flag) - log_total)
    grad_probs = jnp.einsum("qhd,khd->hqk", grad_ctx, values, preferred_element_type=jnp.float32)
    grad_values = jnp.einsum(
        "hqk,qhd->khd",
        attn_probs.astype(jnp.bfloat16),
        grad_ctx,
        preferred_element_type=jnp.float32,
    )
    inner = jnp.sum(grad_probs * attn_probs, axis=-1, keepdims=True)
    grad_scores = (attn_probs * (grad_probs - inner)).astype(jnp.bfloat16)
    grad_queries = jnp.einsum(
        "hqk,khd->qhd", grad_scores, keys_in, preferred_element_type=jnp.float32
    )
    grad_keys = jnp.einsum("hqk,qhd->khd", grad_scores, queries, preferred_element_type=jnp.float32)
    return (
        grad_queries.astype(jnp.bfloat16),
        grad_keys.astype(jnp.bfloat16),
        grad_values.astype(jnp.bfloat16),
    )


def prepare(gathered, w_peaks):
    return tuple(
        (
            squash(gathered[index].astype(jnp.float32), w_peaks[index]).astype(jnp.bfloat16)
            for index in range(4)
        )
    )


def peak_all(values):
    return lax.pmax(peak_of(values), ("dp", "mp"))


def per_device(
    tokens,
    w_qkv,
    w_out,
    w_up,
    w_down,
    b_qv,
    b_up,
    vectors,
    ema_ranges,
    key_mask,
    long_rows,
    grad_out,
):
    row_count = tokens.shape[0]
    quarter = row_count // lax.axis_size("mp")
    row_start = lax.axis_index("mp") * quarter
    blocks = row_count // BLOCK
    w_peaks = lax.pmax(
        (peak_of(w_qkv), peak_of(w_out), peak_of(w_up), peak_of(w_down)), ("dp", "mp")
    )
    gathered = (
        lax.all_gather(w_qkv, "dp", axis=1, tiled=True),
        lax.all_gather(w_out, "dp", axis=1, tiled=True),
        lax.all_gather(w_up, "dp", axis=0, tiled=True),
        lax.all_gather(w_down, "dp", axis=1, tiled=True),
        lax.all_gather(b_qv, "dp", axis=2, tiled=True),
        lax.all_gather(b_up, "dp", axis=1, tiled=True),
        lax.all_gather(vectors, "dp", axis=1, tiled=True),
    )
    qkv_q, out_q, up_q, down_q = prepare(gathered, w_peaks)
    bias_qv = gathered[4].astype(jnp.float32).reshape(2, -1)
    bias_up = gathered[5].astype(jnp.float32).reshape(-1)
    vec = gathered[6].astype(jnp.float32)
    head_width = bias_qv.shape[1]
    heads_here = head_width // HD
    scale_q = HD ** (-0.5)
    tok_float = tokens.astype(jnp.float32)
    peak_tok = peak_all(tok_float)
    tok_quant = squash(tok_float, ema_ranges[0]).astype(jnp.bfloat16)
    projected = jnp.einsum("td,jde->jte", tok_quant, qkv_q, preferred_element_type=jnp.float32)
    queries = ((projected[0] + bias_qv[0]) * scale_q).astype(jnp.bfloat16)
    keys_all = projected[1].astype(jnp.bfloat16)
    values = (projected[2] + bias_qv[1]).astype(jnp.bfloat16)
    shape_four = (blocks, BLOCK, heads_here, HD)
    mask_blocks = key_mask.reshape(blocks, BLOCK)
    block_inputs = (
        queries.reshape(shape_four),
        keys_all.reshape(shape_four),
        values.reshape(shape_four),
        mask_blocks,
        long_rows,
    )
    context, log_total = lax.map(attend_block, block_inputs)
    context = context.reshape(row_count, head_width)
    peak_ctx = peak_all(context)
    ctx_quant = squash(context, ema_ranges[1]).astype(jnp.bfloat16)
    partial_attn = product(ctx_quant, out_q)
    attn = lax.psum_scatter(partial_attn, "mp", scatter_dimension=0, tiled=True) + vec[0]
    first_own = lax.dynamic_slice_in_dim(tok_float, row_start, quarter, 0) + attn
    normed, factor_one = normalize(first_own)
    hidden_in = normed * vec[2] + vec[3]
    hid_quant = lax.all_gather(
        squash(hidden_in, ema_ranges[2]).astype(jnp.bfloat16), "mp", axis=0, tiled=True
    )
    peak_hid = peak_all(hidden_in)
    pre_act = product(hid_quant, up_q) + bias_up
    active = pre_act * 0.5 * (1.0 + lax.erf(pre_act * root_half))
    peak_act = peak_all(active)
    act_quant = squash(active, ema_ranges[3]).astype(jnp.bfloat16)
    branch = (
        lax.psum_scatter(product(act_quant, down_q), "mp", scatter_dimension=0, tiled=True) + vec[1]
    )
    second = first_own + branch
    normed_two, factor_two = normalize(second)
    layer_out = (normed_two * vec[4] + vec[5]).astype(jnp.bfloat16)
    new_ranges = 0.9 * ema_ranges + 0.1 * jnp.stack([peak_tok, peak_ctx, peak_hid, peak_act])
    gathered = (
        lax.all_gather(w_qkv, "dp", axis=1, tiled=True),
        lax.all_gather(w_out, "dp", axis=1, tiled=True),
        lax.all_gather(w_up, "dp", axis=0, tiled=True),
        lax.all_gather(w_down, "dp", axis=1, tiled=True),
        lax.all_gather(b_qv, "dp", axis=2, tiled=True),
        lax.all_gather(b_up, "dp", axis=1, tiled=True),
        lax.all_gather(vectors, "dp", axis=1, tiled=True),
    )
    qkv_q, out_q, up_q, down_q = prepare(gathered, w_peaks)
    grad_y = grad_out.astype(jnp.float32)
    grad_gain_two = jnp.sum(grad_y * normed_two, axis=0)
    grad_shift_two = jnp.sum(grad_y, axis=0)
    grad_second = norm_back(grad_y * vec[4], normed_two, factor_two)
    grad_resid = lax.all_gather(grad_second.astype(jnp.bfloat16), "mp", axis=0, tiled=True).astype(
        grad_second.dtype
    )
    grad_branch = grad_resid.astype(jnp.bfloat16)
    grad_bias_down = jnp.sum(grad_branch.astype(jnp.float32), axis=0)
    grad_down_w = contract_rows(act_quant, grad_branch)
    grad_active = contract_cols(grad_branch, down_q) * slope(active, ema_ranges[3])
    normal_cdf = 0.5 * (1.0 + lax.erf(pre_act * root_half))
    normal_pdf = inv_root_tau * jnp.exp(-0.5 * pre_act * pre_act)
    grad_pre = (grad_active * (normal_cdf + pre_act * normal_pdf)).astype(jnp.bfloat16)
    grad_bias_up = jnp.sum(grad_pre.astype(jnp.float32), axis=0)
    grad_up_w = contract_rows(hid_quant, grad_pre)
    partial_hid = contract_cols(grad_pre, up_q)
    grad_hid_q = lax.psum_scatter(partial_hid, "mp", scatter_dimension=0, tiled=True)
    grad_hidden = grad_hid_q * slope(hidden_in, ema_ranges[2])
    grad_gain_one = jnp.sum(grad_hidden * normed, axis=0)
    grad_shift_one = jnp.sum(grad_hidden, axis=0)
    grad_first = norm_back(grad_hidden * vec[2], normed, factor_one) + grad_second
    grad_attn = lax.all_gather(grad_first.astype(jnp.bfloat16), "mp", axis=0, tiled=True)
    grad_bias_out = jnp.sum(grad_attn.astype(jnp.float32), axis=0)
    grad_out_w = contract_rows(ctx_quant, grad_attn)
    grad_ctx = (contract_cols(grad_attn, out_q) * slope(context, ema_ranges[1])).astype(
        jnp.bfloat16
    )
    back_inputs = block_inputs + (log_total, grad_ctx.reshape(shape_four))
    grad_q, grad_k, grad_v = lax.map(attend_back, back_inputs)
    stacked = jnp.stack(
        [
            grad_q.reshape(row_count, head_width) * jnp.bfloat16(scale_q),
            grad_k.reshape(row_count, head_width),
            grad_v.reshape(row_count, head_width),
        ]
    )
    grad_qkv_w = jnp.einsum("td,jte->jde", tok_quant, stacked, preferred_element_type=jnp.float32)
    stacked_float = stacked.astype(jnp.float32)
    grad_bias_qv = jnp.stack([jnp.sum(stacked_float[0], axis=0), jnp.sum(stacked_float[2], axis=0)])
    part_input = jnp.einsum("jte,jde->td", stacked, qkv_q, preferred_element_type=jnp.float32)
    own_term = part_input * slope(tok_float, ema_ranges[0])
    own_rows = lax.dynamic_slice_in_dim(own_term, row_start, quarter, 0) + grad_first
    own_term = lax.dynamic_update_slice_in_dim(own_term, own_rows, row_start, 0)
    grad_tokens, norm_tail = (
        lax.psum(own_term.astype(jnp.bfloat16), "mp").astype(jnp.float32),
        lax.psum(
            jnp.stack([grad_gain_one, grad_shift_one, grad_gain_two, grad_shift_two]).astype(
                jnp.bfloat16
            ),
            "mp",
        ).astype(jnp.float32),
    )
    grad_vec = jnp.stack(
        [grad_bias_out, grad_bias_down, norm_tail[0], norm_tail[1], norm_tail[2], norm_tail[3]]
    )
    summed = (
        lax.psum_scatter(
            grad_qkv_w * slope(gathered[0].astype(jnp.float32), w_peaks[0]),
            "dp",
            scatter_dimension=1,
            tiled=True,
        ),
        lax.psum_scatter(
            grad_out_w * slope(gathered[1].astype(jnp.float32), w_peaks[1]),
            "dp",
            scatter_dimension=1,
            tiled=True,
        ),
        lax.psum_scatter(
            grad_up_w * slope(gathered[2].astype(jnp.float32), w_peaks[2]),
            "dp",
            scatter_dimension=0,
            tiled=True,
        ),
        lax.psum_scatter(
            grad_down_w * slope(gathered[3].astype(jnp.float32), w_peaks[3]),
            "dp",
            scatter_dimension=1,
            tiled=True,
        ),
        lax.psum_scatter(
            grad_bias_qv.reshape(gathered[4].shape), "dp", scatter_dimension=2, tiled=True
        ),
        lax.psum_scatter(
            grad_bias_up.reshape(gathered[5].shape), "dp", scatter_dimension=1, tiled=True
        ),
        lax.psum_scatter(grad_vec, "dp", scatter_dimension=1, tiled=True),
    )
    return (
        layer_out,
        grad_tokens,
        summed[0],
        summed[1],
        summed[2],
        summed[3],
        summed[4],
        summed[5],
        summed[6],
        new_ranges,
    )


BF = jnp.bfloat16
F32 = jnp.float32
MESH = pl.DeviceIdType.MESH
WIDE = 768
PIECE = 96
AG_CUTS = ((0, 48, 48), (16, 32, 48), (32, 32, 32))
RS_CUTS = ((16, 32, 48), (32, 16, 48), (32, 32, 32))
OWN = 256
HERE = 384


def nn(left, right):
    return lax.dot_general(left, right, (((1,), (0,)), ((), ())), preferred_element_type=F32)


def nt(left, right):
    return lax.dot_general(left, right, (((1,), (1,)), ((), ())), preferred_element_type=F32)


def mul8(value, step):
    return pl.multiple_of(value, step)


def loop(count, body):
    def step(index, carry):
        body(index)
        return carry

    lax.fori_loop(0, count, step, 0)


def layer_kernel(
    h_tok,
    h_qkv,
    h_out,
    h_up,
    h_down,
    h_bqv,
    h_bup,
    h_vec,
    h_rng,
    h_mask,
    h_long,
    h_grad,
    r_layer,
    r_tok,
    r_qkv,
    r_out,
    r_up,
    r_down,
    r_bqv,
    r_bup,
    r_vec,
    r_rng,
    tok,
    w_qkv,
    w_out,
    w_up,
    w_down,
    b_qv,
    b_up,
    vectors,
    mask,
    grad_out,
    o_layer,
    o_tok,
    o_qkv,
    o_out,
    o_up,
    o_down,
    o_bqv,
    o_bup,
    o_vec,
    ranges,
    long_rows,
    o_rng,
    wts,
    wff,
    wc,
    wo,
    rdx,
    rdy,
    rxx,
    ryy,
    rz,
    rzf,
    rz2,
    rzf2,
    rst,
    sm,
    smc,
    smf,
    vec,
    bup,
    bqv,
    xq,
    xqt,
    bias,
    qs,
    ks,
    vs,
    kt,
    vt,
    probs,
    ds,
    ctxt,
    cq,
    slc,
    exa_s,
    exa_r,
    exb_s,
    exb_r,
    hq,
    hqt,
    r1,
    n1,
    rstd1,
    sl1,
    aq,
    fac,
    gu,
    gf,
    rowt,
    gr2,
    gc,
    gct,
    dsum,
    grads,
    gqt,
    gwo,
    tot,
    tot_c,
    tot_x,
    tot_y,
    tot_z,
    link_s,
    zr,
    z2r,
    str_,
    xr,
    yr,
    dr,
    rs_r,
    rf_r,
    sm_s,
    sm_r,
    ex_s,
    ex_r,
    tt_s,
    tt_r,
    gx_s,
    gx_r,
    in_s,
):
    dp = lax.axis_index("dp")
    mp = lax.axis_index("mp")
    z, y = dp // 2, dp % 2
    x, c = mp // 2, mp % 2
    nx, ny, nc = 1 - x, 1 - y, 1 - c
    to_x = (dp, nx * 2 + c)
    to_y = (z * 2 + ny, mp)
    to_c = (dp, x * 2 + nc)
    to_xy = (z * 2 + ny, nx * 2 + c)
    to_z = [None] + [((z + k) % 4 * 2 + y, mp) for k in (1, 2, 3)]
    zk = [z, z + 1 - 2 * (z % 2), 2 - z // 2, 3 - 3 * (z // 2)]
    outer = (z * z - 3 * z + 2) // 2
    to_zk = [None] + [(zk[k] * 2 + y, mp) for k in (1, 2, 3)]
    mine = mul8(c * OWN, OWN)
    theirs = mul8(nc * OWN, OWN)
    started = {}
    moved = {}

    def copy(src, dst, send, recv, device):
        return pltpu.make_async_remote_copy(
            src_ref=src, dst_ref=dst, send_sem=send, recv_sem=recv, device_id=device, device_id_type=MESH
        )

    def send(kind, g, axis, src, dst, recv, device, which=None):
        made = copy(src, dst, kind.at[g, axis], recv, device)
        if which is None:
            made.start()
        else:
            pl.when(outer == which)(made.start)
        rows = math.prod(src.shape[:-1])
        count = moved.setdefault((id(kind), g, axis), [kind.at[g, axis], 0, 0])
        for place in (0, 1):
            if which is None or which == place:
                count[1 + place] += rows

    def sent(kind):
        for key in [key for key in moved if key[0] == id(kind)]:
            sem, inside, ends = moved.pop(key)
            if inside == ends:
                got_rows_of(inside, sem)
            else:
                pl.when(outer == 0)(functools.partial(got_rows_of, inside, sem))
                pl.when(outer == 1)(functools.partial(got_rows_of, ends, sem))

    def arrived(ref, sem):
        copy(ref, ref, link_s.at[0, 0], sem, to_c).wait_recv()

    def got_rows_of(rows, sem):
        arrived(gwo.at[pl.ds(0, rows)], sem)

    def keep(group, made):
        made.start()
        started.setdefault(group, []).append(made)

    def kept(group):
        for made in started.pop(group, []):
            made.wait_send()

    barrier = pltpu.get_barrier_semaphore()
    for device in (to_c, to_x, to_y, to_xy, *to_z[1:]):
        pl.semaphore_signal(barrier, inc=1, device_id=device, device_id_type=MESH)

    base = mul8(x * 512, 512)
    arriving = [
        pltpu.make_async_copy(there, here, in_s.at[i])
        for i, (there, here) in enumerate(
            (
                (h_qkv, w_qkv),
                (h_out, w_out),
                (h_up, w_up),
                (h_down, w_down),
                (h_vec, vectors),
                (h_bup, b_up),
                (h_bqv, b_qv),
                (h_rng, ranges),
                (h_tok.at[pl.ds(base, 512)], tok),
                (h_mask, mask),
                (h_long, long_rows),
                (h_grad, grad_out),
                (h_up, wts.at[1, x, z, y]),
                (h_down, wts.at[2, x, z, y]),
            )
        )
    ]
    for made in arriving:
        made.start()
    leaving = []

    def leave_rows(place):
        part = pl.ds(mul8(place * OWN, OWN), OWN)
        leave(o_tok.at[part], r_tok.at[part])

    def leave(here, there):
        made = pltpu.make_async_copy(here, there, in_s.at[len(leaving)])
        made.start()
        leaving.append(made)

    pl.semaphore_wait(barrier, 7)

    def ag_rows(g, xx, zz, yy, part):
        strip, one, two = AG_CUTS[g]
        first = (0, strip, strip + one, strip)[part]
        return wts.at[g, xx, zz, yy, pl.ds(first, (strip, one, two, one + two)[part])]

    def ag_own(g, part):
        if g == 0:
            return ag_rows(g, x, z, y, part)
        strip, one, two = AG_CUTS[g]
        return (h_up, h_down)[g - 1].at[pl.ds(*((0, strip), None, None, (strip, one + two))[part])]

    def ag_strips(g, zz):
        return wts.at[g, :, zz, :, pl.ds(0, AG_CUTS[g][0])]

    def ag_strip_xy(g):
        own = ag_rows(g, x, z, y, 0)
        for axis, device in ((0, to_x), (1, to_y), (0, to_xy)):
            send(link_s, g, axis, ag_own(g, 0), own, str_.at[g - 1], device)

    def ag_strip_z(g):
        got_rows_of(3 * AG_CUTS[g][0], str_.at[g - 1])
        own = ag_strips(g, z)
        send(link_s, g, 2, own, own, z2r.at[g - 1, 0], to_zk[1])
        send(link_s, g, 2, own, own, z2r.at[g - 1, 1 + outer], to_zk[2])

    def ag_strip_fwd(g):
        for k in (2, 3):
            pl.when(outer == 0)(functools.partial(arrived, ag_strips(g, zk[k]), z2r.at[g - 1, k - 1]))
        for k in (2, 3):
            held = ag_strips(g, zk[k])
            send(link_s, g, 2, held, held, z2r.at[g - 1, k - 1], to_zk[1], 0)

    def ag_strip_got(g):
        arrived(ag_strips(g, zk[1]), z2r.at[g - 1, 0])
        for k in (2, 3):
            pl.when(outer == 1)(functools.partial(arrived, ag_strips(g, zk[k]), z2r.at[g - 1, k - 1]))

    def ag_z_send(g):
        own, held = ag_rows(g, x, z, y, 3), ag_own(g, 3)
        send(link_s, g, 2, held, own, zr.at[g, 0], to_zk[1])
        send(link_s, g, 2, held, own, zr.at[g, 1 + outer], to_zk[2])

    def ag_z_fwd(g, k):
        held = ag_rows(g, x, zk[k], y, 3)
        pl.when(outer == 0)(functools.partial(arrived, held, zr.at[g, k - 1]))
        send(link_s, g, 2, held, held, zr.at[g, k - 1], to_zk[1], 0)

    def ag_z_got(g, k):
        held = ag_rows(g, x, zk[k], y, 3)
        if k == 1:
            arrived(held, zr.at[g, 0])
        elif k > 1:
            pl.when(outer == 1)(functools.partial(arrived, held, zr.at[g, k - 1]))

    def ag_xy_send(g, k, which=None):
        own = ag_rows(g, x, zk[k], y, 3)
        if which is None:
            ag_z_got(g, k)
        held = own if k else ag_own(g, 3)
        send(link_s, g, 0, held, own, xr.at[g, k], to_x, which)
        send(link_s, g, 1, held, own, yr.at[g, k], to_y, which)

    def ag_diag(g, k):
        arrived(ag_rows(g, x, zk[k], ny, 3), yr.at[g, k])
        half = ag_rows(g, x, zk[k], ny, 1)
        send(link_s, g, 0, half, half, dr.at[g], to_x)
        arrived(ag_rows(g, nx, zk[k], y, 3), xr.at[g, k])
        half = ag_rows(g, nx, zk[k], y, 2)
        send(link_s, g, 1, half, half, dr.at[g], to_y)

    def ag_last(g):
        got_rows_of(4 * (PIECE - AG_CUTS[g][0]), dr.at[g])

    ag_strip_xy(1)
    ag_xy_send(1, 0)

    arriving[0].wait()
    arriving[1].wait()
    turned = w_out[...].T
    for j, part in enumerate((w_qkv[0], w_qkv[1], w_qkv[2], turned)):
        wts[0, x, z, y, :, j * 128 : j * 128 + 128] = part[:, 0:128]
        wts[0, x, z, y, :, 512 + j * 64 : 576 + j * 64] = part[:, 128:192]
    ag_z_send(0)
    ag_xy_send(0, 0)

    for made in arriving[2:8]:
        made.wait()
    range_of = [ranges[i] for i in range(4)]
    inv_of = [1.0 / r for r in range_of]

    smf[...] = jnp.zeros((16, 128), F32)
    smf[0:6, 0:96] = vectors[...].astype(F32)
    smf[6:9, 0:32] = b_up[...].astype(F32)
    smf[9:12, 0:8] = b_qv[:, 0, :].astype(F32)
    smf[12:15, 0:8] = b_qv[:, 1, :].astype(F32)
    lane = lax.broadcasted_iota(jnp.int32, (1, 128), 1)
    peak_row = jnp.zeros((1, 128), F32)
    for g, ref in enumerate((w_qkv, w_out, w_up, w_down)):
        most = jnp.abs(ref[...].astype(F32))
        if most.ndim == 3:
            most = jnp.max(most, axis=0)
        most = jnp.max(jnp.max(most, axis=0, keepdims=True), axis=1, keepdims=True)
        peak_row = jnp.where(lane == g, most, peak_row)
    smf[15:16] = peak_row
    sm[x, z, y] = smf[...].astype(BF)

    small_c = copy(sm.at[x, z, y], smc, sm_s.at[0], sm_r.at[0], to_c)
    small_c.start()
    ag_z_send(1)
    small_c.wait()
    smf[15:16] = jnp.maximum(peak_row, smc[...].astype(F32)[15:16])
    sm[x, z, y] = smf[...].astype(BF)
    small_xy = ((nx, y, to_x), (x, ny, to_y), (nx, ny, to_xy))
    for i, (_, _, device) in enumerate(small_xy):
        copy(sm.at[x, z, y], sm.at[x, z, y], sm_s.at[1], sm_r.at[1], device).start()
    ag_strip_xy(2)

    for made in arriving[8:]:
        made.wait()

    def do_tokens(i):
        rows = pl.ds(mul8(i * 128, 128), 128)
        v = tok[pl.ds(mul8(i * 128, 128), 128), :].astype(F32)
        xq[rows, :] = (range_of[0] * jnp.tanh(v * inv_of[0])).astype(BF)

    loop(4, do_tokens)
    def do_turn(j):
        cols = pl.ds(mul8(j * 128, 128), 128)
        xqt[cols, :] = xq[:, cols].T

    loop(6, do_turn)
    ag_xy_send(0, 1)
    ag_z_fwd(0, 2)
    ag_z_fwd(0, 3)

    long_flag = long_rows[x].astype(F32)
    for r in range(4):
        row = mask[pl.ds(x * 4 + r, 1), :].astype(F32)
        column = jnp.broadcast_to(row, (128, 128)).T
        for s in range(4):
            seen = column * (1.0 if r == s else long_flag)
            bias[r * 128 : r * 128 + 128, s * 128 : s * 128 + 128] = jnp.where(seen > 0.5, 0.0, -1e30)

    arrived(sm.at[0, 0:3, 0], sm_r.at[1])
    for k in (1, 2, 3):
        copy(sm.at[:, z], sm.at[:, z], sm_s.at[2], sm_r.at[2], to_z[k]).start()
    ag_strip_z(1)
    ag_z_send(2)
    ag_diag(0, 0)
    ag_z_got(1, 1)
    ag_xy_send(1, 1, 1)
    ag_xy_send(0, 2)
    ag_z_fwd(1, 2)
    ag_diag(0, 1)
    ag_xy_send(0, 3)
    ag_xy_send(1, 1, 0)
    ag_z_fwd(1, 3)
    ag_strip_z(2)
    arrived(sm.at[:, 0:3], sm_r.at[2])
    arrived(sm.at[0, 0:3, 0], sm_s.at[1])
    arrived(sm.at[:, 0:3], sm_s.at[2])

    peaks = jnp.max(sm[...].astype(F32).reshape(16, 16, 128), axis=0)[15:16]
    w_peak = [jnp.max(jnp.where(lane == g, peaks, 0.0)) for g in range(4)]
    w_inv = [1.0 / r for r in w_peak]

    def spread(xx, width, step):
        total = None
        for place in range(8):
            tile = sm[xx, place // 2, place % 2].astype(F32)
            if width > 128:
                tile = jnp.concatenate([tile, jnp.zeros((16, width - 128), F32)], axis=1)
            if place:
                tile = pltpu.roll(tile, place * step, 1)
            total = tile if total is None else total + tile
        return total

    vec[...] = spread(0, WIDE, 96)
    heads = []
    for xx in range(2):
        wide = spread(xx, 256, 32)
        for h in range(3):
            bup[xx : xx + 1, h * 256 : h * 256 + 256] = wide[6 + h : 7 + h, :]
        narrow = spread(xx, 128, 8)
        heads.append((narrow, pltpu.roll(narrow, 64, 1)))
    for j, first in enumerate((9, 12)):
        for xx in range(2):
            bqv[j : j + 1, xx * 128 : xx * 128 + 128] = (
                heads[xx][0][first : first + 1] + heads[xx][1][first + 1 : first + 2]
            )
        bqv[j : j + 1, 256:384] = heads[0][0][first + 2 : first + 3] + heads[1][1][first + 2 : first + 3]

    ag_diag(0, 2)
    ag_xy_send(2, 0)
    ag_strip_fwd(1)
    ag_diag(0, 3)
    ag_xy_send(1, 2)
    ag_xy_send(1, 3)
    ag_diag(1, 0)
    ag_diag(1, 1)
    ag_xy_send(2, 1)

    left = lax.broadcasted_iota(jnp.int32, (PIECE, 128), 1) < 64

    def squash_heads(zz, yy):
        place = zz * 2 + yy
        rows = pl.ds(mul8(place * PIECE, PIECE), PIECE)
        tiles = []
        for xx in range(2):
            v = wts[0, xx, zz, yy].astype(F32)
            inner = [w_peak[0] * jnp.tanh(v[:, t * 128 : t * 128 + 128] * w_inv[0]) for t in (0, 1, 2)]
            inner.append(w_peak[1] * jnp.tanh(v[:, 384:512] * w_inv[1]))
            mixed = jnp.where(left, w_peak[0], w_peak[1])
            mixed_inv = jnp.where(left, w_inv[0], w_inv[1])
            inner.append(w_peak[0] * jnp.tanh(v[:, 512:640] * w_inv[0]))
            inner.append(mixed * jnp.tanh(v[:, 640:768] * mixed_inv))
            tiles.append(inner)
        for t in range(3):
            for xx in range(2):
                wc[rows, t * HERE + xx * 128 : t * HERE + xx * 128 + 128] = tiles[xx][t].astype(BF)
        for xx in range(2):
            wo[rows, xx * 128 : xx * 128 + 128] = tiles[xx][3].astype(BF)
        for t, first, second in ((4, 0, 1), (5, 2, 3)):
            one, two = tiles[0][t], tiles[1][t]
            wc[rows, first * HERE + 256 : first * HERE + 384] = jnp.where(left, one, pltpu.roll(two, 64, 1)).astype(BF)
            other = jnp.where(left, pltpu.roll(one, 64, 1), two).astype(BF)
            if second == 1:
                wc[rows, HERE + 256 : HERE + 384] = other
            else:
                wo[rows, 256:384] = other

    loop(4, lambda zz: squash_heads(zz, y))
    ag_last(0)
    loop(4, lambda zz: squash_heads(zz, ny))
    ag_z_fwd(2, 2)
    ag_z_fwd(2, 3)

    def squash_piece(g, xx, zz, yy):
        v = wts[g, xx, zz, yy].astype(F32)
        wff[g - 1, xx, pl.ds(mul8((zz * 2 + yy) * PIECE, PIECE), PIECE), :] = (
            w_peak[g + 1] * jnp.tanh(v * w_inv[g + 1])
        ).astype(BF)

    def squash_ff(g, xx):
        loop(8, lambda place: squash_piece(g, xx, place // 2, place % 2))

    for j, held in enumerate((qs, ks, vs)):

        got = nn(xq[...], wc[:, j * HERE : (j + 1) * HERE])
        if j == 0:
            got = (got + bqv[0:1, :]) * 0.125
        elif j == 2:
            got = got + bqv[1:2, :]
        held[...] = got.astype(BF)
    ag_diag(1, 2)
    for p in range(3):
        cols = slice(p * 128, p * 128 + 128)
        kt[cols, :] = ks[:, cols].T
        vt[cols, :] = vs[:, cols].T

    half_of = lax.broadcasted_iota(jnp.int32, (1, 128), 1) // 64

    def attend(p):
        cols = pl.ds(mul8(p * 128, 128), 128)
        for e in range(2):
            feats = pl.ds(mul8(p * 128 + e * 64, 64), 64)
            for n in range(2):
                q = qs[n * 256 : n * 256 + 256, cols]
                q = jnp.where(half_of == e, q, jnp.zeros_like(q))
                s = nt(ks[:, cols], q) + bias[:, n * 256 : n * 256 + 256]
                s = jnp.exp(s - jnp.max(s, axis=0, keepdims=True))
                s = (s * (1.0 / jnp.sum(s, axis=0, keepdims=True))).astype(BF)
                probs[p * 2 + e, :, n * 256 : n * 256 + 256] = s
                ctxt[feats, n * 256 : n * 256 + 256] = nn(vt[feats, :], s)

    ag_strip_fwd(2)
    attend(0)
    ag_diag(1, 3)
    ag_xy_send(2, 2)
    attend(1)
    ag_xy_send(2, 3)
    ag_diag(2, 0)
    attend(2)

    for p in range(3):
        cols = slice(p * 128, p * 128 + 128)
        bent = jnp.tanh(ctxt[cols, :].T * inv_of[1])
        cq[:, cols] = (range_of[1] * bent).astype(BF)
        slc[:, cols] = 1.0 - bent * bent
    tot[0] = jnp.zeros((16, WIDE), F32)
    most = jnp.max(jnp.max(jnp.abs(ctxt[...]), axis=0, keepdims=True), axis=1, keepdims=True)
    tot[0, 10:11, :] = jnp.broadcast_to(most, (1, WIDE))

    def out_part(start, held, cols=slice(0, WIDE)):
        held[:, cols] = nt(cq[pl.ds(start, OWN), :], wo[cols, :])

    for i in range(2):
        cols = slice(i * HERE, i * HERE + HERE)
        out_part(theirs, exa_s, cols)
        made = copy(exa_s.at[:, cols], exa_r.at[:, cols], ex_s.at[0], ex_r.at[0], to_c)
        made.start()
    out_part(mine, r1)
    ag_strip_got(1)
    ag_diag(2, 1)
    squash_ff(1, x)
    arrived(exa_r, ex_r.at[0])
    arrived(exa_s, ex_s.at[0])

    def sum_rows(v):
        return jnp.sum(v, axis=0, keepdims=True)

    def mean_of(v):
        return jnp.sum(v, axis=-1, keepdims=True) * (1.0 / WIDE)

    def first_norm(i):
        rows = pl.ds(mul8(i * 128, 128), 128)
        v = tok[pl.ds(mul8(mine + i * 128, 128), 128), :].astype(F32)
        v = v + (r1[rows, :] + exa_r[rows, :] + vec[0:1, :])
        r1[rows, :] = v
        center = v - mean_of(v)
        factor = lax.rsqrt(mean_of(center * center) + 1e-12)
        normed = center * factor
        n1[rows, :] = normed
        rstd1[rows, :] = factor
        h = normed * vec[2:3, :] + vec[3:4, :]
        tot[0, 11:12, :] = jnp.maximum(tot[0, 11:12, :], jnp.max(jnp.abs(h), axis=0, keepdims=True))
        bent = jnp.tanh(h * inv_of[2])
        sl1[rows, :] = 1.0 - bent * bent
        hq[pl.ds(mul8(mine + i * 128, 128), 128), :] = (range_of[2] * bent).astype(BF)

    def half_rows(start, i):
        return pl.ds(mul8(start + i * 128, 128), 128)

    for i in range(2):
        first_norm(i)
        own = hq.at[half_rows(mine, i)]
        copy(own, own, ex_s.at[1], ex_r.at[1], to_c).start()

    def share_rows(held, number):
        own = held.at[pl.ds(mine, OWN)]
        copy(own, own, ex_s.at[1], ex_r.at[number], to_c).start()

    def shared(held):
        arrived(held.at[pl.ds(mine, OWN)], ex_s.at[1])

    def got_rows(held, number):
        arrived(held.at[pl.ds(theirs, OWN)], ex_r.at[number])

    def turn_rows(held, out, start):
        out[:, pl.ds(start, OWN)] = held[pl.ds(start, OWN), :].T

    turn_rows(hq, hqt, mine)
    arrived(hq.at[pl.ds(theirs, OWN)], ex_r.at[1])
    turn_rows(hq, hqt, theirs)

    def expand(xx):
        wide = pl.ds(mul8(xx * WIDE, WIDE), WIDE)

        def body(i):
            rows = pl.ds(mul8(i * 256, 256), 256)
            u = nn(hq[rows, :], wff[0, xx]) + bup[pl.ds(xx, 1), :]
            cdf = 0.5 * (1.0 + lax.erf(u * 0.7071067811865476))
            a = u * cdf
            tot[0, 12:13, :] = jnp.maximum(tot[0, 12:13, :], jnp.max(jnp.abs(a), axis=0, keepdims=True))
            bent = jnp.tanh(a * inv_of[3])
            aq[rows, wide] = (range_of[3] * bent).astype(BF)
            pdf = 0.3989422804014327 * jnp.exp(-0.5 * u * u)
            fac[rows, wide] = ((1.0 - bent * bent) * (cdf + u * pdf)).astype(fac.dtype)

        loop(2, body)

    expand(x)
    ag_diag(2, 2)
    ag_last(1)
    squash_ff(1, nx)
    ag_diag(2, 3)
    expand(nx)
    ag_strip_got(2)

    def down_part(start, held, xx, first, cols=slice(0, WIDE)):
        got = nt(aq[pl.ds(start, OWN), pl.ds(mul8(xx * WIDE, WIDE), WIDE)], wff[1, xx, cols, :])
        held[:, cols] = got if first else held[:, cols] + got

    squash_ff(2, x)
    down_part(theirs, exb_s, x, True)
    down_part(mine, gr2, x, True)
    loop(4, lambda zz: squash_piece(2, nx, zz, y))
    ag_last(2)
    loop(4, lambda zz: squash_piece(2, nx, zz, ny))
    for i in range(2):
        cols = slice(i * HERE, i * HERE + HERE)
        down_part(theirs, exb_s, nx, False, cols)
        made = copy(exb_s.at[:, cols], exb_r.at[:, cols], ex_s.at[0], ex_r.at[2], to_c)
        made.start()
    down_part(mine, gr2, nx, False)
    arrived(exb_r, ex_r.at[2])
    arrived(exb_s, ex_s.at[0])

    def second_norm(i):
        rows = pl.ds(mul8(i * 128, 128), 128)
        v = r1[rows, :] + (gr2[rows, :] + exb_r[rows, :] + vec[1:2, :])
        center = v - mean_of(v)
        factor = lax.rsqrt(mean_of(center * center) + 1e-12)
        normed = center * factor
        o_layer[rows, :] = (normed * vec[4:5, :] + vec[5:6, :]).astype(BF)
        gy = grad_out[rows, :].astype(F32)
        tot[0, 4:5, :] += sum_rows(gy * normed)
        tot[0, 5:6, :] += sum_rows(gy)
        gn = gy * vec[4:5, :]
        back = factor * (gn - mean_of(gn) - normed * mean_of(gn * normed))
        gr2[rows, :] = back
        low = back.astype(BF)
        tot[0, 1:2, :] += sum_rows(low.astype(F32))
        gf[pl.ds(mul8(mine + i * 128, 128), 128), :] = low

    shared(hq)
    for i in range(2):
        second_norm(i)
        own = gf.at[half_rows(mine, i)]
        copy(own, own, ex_s.at[1], ex_r.at[3], to_c).start()
    leave(o_layer, r_layer)
    turn_rows(gf, rowt, mine)
    sent(link_s)
    arrived(gf.at[pl.ds(theirs, OWN)], ex_r.at[3])
    turn_rows(gf, rowt, theirs)

    def rs_rows(g, part):
        strip, one, two = RS_CUTS[g]
        return pl.ds((0, strip, strip + one, strip)[part], (strip, one, two, one + two)[part])

    def rs_part(g, part):
        _, one, two = RS_CUTS[g]
        return pl.ds((0, 0, one, 0)[part], (0, one, two, one + two)[part])

    far_z, near_z = pl.ds(2 - z // 2 * 2, 2), pl.ds(z // 2 * 2, 2)

    def rs_first(g, planes):
        one, far = rs_part(g, 1), pl.ds(0, RS_CUTS[g][2])
        i = 0 if planes is far_z else 2
        send(link_s, g, 0, wts.at[g, nx, planes, ny, rs_rows(g, 1)], rdx.at[g, planes, one], rs_r.at[g, i], to_x)
        send(link_s, g, 1, wts.at[g, nx, planes, ny, rs_rows(g, 2)], rdy.at[g, planes, far], rs_r.at[g, i + 1], to_y)

    def rs_direct_x(g, planes, part):
        i = 4 if planes is far_z else 5
        src = wts.at[g, nx, planes, y, rs_rows(g, part)]
        send(link_s, g, 0, src, rxx.at[g, planes, rs_part(g, part)], rs_r.at[g, i], to_x)

    def rs_direct_y(g, planes, part):
        i = 4 if planes is far_z else 5
        src = wts.at[g, x, planes, ny, rs_rows(g, part)]
        send(link_s, g, 1, src, ryy.at[g, planes, rs_part(g, part)], rs_r.at[g, i], to_y)

    def rs_direct(g, near):
        rs_direct_x(g, far_z, 1)
        if near:
            rs_direct_x(g, near_z, 1)

    def rs_second(g, near):
        rs_direct_y(g, far_z, 2)
        if near:
            rs_direct_y(g, near_z, 2)

    def rs_third_x(g, near):
        one, here = rs_part(g, 1), rs_rows(g, 1)
        for planes, i in ((far_z, 0), (near_z, 2)):
            arrived(rdx.at[g, planes, one], rs_r.at[g, i])
            wts[g, x, planes, ny, here] = (
                wts[g, x, planes, ny, here].astype(F32) + rdx[g, planes, one].astype(F32)
            ).astype(BF)
            rs_direct_y(g, planes, 1)
        if not near:
            rs_direct_y(g, near_z, 2)

    def rs_third_y(g, near):
        here, far = rs_rows(g, 2), pl.ds(0, RS_CUTS[g][2])
        for planes, i in ((far_z, 1), (near_z, 3)):
            arrived(rdy.at[g, planes, far], rs_r.at[g, i])
            wts[g, nx, planes, y, here] = (
                wts[g, nx, planes, y, here].astype(F32) + rdy[g, planes, far].astype(F32)
            ).astype(BF)
            rs_direct_x(g, planes, 2)
        if not near:
            rs_direct_x(g, near_z, 1)

    def plane(g, zz):
        rest, here = rs_rows(g, 3), rs_part(g, 3)
        return wts[g, x, zz, y, rest].astype(F32) + rxx[g, zz, here].astype(F32) + ryy[g, zz, here].astype(F32)

    def rs_fourth(g):
        both, rest = rs_part(g, 3), rs_rows(g, 3)
        got_rows_of(4 * (PIECE - RS_CUTS[g][0]), rs_r.at[g, 4])
        for k in (3, 2):
            wts[g, x, zk[k], y, rest] = plane(g, zk[k]).astype(BF)
            send(link_s, g, 2, wts.at[g, x, zk[k], y, rest], rzf.at[g, k - 2, both], rf_r.at[g, k - 2], to_zk[1], 1)

    def rs_near(g):
        both, rest = rs_part(g, 3), rs_rows(g, 3)
        got_rows_of(4 * (PIECE - RS_CUTS[g][0]), rs_r.at[g, 5])
        wts[g, x, zk[1], y, rest] = plane(g, zk[1]).astype(BF)
        send(link_s, g, 2, wts.at[g, x, zk[1], y, rest], rz.at[g, 0, both], rs_r.at[g, 7], to_zk[1])

    def rs_fifth(g):
        both, rest = rs_part(g, 3), rs_rows(g, 3)
        for k in (3, 2):

            @pl.when(outer == 0)
            def _(k=k):
                arrived(rzf.at[g, k - 2, both], rf_r.at[g, k - 2])
                wts[g, x, zk[k], y, rest] = (
                    wts[g, x, zk[k], y, rest].astype(F32) + rzf[g, k - 2, both].astype(F32)
                ).astype(BF)

            send(link_s, g, 2, wts.at[g, x, zk[k], y, rest], rz.at[g, 1, both], rs_r.at[g, 7], to_zk[k], 0)

    def strips(held, g, place, i):
        here = pl.ds(0, RS_CUTS[g][0])
        return held.at[g, *place, (nx, x)[i] if g == 2 else slice(None), :, here]

    def strips_of(g, zz, i):
        here = pl.ds(0, RS_CUTS[g][0])
        return wts.at[g, (nx, x)[i] if g == 2 else slice(None), zz, :, here]

    def rs_strip_z(g, i):
        for k in (3, 2):
            send(link_s, g, 2, strips_of(g, zk[k], i), strips(rzf2, g, (k - 2,), i), rf_r.at[g, k], to_zk[1], 1)
        send(link_s, g, 2, strips_of(g, zk[1], i), strips(rz2, g, (0,), i), rs_r.at[g, 6], to_zk[1])

    def rs_strip_fwd(g):
        here = pl.ds(0, RS_CUTS[g][0])
        for k in (3, 2):

            @pl.when(outer == 0)
            def _(k=k):
                got_rows_of(4 * RS_CUTS[g][0], rf_r.at[g, k])
                wts[g, :, zk[k], :, here] = (
                    wts[g, :, zk[k], :, here].astype(F32) + rzf2[g, k - 2, :, :, here].astype(F32)
                ).astype(BF)

            whole = wts.at[g, :, zk[k], :, here]
            send(link_s, g, 2, whole, rz2.at[g, 1, :, :, here], rs_r.at[g, 6], to_zk[k], 0)

    def rs_strip_sum(g):
        here = pl.ds(0, RS_CUTS[g][0])
        got_rows_of(8 * RS_CUTS[g][0], rs_r.at[g, 6])
        wts[g, :, z, :, here] = (
            wts[g, :, z, :, here].astype(F32)
            + rz2[g, 0, :, :, here].astype(F32)
            + rz2[g, 1, :, :, here].astype(F32)
        ).astype(BF)

    def rs_strip_send(g):
        here = pl.ds(0, RS_CUTS[g][0])
        for i, (xx, yy, axis, device) in enumerate(((nx, ny, 0, to_xy), (nx, y, 0, to_x), (x, ny, 1, to_y))):
            send(link_s, g, axis, wts.at[g, xx, z, yy, here], rst.at[g, i, here], rs_r.at[g, 7], device)

    def rs_total(g):
        here, both = pl.ds(0, RS_CUTS[g][0]), rs_part(g, 3)
        got_rows_of(2 * PIECE + RS_CUTS[g][0], rs_r.at[g, 7])
        strip = wts[g, x, z, y, here].astype(F32)
        for i in range(3):
            strip = strip + rst[g, i, here].astype(F32)
        total = plane(g, z)
        for k in range(2):
            total = total + rz[g, k, both].astype(F32)
        return jnp.concatenate([strip, total], axis=0)

    def ff_grad_planes(g, turned, held, xx, planes, first):
        rows = pl.ds(mul8(first * 2 * PIECE, 4 * PIECE), 4 * PIECE)
        got = nn(turned[rows, :], held[:, pl.ds(mul8(xx * WIDE, WIDE), WIDE)])
        wts[g, xx, planes] = got.reshape(2, 2, PIECE, WIDE).astype(BF)

    def ff_grad(g, turned, held, xx):
        got = nn(turned[...], held[:, pl.ds(mul8(xx * WIDE, WIDE), WIDE)])
        wts[g, xx] = got.reshape(4, 2, PIECE, WIDE).astype(BF)

    ff_grad_planes(2, rowt, aq, nx, far_z, 2 - z // 2 * 2)
    rs_first(2, far_z)
    ff_grad_planes(2, rowt, aq, nx, near_z, z // 2 * 2)
    rs_first(2, near_z)
    rs_direct(2, True)
    rs_strip_z(2, 0)
    ff_grad(2, rowt, aq, x)
    rs_second(2, True)
    rs_strip_z(2, 1)

    for xx in range(2):

        def hidden_grad(i, xx=xx):
            wide = slice(xx * WIDE, xx * WIDE + WIDE)
            rows = pl.ds(mul8(i * 256, 256), 256)
            got = (nn(gf[rows, :], wff[1, xx]) * fac[rows, wide].astype(F32)).astype(BF)
            gu[rows, wide] = got
            tot[0, 6 + xx : 7 + xx, :] += sum_rows(got.astype(F32))

        loop(2, hidden_grad)
    def up_part(start, held):
        held[...] = nt(gu[pl.ds(start, OWN), 0:WIDE], wff[0, 0]) + nt(
            gu[pl.ds(start, OWN), WIDE : 2 * WIDE], wff[0, 1]
        )

    up_part(theirs, exa_s)
    ex3 = copy(exa_s, exa_r, ex_s.at[0], ex_r.at[4], to_c)
    ex3.start()
    up_part(mine, r1)
    ff_grad(1, hqt, gu, nx)
    rs_third_x(2, True)
    rs_third_y(2, True)
    rs_first(1, far_z)
    rs_first(1, near_z)
    rs_direct(1, True)
    ff_grad(1, hqt, gu, x)
    rs_second(1, True)
    rs_strip_z(1, 0)
    ex3.wait()

    def first_back(i):
        rows = pl.ds(mul8(i * 64, 64), 64)
        normed = n1[rows, :]
        gh = (r1[rows, :] + exa_r[rows, :]) * sl1[rows, :]
        tot[0, 2:3, :] += sum_rows(gh * normed)
        tot[0, 3:4, :] += sum_rows(gh)
        gn = gh * vec[2:3, :]
        back = rstd1[rows, :] * (gn - mean_of(gn) - normed * mean_of(gn * normed)) + gr2[rows, :]
        gr2[rows, :] = back
        low = back.astype(BF)
        tot[0, 0:1, :] += sum_rows(low.astype(F32))
        gf[pl.ds(mul8(mine + i * 64, 64), 64), :] = low

    shared(gf)
    loop(4, first_back)
    share_rows(gf, 5)
    turn_rows(gf, rowt, mine)
    got_rows(gf, 5)
    turn_rows(gf, rowt, theirs)

    gwo[...] = nn(rowt[...], cq[...])
    gc[...] = (nn(gf[...], wo[...]) * slc[...]).astype(BF)
    for p in range(3):
        cols = slice(p * 128, p * 128 + 128)
        gct[cols, :] = gc[:, cols].T
        for e in range(2):
            feats = slice(p * 128 + e * 64, p * 128 + e * 64 + 64)
            dsum[p * 2 + e : p * 2 + e + 1, :] = sum_rows(gct[feats, :].astype(F32) * ctxt[feats, :])

    row_half = lax.broadcasted_iota(jnp.int32, (128, 1), 0) // 64

    def attend_back(p):
        cols = pl.ds(mul8(p * 128, 128), 128)
        grad_k = grad_v = None
        for e in range(2):
            feats = pl.ds(mul8(p * 128 + e * 64, 64), 64)
            for n in range(2):
                part = slice(n * 256, n * 256 + 256)
                g = gct[cols, part]
                g = jnp.where(row_half == e, g, jnp.zeros_like(g))
                dpr = nn(vs[:, cols], g)
                ds[:, part] = (probs[p * 2 + e, :, part].astype(F32) * (dpr - dsum[pl.ds(p * 2 + e, 1), part])).astype(BF)
            g = gc[:, cols]
            g = jnp.where(half_of == e, g, jnp.zeros_like(g))
            more_v = nn(probs[p * 2 + e], g)
            q = qs[:, cols]
            q = jnp.where(half_of == e, q, jnp.zeros_like(q))
            more_k = nn(ds[...], q)
            grad_v = more_v if e == 0 else grad_v + more_v
            grad_k = more_k if e == 0 else grad_k + more_k
            gqt[feats, :] = nn(kt[feats, :], ds[...])
        grads[:, pl.ds(mul8(HERE + p * 128, 128), 128)] = grad_k.astype(BF)
        grads[:, pl.ds(mul8(2 * HERE + p * 128, 128), 128)] = grad_v.astype(BF)
        grads[:, cols] = (gqt[cols, :].astype(BF).astype(F32) * 0.125).T.astype(BF)

    attend_back(0)
    attend_back(1)
    attend_back(2)
    rs_strip_fwd(2)
    rs_fourth(2)
    rs_near(2)
    for j, part in ((0, 0), (2, HERE)):
        tot[0, 8:9, part : part + HERE] = sum_rows(grads[:, j * HERE : (j + 1) * HERE].astype(F32))

    left_four = lax.broadcasted_iota(jnp.int32, (4 * PIECE, 128), 1) < 64

    def head_grad(i):
        rows = pl.ds(mul8(i * 4 * PIECE, 4 * PIECE), 4 * PIECE)
        gq, gk, gv = (nn(xqt[rows, :], grads[:, j * HERE : (j + 1) * HERE]) for j in range(3))
        parts = (gq, gk, gv, gwo[rows, :])

        def put(xx, t, v):
            wts[0, xx, pl.ds(i * 2, 2), :, :, t * 128 : t * 128 + 128] = v.reshape(2, 2, PIECE, 128).astype(BF)

        for xx in range(2):
            for t in range(4):
                put(xx, t, parts[t][:, xx * 128 : xx * 128 + 128])
        for t, first, second in ((4, gq, gk), (5, gv, gwo[rows, :])):
            one, two = first[:, 256:384], second[:, 256:384]
            put(0, t, jnp.where(left_four, one, pltpu.roll(two, 64, 1)))
            put(1, t, jnp.where(left_four, pltpu.roll(one, 64, 1), two))

    def most_x(i):
        v = jnp.abs(tok[pl.ds(mul8(i * 128, 128), 128), :].astype(F32))
        tot[0, 9:10, :] = jnp.maximum(tot[0, 9:10, :], jnp.max(v, axis=0, keepdims=True))

    loop(4, most_x)
    row_of = lax.broadcasted_iota(jnp.int32, (16, 1), 0)
    small = copy(tot.at[0], tot_c, tt_s.at[0], tt_r.at[0], to_c)
    small.start()
    loop(2, head_grad)
    small.wait()
    mixed = jnp.where(row_of < 6, tot[0] + tot_c[...], jnp.maximum(tot[0], tot_c[...]))
    tot[1] = jnp.where((row_of >= 6) & (row_of < 9), tot[0], mixed)
    small = copy(tot.at[1], tot_x, tt_s.at[0], tt_r.at[1], to_x)
    small.start()
    rs_first(0, far_z)
    rs_first(0, near_z)
    rs_direct(0, False)
    rs_second(0, False)
    rs_strip_z(0, 0)

    def token_part(start, held):
        held[...] = nt(grads[pl.ds(start, OWN), :], wc[...])

    token_part(theirs, exb_s)
    ex4 = copy(exb_s, exb_r, ex_s.at[0], ex_r.at[6], to_c)
    ex4.start()
    rs_third_x(1, True)
    rs_third_y(1, True)
    token_part(mine, r1)
    ex4.wait()

    def token_grad(i):
        rows = pl.ds(mul8(i * 64, 64), 64)
        v = tok[pl.ds(mul8(mine + i * 64, 64), 64), :].astype(F32)
        bent = jnp.tanh(v * inv_of[0])
        got = gr2[rows, :] + (r1[rows, :] + exb_r[rows, :]) * (1.0 - bent * bent)
        o_tok[pl.ds(mul8(mp * OWN + i * 64, 64), 64), :] = got.astype(BF)

    loop(4, token_grad)
    own = o_tok.at[pl.ds(mul8(mp * OWN, OWN), OWN)]
    keep("tok", copy(own, own, gx_s.at[1], gx_r.at[1], to_c))
    leave_rows(mp)
    rs_strip_fwd(1)
    small.wait()
    tot[2] = jnp.where(row_of < 9, tot[1] + tot_x[...], jnp.maximum(tot[1], tot_x[...]))
    small = copy(tot.at[2], tot_y, tt_s.at[0], tt_r.at[2], to_y)
    small.start()
    rs_third_x(0, False)
    rs_fifth(2)
    rs_third_y(0, False)
    keep("tok", copy(own, own, gx_s.at[0], gx_r.at[0], to_x))
    for g in (2, 1):
        rs_strip_sum(g)
        rs_strip_send(g)
    rs_strip_fwd(0)
    rs_fourth(1)
    rs_near(1)
    small.wait()
    tot[3] = jnp.where(row_of < 9, tot[2] + tot_y[...], jnp.maximum(tot[2], tot_y[...]))

    def both(one, two):
        return jnp.where(row_of < 9, one + two, jnp.maximum(one, two))

    inward = copy(tot.at[3], tot_z.at[0], tt_s.at[0], tt_r.at[3], to_zk[1])
    across = copy(tot.at[4], tot_z.at[1], tt_s.at[0], tt_r.at[4], to_zk[2])
    outward = copy(tot.at[5], tot_z.at[2], tt_s.at[0], tt_r.at[5], to_zk[1])
    pl.when(outer == 1)(inward.start)
    rs_fourth(0)
    rs_strip_sum(0)
    rs_strip_send(0)
    rs_fifth(1)

    @pl.when(outer == 0)
    def _():
        inward.wait_recv()
        tot[4] = both(tot[3], tot_z[0])
        across.start()

    rs_near(0)

    @pl.when(outer == 0)
    def _():
        across.wait()
        tot[5] = both(tot[4], tot_z[1])
        outward.start()

    rs_fifth(0)
    o_down[...] = rs_total(2) * _slope(w_down[...], w_inv[3])
    leave(o_down, r_down)
    o_up[...] = rs_total(1) * _slope(w_up[...], w_inv[2])
    leave(o_up, r_up)

    far = o_tok.at[pl.ds(mul8((nx * 2 + c) * OWN, OWN), OWN)]
    copy(far, far, gx_s.at[0], gx_r.at[0], to_x).wait_recv()
    keep("tok", copy(far, far, gx_s.at[2], gx_r.at[2], to_c))
    leave_rows(nx * 2 + c)

    @pl.when(outer == 0)
    def _():
        outward.wait_send()

    @pl.when(outer == 1)
    def _():
        inward.wait_send()
        outward.wait_recv()
        tot[5] = tot_z[2]

    done = tot[5]
    back = pltpu.roll(done, (8 - dp) * 96, 1)
    o_vec[...] = back[0:6, 0:96]
    ups = jnp.where(x == 0, done[6:7, :], done[7:8, :])
    for h in range(3):
        tile = jnp.broadcast_to(ups[:, h * 256 : h * 256 + 256], (8, 256))
        o_bup[h : h + 1, :] = pltpu.roll(tile, (8 - dp) * 32, 1)[0:1, 0:32]
    for j in range(2):
        row = jnp.broadcast_to(done[8:9, j * HERE : (j + 1) * HERE], (8, HERE))
        pair = jnp.where(x == 0, row[:, 0:128], row[:, 128:256])
        for h, tile, shift in ((0, pair, 0), (1, pair, 64), (2, row[:, 256:384], 64 * x)):
            o_bqv[h, j : j + 1, :] = pltpu.roll(tile, (256 - shift - dp * 8) % 128, 1)[0:1, 0:8]
    for i in range(4):
        most = jnp.max(done[9 + i : 10 + i, :], axis=1, keepdims=True)
        o_rng[i : i + 1, :] = jnp.broadcast_to(0.9 * range_of[i] + 0.1 * most, (1, 128))

    for here, there in ((o_vec, r_vec), (o_bup, r_bup), (o_bqv, r_bqv), (o_rng, r_rng)):
        leave(here, there)
    near = pl.ds(mul8((x * 2 + nc) * OWN, OWN), OWN)
    copy(o_tok.at[near], o_tok.at[near], gx_s.at[1], gx_r.at[1], to_c).wait_recv()
    leave_rows(x * 2 + nc)
    total = rs_total(0)
    for j in range(4):
        main = total[:, j * 128 : j * 128 + 128]
        pair = total[:, 512 + j // 2 * 128 : 640 + j // 2 * 128]
        if j % 2:
            pair = pltpu.roll(pair, 64, 1)
        whole = jnp.concatenate([main, pair], axis=1)[:, 0:192]
        if j < 3:
            o_qkv[j] = whole * _slope(w_qkv[j], w_inv[0])
        else:
            o_out[...] = whole.T * _slope(w_out[...], w_inv[1])
    leave(o_qkv, r_qkv)
    leave(o_out, r_out)
    far = pl.ds(mul8((nx * 2 + nc) * OWN, OWN), OWN)
    copy(o_tok.at[far], o_tok.at[far], gx_s.at[2], gx_r.at[2], to_c).wait_recv()
    leave_rows(nx * 2 + nc)
    sent(link_s)
    kept("tok")
    shared(gf)
    for made in leaving:
        made.wait()


def _slope(values, inverse):
    bent = jnp.tanh(values.astype(F32) * inverse)
    return 1.0 - bent * bent


def layer_on_chips(
    tokens, w_qkv, w_out, w_up, w_down, b_qv, b_up, vectors, ema_ranges, key_mask, long_rows, grad_out
):
    vmem = pltpu.VMEM
    rows = tokens.shape[0]
    half = rows // 2

    def buffer(*shape, dtype=BF):
        return vmem(shape, dtype)

    def f32(*shape):
        return vmem(shape, F32)

    sems = pltpu.SemaphoreType.DMA
    ins = (w_qkv, w_out, w_up, w_down.T, b_qv.transpose(1, 0, 2), b_up, vectors)
    mask = key_mask.reshape(rows // 128, 128)
    kinds = [
        jax.ShapeDtypeStruct(grad_out.shape, BF),
        jax.ShapeDtypeStruct(tokens.shape, BF),
        *(jax.ShapeDtypeStruct(v.shape, F32) for v in ins),
    ]
    scratch = [
        buffer(half, WIDE),
        *(vmem(v.shape, v.dtype) for v in (*ins, mask, grad_out)),
        *(vmem(v.shape, v.dtype) for v in kinds),
        pltpu.SMEM(ema_ranges.shape, F32),
        pltpu.SMEM(long_rows.shape, jnp.int32),
        f32(8, 128),
        buffer(3, 2, 4, 2, PIECE, WIDE),
        buffer(2, 2, WIDE, WIDE),
        buffer(WIDE, 3 * HERE),
        buffer(WIDE, HERE),
        buffer(3, 4, 48, WIDE),
        buffer(3, 4, 48, WIDE),
        buffer(3, 4, 80, WIDE),
        buffer(3, 4, 80, WIDE),
        buffer(3, 2, 80, WIDE),
        buffer(3, 2, 80, WIDE),
        buffer(3, 2, 2, 2, 32, WIDE),
        buffer(3, 2, 2, 2, 32, WIDE),
        buffer(3, 3, 32, WIDE),
        buffer(2, 4, 2, 16, 128),
        buffer(16, 128),
        f32(16, 128),
        f32(16, WIDE),
        f32(8, WIDE),
        f32(8, HERE),
        buffer(half, WIDE),
        buffer(WIDE, half),
        f32(half, half),
        buffer(half, HERE),
        buffer(half, HERE),
        buffer(half, HERE),
        buffer(HERE, half),
        buffer(HERE, half),
        buffer(6, half, half),
        buffer(half, half),
        f32(HERE, half),
        buffer(half, HERE),
        f32(half, HERE),
        f32(OWN, WIDE),
        f32(OWN, WIDE),
        f32(OWN, WIDE),
        f32(OWN, WIDE),
        buffer(half, WIDE),
        buffer(WIDE, half),
        f32(OWN, WIDE),
        f32(OWN, WIDE),
        f32(OWN, 1),
        f32(OWN, WIDE),
        buffer(half, 2 * WIDE),
        buffer(half, 2 * WIDE),
        buffer(half, 2 * WIDE),
        buffer(half, WIDE),
        buffer(WIDE, half),
        f32(OWN, WIDE),
        buffer(half, HERE),
        buffer(HERE, half),
        f32(8, half),
        buffer(half, 3 * HERE),
        f32(HERE, half),
        f32(WIDE, HERE),
        f32(6, 16, WIDE),
        f32(16, WIDE),
        f32(16, WIDE),
        f32(16, WIDE),
        f32(3, 16, WIDE),
        sems((3, 3)),
        sems((3, 3)),
        sems((2, 3)),
        sems((2,)),
        sems((3, 4)),
        sems((3, 4)),
        sems((3,)),
        sems((3, 8)),
        sems((3, 4)),
        sems((3,)),
        sems((3,)),
        sems((2,)),
        sems((7,)),
        sems((1,)),
        sems((6,)),
        sems((3,)),
        sems((3,)),
        sems((14,)),
    ]
    far = pl.BlockSpec(memory_space=pltpu.HBM)
    outs = pl.pallas_call(
        layer_kernel,
        out_shape=[*kinds, jax.ShapeDtypeStruct((8, 128), F32)],
        in_specs=[far] * 12,
        out_specs=[far] * 10,
        scratch_shapes=scratch,
        compiler_params=pltpu.CompilerParams(
            collective_id=0, has_side_effects=True, vmem_limit_bytes=VMEM_LIMIT
        ),
        name="encoder_layer",
    )(tokens, *ins, ema_ranges, mask, long_rows, grad_out)
    outs = finish(outs, ema_ranges)
    return (*outs[:5], outs[5].T, outs[6].transpose(1, 0, 2), *outs[7:])


def finish_kernel(*refs):
    ins, outs, held, wide, sem = refs[:10], refs[10:20], refs[20:30], refs[30], refs[31]
    step = OWN // 2
    parts = [pl.ds(i * step, step) for i in range(ins[1].shape[0] // step)]
    arriving = [pltpu.make_async_copy(ins[1].at[p], held[1].at[p], sem.at[10 + i]) for i, p in enumerate(parts)]
    moved = [i for i in range(10) if i != 1]
    arriving += [pltpu.make_async_copy(ins[i], held[i], sem.at[i]) for i in moved]
    leaving = [pltpu.make_async_copy(wide.at[p], outs[1].at[p], sem.at[10 + i]) for i, p in enumerate(parts)]
    leaving += [pltpu.make_async_copy(held[i], outs[i], sem.at[i]) for i in moved[:-1]]
    for made in arriving:
        made.start()
    for i, (here, there) in enumerate(zip(arriving, leaving)):
        here.wait()
        if i < len(parts):
            wide[parts[i], :] = held[1][parts[i], :].astype(F32)
        there.start()
    arriving[-1].wait()
    for i in range(4):
        outs[9][i] = held[9][i, 0]
    for made in leaving:
        made.wait()


def finish(held, ranges):
    shape = jax.ShapeDtypeStruct
    far = pl.BlockSpec(memory_space=pltpu.HBM)
    return pl.pallas_call(
        finish_kernel,
        out_shape=[shape(v.shape, F32 if i == 1 else v.dtype) for i, v in enumerate(held[:9])]
        + [shape(ranges.shape, F32)],
        in_specs=[far] * 10,
        out_specs=[far] * 9 + [pl.BlockSpec(memory_space=pltpu.SMEM)],
        scratch_shapes=[pltpu.VMEM(v.shape, v.dtype) for v in held]
        + [pltpu.VMEM(held[1].shape, F32), pltpu.SemaphoreType.DMA((10 + held[1].shape[0] * 2 // OWN,))],
        compiler_params=pltpu.CompilerParams(vmem_limit_bytes=VMEM_LIMIT),
        name="write_results",
    )(*held)


VMEM_LIMIT = 64 * 1024 * 1024


def solution(mesh):
    placed = (
        P("dp", None),
        P(None, "dp", "mp"),
        P("mp", "dp"),
        P("dp", "mp"),
        P("mp", "dp"),
        P(None, "mp", "dp"),
        P("mp", "dp"),
        P(None, "dp"),
        P(),
        P("dp"),
        P("dp"),
        P(("dp", "mp"), None),
    )
    on_chips = dict(mesh.shape) == {"dp": 8, "mp": 4}
    return jax.shard_map(
        layer_on_chips if on_chips else per_device,
        mesh=mesh,
        in_specs=placed,
        out_specs=(
            P(("dp", "mp"), None),
            P("dp", None),
            P(None, "dp", "mp"),
            P("mp", "dp"),
            P("dp", "mp"),
            P("mp", "dp"),
            P(None, "mp", "dp"),
            P("mp", "dp"),
            P(None, "dp"),
            P(),
        ),
        check_vma=False,
    )
```

```python
import functools
import math

import jax
import jax.numpy as jnp
from jax import lax
from jax.experimental import pallas as pl
from jax.experimental.pallas import tpu as pltpu
from jax.sharding import PartitionSpec as P

HD = 64
BLOCK = 512
SEG = 128


eps_norm = 1e-12
root_half = 0.7071067811865476
inv_root_tau = 0.3989422804014327


def squash(values, limit):
    return limit * jnp.tanh(values / limit)


def slope(values, limit):
    bent = jnp.tanh(values / limit)
    return 1.0 - bent * bent


def peak_of(values):
    return jnp.max(jnp.abs(values.astype(jnp.float32)))


def product(left, right):
    return jnp.dot(left, right, preferred_element_type=jnp.float32)


def contract_rows(left, right):
    return lax.dot_general(
        left, right, (((0,), (0,)), ((), ())), preferred_element_type=jnp.float32
    )


def contract_cols(left, right):
    return lax.dot_general(
        left, right, (((1,), (1,)), ((), ())), preferred_element_type=jnp.float32
    )


def normalize(values):
    center = values - jnp.mean(values, axis=-1, keepdims=True)
    factor = lax.rsqrt(jnp.mean(center * center, axis=-1, keepdims=True) + eps_norm)
    return (center * factor, factor)


def norm_back(grad_normed, normed, factor):
    first_mean = jnp.mean(grad_normed, axis=-1, keepdims=True)
    cross_mean = jnp.mean(grad_normed * normed, axis=-1, keepdims=True)
    return factor * (grad_normed - first_mean - normed * cross_mean)


def allowed_keys(live, long_flag):
    places = jnp.arange(BLOCK) // SEG
    return (live[None, :] > 0) & ((long_flag > 0) | (places[:, None] == places[None, :]))


def block_scores(queries, keys_in, live, long_flag):
    scores = jnp.einsum("qhd,khd->hqk", queries, keys_in, preferred_element_type=jnp.float32)
    return jnp.where(allowed_keys(live, long_flag)[None], scores, -1e30)


def attend_block(pieces):
    queries, keys_in, values, live, long_flag = pieces
    scores = block_scores(queries, keys_in, live, long_flag)
    top_score = jnp.max(scores, axis=-1, keepdims=True)
    weights = jnp.exp(scores - top_score)
    totals = jnp.sum(weights, axis=-1, keepdims=True)
    attn_probs = (weights / totals).astype(jnp.bfloat16)
    context = jnp.einsum("hqk,khd->qhd", attn_probs, values, preferred_element_type=jnp.float32)
    return (context, top_score + jnp.log(totals))


def attend_back(pieces):
    queries, keys_in, values, live, long_flag, log_total, grad_ctx = pieces
    attn_probs = jnp.exp(block_scores(queries, keys_in, live, long_flag) - log_total)
    grad_probs = jnp.einsum("qhd,khd->hqk", grad_ctx, values, preferred_element_type=jnp.float32)
    grad_values = jnp.einsum(
        "hqk,qhd->khd",
        attn_probs.astype(jnp.bfloat16),
        grad_ctx,
        preferred_element_type=jnp.float32,
    )
    inner = jnp.sum(grad_probs * attn_probs, axis=-1, keepdims=True)
    grad_scores = (attn_probs * (grad_probs - inner)).astype(jnp.bfloat16)
    grad_queries = jnp.einsum(
        "hqk,khd->qhd", grad_scores, keys_in, preferred_element_type=jnp.float32
    )
    grad_keys = jnp.einsum("hqk,qhd->khd", grad_scores, queries, preferred_element_type=jnp.float32)
    return (
        grad_queries.astype(jnp.bfloat16),
        grad_keys.astype(jnp.bfloat16),
        grad_values.astype(jnp.bfloat16),
    )


def prepare(gathered, w_peaks):
    return tuple(
        (
            squash(gathered[index].astype(jnp.float32), w_peaks[index]).astype(jnp.bfloat16)
            for index in range(4)
        )
    )


def peak_all(values):
    return lax.pmax(peak_of(values), ("dp", "mp"))


def per_device(
    tokens,
    w_qkv,
    w_out,
    w_up,
    w_down,
    b_qv,
    b_up,
    vectors,
    ema_ranges,
    key_mask,
    long_rows,
    grad_out,
):
    row_count = tokens.shape[0]
    quarter = row_count // lax.axis_size("mp")
    row_start = lax.axis_index("mp") * quarter
    blocks = row_count // BLOCK
    w_peaks = lax.pmax(
        (peak_of(w_qkv), peak_of(w_out), peak_of(w_up), peak_of(w_down)), ("dp", "mp")
    )
    gathered = (
        lax.all_gather(w_qkv, "dp", axis=1, tiled=True),
        lax.all_gather(w_out, "dp", axis=1, tiled=True),
        lax.all_gather(w_up, "dp", axis=0, tiled=True),
        lax.all_gather(w_down, "dp", axis=1, tiled=True),
        lax.all_gather(b_qv, "dp", axis=2, tiled=True),
        lax.all_gather(b_up, "dp", axis=1, tiled=True),
        lax.all_gather(vectors, "dp", axis=1, tiled=True),
    )
    qkv_q, out_q, up_q, down_q = prepare(gathered, w_peaks)
    bias_qv = gathered[4].astype(jnp.float32).reshape(2, -1)
    bias_up = gathered[5].astype(jnp.float32).reshape(-1)
    vec = gathered[6].astype(jnp.float32)
    head_width = bias_qv.shape[1]
    heads_here = head_width // HD
    scale_q = HD ** (-0.5)
    tok_float = tokens.astype(jnp.float32)
    peak_tok = peak_all(tok_float)
    tok_quant = squash(tok_float, ema_ranges[0]).astype(jnp.bfloat16)
    projected = jnp.einsum("td,jde->jte", tok_quant, qkv_q, preferred_element_type=jnp.float32)
    queries = ((projected[0] + bias_qv[0]) * scale_q).astype(jnp.bfloat16)
    keys_all = projected[1].astype(jnp.bfloat16)
    values = (projected[2] + bias_qv[1]).astype(jnp.bfloat16)
    shape_four = (blocks, BLOCK, heads_here, HD)
    mask_blocks = key_mask.reshape(blocks, BLOCK)
    block_inputs = (
        queries.reshape(shape_four),
        keys_all.reshape(shape_four),
        values.reshape(shape_four),
        mask_blocks,
        long_rows,
    )
    context, log_total = lax.map(attend_block, block_inputs)
    context = context.reshape(row_count, head_width)
    peak_ctx = peak_all(context)
    ctx_quant = squash(context, ema_ranges[1]).astype(jnp.bfloat16)
    partial_attn = product(ctx_quant, out_q)
    attn = lax.psum_scatter(partial_attn, "mp", scatter_dimension=0, tiled=True) + vec[0]
    first_own = lax.dynamic_slice_in_dim(tok_float, row_start, quarter, 0) + attn
    normed, factor_one = normalize(first_own)
    hidden_in = normed * vec[2] + vec[3]
    hid_quant = lax.all_gather(
        squash(hidden_in, ema_ranges[2]).astype(jnp.bfloat16), "mp", axis=0, tiled=True
    )
    peak_hid = peak_all(hidden_in)
    pre_act = product(hid_quant, up_q) + bias_up
    active = pre_act * 0.5 * (1.0 + lax.erf(pre_act * root_half))
    peak_act = peak_all(active)
    act_quant = squash(active, ema_ranges[3]).astype(jnp.bfloat16)
    branch = (
        lax.psum_scatter(product(act_quant, down_q), "mp", scatter_dimension=0, tiled=True) + vec[1]
    )
    second = first_own + branch
    normed_two, factor_two = normalize(second)
    layer_out = (normed_two * vec[4] + vec[5]).astype(jnp.bfloat16)
    new_ranges = 0.9 * ema_ranges + 0.1 * jnp.stack([peak_tok, peak_ctx, peak_hid, peak_act])
    gathered = (
        lax.all_gather(w_qkv, "dp", axis=1, tiled=True),
        lax.all_gather(w_out, "dp", axis=1, tiled=True),
        lax.all_gather(w_up, "dp", axis=0, tiled=True),
        lax.all_gather(w_down, "dp", axis=1, tiled=True),
        lax.all_gather(b_qv, "dp", axis=2, tiled=True),
        lax.all_gather(b_up, "dp", axis=1, tiled=True),
        lax.all_gather(vectors, "dp", axis=1, tiled=True),
    )
    qkv_q, out_q, up_q, down_q = prepare(gathered, w_peaks)
    grad_y = grad_out.astype(jnp.float32)
    grad_gain_two = jnp.sum(grad_y * normed_two, axis=0)
    grad_shift_two = jnp.sum(grad_y, axis=0)
    grad_second = norm_back(grad_y * vec[4], normed_two, factor_two)
    grad_resid = lax.all_gather(grad_second.astype(jnp.bfloat16), "mp", axis=0, tiled=True).astype(
        grad_second.dtype
    )
    grad_branch = grad_resid.astype(jnp.bfloat16)
    grad_bias_down = jnp.sum(grad_branch.astype(jnp.float32), axis=0)
    grad_down_w = contract_rows(act_quant, grad_branch)
    grad_active = contract_cols(grad_branch, down_q) * slope(active, ema_ranges[3])
    normal_cdf = 0.5 * (1.0 + lax.erf(pre_act * root_half))
    normal_pdf = inv_root_tau * jnp.exp(-0.5 * pre_act * pre_act)
    grad_pre = (grad_active * (normal_cdf + pre_act * normal_pdf)).astype(jnp.bfloat16)
    grad_bias_up = jnp.sum(grad_pre.astype(jnp.float32), axis=0)
    grad_up_w = contract_rows(hid_quant, grad_pre)
    partial_hid = contract_cols(grad_pre, up_q)
    grad_hid_q = lax.psum_scatter(partial_hid, "mp", scatter_dimension=0, tiled=True)
    grad_hidden = grad_hid_q * slope(hidden_in, ema_ranges[2])
    grad_gain_one = jnp.sum(grad_hidden * normed, axis=0)
    grad_shift_one = jnp.sum(grad_hidden, axis=0)
    grad_first = norm_back(grad_hidden * vec[2], normed, factor_one) + grad_second
    grad_attn = lax.all_gather(grad_first.astype(jnp.bfloat16), "mp", axis=0, tiled=True)
    grad_bias_out = jnp.sum(grad_attn.astype(jnp.float32), axis=0)
    grad_out_w = contract_rows(ctx_quant, grad_attn)
    grad_ctx = (contract_cols(grad_attn, out_q) * slope(context, ema_ranges[1])).astype(
        jnp.bfloat16
    )
    back_inputs = block_inputs + (log_total, grad_ctx.reshape(shape_four))
    grad_q, grad_k, grad_v = lax.map(attend_back, back_inputs)
    stacked = jnp.stack(
        [
            grad_q.reshape(row_count, head_width) * jnp.bfloat16(scale_q),
            grad_k.reshape(row_count, head_width),
            grad_v.reshape(row_count, head_width),
        ]
    )
    grad_qkv_w = jnp.einsum("td,jte->jde", tok_quant, stacked, preferred_element_type=jnp.float32)
    stacked_float = stacked.astype(jnp.float32)
    grad_bias_qv = jnp.stack([jnp.sum(stacked_float[0], axis=0), jnp.sum(stacked_float[2], axis=0)])
    part_input = jnp.einsum("jte,jde->td", stacked, qkv_q, preferred_element_type=jnp.float32)
    own_term = part_input * slope(tok_float, ema_ranges[0])
    own_rows = lax.dynamic_slice_in_dim(own_term, row_start, quarter, 0) + grad_first
    own_term = lax.dynamic_update_slice_in_dim(own_term, own_rows, row_start, 0)
    grad_tokens, norm_tail = (
        lax.psum(own_term.astype(jnp.bfloat16), "mp").astype(jnp.float32),
        lax.psum(
            jnp.stack([grad_gain_one, grad_shift_one, grad_gain_two, grad_shift_two]).astype(
                jnp.bfloat16
            ),
            "mp",
        ).astype(jnp.float32),
    )
    grad_vec = jnp.stack(
        [grad_bias_out, grad_bias_down, norm_tail[0], norm_tail[1], norm_tail[2], norm_tail[3]]
    )
    summed = (
        lax.psum_scatter(
            grad_qkv_w * slope(gathered[0].astype(jnp.float32), w_peaks[0]),
            "dp",
            scatter_dimension=1,
            tiled=True,
        ),
        lax.psum_scatter(
            grad_out_w * slope(gathered[1].astype(jnp.float32), w_peaks[1]),
            "dp",
            scatter_dimension=1,
            tiled=True,
        ),
        lax.psum_scatter(
            grad_up_w * slope(gathered[2].astype(jnp.float32), w_peaks[2]),
            "dp",
            scatter_dimension=0,
            tiled=True,
        ),
        lax.psum_scatter(
            grad_down_w * slope(gathered[3].astype(jnp.float32), w_peaks[3]),
            "dp",
            scatter_dimension=1,
            tiled=True,
        ),
        lax.psum_scatter(
            grad_bias_qv.reshape(gathered[4].shape), "dp", scatter_dimension=2, tiled=True
        ),
        lax.psum_scatter(
            grad_bias_up.reshape(gathered[5].shape), "dp", scatter_dimension=1, tiled=True
        ),
        lax.psum_scatter(grad_vec, "dp", scatter_dimension=1, tiled=True),
    )
    return (
        layer_out,
        grad_tokens,
        summed[0],
        summed[1],
        summed[2],
        summed[3],
        summed[4],
        summed[5],
        summed[6],
        new_ranges,
    )


BF = jnp.bfloat16
F32 = jnp.float32
MESH = pl.DeviceIdType.MESH
WIDE = 768
PIECE = 96
AG_CUTS = ((0, 48, 48), (16, 32, 48), (32, 32, 32))
RS_CUTS = ((16, 32, 48), (32, 16, 48), (32, 32, 32))
OWN = 256
HERE = 384


def nn(left, right):
    return lax.dot_general(left, right, (((1,), (0,)), ((), ())), preferred_element_type=F32)


def nt(left, right):
    return lax.dot_general(left, right, (((1,), (1,)), ((), ())), preferred_element_type=F32)


def mul8(value, step):
    return pl.multiple_of(value, step)


def loop(count, body):
    def step(index, carry):
        body(index)
        return carry

    lax.fori_loop(0, count, step, 0)


def layer_kernel(
    h_tok,
    h_qkv,
    h_out,
    h_up,
    h_down,
    h_bqv,
    h_bup,
    h_vec,
    h_rng,
    h_mask,
    h_long,
    h_grad,
    r_layer,
    r_tok,
    r_qkv,
    r_out,
    r_up,
    r_down,
    r_bqv,
    r_bup,
    r_vec,
    r_rng,
    tok,
    w_qkv,
    w_out,
    w_up,
    w_down,
    b_qv,
    b_up,
    vectors,
    mask,
    grad_out,
    o_layer,
    o_tok,
    o_qkv,
    o_out,
    o_up,
    o_down,
    o_bqv,
    o_bup,
    o_vec,
    ranges,
    long_rows,
    o_rng,
    wts,
    wff,
    wc,
    wo,
    rdx,
    rdy,
    rxx,
    ryy,
    rz,
    rzf,
    rz2,
    rzf2,
    rst,
    sm,
    smc,
    smf,
    vec,
    bup,
    bqv,
    xq,
    xqt,
    bias,
    qs,
    ks,
    vs,
    kt,
    vt,
    probs,
    ds,
    ctxt,
    cq,
    slc,
    exa_s,
    exa_r,
    exb_s,
    exb_r,
    low_s,
    low_r,
    hq,
    hqt,
    r1,
    n1,
    rstd1,
    sl1,
    aq,
    fac,
    gu,
    gf,
    rowt,
    gr2,
    gc,
    gct,
    dsum,
    grads,
    gqt,
    gwo,
    tot,
    tot_c,
    tot_x,
    tot_y,
    tot_z,
    link_s,
    zr,
    z2r,
    str_,
    xr,
    yr,
    dr,
    rs_r,
    rf_r,
    sm_s,
    sm_r,
    ex_s,
    ex_r,
    tt_s,
    tt_r,
    gx_s,
    gx_r,
    in_s,
):
    dp = lax.axis_index("dp")
    mp = lax.axis_index("mp")
    z, y = dp // 2, dp % 2
    x, c = mp // 2, mp % 2
    nx, ny, nc = 1 - x, 1 - y, 1 - c
    to_x = (dp, nx * 2 + c)
    to_y = (z * 2 + ny, mp)
    to_c = (dp, x * 2 + nc)
    to_xy = (z * 2 + ny, nx * 2 + c)
    to_z = [None] + [((z + k) % 4 * 2 + y, mp) for k in (1, 2, 3)]
    zk = [z, z + 1 - 2 * (z % 2), 2 - z // 2, 3 - 3 * (z // 2)]
    outer = (z * z - 3 * z + 2) // 2
    to_zk = [None] + [(zk[k] * 2 + y, mp) for k in (1, 2, 3)]
    mine = mul8(c * OWN, OWN)
    theirs = mul8(nc * OWN, OWN)
    started = {}
    moved = {}

    def copy(src, dst, send, recv, device):
        return pltpu.make_async_remote_copy(
            src_ref=src, dst_ref=dst, send_sem=send, recv_sem=recv, device_id=device, device_id_type=MESH
        )

    def send(kind, g, axis, src, dst, recv, device, which=None):
        made = copy(src, dst, kind.at[g, axis], recv, device)
        if which is None:
            made.start()
        else:
            pl.when(outer == which)(made.start)
        rows = math.prod(src.shape[:-1])
        count = moved.setdefault((id(kind), g, axis), [kind.at[g, axis], 0, 0])
        for place in (0, 1):
            if which is None or which == place:
                count[1 + place] += rows

    def sent(kind):
        for key in [key for key in moved if key[0] == id(kind)]:
            sem, inside, ends = moved.pop(key)
            if inside == ends:
                got_rows_of(inside, sem)
            else:
                pl.when(outer == 0)(functools.partial(got_rows_of, inside, sem))
                pl.when(outer == 1)(functools.partial(got_rows_of, ends, sem))

    def arrived(ref, sem):
        copy(ref, ref, link_s.at[0, 0], sem, to_c).wait_recv()

    def got_rows_of(rows, sem):
        arrived(gwo.at[pl.ds(0, rows)], sem)

    def keep(group, made):
        made.start()
        started.setdefault(group, []).append(made)

    def kept(group):
        for made in started.pop(group, []):
            made.wait_send()

    barrier = pltpu.get_barrier_semaphore()
    for device in (to_c, to_x, to_y, to_xy, *to_z[1:]):
        pl.semaphore_signal(barrier, inc=1, device_id=device, device_id_type=MESH)

    base = mul8(x * 512, 512)
    arriving = [
        pltpu.make_async_copy(there, here, in_s.at[i])
        for i, (there, here) in enumerate(
            (
                (h_qkv, w_qkv),
                (h_out, w_out),
                (h_up, w_up),
                (h_down, w_down),
                (h_vec, vectors),
                (h_bup, b_up),
                (h_bqv, b_qv),
                (h_rng, ranges),
                (h_tok.at[pl.ds(base, 512)], tok),
                (h_mask, mask),
                (h_long, long_rows),
                (h_grad, grad_out),
                (h_up, wts.at[1, x, z, y]),
                (h_down, wts.at[2, x, z, y]),
            )
        )
    ]
    for made in arriving:
        made.start()
    leaving = []

    def leave_rows(place):
        part = pl.ds(mul8(place * OWN, OWN), OWN)
        leave(o_tok.at[part], r_tok.at[part])

    def leave(here, there):
        made = pltpu.make_async_copy(here, there, in_s.at[len(leaving)])
        made.start()
        leaving.append(made)

    pl.semaphore_wait(barrier, 7)

    def ag_rows(g, xx, zz, yy, part):
        strip, one, two = AG_CUTS[g]
        first = (0, strip, strip + one, strip)[part]
        return wts.at[g, xx, zz, yy, pl.ds(first, (strip, one, two, one + two)[part])]

    def ag_own(g, part):
        if g == 0:
            return ag_rows(g, x, z, y, part)
        strip, one, two = AG_CUTS[g]
        return (h_up, h_down)[g - 1].at[pl.ds(*((0, strip), None, None, (strip, one + two))[part])]

    def ag_strips(g, zz):
        return wts.at[g, :, zz, :, pl.ds(0, AG_CUTS[g][0])]

    def ag_strip_xy(g):
        own = ag_rows(g, x, z, y, 0)
        for axis, device in ((0, to_x), (1, to_y)):
            send(link_s, g, axis, ag_own(g, 0), own, str_.at[g - 1, int(axis != g - 1)], device)

    def ag_strip_relay(g):
        held = ag_rows(g, nx, z, y, 0) if g == 1 else ag_rows(g, x, z, ny, 0)
        arrived(held, str_.at[g - 1, 0])
        send(link_s, g, 2 - g, held, held, str_.at[g - 1, 1], (to_y, to_x)[g - 1])

    def ag_strip_z(g):
        got_rows_of(2 * AG_CUTS[g][0], str_.at[g - 1, 1])
        own = ag_strips(g, z)
        send(link_s, g, 2, own, own, z2r.at[g - 1, 0], to_zk[1])
        send(link_s, g, 2, own, own, z2r.at[g - 1, 1 + outer], to_zk[2])

    def ag_strip_fwd(g):
        for k in (2, 3):
            pl.when(outer == 0)(functools.partial(arrived, ag_strips(g, zk[k]), z2r.at[g - 1, k - 1]))
        for k in (2, 3):
            held = ag_strips(g, zk[k])
            send(link_s, g, 2, held, held, z2r.at[g - 1, k - 1], to_zk[1], 0)

    def ag_strip_got(g):
        arrived(ag_strips(g, zk[1]), z2r.at[g - 1, 0])
        for k in (2, 3):
            pl.when(outer == 1)(functools.partial(arrived, ag_strips(g, zk[k]), z2r.at[g - 1, k - 1]))

    def ag_z_send(g):
        own, held = ag_rows(g, x, z, y, 3), ag_own(g, 3)
        send(link_s, g, 2, held, own, zr.at[g, 0], to_zk[1])
        send(link_s, g, 2, held, own, zr.at[g, 1 + outer], to_zk[2])

    def ag_z_fwd(g, k):
        held = ag_rows(g, x, zk[k], y, 3)
        pl.when(outer == 0)(functools.partial(arrived, held, zr.at[g, k - 1]))
        send(link_s, g, 2, held, held, zr.at[g, k - 1], to_zk[1], 0)

    def ag_z_got(g, k):
        held = ag_rows(g, x, zk[k], y, 3)
        if k == 1:
            arrived(held, zr.at[g, 0])
        elif k > 1:
            pl.when(outer == 1)(functools.partial(arrived, held, zr.at[g, k - 1]))

    def ag_xy_send(g, k, which=None):
        own = ag_rows(g, x, zk[k], y, 3)
        if which is None:
            ag_z_got(g, k)
        held = own if k else ag_own(g, 3)
        send(link_s, g, 0, held, own, xr.at[g, k], to_x, which)
        send(link_s, g, 1, held, own, yr.at[g, k], to_y, which)

    def ag_diag(g, k):
        arrived(ag_rows(g, x, zk[k], ny, 3), yr.at[g, k])
        half = ag_rows(g, x, zk[k], ny, 1)
        send(link_s, g, 0, half, half, dr.at[g + k if g == 2 else g], to_x)
        arrived(ag_rows(g, nx, zk[k], y, 3), xr.at[g, k])
        half = ag_rows(g, nx, zk[k], y, 2)
        send(link_s, g, 1, half, half, dr.at[g + k if g == 2 else g], to_y)

    def ag_last(g, k=0, pieces=4):
        got_rows_of(pieces * (PIECE - AG_CUTS[g][0]), dr.at[g + k])

    ag_strip_xy(1)
    ag_xy_send(1, 0)

    arriving[0].wait()
    arriving[1].wait()
    turned = w_out[...].T
    for j, part in enumerate((w_qkv[0], w_qkv[1], w_qkv[2], turned)):
        wts[0, x, z, y, :, j * 128 : j * 128 + 128] = part[:, 0:128]
        wts[0, x, z, y, :, 512 + j * 64 : 576 + j * 64] = part[:, 128:192]
    ag_z_send(0)
    ag_xy_send(0, 0)

    for made in arriving[2:8]:
        made.wait()
    range_of = [ranges[i] for i in range(4)]
    inv_of = [1.0 / r for r in range_of]

    smf[...] = jnp.zeros((16, 128), F32)
    smf[0:6, 0:96] = vectors[...].astype(F32)
    smf[6:9, 0:32] = b_up[...].astype(F32)
    smf[9:12, 0:8] = b_qv[:, 0, :].astype(F32)
    smf[12:15, 0:8] = b_qv[:, 1, :].astype(F32)
    lane = lax.broadcasted_iota(jnp.int32, (1, 128), 1)
    peak_row = jnp.zeros((1, 128), F32)
    for g, ref in enumerate((w_qkv, w_out, w_up, w_down)):
        most = jnp.abs(ref[...].astype(F32))
        if most.ndim == 3:
            most = jnp.max(most, axis=0)
        most = jnp.max(jnp.max(most, axis=0, keepdims=True), axis=1, keepdims=True)
        peak_row = jnp.where(lane == g, most, peak_row)
    smf[15:16] = peak_row
    sm[x, z, y] = smf[...].astype(BF)

    small_c = copy(sm.at[x, z, y], smc, sm_s.at[0], sm_r.at[0], to_c)
    small_c.start()
    ag_z_send(1)
    small_c.wait()
    smf[15:16] = jnp.maximum(peak_row, smc[...].astype(F32)[15:16])
    sm[x, z, y] = smf[...].astype(BF)
    small_xy = ((nx, y, to_x), (x, ny, to_y), (nx, ny, to_xy))
    for i, (_, _, device) in enumerate(small_xy):
        copy(sm.at[x, z, y], sm.at[x, z, y], sm_s.at[1], sm_r.at[1], device).start()
    ag_strip_xy(2)

    for made in arriving[8:]:
        made.wait()

    def do_tokens(i):
        rows = pl.ds(mul8(i * 128, 128), 128)
        v = tok[pl.ds(mul8(i * 128, 128), 128), :].astype(F32)
        xq[rows, :] = (range_of[0] * jnp.tanh(v * inv_of[0])).astype(BF)

    loop(4, do_tokens)
    def do_turn(j):
        cols = pl.ds(mul8(j * 128, 128), 128)
        xqt[cols, :] = xq[:, cols].T

    loop(6, do_turn)
    ag_strip_relay(1)
    ag_xy_send(0, 1)
    ag_z_fwd(0, 2)
    ag_z_fwd(0, 3)

    long_flag = long_rows[x].astype(F32)
    for r in range(4):
        row = mask[pl.ds(x * 4 + r, 1), :].astype(F32)
        column = jnp.broadcast_to(row, (128, 128)).T
        for s in range(4):
            seen = column * (1.0 if r == s else long_flag)
            bias[r * 128 : r * 128 + 128, s * 128 : s * 128 + 128] = jnp.where(seen > 0.5, 0.0, -1e30)

    arrived(sm.at[0, 0:3, 0], sm_r.at[1])
    for k in (1, 2, 3):
        copy(sm.at[:, z], sm.at[:, z], sm_s.at[2], sm_r.at[2], to_z[k]).start()
    ag_strip_relay(2)
    ag_strip_z(1)
    ag_z_send(2)
    ag_diag(0, 0)
    ag_z_got(1, 1)
    ag_xy_send(1, 1, 1)
    ag_xy_send(0, 2)
    ag_z_fwd(1, 2)
    ag_diag(0, 1)
    ag_xy_send(0, 3)
    ag_xy_send(1, 1, 0)
    ag_z_fwd(1, 3)
    arrived(sm.at[:, 0:3], sm_r.at[2])
    arrived(sm.at[0, 0:3, 0], sm_s.at[1])
    arrived(sm.at[:, 0:3], sm_s.at[2])

    peaks = jnp.max(sm[...].astype(F32).reshape(16, 16, 128), axis=0)[15:16]
    w_peak = [jnp.max(jnp.where(lane == g, peaks, 0.0)) for g in range(4)]
    w_inv = [1.0 / r for r in w_peak]

    def spread(xx, width, step):
        total = None
        for place in range(8):
            tile = sm[xx, place // 2, place % 2].astype(F32)
            if width > 128:
                tile = jnp.concatenate([tile, jnp.zeros((16, width - 128), F32)], axis=1)
            if place:
                tile = pltpu.roll(tile, place * step, 1)
            total = tile if total is None else total + tile
        return total

    vec[...] = spread(0, WIDE, 96)
    heads = []
    for xx in range(2):
        wide = spread(xx, 256, 32)
        for h in range(3):
            bup[xx : xx + 1, h * 256 : h * 256 + 256] = wide[6 + h : 7 + h, :]
        narrow = spread(xx, 128, 8)
        heads.append((narrow, pltpu.roll(narrow, 64, 1)))
    for j, first in enumerate((9, 12)):
        for xx in range(2):
            bqv[j : j + 1, xx * 128 : xx * 128 + 128] = (
                heads[xx][0][first : first + 1] + heads[xx][1][first + 1 : first + 2]
            )
        bqv[j : j + 1, 256:384] = heads[0][0][first + 2 : first + 3] + heads[1][1][first + 2 : first + 3]

    ag_diag(0, 2)
    ag_strip_z(2)
    ag_xy_send(2, 0)
    ag_strip_fwd(1)
    ag_diag(0, 3)
    ag_xy_send(1, 2)
    ag_xy_send(1, 3)
    ag_diag(1, 0)
    ag_diag(1, 1)
    ag_xy_send(2, 1)

    left = lax.broadcasted_iota(jnp.int32, (PIECE, 128), 1) < 64

    def squash_heads(zz, yy):
        place = zz * 2 + yy
        rows = pl.ds(mul8(place * PIECE, PIECE), PIECE)
        tiles = []
        for xx in range(2):
            v = wts[0, xx, zz, yy].astype(F32)
            inner = [w_peak[0] * jnp.tanh(v[:, t * 128 : t * 128 + 128] * w_inv[0]) for t in (0, 1, 2)]
            inner.append(w_peak[1] * jnp.tanh(v[:, 384:512] * w_inv[1]))
            mixed = jnp.where(left, w_peak[0], w_peak[1])
            mixed_inv = jnp.where(left, w_inv[0], w_inv[1])
            inner.append(w_peak[0] * jnp.tanh(v[:, 512:640] * w_inv[0]))
            inner.append(mixed * jnp.tanh(v[:, 640:768] * mixed_inv))
            tiles.append(inner)
        for t in range(3):
            for xx in range(2):
                wc[rows, t * HERE + xx * 128 : t * HERE + xx * 128 + 128] = tiles[xx][t].astype(BF)
        for xx in range(2):
            wo[rows, xx * 128 : xx * 128 + 128] = tiles[xx][3].astype(BF)
        for t, first, second in ((4, 0, 1), (5, 2, 3)):
            one, two = tiles[0][t], tiles[1][t]
            wc[rows, first * HERE + 256 : first * HERE + 384] = jnp.where(left, one, pltpu.roll(two, 64, 1)).astype(BF)
            other = jnp.where(left, pltpu.roll(one, 64, 1), two).astype(BF)
            if second == 1:
                wc[rows, HERE + 256 : HERE + 384] = other
            else:
                wo[rows, 256:384] = other

    loop(4, lambda zz: squash_heads(zz, y))
    ag_last(0)
    loop(4, lambda zz: squash_heads(zz, ny))
    ag_z_fwd(2, 2)
    ag_z_fwd(2, 3)

    def squash_piece(g, xx, zz, yy):
        v = wts[g, xx, zz, yy].astype(F32)
        wff[g - 1, xx, pl.ds(mul8((zz * 2 + yy) * PIECE, PIECE), PIECE), :] = (
            w_peak[g + 1] * jnp.tanh(v * w_inv[g + 1])
        ).astype(BF)

    def squash_ff(g, xx):
        loop(8, lambda place: squash_piece(g, xx, place // 2, place % 2))

    for j, held in enumerate((qs, ks, vs)):

        got = nn(xq[...], wc[:, j * HERE : (j + 1) * HERE])
        if j == 0:
            got = (got + bqv[0:1, :]) * 0.125
        elif j == 2:
            got = got + bqv[1:2, :]
        held[...] = got.astype(BF)
    ag_diag(1, 2)
    for p in range(3):
        cols = slice(p * 128, p * 128 + 128)
        kt[cols, :] = ks[:, cols].T
        vt[cols, :] = vs[:, cols].T

    half_of = lax.broadcasted_iota(jnp.int32, (1, 128), 1) // 64

    def attend(p):
        cols = pl.ds(mul8(p * 128, 128), 128)
        for e in range(2):
            feats = pl.ds(mul8(p * 128 + e * 64, 64), 64)
            q = qs[:, cols]
            q = jnp.where(half_of == e, q, jnp.zeros_like(q))
            s = nt(ks[:, cols], q) + bias[...]
            s = jnp.exp(s - jnp.max(s, axis=0, keepdims=True))
            s = (s * (1.0 / jnp.sum(s, axis=0, keepdims=True))).astype(BF)
            probs[p * 2 + e] = s
            ctxt[feats, :] = nn(vt[feats, :], s)

    ag_strip_fwd(2)
    attend(0)
    ag_diag(1, 3)
    ag_xy_send(2, 2)
    attend(1)
    ag_xy_send(2, 3)
    ag_diag(2, 0)
    attend(2)

    for p in range(3):
        cols = slice(p * 128, p * 128 + 128)
        bent = jnp.tanh(ctxt[cols, :].T * inv_of[1])
        cq[:, cols] = (range_of[1] * bent).astype(BF)
        slc[:, cols] = 1.0 - bent * bent
    tot[0] = jnp.zeros((16, WIDE), F32)
    most = jnp.max(jnp.max(jnp.abs(ctxt[...]), axis=0, keepdims=True), axis=1, keepdims=True)
    tot[0, 10:11, :] = jnp.broadcast_to(most, (1, WIDE))

    def out_part(start, held, cols=slice(0, WIDE)):
        held[:, cols] = nt(cq[pl.ds(start, OWN), :], wo[cols, :])

    for i in range(2):
        cols = slice(i * HERE, i * HERE + HERE)
        out_part(theirs, exa_s, cols)
        made = copy(exa_s.at[:, cols], exa_r.at[:, cols], ex_s.at[0], ex_r.at[0], to_c)
        made.start()
    out_part(mine, r1)
    ag_strip_got(1)
    ag_diag(2, 1)
    squash_ff(1, x)
    arrived(exa_r, ex_r.at[0])
    arrived(exa_s, ex_s.at[0])

    def sum_rows(v):
        return jnp.sum(v, axis=0, keepdims=True)

    def mean_of(v):
        return jnp.sum(v, axis=-1, keepdims=True) * (1.0 / WIDE)

    def first_norm(i):
        rows = pl.ds(mul8(i * 128, 128), 128)
        v = tok[pl.ds(mul8(mine + i * 128, 128), 128), :].astype(F32)
        v = v + (r1[rows, :] + exa_r[rows, :] + vec[0:1, :])
        r1[rows, :] = v
        center = v - mean_of(v)
        factor = lax.rsqrt(mean_of(center * center) + 1e-12)
        normed = center * factor
        n1[rows, :] = normed
        rstd1[rows, :] = factor
        h = normed * vec[2:3, :] + vec[3:4, :]
        tot[0, 11:12, :] = jnp.maximum(tot[0, 11:12, :], jnp.max(jnp.abs(h), axis=0, keepdims=True))
        bent = jnp.tanh(h * inv_of[2])
        sl1[rows, :] = 1.0 - bent * bent
        hq[pl.ds(mul8(mine + i * 128, 128), 128), :] = (range_of[2] * bent).astype(BF)

    def half_rows(start, i):
        return pl.ds(mul8(start + i * 128, 128), 128)

    for i in range(2):
        first_norm(i)
        own = hq.at[half_rows(mine, i)]
        copy(own, own, ex_s.at[1], ex_r.at[1], to_c).start()

    def share_rows(held, number):
        own = held.at[pl.ds(mine, OWN)]
        copy(own, own, ex_s.at[1], ex_r.at[number], to_c).start()

    def shared(held):
        arrived(held.at[pl.ds(mine, OWN)], ex_s.at[1])

    def got_rows(held, number):
        arrived(held.at[pl.ds(theirs, OWN)], ex_r.at[number])

    def turn_rows(held, out, start):
        out[:, pl.ds(start, OWN)] = held[pl.ds(start, OWN), :].T

    turn_rows(hq, hqt, mine)
    arrived(hq.at[pl.ds(theirs, OWN)], ex_r.at[1])
    turn_rows(hq, hqt, theirs)

    def expand(xx, between=None):
        wide = pl.ds(mul8(xx * WIDE, WIDE), WIDE)

        def body(i):
            rows = pl.ds(mul8(i * 256, 256), 256)
            u = nn(hq[rows, :], wff[0, xx]) + bup[pl.ds(xx, 1), :]
            cdf = 0.5 * (1.0 + lax.erf(u * 0.7071067811865476))
            a = u * cdf
            tot[0, 12:13, :] = jnp.maximum(tot[0, 12:13, :], jnp.max(jnp.abs(a), axis=0, keepdims=True))
            bent = jnp.tanh(a * inv_of[3])
            aq[rows, wide] = (range_of[3] * bent).astype(BF)
            pdf = 0.3989422804014327 * jnp.exp(-0.5 * u * u)
            fac[rows, wide] = ((1.0 - bent * bent) * (cdf + u * pdf)).astype(fac.dtype)

        body(0)
        if between is not None:
            between()
        body(1)

    expand(x)
    ag_diag(2, 2)
    ag_last(1)
    squash_ff(1, nx)
    expand(nx, functools.partial(ag_diag, 2, 3))
    ag_strip_got(2)

    def down_part(start, held, xx, first, cols=slice(0, WIDE)):
        got = nt(aq[pl.ds(start, OWN), pl.ds(mul8(xx * WIDE, WIDE), WIDE)], wff[1, xx, cols, :])
        held[:, cols] = got if first else held[:, cols] + got

    squash_ff(2, x)
    down_part(theirs, exb_s, x, True)
    down_part(mine, gr2, x, True)
    loop(4, lambda zz: squash_piece(2, nx, zz, y))
    for k in range(4):
        ag_last(2, k, 1)
        squash_piece(2, nx, zk[k], ny)
    for i in range(2):
        cols = slice(i * HERE, i * HERE + HERE)
        down_part(theirs, exb_s, nx, False, cols)
        low_s[:, cols] = exb_s[:, cols].astype(BF)
        copy(low_s.at[:, cols], low_r.at[:, cols], ex_s.at[0], ex_r.at[2], to_c).start()
    down_part(mine, gr2, nx, False)
    arrived(low_r, ex_r.at[2])
    arrived(low_s, ex_s.at[0])

    def second_norm(i):
        rows = pl.ds(mul8(i * 128, 128), 128)
        v = r1[rows, :] + (gr2[rows, :] + low_r[rows, :].astype(F32) + vec[1:2, :])
        center = v - mean_of(v)
        factor = lax.rsqrt(mean_of(center * center) + 1e-12)
        normed = center * factor
        o_layer[rows, :] = (normed * vec[4:5, :] + vec[5:6, :]).astype(BF)
        gy = grad_out[rows, :].astype(F32)
        tot[0, 4:5, :] += sum_rows(gy * normed)
        tot[0, 5:6, :] += sum_rows(gy)
        gn = gy * vec[4:5, :]
        back = factor * (gn - mean_of(gn) - normed * mean_of(gn * normed))
        gr2[rows, :] = back
        low = back.astype(BF)
        tot[0, 1:2, :] += sum_rows(low.astype(F32))
        gf[pl.ds(mul8(mine + i * 128, 128), 128), :] = low

    shared(hq)
    for i in range(2):
        second_norm(i)
        own = gf.at[half_rows(mine, i)]
        copy(own, own, ex_s.at[1], ex_r.at[3], to_c).start()
    leave(o_layer, r_layer)
    turn_rows(gf, rowt, mine)
    sent(link_s)
    arrived(gf.at[pl.ds(theirs, OWN)], ex_r.at[3])
    turn_rows(gf, rowt, theirs)

    def rs_rows(g, part):
        strip, one, two = RS_CUTS[g]
        return pl.ds((0, strip, strip + one, strip)[part], (strip, one, two, one + two)[part])

    def rs_part(g, part):
        _, one, two = RS_CUTS[g]
        return pl.ds((0, 0, one, 0)[part], (0, one, two, one + two)[part])

    far_z, near_z = pl.ds(2 - z // 2 * 2, 2), pl.ds(z // 2 * 2, 2)

    def rs_first(g, planes):
        one, far = rs_part(g, 1), pl.ds(0, RS_CUTS[g][2])
        i = 0 if planes is far_z else 2
        send(link_s, g, 0, wts.at[g, nx, planes, ny, rs_rows(g, 1)], rdx.at[g, planes, one], rs_r.at[g, i], to_x)
        send(link_s, g, 1, wts.at[g, nx, planes, ny, rs_rows(g, 2)], rdy.at[g, planes, far], rs_r.at[g, i + 1], to_y)

    def rs_direct_x(g, planes, part):
        i = 4 if planes is far_z else 5
        src = wts.at[g, nx, planes, y, rs_rows(g, part)]
        send(link_s, g, 0, src, rxx.at[g, planes, rs_part(g, part)], rs_r.at[g, i], to_x)

    def rs_direct_y(g, planes, part):
        i = 4 if planes is far_z else 5
        src = wts.at[g, x, planes, ny, rs_rows(g, part)]
        send(link_s, g, 1, src, ryy.at[g, planes, rs_part(g, part)], rs_r.at[g, i], to_y)

    def rs_direct(g, near):
        rs_direct_x(g, far_z, 1)
        if near:
            rs_direct_x(g, near_z, 1)

    def rs_second(g, near):
        rs_direct_y(g, far_z, 2)
        if near:
            rs_direct_y(g, near_z, 2)

    def rs_third_x(g, near):
        one, here = rs_part(g, 1), rs_rows(g, 1)
        for planes, i in ((far_z, 0), (near_z, 2)):
            arrived(rdx.at[g, planes, one], rs_r.at[g, i])
            wts[g, x, planes, ny, here] = (
                wts[g, x, planes, ny, here].astype(F32) + rdx[g, planes, one].astype(F32)
            ).astype(BF)
            rs_direct_y(g, planes, 1)
        if not near:
            rs_direct_y(g, near_z, 2)

    def rs_third_y(g, near):
        here, far = rs_rows(g, 2), pl.ds(0, RS_CUTS[g][2])
        for planes, i in ((far_z, 1), (near_z, 3)):
            arrived(rdy.at[g, planes, far], rs_r.at[g, i])
            wts[g, nx, planes, y, here] = (
                wts[g, nx, planes, y, here].astype(F32) + rdy[g, planes, far].astype(F32)
            ).astype(BF)
            rs_direct_x(g, planes, 2)
        if not near:
            rs_direct_x(g, near_z, 1)

    def plane(g, zz):
        rest, here = rs_rows(g, 3), rs_part(g, 3)
        return wts[g, x, zz, y, rest].astype(F32) + rxx[g, zz, here].astype(F32) + ryy[g, zz, here].astype(F32)

    def rs_fourth(g):
        both, rest = rs_part(g, 3), rs_rows(g, 3)
        got_rows_of(4 * (PIECE - RS_CUTS[g][0]), rs_r.at[g, 4])
        for k in (3, 2):
            wts[g, x, zk[k], y, rest] = plane(g, zk[k]).astype(BF)
            send(link_s, g, 2, wts.at[g, x, zk[k], y, rest], rzf.at[g, k - 2, both], rf_r.at[g, k - 2], to_zk[1], 1)

    def rs_near(g):
        both, rest = rs_part(g, 3), rs_rows(g, 3)
        got_rows_of(4 * (PIECE - RS_CUTS[g][0]), rs_r.at[g, 5])
        wts[g, x, zk[1], y, rest] = plane(g, zk[1]).astype(BF)
        send(link_s, g, 2, wts.at[g, x, zk[1], y, rest], rz.at[g, 0, both], rs_r.at[g, 7], to_zk[1])

    def rs_fifth(g):
        both, rest = rs_part(g, 3), rs_rows(g, 3)
        for k in (3, 2):

            @pl.when(outer == 0)
            def _(k=k):
                arrived(rzf.at[g, k - 2, both], rf_r.at[g, k - 2])
                wts[g, x, zk[k], y, rest] = (
                    wts[g, x, zk[k], y, rest].astype(F32) + rzf[g, k - 2, both].astype(F32)
                ).astype(BF)

            send(link_s, g, 2, wts.at[g, x, zk[k], y, rest], rz.at[g, 1, both], rs_r.at[g, 7], to_zk[k], 0)

    def strips(held, g, place, i):
        here = pl.ds(0, RS_CUTS[g][0])
        return held.at[g, *place, (nx, x)[i] if g == 2 else slice(None), :, here]

    def strips_of(g, zz, i):
        here = pl.ds(0, RS_CUTS[g][0])
        return wts.at[g, (nx, x)[i] if g == 2 else slice(None), zz, :, here]

    def rs_strip_z(g, i):
        for k in (3, 2):
            send(link_s, g, 2, strips_of(g, zk[k], i), strips(rzf2, g, (k - 2,), i), rf_r.at[g, k], to_zk[1], 1)
        send(link_s, g, 2, strips_of(g, zk[1], i), strips(rz2, g, (0,), i), rs_r.at[g, 6], to_zk[1])

    def rs_strip_fwd(g):
        here = pl.ds(0, RS_CUTS[g][0])
        for k in (3, 2):

            @pl.when(outer == 0)
            def _(k=k):
                got_rows_of(4 * RS_CUTS[g][0], rf_r.at[g, k])
                wts[g, :, zk[k], :, here] = (
                    wts[g, :, zk[k], :, here].astype(F32) + rzf2[g, k - 2, :, :, here].astype(F32)
                ).astype(BF)

            whole = wts.at[g, :, zk[k], :, here]
            send(link_s, g, 2, whole, rz2.at[g, 1, :, :, here], rs_r.at[g, 6], to_zk[k], 0)

    def rs_strip_sum(g):
        here = pl.ds(0, RS_CUTS[g][0])
        got_rows_of(8 * RS_CUTS[g][0], rs_r.at[g, 6])
        wts[g, :, z, :, here] = (
            wts[g, :, z, :, here].astype(F32)
            + rz2[g, 0, :, :, here].astype(F32)
            + rz2[g, 1, :, :, here].astype(F32)
        ).astype(BF)

    def rs_strip_send(g):
        here = pl.ds(0, RS_CUTS[g][0])
        for i, (xx, yy, axis, device) in enumerate(((nx, ny, 0, to_xy), (nx, y, 0, to_x), (x, ny, 1, to_y))):
            send(link_s, g, axis, wts.at[g, xx, z, yy, here], rst.at[g, i, here], rs_r.at[g, 7], device)

    def rs_total(g):
        here, both = pl.ds(0, RS_CUTS[g][0]), rs_part(g, 3)
        got_rows_of(2 * PIECE + RS_CUTS[g][0], rs_r.at[g, 7])
        strip = wts[g, x, z, y, here].astype(F32)
        for i in range(3):
            strip = strip + rst[g, i, here].astype(F32)
        total = plane(g, z)
        for k in range(2):
            total = total + rz[g, k, both].astype(F32)
        return jnp.concatenate([strip, total], axis=0)

    def ff_grad_planes(g, turned, held, xx, planes, first):
        rows = pl.ds(mul8(first * 2 * PIECE, 4 * PIECE), 4 * PIECE)
        got = nn(turned[rows, :], held[:, pl.ds(mul8(xx * WIDE, WIDE), WIDE)])
        wts[g, xx, planes] = got.reshape(2, 2, PIECE, WIDE).astype(BF)

    def ff_grad(g, turned, held, xx):
        got = nn(turned[...], held[:, pl.ds(mul8(xx * WIDE, WIDE), WIDE)])
        wts[g, xx] = got.reshape(4, 2, PIECE, WIDE).astype(BF)

    ff_grad_planes(2, rowt, aq, nx, far_z, 2 - z // 2 * 2)
    rs_first(2, far_z)
    ff_grad_planes(2, rowt, aq, nx, near_z, z // 2 * 2)
    rs_first(2, near_z)
    rs_direct(2, True)
    rs_strip_z(2, 0)
    ff_grad(2, rowt, aq, x)
    rs_second(2, True)
    rs_strip_z(2, 1)

    for xx in range(2):

        def hidden_grad(i, xx=xx):
            wide = slice(xx * WIDE, xx * WIDE + WIDE)
            rows = pl.ds(mul8(i * 256, 256), 256)
            got = (nn(gf[rows, :], wff[1, xx]) * fac[rows, wide].astype(F32)).astype(BF)
            gu[rows, wide] = got
            tot[0, 6 + xx : 7 + xx, :] += sum_rows(got.astype(F32))

        loop(2, hidden_grad)
    def up_part(start, held):
        held[...] = nt(gu[pl.ds(start, OWN), 0:WIDE], wff[0, 0]) + nt(
            gu[pl.ds(start, OWN), WIDE : 2 * WIDE], wff[0, 1]
        )

    up_part(theirs, exa_s)
    ex3 = copy(exa_s, exa_r, ex_s.at[0], ex_r.at[4], to_c)
    ex3.start()
    up_part(mine, r1)
    ff_grad(1, hqt, gu, nx)
    rs_third_x(2, True)
    rs_third_y(2, True)
    rs_first(1, far_z)
    rs_first(1, near_z)
    rs_direct(1, True)
    ff_grad(1, hqt, gu, x)
    rs_second(1, True)
    rs_strip_z(1, 0)
    ex3.wait()

    def first_back(i):
        rows = pl.ds(mul8(i * 64, 64), 64)
        normed = n1[rows, :]
        gh = (r1[rows, :] + exa_r[rows, :]) * sl1[rows, :]
        tot[0, 2:3, :] += sum_rows(gh * normed)
        tot[0, 3:4, :] += sum_rows(gh)
        gn = gh * vec[2:3, :]
        back = rstd1[rows, :] * (gn - mean_of(gn) - normed * mean_of(gn * normed)) + gr2[rows, :]
        gr2[rows, :] = back
        low = back.astype(BF)
        tot[0, 0:1, :] += sum_rows(low.astype(F32))
        gf[pl.ds(mul8(mine + i * 64, 64), 64), :] = low

    shared(gf)
    loop(4, first_back)
    share_rows(gf, 5)
    turn_rows(gf, rowt, mine)
    got_rows(gf, 5)
    turn_rows(gf, rowt, theirs)

    gwo[...] = nn(rowt[...], cq[...])
    gc[...] = (nn(gf[...], wo[...]) * slc[...]).astype(BF)
    for p in range(3):
        cols = slice(p * 128, p * 128 + 128)
        gct[cols, :] = gc[:, cols].T
        for e in range(2):
            feats = slice(p * 128 + e * 64, p * 128 + e * 64 + 64)
            dsum[p * 2 + e : p * 2 + e + 1, :] = sum_rows(gct[feats, :].astype(F32) * ctxt[feats, :])

    row_half = lax.broadcasted_iota(jnp.int32, (128, 1), 0) // 64

    def attend_back(p):
        cols = pl.ds(mul8(p * 128, 128), 128)
        grad_k = grad_v = None
        for e in range(2):
            feats = pl.ds(mul8(p * 128 + e * 64, 64), 64)
            g = gct[cols, :]
            g = jnp.where(row_half == e, g, jnp.zeros_like(g))
            dpr = nn(vs[:, cols], g)
            ds[...] = (probs[p * 2 + e].astype(F32) * (dpr - dsum[pl.ds(p * 2 + e, 1), :])).astype(BF)
            g = gc[:, cols]
            g = jnp.where(half_of == e, g, jnp.zeros_like(g))
            more_v = nn(probs[p * 2 + e], g)
            q = qs[:, cols]
            q = jnp.where(half_of == e, q, jnp.zeros_like(q))
            more_k = nn(ds[...], q)
            grad_v = more_v if e == 0 else grad_v + more_v
            grad_k = more_k if e == 0 else grad_k + more_k
            gqt[feats, :] = nn(kt[feats, :], ds[...])
        grads[:, pl.ds(mul8(HERE + p * 128, 128), 128)] = grad_k.astype(BF)
        grads[:, pl.ds(mul8(2 * HERE + p * 128, 128), 128)] = grad_v.astype(BF)
        grads[:, cols] = (gqt[cols, :].astype(BF).astype(F32) * 0.125).T.astype(BF)

    attend_back(0)
    attend_back(1)
    attend_back(2)
    rs_strip_fwd(2)
    rs_fourth(2)
    rs_near(2)
    for j, part in ((0, 0), (2, HERE)):
        tot[0, 8:9, part : part + HERE] = sum_rows(grads[:, j * HERE : (j + 1) * HERE].astype(F32))

    left_four = lax.broadcasted_iota(jnp.int32, (4 * PIECE, 128), 1) < 64

    def head_grad(i):
        rows = pl.ds(mul8(i * 4 * PIECE, 4 * PIECE), 4 * PIECE)
        gq, gk, gv = (nn(xqt[rows, :], grads[:, j * HERE : (j + 1) * HERE]) for j in range(3))
        parts = (gq, gk, gv, gwo[rows, :])

        def put(xx, t, v):
            wts[0, xx, pl.ds(i * 2, 2), :, :, t * 128 : t * 128 + 128] = v.reshape(2, 2, PIECE, 128).astype(BF)

        for xx in range(2):
            for t in range(4):
                put(xx, t, parts[t][:, xx * 128 : xx * 128 + 128])
        for t, first, second in ((4, gq, gk), (5, gv, gwo[rows, :])):
            one, two = first[:, 256:384], second[:, 256:384]
            put(0, t, jnp.where(left_four, one, pltpu.roll(two, 64, 1)))
            put(1, t, jnp.where(left_four, pltpu.roll(one, 64, 1), two))

    def most_x(i):
        v = jnp.abs(tok[pl.ds(mul8(i * 128, 128), 128), :].astype(F32))
        tot[0, 9:10, :] = jnp.maximum(tot[0, 9:10, :], jnp.max(v, axis=0, keepdims=True))

    loop(4, most_x)
    row_of = lax.broadcasted_iota(jnp.int32, (16, 1), 0)
    small = copy(tot.at[0], tot_c, tt_s.at[0], tt_r.at[0], to_c)
    small.start()
    loop(2, head_grad)
    small.wait()
    mixed = jnp.where(row_of < 6, tot[0] + tot_c[...], jnp.maximum(tot[0], tot_c[...]))
    tot[1] = jnp.where((row_of >= 6) & (row_of < 9), tot[0], mixed)
    small = copy(tot.at[1], tot_x, tt_s.at[0], tt_r.at[1], to_x)
    small.start()
    rs_first(0, far_z)
    rs_first(0, near_z)
    rs_direct(0, False)
    rs_second(0, False)
    rs_strip_z(0, 0)

    def token_part(start, held):
        held[...] = nt(grads[pl.ds(start, OWN), :], wc[...])

    token_part(theirs, exb_s)
    ex4 = copy(exb_s, exb_r, ex_s.at[0], ex_r.at[6], to_c)
    ex4.start()
    rs_third_x(1, True)
    rs_third_y(1, True)
    token_part(mine, r1)
    ex4.wait()

    def token_grad(i):
        rows = pl.ds(mul8(i * 64, 64), 64)
        v = tok[pl.ds(mul8(mine + i * 64, 64), 64), :].astype(F32)
        bent = jnp.tanh(v * inv_of[0])
        got = gr2[rows, :] + (r1[rows, :] + exb_r[rows, :]) * (1.0 - bent * bent)
        o_tok[pl.ds(mul8(mp * OWN + i * 64, 64), 64), :] = got.astype(BF)

    loop(4, token_grad)
    own = o_tok.at[pl.ds(mul8(mp * OWN, OWN), OWN)]
    keep("tok", copy(own, own, gx_s.at[1], gx_r.at[1], to_c))
    leave_rows(mp)
    rs_strip_fwd(1)
    small.wait()
    tot[2] = jnp.where(row_of < 9, tot[1] + tot_x[...], jnp.maximum(tot[1], tot_x[...]))
    small = copy(tot.at[2], tot_y, tt_s.at[0], tt_r.at[2], to_y)
    small.start()
    rs_third_x(0, False)
    rs_fifth(2)
    rs_third_y(0, False)
    keep("tok", copy(own, own, gx_s.at[0], gx_r.at[0], to_x))
    for g in (2, 1):
        rs_strip_sum(g)
        rs_strip_send(g)
    rs_strip_fwd(0)
    rs_fourth(1)
    small.wait()
    tot[3] = jnp.where(row_of < 9, tot[2] + tot_y[...], jnp.maximum(tot[2], tot_y[...]))

    def both(one, two):
        return jnp.where(row_of < 9, one + two, jnp.maximum(one, two))

    inward = copy(tot.at[3], tot_z.at[0], tt_s.at[0], tt_r.at[3], to_zk[1])
    across = copy(tot.at[4], tot_z.at[1], tt_s.at[0], tt_r.at[4], to_zk[2])
    outward = copy(tot.at[5], tot_z.at[2], tt_s.at[0], tt_r.at[5], to_zk[1])
    pl.when(outer == 1)(inward.start)
    rs_fourth(0)
    rs_near(1)
    rs_strip_sum(0)
    rs_strip_send(0)
    rs_fifth(1)

    @pl.when(outer == 0)
    def _():
        inward.wait_recv()
        tot[4] = both(tot[3], tot_z[0])
        across.start()

    rs_near(0)

    @pl.when(outer == 0)
    def _():
        across.wait()
        tot[5] = both(tot[4], tot_z[1])
        outward.start()

    rs_fifth(0)
    far = o_tok.at[pl.ds(mul8((nx * 2 + c) * OWN, OWN), OWN)]
    copy(far, far, gx_s.at[0], gx_r.at[0], to_x).wait_recv()
    keep("tok", copy(far, far, gx_s.at[2], gx_r.at[2], to_c))
    leave_rows(nx * 2 + c)

    o_down[...] = rs_total(2) * _slope(w_down[...], w_inv[3])
    leave(o_down, r_down)
    o_up[...] = rs_total(1) * _slope(w_up[...], w_inv[2])
    leave(o_up, r_up)

    @pl.when(outer == 0)
    def _():
        outward.wait_send()

    @pl.when(outer == 1)
    def _():
        inward.wait_send()
        outward.wait_recv()
        tot[5] = tot_z[2]

    done = tot[5]
    back = pltpu.roll(done, (8 - dp) * 96, 1)
    o_vec[...] = back[0:6, 0:96]
    ups = jnp.where(x == 0, done[6:7, :], done[7:8, :])
    for h in range(3):
        tile = jnp.broadcast_to(ups[:, h * 256 : h * 256 + 256], (8, 256))
        o_bup[h : h + 1, :] = pltpu.roll(tile, (8 - dp) * 32, 1)[0:1, 0:32]
    for j in range(2):
        row = jnp.broadcast_to(done[8:9, j * HERE : (j + 1) * HERE], (8, HERE))
        pair = jnp.where(x == 0, row[:, 0:128], row[:, 128:256])
        for h, tile, shift in ((0, pair, 0), (1, pair, 64), (2, row[:, 256:384], 64 * x)):
            o_bqv[h, j : j + 1, :] = pltpu.roll(tile, (256 - shift - dp * 8) % 128, 1)[0:1, 0:8]
    for i in range(4):
        most = jnp.max(done[9 + i : 10 + i, :], axis=1, keepdims=True)
        o_rng[i : i + 1, :] = jnp.broadcast_to(0.9 * range_of[i] + 0.1 * most, (1, 128))

    for here, there in ((o_vec, r_vec), (o_bup, r_bup), (o_bqv, r_bqv), (o_rng, r_rng)):
        leave(here, there)
    near = pl.ds(mul8((x * 2 + nc) * OWN, OWN), OWN)
    copy(o_tok.at[near], o_tok.at[near], gx_s.at[1], gx_r.at[1], to_c).wait_recv()
    leave_rows(x * 2 + nc)
    total = rs_total(0)
    for j in range(4):
        main = total[:, j * 128 : j * 128 + 128]
        pair = total[:, 512 + j // 2 * 128 : 640 + j // 2 * 128]
        if j % 2:
            pair = pltpu.roll(pair, 64, 1)
        whole = jnp.concatenate([main, pair], axis=1)[:, 0:192]
        if j < 3:
            o_qkv[j] = whole * _slope(w_qkv[j], w_inv[0])
        else:
            o_out[...] = whole.T * _slope(w_out[...], w_inv[1])
    leave(o_qkv, r_qkv)
    leave(o_out, r_out)
    far = pl.ds(mul8((nx * 2 + nc) * OWN, OWN), OWN)
    copy(o_tok.at[far], o_tok.at[far], gx_s.at[2], gx_r.at[2], to_c).wait_recv()
    leave_rows(nx * 2 + nc)
    sent(link_s)
    kept("tok")
    shared(gf)
    for made in leaving:
        made.wait()


def _slope(values, inverse):
    bent = jnp.tanh(values.astype(F32) * inverse)
    return 1.0 - bent * bent


def layer_on_chips(
    tokens, w_qkv, w_out, w_up, w_down, b_qv, b_up, vectors, ema_ranges, key_mask, long_rows, grad_out
):
    vmem = pltpu.VMEM
    rows = tokens.shape[0]
    half = rows // 2

    def buffer(*shape, dtype=BF):
        return vmem(shape, dtype)

    def f32(*shape):
        return vmem(shape, F32)

    sems = pltpu.SemaphoreType.DMA
    ins = (w_qkv, w_out, w_up, w_down.T, b_qv.transpose(1, 0, 2), b_up, vectors)
    mask = key_mask.reshape(rows // 128, 128)
    kinds = [
        jax.ShapeDtypeStruct(grad_out.shape, BF),
        jax.ShapeDtypeStruct(tokens.shape, BF),
        *(jax.ShapeDtypeStruct(v.shape, F32) for v in ins),
    ]
    scratch = [
        buffer(half, WIDE),
        *(vmem(v.shape, v.dtype) for v in (*ins, mask, grad_out)),
        *(vmem(v.shape, v.dtype) for v in kinds),
        pltpu.SMEM(ema_ranges.shape, F32),
        pltpu.SMEM(long_rows.shape, jnp.int32),
        f32(8, 128),
        buffer(3, 2, 4, 2, PIECE, WIDE),
        buffer(2, 2, WIDE, WIDE),
        buffer(WIDE, 3 * HERE),
        buffer(WIDE, HERE),
        buffer(3, 4, 48, WIDE),
        buffer(3, 4, 48, WIDE),
        buffer(3, 4, 80, WIDE),
        buffer(3, 4, 80, WIDE),
        buffer(3, 2, 80, WIDE),
        buffer(3, 2, 80, WIDE),
        buffer(3, 2, 2, 2, 32, WIDE),
        buffer(3, 2, 2, 2, 32, WIDE),
        buffer(3, 3, 32, WIDE),
        buffer(2, 4, 2, 16, 128),
        buffer(16, 128),
        f32(16, 128),
        f32(16, WIDE),
        f32(8, WIDE),
        f32(8, HERE),
        buffer(half, WIDE),
        buffer(WIDE, half),
        f32(half, half),
        buffer(half, HERE),
        buffer(half, HERE),
        buffer(half, HERE),
        buffer(HERE, half),
        buffer(HERE, half),
        buffer(6, half, half),
        buffer(half, half),
        f32(HERE, half),
        buffer(half, HERE),
        f32(half, HERE),
        f32(OWN, WIDE),
        f32(OWN, WIDE),
        f32(OWN, WIDE),
        f32(OWN, WIDE),
        buffer(OWN, WIDE),
        buffer(OWN, WIDE),
        buffer(half, WIDE),
        buffer(WIDE, half),
        f32(OWN, WIDE),
        f32(OWN, WIDE),
        f32(OWN, 1),
        f32(OWN, WIDE),
        buffer(half, 2 * WIDE),
        buffer(half, 2 * WIDE),
        buffer(half, 2 * WIDE),
        buffer(half, WIDE),
        buffer(WIDE, half),
        f32(OWN, WIDE),
        buffer(half, HERE),
        buffer(HERE, half),
        f32(8, half),
        buffer(half, 3 * HERE),
        f32(HERE, half),
        f32(WIDE, HERE),
        f32(6, 16, WIDE),
        f32(16, WIDE),
        f32(16, WIDE),
        f32(16, WIDE),
        f32(3, 16, WIDE),
        sems((3, 3)),
        sems((3, 3)),
        sems((2, 3)),
        sems((2, 2)),
        sems((3, 4)),
        sems((3, 4)),
        sems((6,)),
        sems((3, 8)),
        sems((3, 4)),
        sems((3,)),
        sems((3,)),
        sems((2,)),
        sems((7,)),
        sems((1,)),
        sems((6,)),
        sems((3,)),
        sems((3,)),
        sems((14,)),
    ]
    far = pl.BlockSpec(memory_space=pltpu.HBM)
    outs = pl.pallas_call(
        layer_kernel,
        out_shape=[*kinds, jax.ShapeDtypeStruct((8, 128), F32)],
        in_specs=[far] * 12,
        out_specs=[far] * 10,
        scratch_shapes=scratch,
        compiler_params=pltpu.CompilerParams(
            collective_id=0, has_side_effects=True, vmem_limit_bytes=VMEM_LIMIT
        ),
        name="encoder_layer",
    )(tokens, *ins, ema_ranges, mask, long_rows, grad_out)
    outs = finish(outs, ema_ranges)
    return (*outs[:5], outs[5].T, outs[6].transpose(1, 0, 2), *outs[7:])


def finish_kernel(*refs):
    ins, outs, held, wide, sem = refs[:10], refs[10:20], refs[20:30], refs[30], refs[31]
    step = OWN // 2
    parts = [pl.ds(i * step, step) for i in range(ins[1].shape[0] // step)]
    arriving = [pltpu.make_async_copy(ins[1].at[p], held[1].at[p], sem.at[10 + i]) for i, p in enumerate(parts)]
    moved = [i for i in range(10) if i != 1]
    arriving += [pltpu.make_async_copy(ins[i], held[i], sem.at[i]) for i in moved]
    leaving = [pltpu.make_async_copy(wide.at[p], outs[1].at[p], sem.at[10 + i]) for i, p in enumerate(parts)]
    leaving += [pltpu.make_async_copy(held[i], outs[i], sem.at[i]) for i in moved[:-1]]
    for made in arriving:
        made.start()
    for i, (here, there) in enumerate(zip(arriving, leaving)):
        here.wait()
        if i < len(parts):
            wide[parts[i], :] = held[1][parts[i], :].astype(F32)
        there.start()
    arriving[-1].wait()
    for i in range(4):
        outs[9][i] = held[9][i, 0]
    for made in leaving:
        made.wait()


def finish(held, ranges):
    shape = jax.ShapeDtypeStruct
    far = pl.BlockSpec(memory_space=pltpu.HBM)
    return pl.pallas_call(
        finish_kernel,
        out_shape=[shape(v.shape, F32 if i == 1 else v.dtype) for i, v in enumerate(held[:9])]
        + [shape(ranges.shape, F32)],
        in_specs=[far] * 10,
        out_specs=[far] * 9 + [pl.BlockSpec(memory_space=pltpu.SMEM)],
        scratch_shapes=[pltpu.VMEM(v.shape, v.dtype) for v in held]
        + [pltpu.VMEM(held[1].shape, F32), pltpu.SemaphoreType.DMA((10 + held[1].shape[0] * 2 // OWN,))],
        compiler_params=pltpu.CompilerParams(vmem_limit_bytes=VMEM_LIMIT),
        name="write_results",
    )(*held)


VMEM_LIMIT = 64 * 1024 * 1024


def solution(mesh):
    placed = (
        P("dp", None),
        P(None, "dp", "mp"),
        P("mp", "dp"),
        P("dp", "mp"),
        P("mp", "dp"),
        P(None, "mp", "dp"),
        P("mp", "dp"),
        P(None, "dp"),
        P(),
        P("dp"),
        P("dp"),
        P(("dp", "mp"), None),
    )
    on_chips = dict(mesh.shape) == {"dp": 8, "mp": 4}
    return jax.shard_map(
        layer_on_chips if on_chips else per_device,
        mesh=mesh,
        in_specs=placed,
        out_specs=(
            P(("dp", "mp"), None),
            P("dp", None),
            P(None, "dp", "mp"),
            P("mp", "dp"),
            P("dp", "mp"),
            P("mp", "dp"),
            P(None, "mp", "dp"),
            P("mp", "dp"),
            P(None, "dp"),
            P(),
        ),
        check_vma=False,
    )
```

```python
import functools
import math

import jax
import jax.numpy as jnp
from jax import lax
from jax.experimental import pallas as pl
from jax.experimental.pallas import tpu as pltpu
from jax.sharding import PartitionSpec as P

HD = 64
BLOCK = 512
SEG = 128


eps_norm = 1e-12
root_half = 0.7071067811865476
inv_root_tau = 0.3989422804014327


def squash(values, limit):
    return limit * jnp.tanh(values / limit)


def slope(values, limit):
    bent = jnp.tanh(values / limit)
    return 1.0 - bent * bent


def peak_of(values):
    return jnp.max(jnp.abs(values.astype(jnp.float32)))


def product(left, right):
    return jnp.dot(left, right, preferred_element_type=jnp.float32)


def contract_rows(left, right):
    return lax.dot_general(
        left, right, (((0,), (0,)), ((), ())), preferred_element_type=jnp.float32
    )


def contract_cols(left, right):
    return lax.dot_general(
        left, right, (((1,), (1,)), ((), ())), preferred_element_type=jnp.float32
    )


def normalize(values):
    center = values - jnp.mean(values, axis=-1, keepdims=True)
    factor = lax.rsqrt(jnp.mean(center * center, axis=-1, keepdims=True) + eps_norm)
    return (center * factor, factor)


def norm_back(grad_normed, normed, factor):
    first_mean = jnp.mean(grad_normed, axis=-1, keepdims=True)
    cross_mean = jnp.mean(grad_normed * normed, axis=-1, keepdims=True)
    return factor * (grad_normed - first_mean - normed * cross_mean)


def allowed_keys(live, long_flag):
    places = jnp.arange(BLOCK) // SEG
    return (live[None, :] > 0) & ((long_flag > 0) | (places[:, None] == places[None, :]))


def block_scores(queries, keys_in, live, long_flag):
    scores = jnp.einsum("qhd,khd->hqk", queries, keys_in, preferred_element_type=jnp.float32)
    return jnp.where(allowed_keys(live, long_flag)[None], scores, -1e30)


def attend_block(pieces):
    queries, keys_in, values, live, long_flag = pieces
    scores = block_scores(queries, keys_in, live, long_flag)
    top_score = jnp.max(scores, axis=-1, keepdims=True)
    weights = jnp.exp(scores - top_score)
    totals = jnp.sum(weights, axis=-1, keepdims=True)
    attn_probs = (weights / totals).astype(jnp.bfloat16)
    context = jnp.einsum("hqk,khd->qhd", attn_probs, values, preferred_element_type=jnp.float32)
    return (context, top_score + jnp.log(totals))


def attend_back(pieces):
    queries, keys_in, values, live, long_flag, log_total, grad_ctx = pieces
    attn_probs = jnp.exp(block_scores(queries, keys_in, live, long_flag) - log_total)
    grad_probs = jnp.einsum("qhd,khd->hqk", grad_ctx, values, preferred_element_type=jnp.float32)
    grad_values = jnp.einsum(
        "hqk,qhd->khd",
        attn_probs.astype(jnp.bfloat16),
        grad_ctx,
        preferred_element_type=jnp.float32,
    )
    inner = jnp.sum(grad_probs * attn_probs, axis=-1, keepdims=True)
    grad_scores = (attn_probs * (grad_probs - inner)).astype(jnp.bfloat16)
    grad_queries = jnp.einsum(
        "hqk,khd->qhd", grad_scores, keys_in, preferred_element_type=jnp.float32
    )
    grad_keys = jnp.einsum("hqk,qhd->khd", grad_scores, queries, preferred_element_type=jnp.float32)
    return (
        grad_queries.astype(jnp.bfloat16),
        grad_keys.astype(jnp.bfloat16),
        grad_values.astype(jnp.bfloat16),
    )


def prepare(gathered, w_peaks):
    return tuple(
        (
            squash(gathered[index].astype(jnp.float32), w_peaks[index]).astype(jnp.bfloat16)
            for index in range(4)
        )
    )


def peak_all(values):
    return lax.pmax(peak_of(values), ("dp", "mp"))


def per_device(
    tokens,
    w_qkv,
    w_out,
    w_up,
    w_down,
    b_qv,
    b_up,
    vectors,
    ema_ranges,
    key_mask,
    long_rows,
    grad_out,
):
    row_count = tokens.shape[0]
    quarter = row_count // lax.axis_size("mp")
    row_start = lax.axis_index("mp") * quarter
    blocks = row_count // BLOCK
    w_peaks = lax.pmax(
        (peak_of(w_qkv), peak_of(w_out), peak_of(w_up), peak_of(w_down)), ("dp", "mp")
    )
    gathered = (
        lax.all_gather(w_qkv, "dp", axis=1, tiled=True),
        lax.all_gather(w_out, "dp", axis=1, tiled=True),
        lax.all_gather(w_up, "dp", axis=0, tiled=True),
        lax.all_gather(w_down, "dp", axis=1, tiled=True),
        lax.all_gather(b_qv, "dp", axis=2, tiled=True),
        lax.all_gather(b_up, "dp", axis=1, tiled=True),
        lax.all_gather(vectors, "dp", axis=1, tiled=True),
    )
    qkv_q, out_q, up_q, down_q = prepare(gathered, w_peaks)
    bias_qv = gathered[4].astype(jnp.float32).reshape(2, -1)
    bias_up = gathered[5].astype(jnp.float32).reshape(-1)
    vec = gathered[6].astype(jnp.float32)
    head_width = bias_qv.shape[1]
    heads_here = head_width // HD
    scale_q = HD ** (-0.5)
    tok_float = tokens.astype(jnp.float32)
    peak_tok = peak_all(tok_float)
    tok_quant = squash(tok_float, ema_ranges[0]).astype(jnp.bfloat16)
    projected = jnp.einsum("td,jde->jte", tok_quant, qkv_q, preferred_element_type=jnp.float32)
    queries = ((projected[0] + bias_qv[0]) * scale_q).astype(jnp.bfloat16)
    keys_all = projected[1].astype(jnp.bfloat16)
    values = (projected[2] + bias_qv[1]).astype(jnp.bfloat16)
    shape_four = (blocks, BLOCK, heads_here, HD)
    mask_blocks = key_mask.reshape(blocks, BLOCK)
    block_inputs = (
        queries.reshape(shape_four),
        keys_all.reshape(shape_four),
        values.reshape(shape_four),
        mask_blocks,
        long_rows,
    )
    context, log_total = lax.map(attend_block, block_inputs)
    context = context.reshape(row_count, head_width)
    peak_ctx = peak_all(context)
    ctx_quant = squash(context, ema_ranges[1]).astype(jnp.bfloat16)
    partial_attn = product(ctx_quant, out_q)
    attn = lax.psum_scatter(partial_attn, "mp", scatter_dimension=0, tiled=True) + vec[0]
    first_own = lax.dynamic_slice_in_dim(tok_float, row_start, quarter, 0) + attn
    normed, factor_one = normalize(first_own)
    hidden_in = normed * vec[2] + vec[3]
    hid_quant = lax.all_gather(
        squash(hidden_in, ema_ranges[2]).astype(jnp.bfloat16), "mp", axis=0, tiled=True
    )
    peak_hid = peak_all(hidden_in)
    pre_act = product(hid_quant, up_q) + bias_up
    active = pre_act * 0.5 * (1.0 + lax.erf(pre_act * root_half))
    peak_act = peak_all(active)
    act_quant = squash(active, ema_ranges[3]).astype(jnp.bfloat16)
    branch = (
        lax.psum_scatter(product(act_quant, down_q), "mp", scatter_dimension=0, tiled=True) + vec[1]
    )
    second = first_own + branch
    normed_two, factor_two = normalize(second)
    layer_out = (normed_two * vec[4] + vec[5]).astype(jnp.bfloat16)
    new_ranges = 0.9 * ema_ranges + 0.1 * jnp.stack([peak_tok, peak_ctx, peak_hid, peak_act])
    gathered = (
        lax.all_gather(w_qkv, "dp", axis=1, tiled=True),
        lax.all_gather(w_out, "dp", axis=1, tiled=True),
        lax.all_gather(w_up, "dp", axis=0, tiled=True),
        lax.all_gather(w_down, "dp", axis=1, tiled=True),
        lax.all_gather(b_qv, "dp", axis=2, tiled=True),
        lax.all_gather(b_up, "dp", axis=1, tiled=True),
        lax.all_gather(vectors, "dp", axis=1, tiled=True),
    )
    qkv_q, out_q, up_q, down_q = prepare(gathered, w_peaks)
    grad_y = grad_out.astype(jnp.float32)
    grad_gain_two = jnp.sum(grad_y * normed_two, axis=0)
    grad_shift_two = jnp.sum(grad_y, axis=0)
    grad_second = norm_back(grad_y * vec[4], normed_two, factor_two)
    grad_resid = lax.all_gather(grad_second.astype(jnp.bfloat16), "mp", axis=0, tiled=True).astype(
        grad_second.dtype
    )
    grad_branch = grad_resid.astype(jnp.bfloat16)
    grad_bias_down = jnp.sum(grad_branch.astype(jnp.float32), axis=0)
    grad_down_w = contract_rows(act_quant, grad_branch)
    grad_active = contract_cols(grad_branch, down_q) * slope(active, ema_ranges[3])
    normal_cdf = 0.5 * (1.0 + lax.erf(pre_act * root_half))
    normal_pdf = inv_root_tau * jnp.exp(-0.5 * pre_act * pre_act)
    grad_pre = (grad_active * (normal_cdf + pre_act * normal_pdf)).astype(jnp.bfloat16)
    grad_bias_up = jnp.sum(grad_pre.astype(jnp.float32), axis=0)
    grad_up_w = contract_rows(hid_quant, grad_pre)
    partial_hid = contract_cols(grad_pre, up_q)
    grad_hid_q = lax.psum_scatter(partial_hid, "mp", scatter_dimension=0, tiled=True)
    grad_hidden = grad_hid_q * slope(hidden_in, ema_ranges[2])
    grad_gain_one = jnp.sum(grad_hidden * normed, axis=0)
    grad_shift_one = jnp.sum(grad_hidden, axis=0)
    grad_first = norm_back(grad_hidden * vec[2], normed, factor_one) + grad_second
    grad_attn = lax.all_gather(grad_first.astype(jnp.bfloat16), "mp", axis=0, tiled=True)
    grad_bias_out = jnp.sum(grad_attn.astype(jnp.float32), axis=0)
    grad_out_w = contract_rows(ctx_quant, grad_attn)
    grad_ctx = (contract_cols(grad_attn, out_q) * slope(context, ema_ranges[1])).astype(
        jnp.bfloat16
    )
    back_inputs = block_inputs + (log_total, grad_ctx.reshape(shape_four))
    grad_q, grad_k, grad_v = lax.map(attend_back, back_inputs)
    stacked = jnp.stack(
        [
            grad_q.reshape(row_count, head_width) * jnp.bfloat16(scale_q),
            grad_k.reshape(row_count, head_width),
            grad_v.reshape(row_count, head_width),
        ]
    )
    grad_qkv_w = jnp.einsum("td,jte->jde", tok_quant, stacked, preferred_element_type=jnp.float32)
    stacked_float = stacked.astype(jnp.float32)
    grad_bias_qv = jnp.stack([jnp.sum(stacked_float[0], axis=0), jnp.sum(stacked_float[2], axis=0)])
    part_input = jnp.einsum("jte,jde->td", stacked, qkv_q, preferred_element_type=jnp.float32)
    own_term = part_input * slope(tok_float, ema_ranges[0])
    own_rows = lax.dynamic_slice_in_dim(own_term, row_start, quarter, 0) + grad_first
    own_term = lax.dynamic_update_slice_in_dim(own_term, own_rows, row_start, 0)
    grad_tokens, norm_tail = (
        lax.psum(own_term.astype(jnp.bfloat16), "mp").astype(jnp.float32),
        lax.psum(
            jnp.stack([grad_gain_one, grad_shift_one, grad_gain_two, grad_shift_two]).astype(
                jnp.bfloat16
            ),
            "mp",
        ).astype(jnp.float32),
    )
    grad_vec = jnp.stack(
        [grad_bias_out, grad_bias_down, norm_tail[0], norm_tail[1], norm_tail[2], norm_tail[3]]
    )
    summed = (
        lax.psum_scatter(
            grad_qkv_w * slope(gathered[0].astype(jnp.float32), w_peaks[0]),
            "dp",
            scatter_dimension=1,
            tiled=True,
        ),
        lax.psum_scatter(
            grad_out_w * slope(gathered[1].astype(jnp.float32), w_peaks[1]),
            "dp",
            scatter_dimension=1,
            tiled=True,
        ),
        lax.psum_scatter(
            grad_up_w * slope(gathered[2].astype(jnp.float32), w_peaks[2]),
            "dp",
            scatter_dimension=0,
            tiled=True,
        ),
        lax.psum_scatter(
            grad_down_w * slope(gathered[3].astype(jnp.float32), w_peaks[3]),
            "dp",
            scatter_dimension=1,
            tiled=True,
        ),
        lax.psum_scatter(
            grad_bias_qv.reshape(gathered[4].shape), "dp", scatter_dimension=2, tiled=True
        ),
        lax.psum_scatter(
            grad_bias_up.reshape(gathered[5].shape), "dp", scatter_dimension=1, tiled=True
        ),
        lax.psum_scatter(grad_vec, "dp", scatter_dimension=1, tiled=True),
    )
    return (
        layer_out,
        grad_tokens,
        summed[0],
        summed[1],
        summed[2],
        summed[3],
        summed[4],
        summed[5],
        summed[6],
        new_ranges,
    )


BF = jnp.bfloat16
F32 = jnp.float32
MESH = pl.DeviceIdType.MESH
WIDE = 768
PIECE = 96
AG_CUTS = ((0, 48, 48), (16, 32, 48), (32, 32, 32))
RS_CUTS = ((16, 32, 48), (32, 16, 48), (32, 32, 32))
OWN = 256
HERE = 384


def nn(left, right):
    return lax.dot_general(left, right, (((1,), (0,)), ((), ())), preferred_element_type=F32)


def nt(left, right):
    return lax.dot_general(left, right, (((1,), (1,)), ((), ())), preferred_element_type=F32)


def mul8(value, step):
    return pl.multiple_of(value, step)


def loop(count, body):
    def step(index, carry):
        body(index)
        return carry

    lax.fori_loop(0, count, step, 0)


def layer_kernel(
    h_tok,
    h_qkv,
    h_out,
    h_up,
    h_down,
    h_bqv,
    h_bup,
    h_vec,
    h_rng,
    h_mask,
    h_long,
    h_grad,
    r_layer,
    r_tok,
    r_qkv,
    r_out,
    r_up,
    r_down,
    r_bqv,
    r_bup,
    r_vec,
    r_rng,
    tok,
    w_qkv,
    w_out,
    w_up,
    w_down,
    b_qv,
    b_up,
    vectors,
    mask,
    grad_out,
    o_layer,
    o_tok,
    o_qkv,
    o_out,
    o_up,
    o_down,
    o_bqv,
    o_bup,
    o_vec,
    ranges,
    long_rows,
    o_rng,
    wts,
    wff,
    wc,
    wo,
    rdx,
    rdy,
    rxx,
    ryy,
    rz,
    rzf,
    rz2,
    rzf2,
    rst,
    sm,
    smc,
    smf,
    vec,
    bup,
    bqv,
    xq,
    xqt,
    bias,
    qs,
    ks,
    vs,
    kt,
    vt,
    probs,
    ds,
    ctxt,
    cq,
    slc,
    exa_s,
    exa_r,
    exb_s,
    exb_r,
    low_s,
    low_r,
    hq,
    hqt,
    r1,
    n1,
    rstd1,
    sl1,
    aq,
    fac,
    gu,
    gf,
    rowt,
    gr2,
    gc,
    gct,
    dsum,
    grads,
    gqt,
    gwo,
    tot,
    tot_c,
    tot_x,
    tot_y,
    tot_z,
    link_s,
    zr,
    z2r,
    str_,
    xr,
    yr,
    dr,
    rs_r,
    rf_r,
    sm_s,
    sm_r,
    ex_s,
    ex_r,
    tt_s,
    tt_r,
    gx_s,
    gx_r,
    in_s,
):
    dp = lax.axis_index("dp")
    mp = lax.axis_index("mp")
    z, y = dp // 2, dp % 2
    x, c = mp // 2, mp % 2
    nx, ny, nc = 1 - x, 1 - y, 1 - c
    to_x = (dp, nx * 2 + c)
    to_y = (z * 2 + ny, mp)
    to_c = (dp, x * 2 + nc)
    to_xy = (z * 2 + ny, nx * 2 + c)
    to_z = [None] + [((z + k) % 4 * 2 + y, mp) for k in (1, 2, 3)]
    zk = [z, z + 1 - 2 * (z % 2), 2 - z // 2, 3 - 3 * (z // 2)]
    outer = (z * z - 3 * z + 2) // 2
    to_zk = [None] + [(zk[k] * 2 + y, mp) for k in (1, 2, 3)]
    mine = mul8(c * OWN, OWN)
    theirs = mul8(nc * OWN, OWN)
    started = {}
    moved = {}

    def copy(src, dst, send, recv, device):
        return pltpu.make_async_remote_copy(
            src_ref=src, dst_ref=dst, send_sem=send, recv_sem=recv, device_id=device, device_id_type=MESH
        )

    def send(kind, g, axis, src, dst, recv, device, which=None):
        made = copy(src, dst, kind.at[g, axis], recv, device)
        if which is None:
            made.start()
        else:
            pl.when(outer == which)(made.start)
        rows = math.prod(src.shape[:-1])
        count = moved.setdefault((id(kind), g, axis), [kind.at[g, axis], 0, 0])
        for place in (0, 1):
            if which is None or which == place:
                count[1 + place] += rows

    def sent(kind):
        for key in [key for key in moved if key[0] == id(kind)]:
            sem, inside, ends = moved.pop(key)
            if inside == ends:
                got_rows_of(inside, sem)
            else:
                pl.when(outer == 0)(functools.partial(got_rows_of, inside, sem))
                pl.when(outer == 1)(functools.partial(got_rows_of, ends, sem))

    def arrived(ref, sem):
        copy(ref, ref, link_s.at[0, 0], sem, to_c).wait_recv()

    def got_rows_of(rows, sem):
        arrived(gwo.at[pl.ds(0, rows)], sem)

    def keep(group, made):
        made.start()
        started.setdefault(group, []).append(made)

    def kept(group):
        for made in started.pop(group, []):
            made.wait_send()

    barrier = pltpu.get_barrier_semaphore()
    for device in (to_c, to_x, to_y, to_xy, *to_z[1:]):
        pl.semaphore_signal(barrier, inc=1, device_id=device, device_id_type=MESH)

    base = mul8(x * 512, 512)
    arriving = [
        pltpu.make_async_copy(there, here, in_s.at[i])
        for i, (there, here) in enumerate(
            (
                (h_qkv, w_qkv),
                (h_out, w_out),
                (h_up, w_up),
                (h_down, w_down),
                (h_vec, vectors),
                (h_bup, b_up),
                (h_bqv, b_qv),
                (h_rng, ranges),
                (h_tok.at[pl.ds(base, 512)], tok),
                (h_mask, mask),
                (h_long, long_rows),
                (h_grad, grad_out),
                (h_up, wts.at[1, x, z, y]),
                (h_down, wts.at[2, x, z, y]),
            )
        )
    ]
    for made in arriving:
        made.start()
    leaving = []

    def leave_rows(place):
        part = pl.ds(mul8(place * OWN, OWN), OWN)
        leave(o_tok.at[part], r_tok.at[part])

    def leave(here, there):
        made = pltpu.make_async_copy(here, there, in_s.at[len(leaving)])
        made.start()
        leaving.append(made)

    pl.semaphore_wait(barrier, 7)

    def ag_rows(g, xx, zz, yy, part):
        strip, one, two = AG_CUTS[g]
        first = (0, strip, strip + one, strip)[part]
        return wts.at[g, xx, zz, yy, pl.ds(first, (strip, one, two, one + two)[part])]

    def ag_own(g, part):
        if g == 0:
            return ag_rows(g, x, z, y, part)
        strip, one, two = AG_CUTS[g]
        return (h_up, h_down)[g - 1].at[pl.ds(*((0, strip), None, None, (strip, one + two))[part])]

    def ag_strips(g, zz):
        return wts.at[g, :, zz, :, pl.ds(0, AG_CUTS[g][0])]

    def ag_strip_xy(g):
        own = ag_rows(g, x, z, y, 0)
        for axis, device in ((0, to_x), (1, to_y)):
            send(link_s, g, axis, ag_own(g, 0), own, str_.at[g - 1, int(axis != g - 1)], device)

    def ag_strip_relay(g):
        held = ag_rows(g, nx, z, y, 0) if g == 1 else ag_rows(g, x, z, ny, 0)
        arrived(held, str_.at[g - 1, 0])
        send(link_s, g, 2 - g, held, held, str_.at[g - 1, 1], (to_y, to_x)[g - 1])

    def ag_strip_z(g):
        got_rows_of(2 * AG_CUTS[g][0], str_.at[g - 1, 1])
        own = ag_strips(g, z)
        send(link_s, g, 2, own, own, z2r.at[g - 1, 0], to_zk[1])
        send(link_s, g, 2, own, own, z2r.at[g - 1, 1 + outer], to_zk[2])

    def ag_strip_fwd(g):
        for k in (2, 3):
            pl.when(outer == 0)(functools.partial(arrived, ag_strips(g, zk[k]), z2r.at[g - 1, k - 1]))
        for k in (2, 3):
            held = ag_strips(g, zk[k])
            send(link_s, g, 2, held, held, z2r.at[g - 1, k - 1], to_zk[1], 0)

    def ag_strip_got(g):
        arrived(ag_strips(g, zk[1]), z2r.at[g - 1, 0])
        for k in (2, 3):
            pl.when(outer == 1)(functools.partial(arrived, ag_strips(g, zk[k]), z2r.at[g - 1, k - 1]))

    def ag_z_send(g):
        own, held = ag_rows(g, x, z, y, 3), ag_own(g, 3)
        send(link_s, g, 2, held, own, zr.at[g, 0], to_zk[1])
        send(link_s, g, 2, held, own, zr.at[g, 1 + outer], to_zk[2])

    def ag_z_fwd(g, k):
        held = ag_rows(g, x, zk[k], y, 3)
        pl.when(outer == 0)(functools.partial(arrived, held, zr.at[g, k - 1]))
        send(link_s, g, 2, held, held, zr.at[g, k - 1], to_zk[1], 0)

    def ag_z_got(g, k):
        held = ag_rows(g, x, zk[k], y, 3)
        if k == 1:
            arrived(held, zr.at[g, 0])
        elif k > 1:
            pl.when(outer == 1)(functools.partial(arrived, held, zr.at[g, k - 1]))

    def ag_xy_send(g, k, which=None):
        own = ag_rows(g, x, zk[k], y, 3)
        if which is None:
            ag_z_got(g, k)
        held = own if k else ag_own(g, 3)
        send(link_s, g, 0, held, own, xr.at[g, k], to_x, which)
        send(link_s, g, 1, held, own, yr.at[g, k], to_y, which)

    def ag_diag(g, k):
        arrived(ag_rows(g, x, zk[k], ny, 3), yr.at[g, k])
        half = ag_rows(g, x, zk[k], ny, 1)
        send(link_s, g, 0, half, half, dr.at[g + k if g == 2 else g], to_x)
        arrived(ag_rows(g, nx, zk[k], y, 3), xr.at[g, k])
        half = ag_rows(g, nx, zk[k], y, 2)
        send(link_s, g, 1, half, half, dr.at[g + k if g == 2 else g], to_y)

    def ag_last(g, k=0, pieces=4):
        got_rows_of(pieces * (PIECE - AG_CUTS[g][0]), dr.at[g + k])

    ag_strip_xy(1)
    ag_xy_send(1, 0)

    arriving[0].wait()
    arriving[1].wait()
    turned = w_out[...].T
    for j, part in enumerate((w_qkv[0], w_qkv[1], w_qkv[2], turned)):
        wts[0, x, z, y, :, j * 128 : j * 128 + 128] = part[:, 0:128]
        wts[0, x, z, y, :, 512 + j * 64 : 576 + j * 64] = part[:, 128:192]
    ag_z_send(0)
    ag_xy_send(0, 0)

    for made in arriving[2:8]:
        made.wait()
    range_of = [ranges[i] for i in range(4)]
    inv_of = [1.0 / r for r in range_of]

    smf[...] = jnp.zeros((16, 128), F32)
    smf[0:6, 0:96] = vectors[...].astype(F32)
    smf[6:9, 0:32] = b_up[...].astype(F32)
    smf[9:12, 0:8] = b_qv[:, 0, :].astype(F32)
    smf[12:15, 0:8] = b_qv[:, 1, :].astype(F32)
    lane = lax.broadcasted_iota(jnp.int32, (1, 128), 1)
    peak_row = jnp.zeros((1, 128), F32)
    for g, ref in enumerate((w_qkv, w_out, w_up, w_down)):
        most = jnp.abs(ref[...].astype(F32))
        if most.ndim == 3:
            most = jnp.max(most, axis=0)
        most = jnp.max(jnp.max(most, axis=0, keepdims=True), axis=1, keepdims=True)
        peak_row = jnp.where(lane == g, most, peak_row)
    smf[15:16] = peak_row
    sm[x, z, y] = smf[...].astype(BF)

    small_c = copy(sm.at[x, z, y], smc, sm_s.at[0], sm_r.at[0], to_c)
    small_c.start()
    ag_z_send(1)
    small_c.wait()
    smf[15:16] = jnp.maximum(peak_row, smc[...].astype(F32)[15:16])
    sm[x, z, y] = smf[...].astype(BF)
    small_xy = ((nx, y, to_x), (x, ny, to_y), (nx, ny, to_xy))
    for i, (_, _, device) in enumerate(small_xy):
        copy(sm.at[x, z, y], sm.at[x, z, y], sm_s.at[1], sm_r.at[1], device).start()
    ag_strip_xy(2)

    for made in arriving[8:]:
        made.wait()

    def do_tokens(i):
        rows = pl.ds(mul8(i * 128, 128), 128)
        v = tok[pl.ds(mul8(i * 128, 128), 128), :].astype(F32)
        xq[rows, :] = (range_of[0] * jnp.tanh(v * inv_of[0])).astype(BF)

    loop(4, do_tokens)
    def do_turn(j):
        cols = pl.ds(mul8(j * 128, 128), 128)
        xqt[cols, :] = xq[:, cols].T

    loop(6, do_turn)
    ag_strip_relay(1)
    ag_xy_send(0, 1)
    ag_z_fwd(0, 2)
    ag_z_fwd(0, 3)

    long_flag = long_rows[x].astype(F32)
    for r in range(4):
        row = mask[pl.ds(x * 4 + r, 1), :].astype(F32)
        column = jnp.broadcast_to(row, (128, 128)).T
        for s in range(4):
            seen = column * (1.0 if r == s else long_flag)
            bias[r * 128 : r * 128 + 128, s * 128 : s * 128 + 128] = jnp.where(seen > 0.5, 0.0, -1e30)

    arrived(sm.at[0, 0:3, 0], sm_r.at[1])
    for k in (1, 2, 3):
        copy(sm.at[:, z], sm.at[:, z], sm_s.at[2], sm_r.at[2], to_z[k]).start()
    ag_strip_relay(2)
    ag_strip_z(1)
    ag_z_send(2)
    ag_diag(0, 0)
    ag_z_got(1, 1)
    ag_xy_send(1, 1, 1)
    ag_xy_send(0, 2)
    ag_z_fwd(1, 2)
    ag_diag(0, 1)
    ag_xy_send(0, 3)
    ag_xy_send(1, 1, 0)
    ag_z_fwd(1, 3)
    arrived(sm.at[:, 0:3], sm_r.at[2])
    arrived(sm.at[0, 0:3, 0], sm_s.at[1])
    arrived(sm.at[:, 0:3], sm_s.at[2])

    peaks = jnp.max(sm[...].astype(F32).reshape(16, 16, 128), axis=0)[15:16]
    w_peak = [jnp.max(jnp.where(lane == g, peaks, 0.0)) for g in range(4)]
    w_inv = [1.0 / r for r in w_peak]

    def spread(xx, width, step):
        total = None
        for place in range(8):
            tile = sm[xx, place // 2, place % 2].astype(F32)
            if width > 128:
                tile = jnp.concatenate([tile, jnp.zeros((16, width - 128), F32)], axis=1)
            if place:
                tile = pltpu.roll(tile, place * step, 1)
            total = tile if total is None else total + tile
        return total

    vec[...] = spread(0, WIDE, 96)
    heads = []
    for xx in range(2):
        wide = spread(xx, 256, 32)
        for h in range(3):
            bup[xx : xx + 1, h * 256 : h * 256 + 256] = wide[6 + h : 7 + h, :]
        narrow = spread(xx, 128, 8)
        heads.append((narrow, pltpu.roll(narrow, 64, 1)))
    for j, first in enumerate((9, 12)):
        for xx in range(2):
            bqv[j : j + 1, xx * 128 : xx * 128 + 128] = (
                heads[xx][0][first : first + 1] + heads[xx][1][first + 1 : first + 2]
            )
        bqv[j : j + 1, 256:384] = heads[0][0][first + 2 : first + 3] + heads[1][1][first + 2 : first + 3]

    ag_diag(0, 2)
    ag_strip_z(2)
    ag_xy_send(2, 0)
    ag_strip_fwd(1)
    ag_diag(0, 3)
    ag_xy_send(1, 2)
    ag_xy_send(1, 3)
    ag_diag(1, 0)
    ag_diag(1, 1)
    ag_xy_send(2, 1)

    left = lax.broadcasted_iota(jnp.int32, (PIECE, 128), 1) < 64

    def squash_heads(zz, yy):
        place = zz * 2 + yy
        rows = pl.ds(mul8(place * PIECE, PIECE), PIECE)
        tiles = []
        for xx in range(2):
            v = wts[0, xx, zz, yy].astype(F32)
            inner = [w_peak[0] * jnp.tanh(v[:, t * 128 : t * 128 + 128] * w_inv[0]) for t in (0, 1, 2)]
            inner.append(w_peak[1] * jnp.tanh(v[:, 384:512] * w_inv[1]))
            mixed = jnp.where(left, w_peak[0], w_peak[1])
            mixed_inv = jnp.where(left, w_inv[0], w_inv[1])
            inner.append(w_peak[0] * jnp.tanh(v[:, 512:640] * w_inv[0]))
            inner.append(mixed * jnp.tanh(v[:, 640:768] * mixed_inv))
            tiles.append(inner)
        for t in range(3):
            for xx in range(2):
                wc[rows, t * HERE + xx * 128 : t * HERE + xx * 128 + 128] = tiles[xx][t].astype(BF)
        for xx in range(2):
            wo[rows, xx * 128 : xx * 128 + 128] = tiles[xx][3].astype(BF)
        for t, first, second in ((4, 0, 1), (5, 2, 3)):
            one, two = tiles[0][t], tiles[1][t]
            wc[rows, first * HERE + 256 : first * HERE + 384] = jnp.where(left, one, pltpu.roll(two, 64, 1)).astype(BF)
            other = jnp.where(left, pltpu.roll(one, 64, 1), two).astype(BF)
            if second == 1:
                wc[rows, HERE + 256 : HERE + 384] = other
            else:
                wo[rows, 256:384] = other

    loop(4, lambda zz: squash_heads(zz, y))
    ag_last(0)
    loop(4, lambda zz: squash_heads(zz, ny))
    ag_z_fwd(2, 2)
    ag_z_fwd(2, 3)

    def squash_piece(g, xx, zz, yy):
        v = wts[g, xx, zz, yy].astype(F32)
        wff[g - 1, xx, pl.ds(mul8((zz * 2 + yy) * PIECE, PIECE), PIECE), :] = (
            w_peak[g + 1] * jnp.tanh(v * w_inv[g + 1])
        ).astype(BF)

    def squash_ff(g, xx):
        loop(8, lambda place: squash_piece(g, xx, place // 2, place % 2))

    for j, held in enumerate((qs, ks, vs)):

        got = nn(xq[...], wc[:, j * HERE : (j + 1) * HERE])
        if j == 0:
            got = (got + bqv[0:1, :]) * 0.125
        elif j == 2:
            got = got + bqv[1:2, :]
        held[...] = got.astype(BF)
    ag_diag(1, 2)
    for p in range(3):
        cols = slice(p * 128, p * 128 + 128)
        kt[cols, :] = ks[:, cols].T
        vt[cols, :] = vs[:, cols].T

    half_of = lax.broadcasted_iota(jnp.int32, (1, 128), 1) // 64

    def attend(p):
        cols = pl.ds(mul8(p * 128, 128), 128)
        for e in range(2):
            feats = pl.ds(mul8(p * 128 + e * 64, 64), 64)
            q = qs[:, cols]
            q = jnp.where(half_of == e, q, jnp.zeros_like(q))
            s = nt(ks[:, cols], q) + bias[...]
            s = jnp.exp(s - jnp.max(s, axis=0, keepdims=True))
            s = (s * (1.0 / jnp.sum(s, axis=0, keepdims=True))).astype(BF)
            probs[p * 2 + e] = s
            ctxt[feats, :] = nn(vt[feats, :], s)

    ag_strip_fwd(2)
    attend(0)
    ag_diag(1, 3)
    ag_xy_send(2, 2)
    attend(1)
    ag_xy_send(2, 3)
    ag_diag(2, 0)
    attend(2)

    for p in range(3):
        cols = slice(p * 128, p * 128 + 128)
        bent = jnp.tanh(ctxt[cols, :].T * inv_of[1])
        cq[:, cols] = (range_of[1] * bent).astype(BF)
        slc[:, cols] = 1.0 - bent * bent
    tot[0] = jnp.zeros((16, WIDE), F32)
    most = jnp.max(jnp.max(jnp.abs(ctxt[...]), axis=0, keepdims=True), axis=1, keepdims=True)
    tot[0, 10:11, :] = jnp.broadcast_to(most, (1, WIDE))

    def out_part(start, held, cols=slice(0, WIDE)):
        held[:, cols] = nt(cq[pl.ds(start, OWN), :], wo[cols, :])

    for i in range(2):
        cols = slice(i * HERE, i * HERE + HERE)
        out_part(theirs, exa_s, cols)
        made = copy(exa_s.at[:, cols], exa_r.at[:, cols], ex_s.at[0], ex_r.at[0], to_c)
        made.start()
    out_part(mine, r1)
    ag_strip_got(1)
    ag_diag(2, 1)
    squash_ff(1, x)
    arrived(exa_r, ex_r.at[0])
    arrived(exa_s, ex_s.at[0])

    def sum_rows(v):
        return jnp.sum(v, axis=0, keepdims=True)

    def mean_of(v):
        return jnp.sum(v, axis=-1, keepdims=True) * (1.0 / WIDE)

    def first_norm(i):
        rows = pl.ds(mul8(i * 128, 128), 128)
        v = tok[pl.ds(mul8(mine + i * 128, 128), 128), :].astype(F32)
        v = v + (r1[rows, :] + exa_r[rows, :] + vec[0:1, :])
        r1[rows, :] = v
        center = v - mean_of(v)
        factor = lax.rsqrt(mean_of(center * center) + 1e-12)
        normed = center * factor
        n1[rows, :] = normed
        rstd1[rows, :] = factor
        h = normed * vec[2:3, :] + vec[3:4, :]
        tot[0, 11:12, :] = jnp.maximum(tot[0, 11:12, :], jnp.max(jnp.abs(h), axis=0, keepdims=True))
        bent = jnp.tanh(h * inv_of[2])
        sl1[rows, :] = 1.0 - bent * bent
        hq[pl.ds(mul8(mine + i * 128, 128), 128), :] = (range_of[2] * bent).astype(BF)

    def half_rows(start, i):
        return pl.ds(mul8(start + i * 128, 128), 128)

    for i in range(2):
        first_norm(i)
        own = hq.at[half_rows(mine, i)]
        copy(own, own, ex_s.at[1], ex_r.at[1], to_c).start()

    def share_rows(held, number):
        own = held.at[pl.ds(mine, OWN)]
        copy(own, own, ex_s.at[1], ex_r.at[number], to_c).start()

    def shared(held):
        arrived(held.at[pl.ds(mine, OWN)], ex_s.at[1])

    def got_rows(held, number):
        arrived(held.at[pl.ds(theirs, OWN)], ex_r.at[number])

    def turn_rows(held, out, start):
        out[:, pl.ds(start, OWN)] = held[pl.ds(start, OWN), :].T

    turn_rows(hq, hqt, mine)
    arrived(hq.at[pl.ds(theirs, OWN)], ex_r.at[1])
    turn_rows(hq, hqt, theirs)

    def expand(xx, between=None):
        wide = pl.ds(mul8(xx * WIDE, WIDE), WIDE)

        def body(i):
            rows = pl.ds(mul8(i * 256, 256), 256)
            u = nn(hq[rows, :], wff[0, xx]) + bup[pl.ds(xx, 1), :]
            cdf = 0.5 * (1.0 + lax.erf(u * 0.7071067811865476))
            a = u * cdf
            tot[0, 12:13, :] = jnp.maximum(tot[0, 12:13, :], jnp.max(jnp.abs(a), axis=0, keepdims=True))
            bent = jnp.tanh(a * inv_of[3])
            aq[rows, wide] = (range_of[3] * bent).astype(BF)
            pdf = 0.3989422804014327 * jnp.exp(-0.5 * u * u)
            fac[rows, wide] = ((1.0 - bent * bent) * (cdf + u * pdf)).astype(fac.dtype)

        body(0)
        if between is not None:
            between()
        body(1)

    expand(x)
    ag_diag(2, 2)
    ag_last(1)
    squash_ff(1, nx)
    expand(nx, functools.partial(ag_diag, 2, 3))
    ag_strip_got(2)

    def down_part(start, held, xx, first, cols=slice(0, WIDE)):
        got = nt(aq[pl.ds(start, OWN), pl.ds(mul8(xx * WIDE, WIDE), WIDE)], wff[1, xx, cols, :])
        held[:, cols] = got if first else held[:, cols] + got

    squash_ff(2, x)
    down_part(theirs, exb_s, x, True)
    down_part(mine, gr2, x, True)
    loop(4, lambda zz: squash_piece(2, nx, zz, y))
    for k in range(4):
        ag_last(2, k, 1)
        squash_piece(2, nx, zk[k], ny)
    for i in range(2):
        cols = slice(i * HERE, i * HERE + HERE)
        down_part(theirs, exb_s, nx, False, cols)
        low_s[:, cols] = exb_s[:, cols].astype(BF)
        copy(low_s.at[:, cols], low_r.at[:, cols], ex_s.at[0], ex_r.at[2], to_c).start()
    down_part(mine, gr2, nx, False)
    arrived(low_r, ex_r.at[2])
    arrived(low_s, ex_s.at[0])

    def second_norm(i):
        rows = pl.ds(mul8(i * 128, 128), 128)
        v = r1[rows, :] + (gr2[rows, :] + low_r[rows, :].astype(F32) + vec[1:2, :])
        center = v - mean_of(v)
        factor = lax.rsqrt(mean_of(center * center) + 1e-12)
        normed = center * factor
        o_layer[rows, :] = (normed * vec[4:5, :] + vec[5:6, :]).astype(BF)
        gy = grad_out[rows, :].astype(F32)
        tot[0, 4:5, :] += sum_rows(gy * normed)
        tot[0, 5:6, :] += sum_rows(gy)
        gn = gy * vec[4:5, :]
        back = factor * (gn - mean_of(gn) - normed * mean_of(gn * normed))
        gr2[rows, :] = back
        low = back.astype(BF)
        tot[0, 1:2, :] += sum_rows(low.astype(F32))
        gf[pl.ds(mul8(mine + i * 128, 128), 128), :] = low

    shared(hq)
    for i in range(2):
        second_norm(i)
        own = gf.at[half_rows(mine, i)]
        copy(own, own, ex_s.at[1], ex_r.at[3], to_c).start()
    leave(o_layer, r_layer)
    turn_rows(gf, rowt, mine)
    sent(link_s)

    far_rows = pl.ds(mul8((2 - z // 2 * 2) * 2 * PIECE, 4 * PIECE), 4 * PIECE)
    far_hidden = pl.ds(mul8(nx * WIDE, WIDE), WIDE)

    def far_part(start):
        return nn(rowt[far_rows, pl.ds(start, OWN)], aq[pl.ds(start, OWN), far_hidden])

    own_part = far_part(mine)
    exb_s[...] = own_part[0:OWN, :]
    exb_r[0 : HERE - OWN, :] = own_part[OWN:HERE, :]
    arrived(gf.at[pl.ds(theirs, OWN)], ex_r.at[3])
    turn_rows(gf, rowt, theirs)

    def rs_rows(g, part):
        strip, one, two = RS_CUTS[g]
        return pl.ds((0, strip, strip + one, strip)[part], (strip, one, two, one + two)[part])

    def rs_part(g, part):
        _, one, two = RS_CUTS[g]
        return pl.ds((0, 0, one, 0)[part], (0, one, two, one + two)[part])

    far_z, near_z = pl.ds(2 - z // 2 * 2, 2), pl.ds(z // 2 * 2, 2)

    def rs_first(g, planes):
        one, far = rs_part(g, 1), pl.ds(0, RS_CUTS[g][2])
        i = 0 if planes is far_z else 2
        send(link_s, g, 0, wts.at[g, nx, planes, ny, rs_rows(g, 1)], rdx.at[g, planes, one], rs_r.at[g, i], to_x)
        send(link_s, g, 1, wts.at[g, nx, planes, ny, rs_rows(g, 2)], rdy.at[g, planes, far], rs_r.at[g, i + 1], to_y)

    def rs_direct_x(g, planes, part):
        i = 4 if planes is far_z else 5
        src = wts.at[g, nx, planes, y, rs_rows(g, part)]
        send(link_s, g, 0, src, rxx.at[g, planes, rs_part(g, part)], rs_r.at[g, i], to_x)

    def rs_direct_y(g, planes, part):
        i = 4 if planes is far_z else 5
        src = wts.at[g, x, planes, ny, rs_rows(g, part)]
        send(link_s, g, 1, src, ryy.at[g, planes, rs_part(g, part)], rs_r.at[g, i], to_y)

    def rs_direct(g, near):
        rs_direct_x(g, far_z, 1)
        if near:
            rs_direct_x(g, near_z, 1)

    def rs_second(g, near):
        rs_direct_y(g, far_z, 2)
        if near:
            rs_direct_y(g, near_z, 2)

    def rs_third_x(g, near):
        one, here = rs_part(g, 1), rs_rows(g, 1)
        for planes, i in ((far_z, 0), (near_z, 2)):
            arrived(rdx.at[g, planes, one], rs_r.at[g, i])
            wts[g, x, planes, ny, here] = (
                wts[g, x, planes, ny, here].astype(F32) + rdx[g, planes, one].astype(F32)
            ).astype(BF)
            rs_direct_y(g, planes, 1)
        if not near:
            rs_direct_y(g, near_z, 2)

    def rs_third_y(g, near):
        here, far = rs_rows(g, 2), pl.ds(0, RS_CUTS[g][2])
        for planes, i in ((far_z, 1), (near_z, 3)):
            arrived(rdy.at[g, planes, far], rs_r.at[g, i])
            wts[g, nx, planes, y, here] = (
                wts[g, nx, planes, y, here].astype(F32) + rdy[g, planes, far].astype(F32)
            ).astype(BF)
            rs_direct_x(g, planes, 2)
        if not near:
            rs_direct_x(g, near_z, 1)

    def plane(g, zz):
        rest, here = rs_rows(g, 3), rs_part(g, 3)
        return wts[g, x, zz, y, rest].astype(F32) + rxx[g, zz, here].astype(F32) + ryy[g, zz, here].astype(F32)

    def rs_fourth(g):
        both, rest = rs_part(g, 3), rs_rows(g, 3)
        got_rows_of(4 * (PIECE - RS_CUTS[g][0]), rs_r.at[g, 4])
        for k in (3, 2):
            wts[g, x, zk[k], y, rest] = plane(g, zk[k]).astype(BF)
            send(link_s, g, 2, wts.at[g, x, zk[k], y, rest], rzf.at[g, k - 2, both], rf_r.at[g, k - 2], to_zk[1], 1)

    def rs_near(g):
        both, rest = rs_part(g, 3), rs_rows(g, 3)
        got_rows_of(4 * (PIECE - RS_CUTS[g][0]), rs_r.at[g, 5])
        wts[g, x, zk[1], y, rest] = plane(g, zk[1]).astype(BF)
        send(link_s, g, 2, wts.at[g, x, zk[1], y, rest], rz.at[g, 0, both], rs_r.at[g, 7], to_zk[1])

    def rs_fifth(g):
        both, rest = rs_part(g, 3), rs_rows(g, 3)
        for k in (3, 2):

            @pl.when(outer == 0)
            def _(k=k):
                arrived(rzf.at[g, k - 2, both], rf_r.at[g, k - 2])
                wts[g, x, zk[k], y, rest] = (
                    wts[g, x, zk[k], y, rest].astype(F32) + rzf[g, k - 2, both].astype(F32)
                ).astype(BF)

            send(link_s, g, 2, wts.at[g, x, zk[k], y, rest], rz.at[g, 1, both], rs_r.at[g, 7], to_zk[k], 0)

    def strips(held, g, place, i):
        here = pl.ds(0, RS_CUTS[g][0])
        return held.at[g, *place, (nx, x)[i] if g == 2 else slice(None), :, here]

    def strips_of(g, zz, i):
        here = pl.ds(0, RS_CUTS[g][0])
        return wts.at[g, (nx, x)[i] if g == 2 else slice(None), zz, :, here]

    def rs_strip_z(g, i):
        for k in (3, 2):
            send(link_s, g, 2, strips_of(g, zk[k], i), strips(rzf2, g, (k - 2,), i), rf_r.at[g, k], to_zk[1], 1)
        send(link_s, g, 2, strips_of(g, zk[1], i), strips(rz2, g, (0,), i), rs_r.at[g, 6], to_zk[1])

    def rs_strip_fwd(g):
        here = pl.ds(0, RS_CUTS[g][0])
        for k in (3, 2):

            @pl.when(outer == 0)
            def _(k=k):
                got_rows_of(4 * RS_CUTS[g][0], rf_r.at[g, k])
                wts[g, :, zk[k], :, here] = (
                    wts[g, :, zk[k], :, here].astype(F32) + rzf2[g, k - 2, :, :, here].astype(F32)
                ).astype(BF)

            whole = wts.at[g, :, zk[k], :, here]
            send(link_s, g, 2, whole, rz2.at[g, 1, :, :, here], rs_r.at[g, 6], to_zk[k], 0)

    def rs_strip_sum(g):
        here = pl.ds(0, RS_CUTS[g][0])
        got_rows_of(8 * RS_CUTS[g][0], rs_r.at[g, 6])
        wts[g, :, z, :, here] = (
            wts[g, :, z, :, here].astype(F32)
            + rz2[g, 0, :, :, here].astype(F32)
            + rz2[g, 1, :, :, here].astype(F32)
        ).astype(BF)

    def rs_strip_send(g):
        here = pl.ds(0, RS_CUTS[g][0])
        for i, (xx, yy, axis, device) in enumerate(((nx, ny, 0, to_xy), (nx, y, 0, to_x), (x, ny, 1, to_y))):
            send(link_s, g, axis, wts.at[g, xx, z, yy, here], rst.at[g, i, here], rs_r.at[g, 7], device)

    def rs_total(g):
        here, both = pl.ds(0, RS_CUTS[g][0]), rs_part(g, 3)
        got_rows_of(2 * PIECE + RS_CUTS[g][0], rs_r.at[g, 7])
        strip = wts[g, x, z, y, here].astype(F32)
        for i in range(3):
            strip = strip + rst[g, i, here].astype(F32)
        total = plane(g, z)
        for k in range(2):
            total = total + rz[g, k, both].astype(F32)
        return jnp.concatenate([strip, total], axis=0)

    def ff_grad_planes(g, turned, held, xx, planes, first):
        rows = pl.ds(mul8(first * 2 * PIECE, 4 * PIECE), 4 * PIECE)
        got = nn(turned[rows, :], held[:, pl.ds(mul8(xx * WIDE, WIDE), WIDE)])
        wts[g, xx, planes] = got.reshape(2, 2, PIECE, WIDE).astype(BF)

    def ff_grad(g, turned, held, xx):
        got = nn(turned[...], held[:, pl.ds(mul8(xx * WIDE, WIDE), WIDE)])
        wts[g, xx] = got.reshape(4, 2, PIECE, WIDE).astype(BF)

    other_part = far_part(theirs)
    own_part = jnp.concatenate([exb_s[...], exb_r[0 : HERE - OWN, :]], axis=0)
    wts[2, nx, far_z] = (own_part + other_part).reshape(2, 2, PIECE, WIDE).astype(BF)
    rs_first(2, far_z)
    ff_grad_planes(2, rowt, aq, nx, near_z, z // 2 * 2)
    rs_first(2, near_z)
    rs_direct(2, True)
    rs_strip_z(2, 0)
    ff_grad(2, rowt, aq, x)
    rs_second(2, True)
    rs_strip_z(2, 1)

    for xx in range(2):

        def hidden_grad(i, xx=xx):
            wide = slice(xx * WIDE, xx * WIDE + WIDE)
            rows = pl.ds(mul8(i * 256, 256), 256)
            got = (nn(gf[rows, :], wff[1, xx]) * fac[rows, wide].astype(F32)).astype(BF)
            gu[rows, wide] = got
            tot[0, 6 + xx : 7 + xx, :] += sum_rows(got.astype(F32))

        loop(2, hidden_grad)
    def up_part(start, held):
        held[...] = nt(gu[pl.ds(start, OWN), 0:WIDE], wff[0, 0]) + nt(
            gu[pl.ds(start, OWN), WIDE : 2 * WIDE], wff[0, 1]
        )

    up_part(theirs, exa_s)
    ex3 = copy(exa_s, exa_r, ex_s.at[0], ex_r.at[4], to_c)
    ex3.start()
    up_part(mine, r1)
    ff_grad(1, hqt, gu, nx)
    rs_third_x(2, True)
    rs_third_y(2, True)
    rs_first(1, far_z)
    rs_first(1, near_z)
    rs_direct(1, True)
    ff_grad(1, hqt, gu, x)
    rs_second(1, True)
    rs_strip_z(1, 0)
    ex3.wait()

    def first_back(i):
        rows = pl.ds(mul8(i * 64, 64), 64)
        normed = n1[rows, :]
        gh = (r1[rows, :] + exa_r[rows, :]) * sl1[rows, :]
        tot[0, 2:3, :] += sum_rows(gh * normed)
        tot[0, 3:4, :] += sum_rows(gh)
        gn = gh * vec[2:3, :]
        back = rstd1[rows, :] * (gn - mean_of(gn) - normed * mean_of(gn * normed)) + gr2[rows, :]
        gr2[rows, :] = back
        low = back.astype(BF)
        tot[0, 0:1, :] += sum_rows(low.astype(F32))
        gf[pl.ds(mul8(mine + i * 64, 64), 64), :] = low

    shared(gf)
    loop(4, first_back)
    share_rows(gf, 5)
    turn_rows(gf, rowt, mine)
    got_rows(gf, 5)
    turn_rows(gf, rowt, theirs)

    gwo[...] = nn(rowt[...], cq[...])
    gc[...] = (nn(gf[...], wo[...]) * slc[...]).astype(BF)
    for p in range(3):
        cols = slice(p * 128, p * 128 + 128)
        gct[cols, :] = gc[:, cols].T
        for e in range(2):
            feats = slice(p * 128 + e * 64, p * 128 + e * 64 + 64)
            dsum[p * 2 + e : p * 2 + e + 1, :] = sum_rows(gct[feats, :].astype(F32) * ctxt[feats, :])

    row_half = lax.broadcasted_iota(jnp.int32, (128, 1), 0) // 64

    def attend_back(p):
        cols = pl.ds(mul8(p * 128, 128), 128)
        grad_k = grad_v = None
        for e in range(2):
            feats = pl.ds(mul8(p * 128 + e * 64, 64), 64)
            g = gct[cols, :]
            g = jnp.where(row_half == e, g, jnp.zeros_like(g))
            dpr = nn(vs[:, cols], g)
            ds[...] = (probs[p * 2 + e].astype(F32) * (dpr - dsum[pl.ds(p * 2 + e, 1), :])).astype(BF)
            g = gc[:, cols]
            g = jnp.where(half_of == e, g, jnp.zeros_like(g))
            more_v = nn(probs[p * 2 + e], g)
            q = qs[:, cols]
            q = jnp.where(half_of == e, q, jnp.zeros_like(q))
            more_k = nn(ds[...], q)
            grad_v = more_v if e == 0 else grad_v + more_v
            grad_k = more_k if e == 0 else grad_k + more_k
            gqt[feats, :] = nn(kt[feats, :], ds[...])
        grads[:, pl.ds(mul8(HERE + p * 128, 128), 128)] = grad_k.astype(BF)
        grads[:, pl.ds(mul8(2 * HERE + p * 128, 128), 128)] = grad_v.astype(BF)
        grads[:, cols] = (gqt[cols, :].astype(BF).astype(F32) * 0.125).T.astype(BF)

    attend_back(0)
    attend_back(1)
    attend_back(2)
    rs_strip_fwd(2)
    rs_fourth(2)
    rs_near(2)
    for j, part in ((0, 0), (2, HERE)):
        tot[0, 8:9, part : part + HERE] = sum_rows(grads[:, j * HERE : (j + 1) * HERE].astype(F32))

    left_four = lax.broadcasted_iota(jnp.int32, (4 * PIECE, 128), 1) < 64

    def head_grad(i):
        rows = pl.ds(mul8(i * 4 * PIECE, 4 * PIECE), 4 * PIECE)
        gq, gk, gv = (nn(xqt[rows, :], grads[:, j * HERE : (j + 1) * HERE]) for j in range(3))
        parts = (gq, gk, gv, gwo[rows, :])

        def put(xx, t, v):
            wts[0, xx, pl.ds(i * 2, 2), :, :, t * 128 : t * 128 + 128] = v.reshape(2, 2, PIECE, 128).astype(BF)

        for xx in range(2):
            for t in range(4):
                put(xx, t, parts[t][:, xx * 128 : xx * 128 + 128])
        for t, first, second in ((4, gq, gk), (5, gv, gwo[rows, :])):
            one, two = first[:, 256:384], second[:, 256:384]
            put(0, t, jnp.where(left_four, one, pltpu.roll(two, 64, 1)))
            put(1, t, jnp.where(left_four, pltpu.roll(one, 64, 1), two))

    def most_x(i):
        v = jnp.abs(tok[pl.ds(mul8(i * 128, 128), 128), :].astype(F32))
        tot[0, 9:10, :] = jnp.maximum(tot[0, 9:10, :], jnp.max(v, axis=0, keepdims=True))

    loop(4, most_x)
    row_of = lax.broadcasted_iota(jnp.int32, (16, 1), 0)
    small = copy(tot.at[0], tot_c, tt_s.at[0], tt_r.at[0], to_c)
    small.start()
    loop(2, head_grad)
    small.wait()
    mixed = jnp.where(row_of < 6, tot[0] + tot_c[...], jnp.maximum(tot[0], tot_c[...]))
    tot[1] = jnp.where((row_of >= 6) & (row_of < 9), tot[0], mixed)
    small = copy(tot.at[1], tot_x, tt_s.at[0], tt_r.at[1], to_x)
    small.start()
    rs_first(0, far_z)
    rs_first(0, near_z)
    rs_direct(0, False)
    rs_second(0, False)
    rs_strip_z(0, 0)

    def token_part(start, held):
        held[...] = nt(grads[pl.ds(start, OWN), :], wc[...])

    token_part(theirs, exb_s)
    ex4 = copy(exb_s, exb_r, ex_s.at[0], ex_r.at[6], to_c)
    ex4.start()
    rs_third_x(1, True)
    rs_third_y(1, True)
    token_part(mine, r1)
    ex4.wait()

    def token_grad(i):
        rows = pl.ds(mul8(i * 64, 64), 64)
        v = tok[pl.ds(mul8(mine + i * 64, 64), 64), :].astype(F32)
        bent = jnp.tanh(v * inv_of[0])
        got = gr2[rows, :] + (r1[rows, :] + exb_r[rows, :]) * (1.0 - bent * bent)
        o_tok[pl.ds(mul8(mp * OWN + i * 64, 64), 64), :] = got.astype(BF)

    loop(4, token_grad)
    own = o_tok.at[pl.ds(mul8(mp * OWN, OWN), OWN)]
    keep("tok", copy(own, own, gx_s.at[1], gx_r.at[1], to_c))
    leave_rows(mp)
    rs_strip_fwd(1)
    small.wait()
    tot[2] = jnp.where(row_of < 9, tot[1] + tot_x[...], jnp.maximum(tot[1], tot_x[...]))
    small = copy(tot.at[2], tot_y, tt_s.at[0], tt_r.at[2], to_y)
    small.start()
    rs_third_x(0, False)
    rs_fifth(2)
    rs_third_y(0, False)
    keep("tok", copy(own, own, gx_s.at[0], gx_r.at[0], to_x))
    for g in (2, 1):
        rs_strip_sum(g)
        rs_strip_send(g)
    rs_strip_fwd(0)
    rs_fourth(1)
    small.wait()
    tot[3] = jnp.where(row_of < 9, tot[2] + tot_y[...], jnp.maximum(tot[2], tot_y[...]))

    def both(one, two):
        return jnp.where(row_of < 9, one + two, jnp.maximum(one, two))

    inward = copy(tot.at[3], tot_z.at[0], tt_s.at[0], tt_r.at[3], to_zk[1])
    across = copy(tot.at[4], tot_z.at[1], tt_s.at[0], tt_r.at[4], to_zk[2])
    outward = copy(tot.at[5], tot_z.at[2], tt_s.at[0], tt_r.at[5], to_zk[1])
    pl.when(outer == 1)(inward.start)
    rs_fourth(0)
    rs_near(1)
    rs_strip_sum(0)
    rs_strip_send(0)
    rs_fifth(1)

    @pl.when(outer == 0)
    def _():
        inward.wait_recv()
        tot[4] = both(tot[3], tot_z[0])
        across.start()

    rs_near(0)

    @pl.when(outer == 0)
    def _():
        across.wait()
        tot[5] = both(tot[4], tot_z[1])
        outward.start()

    rs_fifth(0)
    far = o_tok.at[pl.ds(mul8((nx * 2 + c) * OWN, OWN), OWN)]
    copy(far, far, gx_s.at[0], gx_r.at[0], to_x).wait_recv()
    keep("tok", copy(far, far, gx_s.at[2], gx_r.at[2], to_c))
    leave_rows(nx * 2 + c)

    o_down[...] = rs_total(2) * _slope(w_down[...], w_inv[3])
    leave(o_down, r_down)
    o_up[...] = rs_total(1) * _slope(w_up[...], w_inv[2])
    leave(o_up, r_up)

    @pl.when(outer == 0)
    def _():
        outward.wait_send()

    @pl.when(outer == 1)
    def _():
        inward.wait_send()
        outward.wait_recv()
        tot[5] = tot_z[2]

    done = tot[5]
    back = pltpu.roll(done, (8 - dp) * 96, 1)
    o_vec[...] = back[0:6, 0:96]
    ups = jnp.where(x == 0, done[6:7, :], done[7:8, :])
    for h in range(3):
        tile = jnp.broadcast_to(ups[:, h * 256 : h * 256 + 256], (8, 256))
        o_bup[h : h + 1, :] = pltpu.roll(tile, (8 - dp) * 32, 1)[0:1, 0:32]
    for j in range(2):
        row = jnp.broadcast_to(done[8:9, j * HERE : (j + 1) * HERE], (8, HERE))
        pair = jnp.where(x == 0, row[:, 0:128], row[:, 128:256])
        for h, tile, shift in ((0, pair, 0), (1, pair, 64), (2, row[:, 256:384], 64 * x)):
            o_bqv[h, j : j + 1, :] = pltpu.roll(tile, (256 - shift - dp * 8) % 128, 1)[0:1, 0:8]
    for i in range(4):
        most = jnp.max(done[9 + i : 10 + i, :], axis=1, keepdims=True)
        o_rng[i : i + 1, :] = jnp.broadcast_to(0.9 * range_of[i] + 0.1 * most, (1, 128))

    for here, there in ((o_vec, r_vec), (o_bup, r_bup), (o_bqv, r_bqv), (o_rng, r_rng)):
        leave(here, there)
    near = pl.ds(mul8((x * 2 + nc) * OWN, OWN), OWN)
    copy(o_tok.at[near], o_tok.at[near], gx_s.at[1], gx_r.at[1], to_c).wait_recv()
    leave_rows(x * 2 + nc)
    total = rs_total(0)
    for j in range(4):
        main = total[:, j * 128 : j * 128 + 128]
        pair = total[:, 512 + j // 2 * 128 : 640 + j // 2 * 128]
        if j % 2:
            pair = pltpu.roll(pair, 64, 1)
        whole = jnp.concatenate([main, pair], axis=1)[:, 0:192]
        if j < 3:
            o_qkv[j] = whole * _slope(w_qkv[j], w_inv[0])
        else:
            o_out[...] = whole.T * _slope(w_out[...], w_inv[1])
    leave(o_qkv, r_qkv)
    leave(o_out, r_out)
    far = pl.ds(mul8((nx * 2 + nc) * OWN, OWN), OWN)
    copy(o_tok.at[far], o_tok.at[far], gx_s.at[2], gx_r.at[2], to_c).wait_recv()
    leave_rows(nx * 2 + nc)
    sent(link_s)
    kept("tok")
    shared(gf)
    for made in leaving:
        made.wait()


def _slope(values, inverse):
    bent = jnp.tanh(values.astype(F32) * inverse)
    return 1.0 - bent * bent


def layer_on_chips(
    tokens, w_qkv, w_out, w_up, w_down, b_qv, b_up, vectors, ema_ranges, key_mask, long_rows, grad_out
):
    vmem = pltpu.VMEM
    rows = tokens.shape[0]
    half = rows // 2

    def buffer(*shape, dtype=BF):
        return vmem(shape, dtype)

    def f32(*shape):
        return vmem(shape, F32)

    sems = pltpu.SemaphoreType.DMA
    ins = (w_qkv, w_out, w_up, w_down.T, b_qv.transpose(1, 0, 2), b_up, vectors)
    mask = key_mask.reshape(rows // 128, 128)
    kinds = [
        jax.ShapeDtypeStruct(grad_out.shape, BF),
        jax.ShapeDtypeStruct(tokens.shape, BF),
        *(jax.ShapeDtypeStruct(v.shape, F32) for v in ins),
    ]
    scratch = [
        buffer(half, WIDE),
        *(vmem(v.shape, v.dtype) for v in (*ins, mask, grad_out)),
        *(vmem(v.shape, v.dtype) for v in kinds),
        pltpu.SMEM(ema_ranges.shape, F32),
        pltpu.SMEM(long_rows.shape, jnp.int32),
        f32(8, 128),
        buffer(3, 2, 4, 2, PIECE, WIDE),
        buffer(2, 2, WIDE, WIDE),
        buffer(WIDE, 3 * HERE),
        buffer(WIDE, HERE),
        buffer(3, 4, 48, WIDE),
        buffer(3, 4, 48, WIDE),
        buffer(3, 4, 80, WIDE),
        buffer(3, 4, 80, WIDE),
        buffer(3, 2, 80, WIDE),
        buffer(3, 2, 80, WIDE),
        buffer(3, 2, 2, 2, 32, WIDE),
        buffer(3, 2, 2, 2, 32, WIDE),
        buffer(3, 3, 32, WIDE),
        buffer(2, 4, 2, 16, 128),
        buffer(16, 128),
        f32(16, 128),
        f32(16, WIDE),
        f32(8, WIDE),
        f32(8, HERE),
        buffer(half, WIDE),
        buffer(WIDE, half),
        f32(half, half),
        buffer(half, HERE),
        buffer(half, HERE),
        buffer(half, HERE),
        buffer(HERE, half),
        buffer(HERE, half),
        buffer(6, half, half),
        buffer(half, half),
        f32(HERE, half),
        buffer(half, HERE),
        f32(half, HERE),
        f32(OWN, WIDE),
        f32(OWN, WIDE),
        f32(OWN, WIDE),
        f32(OWN, WIDE),
        buffer(OWN, WIDE),
        buffer(OWN, WIDE),
        buffer(half, WIDE),
        buffer(WIDE, half),
        f32(OWN, WIDE),
        f32(OWN, WIDE),
        f32(OWN, 1),
        f32(OWN, WIDE),
        buffer(half, 2 * WIDE),
        buffer(half, 2 * WIDE),
        buffer(half, 2 * WIDE),
        buffer(half, WIDE),
        buffer(WIDE, half),
        f32(OWN, WIDE),
        buffer(half, HERE),
        buffer(HERE, half),
        f32(8, half),
        buffer(half, 3 * HERE),
        f32(HERE, half),
        f32(WIDE, HERE),
        f32(6, 16, WIDE),
        f32(16, WIDE),
        f32(16, WIDE),
        f32(16, WIDE),
        f32(3, 16, WIDE),
        sems((3, 3)),
        sems((3, 3)),
        sems((2, 3)),
        sems((2, 2)),
        sems((3, 4)),
        sems((3, 4)),
        sems((6,)),
        sems((3, 8)),
        sems((3, 4)),
        sems((3,)),
        sems((3,)),
        sems((2,)),
        sems((7,)),
        sems((1,)),
        sems((6,)),
        sems((3,)),
        sems((3,)),
        sems((14,)),
    ]
    far = pl.BlockSpec(memory_space=pltpu.HBM)
    outs = pl.pallas_call(
        layer_kernel,
        out_shape=[*kinds, jax.ShapeDtypeStruct((8, 128), F32)],
        in_specs=[far] * 12,
        out_specs=[far] * 10,
        scratch_shapes=scratch,
        compiler_params=pltpu.CompilerParams(
            collective_id=0, has_side_effects=True, vmem_limit_bytes=VMEM_LIMIT
        ),
        name="encoder_layer",
    )(tokens, *ins, ema_ranges, mask, long_rows, grad_out)
    outs = finish(outs, ema_ranges)
    return (*outs[:5], outs[5].T, outs[6].transpose(1, 0, 2), *outs[7:])


def finish_kernel(*refs):
    ins, outs, held, wide, sem = refs[:10], refs[10:20], refs[20:30], refs[30], refs[31]
    step = OWN // 2
    parts = [pl.ds(i * step, step) for i in range(ins[1].shape[0] // step)]
    arriving = [pltpu.make_async_copy(ins[1].at[p], held[1].at[p], sem.at[10 + i]) for i, p in enumerate(parts)]
    moved = [i for i in range(10) if i != 1]
    arriving += [pltpu.make_async_copy(ins[i], held[i], sem.at[i]) for i in moved]
    leaving = [pltpu.make_async_copy(wide.at[p], outs[1].at[p], sem.at[10 + i]) for i, p in enumerate(parts)]
    leaving += [pltpu.make_async_copy(held[i], outs[i], sem.at[i]) for i in moved[:-1]]
    for made in arriving:
        made.start()
    for i, (here, there) in enumerate(zip(arriving, leaving)):
        here.wait()
        if i < len(parts):
            wide[parts[i], :] = held[1][parts[i], :].astype(F32)
        there.start()
    arriving[-1].wait()
    for i in range(4):
        outs[9][i] = held[9][i, 0]
    for made in leaving:
        made.wait()


def finish(held, ranges):
    shape = jax.ShapeDtypeStruct
    far = pl.BlockSpec(memory_space=pltpu.HBM)
    return pl.pallas_call(
        finish_kernel,
        out_shape=[shape(v.shape, F32 if i == 1 else v.dtype) for i, v in enumerate(held[:9])]
        + [shape(ranges.shape, F32)],
        in_specs=[far] * 10,
        out_specs=[far] * 9 + [pl.BlockSpec(memory_space=pltpu.SMEM)],
        scratch_shapes=[pltpu.VMEM(v.shape, v.dtype) for v in held]
        + [pltpu.VMEM(held[1].shape, F32), pltpu.SemaphoreType.DMA((10 + held[1].shape[0] * 2 // OWN,))],
        compiler_params=pltpu.CompilerParams(vmem_limit_bytes=VMEM_LIMIT),
        name="write_results",
    )(*held)


VMEM_LIMIT = 64 * 1024 * 1024


def solution(mesh):
    placed = (
        P("dp", None),
        P(None, "dp", "mp"),
        P("mp", "dp"),
        P("dp", "mp"),
        P("mp", "dp"),
        P(None, "mp", "dp"),
        P("mp", "dp"),
        P(None, "dp"),
        P(),
        P("dp"),
        P("dp"),
        P(("dp", "mp"), None),
    )
    on_chips = dict(mesh.shape) == {"dp": 8, "mp": 4}
    return jax.shard_map(
        layer_on_chips if on_chips else per_device,
        mesh=mesh,
        in_specs=placed,
        out_specs=(
            P(("dp", "mp"), None),
            P("dp", None),
            P(None, "dp", "mp"),
            P("mp", "dp"),
            P("dp", "mp"),
            P("mp", "dp"),
            P(None, "mp", "dp"),
            P("mp", "dp"),
            P(None, "dp"),
            P(),
        ),
        check_vma=False,
    )
```
